32 devices in a mesh: dp: 16 (over z, y, x), fsdp: 2 (over core).
Axes of the slice: x: 2, y: 2, z: 4, core: 2. Of those that a mesh axis runs over, the one named last changes fastest.
Arguments:
- prompt_states: bfloat16 [32, 1024, 1024], P('dp', 'fsdp'), may hold values from -6 to 6
- branch_states: bfloat16 [32, 2, 128, 1024], P('dp', 'fsdp'), may hold values from -6 to 6
- encoder_states: bfloat16 [32, 256, 1024], P('dp', 'fsdp'), may hold values from -6 to 6
- branch_start: int32 [32, 2], P('dp', 'fsdp'), may hold values from 512 to 1024, as said below
- bucket_table: int32 [1152], replicated, may hold values from 0 to 31, as said below
- prompt_cotangent: bfloat16 [32, 1024, 1024], P('dp', 'fsdp'), may hold values from -6 to 6
- branch_cotangent: bfloat16 [32, 2, 128, 1024], P('dp', 'fsdp'), may hold values from -6 to 6
- projections: float32 [6, 1024, 1024], P(None, ('dp', 'fsdp')), may hold values from -0.1875 to 0.1875
- projections_first: float32 [6, 1024, 1024], P(None, ('dp', 'fsdp')), may hold values from -0.00015258789 to 0.00015258789
- projections_second: float32 [6, 1024, 1024], P(None, ('dp', 'fsdp')), may hold values from 5.868765e-11 to 2.347506e-10
- combiners: float32 [2, 1024, 1024], P(None, ('dp', 'fsdp')), may hold values from -1 to 1
- combiners_first: float32 [2, 1024, 1024], P(None, ('dp', 'fsdp')), may hold values from -7.6293945e-05 to 7.6293945e-05
- combiners_second: float32 [2, 1024, 1024], P(None, ('dp', 'fsdp')), may hold values from 1.173753e-11 to 4.695012e-11
- expansion: float32 [2, 1024, 2816], P(None, ('dp', 'fsdp')), may hold values from -0.1875 to 0.1875
- expansion_first: float32 [2, 1024, 2816], P(None, ('dp', 'fsdp')), may hold values from -0.00015258789 to 0.00015258789
- expansion_second: float32 [2, 1024, 2816], P(None, ('dp', 'fsdp')), may hold values from 5.868765e-11 to 2.347506e-10
- contraction: float32 [2816, 1024], P(('dp', 'fsdp')), may hold values from -0.109375 to 0.109375
- contraction_first: float32 [2816, 1024], P(('dp', 'fsdp')), may hold values from -0.00015258789 to 0.00015258789
- contraction_second: float32 [2816, 1024], P(('dp', 'fsdp')), may hold values from 5.868765e-11 to 2.347506e-10
- norm_gains: float32 [3, 1024], replicated
- gains_first: float32 [3, 1024], replicated, may hold values from -0.00061035156 to 0.00061035156
- gains_second: float32 [3, 1024], replicated, may hold values from 9.390024e-10 to 3.7560097e-09
- position_bias: float32 [32, 16], replicated, may hold values from -4 to 4
- bias_first: float32 [32, 16], replicated, may hold values from -0.0004272461 to 0.0004272461
- bias_second: float32 [32, 16], replicated, may hold values from 2.9343825e-10 to 1.173753e-09
Outputs:
- prompt_output: bfloat16 [32, 1024, 1024], P('dp', 'fsdp')
- branch_output: bfloat16 [32, 2, 128, 1024], P('dp', 'fsdp')
- prompt_grad: float32 [32, 1024, 1024], P('dp', 'fsdp')
- branch_grad: float32 [32, 2, 128, 1024], P('dp', 'fsdp')
- encoder_grad: float32 [32, 256, 1024], P('dp', 'fsdp')
- grad_norm: float32 [], replicated
- projections_new: float32 [6, 1024, 1024], P(None, ('dp', 'fsdp'))
- projections_first_new: float32 [6, 1024, 1024], P(None, ('dp', 'fsdp'))
- projections_second_new: float32 [6, 1024, 1024], P(None, ('dp', 'fsdp'))
- combiners_new: float32 [2, 1024, 1024], P(None, ('dp', 'fsdp'))
- combiners_first_new: float32 [2, 1024, 1024], P(None, ('dp', 'fsdp'))
- combiners_second_new: float32 [2, 1024, 1024], P(None, ('dp', 'fsdp'))
- expansion_new: float32 [2, 1024, 2816], P(None, ('dp', 'fsdp'))
- expansion_first_new: float32 [2, 1024, 2816], P(None, ('dp', 'fsdp'))
- expansion_second_new: float32 [2, 1024, 2816], P(None, ('dp', 'fsdp'))
- contraction_new: float32 [2816, 1024], P(('dp', 'fsdp'))
- contraction_first_new: float32 [2816, 1024], P(('dp', 'fsdp'))
- contraction_second_new: float32 [2816, 1024], P(('dp', 'fsdp'))
- gains_new: float32 [3, 1024], replicated
- gains_first_new: float32 [3, 1024], replicated
- gains_second_new: float32 [3, 1024], replicated
- bias_new: float32 [32, 16], replicated
- bias_first_new: float32 [32, 16], replicated
- bias_second_new: float32 [32, 16], replicated
- projections_copy: bfloat16 [6, 1024, 1024], P(None, ('dp', 'fsdp'))
- combiners_copy: bfloat16 [2, 1024, 1024], P(None, ('dp', 'fsdp'))
- expansion_copy: bfloat16 [2, 1024, 2816], P(None, ('dp', 'fsdp'))
- contraction_copy: bfloat16 [2816, 1024], P(('dp', 'fsdp'))
The draws below stay inside these ranges and needn't reach their ends.
Inputs may be any that keep to these rules, and one draw needn't show every extreme that they name: `bucket_table`: nondecreasing in the distance, 0 at distance 0 and 31 at the largest distance. `branch_start`: in every group one branch continues the whole prompt.
All inputs are finite; a program needn't handle non-finite values.
Results may differ from the reference program's by a relative error of at most 0.022.
The reference program's roundings to bfloat16 on the way count: a program that leaves them out, or rounds other values in their place, can miss the bound.
Values may be sent and summed in bfloat16 or wider, within the bound.
No kernel may reach another device: no remote copies, remote signals or barrier semaphores. Data moves between devices by JAX's collectives and lax.ppermute only.
A program may use at most 576 MiB of HBM per device.

```python
import math
import jax
import jax.numpy as jnp
from jax import lax

D = 1024
FF = 2816
HEADS = 16
HD = 64
BUCKETS = 32
PROMPT = 1024
ENC = 256
CONT_LEN = 128
STEP = 10
GROUPS = 32
CONTS = 2


def draw_norm_gains(key, part):
    key = jax.random.fold_in(key, 11)
    place = jnp.arange(D, dtype=jnp.float32) / D
    base = 0.6 * 3.0 ** place
    jitter = jax.random.uniform(key, (3, D), minval=0.8, maxval=1.25)
    return (base[None, :] * jitter).astype(jnp.float32)


def draw_bucket_table(key, part):
    key = jax.random.fold_in(key, 12)
    span = PROMPT + CONT_LEN
    order = jax.random.permutation(key, span - 1) + 1
    marks = order[:BUCKETS - 1]
    place = jnp.arange(span, dtype=jnp.int32)
    return jnp.sum((place[:, None] >= marks[None, :]).astype(jnp.int32), axis=1).astype(jnp.int32)


def draw_branch_start(key, part):
    key = jax.random.fold_in(key, 13)
    first_key, second_key = jax.random.split(key)
    starts = jax.random.randint(first_key, (GROUPS, CONTS), PROMPT // 2, PROMPT + 1)
    chosen = jax.random.randint(second_key, (GROUPS,), 0, CONTS)
    whole = jnp.arange(CONTS, dtype=jnp.int32)[None, :] == chosen[:, None]
    return jnp.where(whole, PROMPT, starts).astype(jnp.int32)


def steps_of(own_key, dims, shards, least, top_value):
    def one(position, parts):
        steps = jax.random.uniform(jax.random.fold_in(jax.random.fold_in(own_key, 6), position), (parts,), jnp.float32, least / len(shards), top_value / len(shards))
        return jnp.repeat(jnp.exp(steps), dims[position] // parts).reshape((-1,) + (1,) * (len(dims) - position - 1))

    level = one(*shards[0])
    for cut in shards[1:]:
        level = level * one(*cut)
    return level


def normal_values(key, shape, deviation, limit, pieces=(), kind=jnp.bfloat16):
    drawn = jax.random.normal(key, shape, jnp.float32) * deviation
    if len(pieces) > 0:
        drawn = steps_of(key, shape, pieces, -0.22, 0.18) * drawn
    return jnp.clip(drawn, min=-limit, max=limit).astype(kind)


def setup_inputs(seed: int = 0) -> dict:
    keys = jax.random.split(jax.random.key(seed), 26)
    prompt_states = normal_values(keys[0], (GROUPS, PROMPT, D), 1.0, 6.0, ((0, 16), (1, 2)))
    branch_states = normal_values(keys[1], (GROUPS, CONTS, CONT_LEN, D), 1.0, 6.0, ((0, 16), (1, 2)))
    encoder_states = normal_values(keys[2], (GROUPS, ENC, D), 1.0, 6.0, ((0, 16), (1, 2)))
    branch_start = draw_branch_start(jax.random.fold_in(keys[25], 71), 0)
    bucket_table = draw_bucket_table(jax.random.fold_in(keys[25], 71), 0)
    prompt_cotangent = normal_values(keys[5], (GROUPS, PROMPT, D), 1.0, 6.0, ((0, 16), (1, 2)))
    branch_cotangent = normal_values(keys[6], (GROUPS, CONTS, CONT_LEN, D), 1.0, 6.0, ((0, 16), (1, 2)))
    projections = normal_values(keys[7], (6, D, D), D ** -0.5, 0.1875, ((1, 32),), jnp.float32)
    projections_first = normal_values(keys[8], (6, D, D), (0.111 * (8 * D * D + 3 * D * FF) ** -0.5), 0.00015258789, ((1, 32),), jnp.float32)
    projections_second = jnp.clip(jnp.exp(math.log(2.3475060784150514e-10) - 1.3862944 * jax.random.uniform(keys[9], (6, D, D), jnp.float32) ** steps_of(keys[9], (6, D, D), ((1, 32),), -0.2, 0.2)), 5.868765196037629e-11, 2.3475060784150514e-10)
    combiners = normal_values(keys[10], (2, D, D), (D // 32) ** -0.5, 1.0, ((1, 32),), jnp.float32)
    combiners_first = normal_values(keys[11], (2, D, D), (0.05 * (8 * D * D + 3 * D * FF) ** -0.5), 7.62939453125e-05, ((1, 32),), jnp.float32)
    combiners_second = jnp.clip(jnp.exp(math.log(4.695012087441164e-11) - 1.3862944 * jax.random.uniform(keys[12], (2, D, D), jnp.float32) ** steps_of(keys[12], (2, D, D), ((1, 32),), -0.2, 0.2)), 1.173753021860291e-11, 4.695012087441164e-11)
    expansion = normal_values(keys[13], (2, D, FF), D ** -0.5, 0.1875, ((1, 32),), jnp.float32)
    expansion_first = normal_values(keys[14], (2, D, FF), (0.111 * (8 * D * D + 3 * D * FF) ** -0.5), 0.00015258789, ((1, 32),), jnp.float32)
    expansion_second = jnp.clip(jnp.exp(math.log(2.3475060784150514e-10) - 1.3862944 * jax.random.uniform(keys[15], (2, D, FF), jnp.float32) ** steps_of(keys[15], (2, D, FF), ((1, 32),), -0.2, 0.2)), 5.868765196037629e-11, 2.3475060784150514e-10)
    contraction = normal_values(keys[16], (FF, D), FF ** -0.5, 0.109375, ((0, 32),), jnp.float32)
    contraction_first = normal_values(keys[17], (FF, D), (0.111 * (8 * D * D + 3 * D * FF) ** -0.5), 0.00015258789, ((0, 32),), jnp.float32)
    contraction_second = jnp.clip(jnp.exp(math.log(2.3475060784150514e-10) - 1.3862944 * jax.random.uniform(keys[18], (FF, D), jnp.float32) ** steps_of(keys[18], (FF, D), ((0, 32),), -0.2, 0.2)), 5.868765196037629e-11, 2.3475060784150514e-10)
    norm_gains = draw_norm_gains(jax.random.fold_in(keys[25], 71), 0)
    gains_first = normal_values(keys[20], (3, D), (0.444 * (8 * D * D + 3 * D * FF) ** -0.5), 0.00061035156, (), jnp.float32)
    gains_second = jnp.clip(jnp.exp(jax.random.uniform(keys[21], (3, D), jnp.float32, math.log(9.390024313660206e-10), math.log(3.756009725464082e-09))), 9.390024313660206e-10, 3.756009725464082e-09)
    position_bias = normal_values(keys[22], (BUCKETS, HEADS), 1.0, 4.0, (), jnp.float32)
    bias_first = normal_values(keys[23], (BUCKETS, HEADS), (0.3 * (8 * D * D + 3 * D * FF) ** -0.5), 0.0004272461, (), jnp.float32)
    bias_second = jnp.clip(jnp.exp(jax.random.uniform(keys[24], (BUCKETS, HEADS), jnp.float32, math.log(2.934382459240936e-10), math.log(1.1737529836963745e-09))), 2.934382459240936e-10, 1.1737529836963745e-09)
    return {"prompt_states": prompt_states, "branch_states": branch_states, "encoder_states": encoder_states, "branch_start": branch_start, "bucket_table": bucket_table, "prompt_cotangent": prompt_cotangent, "branch_cotangent": branch_cotangent, "projections": projections, "projections_first": projections_first, "projections_second": projections_second, "combiners": combiners, "combiners_first": combiners_first, "combiners_second": combiners_second, "expansion": expansion, "expansion_first": expansion_first, "expansion_second": expansion_second, "contraction": contraction, "contraction_first": contraction_first, "contraction_second": contraction_second, "norm_gains": norm_gains, "gains_first": gains_first, "gains_second": gains_second, "position_bias": position_bias, "bias_first": bias_first, "bias_second": bias_second}


EPS = 1e-06
CLIP = 1.0
BETA_ONE = 0.9
BETA_TWO = 0.999
ADAM_EPS = 1e-08
DECAY = 0.01
RATES = (0.05, 0.3, 0.05, 0.03, 1.0, 1.0)
MASKED = -1e+30

@jax.custom_vjp
def low(v):
    return lax.optimization_barrier(v.astype(jnp.bfloat16)).astype(jnp.float32)

@jax.custom_vjp
def low_back(v):
    return v

def low_keep(v):
    return (low(v), None)

def low_pass(kept, grad):
    return (grad,)

def back_keep(v):
    return (v, None)

def back_low(kept, grad):
    return (low(grad),)
low.defvjp(low_keep, low_pass)
low_back.defvjp(back_keep, back_low)

def both_ways(value):
    return low_back(low(value))

def matmul(left, right):
    return jnp.matmul(left, right, precision=lax.Precision.HIGHEST)

def norm_rows(stream, gain):
    return stream * lax.rsqrt(lax.optimization_barrier(jnp.mean(stream * stream, axis=-1, keepdims=True)) + EPS) * gain

def gelu_mix(gate, up_value):
    inner = 0.7978845608028654 * (gate + 0.044715 * gate * gate * gate)
    return 0.5 * gate * (1.0 + jnp.tanh(inner)) * up_value

def attend(queries, key_rows, value_rows, bias, pair_mask):
    count = queries.shape[0]
    qh = queries.reshape(count, HEADS, HD)
    kh = key_rows.reshape(-1, HEADS, HD)
    vh = value_rows.reshape(-1, HEADS, HD)
    product = low_back(jnp.einsum('rhd,khd->hrk', qh, kh, precision=lax.Precision.HIGHEST))
    scores = jnp.where(pair_mask[None], product * HD ** (-0.5) + bias, MASKED)
    row_max = lax.optimization_barrier(jnp.max(scores, axis=-1, keepdims=True))
    expo = jnp.exp(scores - row_max)
    probs = expo / lax.optimization_barrier(jnp.sum(expo, axis=-1, keepdims=True))
    mixed = jnp.einsum('hrk,khd->rhd', low(probs), vh, precision=lax.Precision.HIGHEST)
    return both_ways(mixed.reshape(count, D))

def layer(params, prompt, branches, encoder, starts, bucket_table):
    projections, combiners, expansion, contraction, norm_gains, position_bias = params
    w_proj = low(projections)
    w_comb = low(combiners)
    w_exp = low(expansion)
    w_con = low(contraction)
    dist_count = bucket_table.shape[0]
    per_distance = jnp.take(position_bias, bucket_table, axis=0).T
    stream = jnp.concatenate([prompt, branches.reshape(-1, D)], axis=0)
    input_one = low(norm_rows(stream, norm_gains[0]))
    queries = both_ways(matmul(input_one, w_proj[0]))
    key_rows = both_ways(matmul(input_one, w_proj[1]))
    value_rows = both_ways(matmul(input_one, w_proj[2]))
    prompt_pos = jnp.arange(PROMPT, dtype=jnp.int32)
    distance = prompt_pos[:, None] - prompt_pos[None, :]
    bias = jnp.take(per_distance, jnp.maximum(distance, 0), axis=1)
    mixed_prompt = jax.checkpoint(attend)(queries[:PROMPT], key_rows[:PROMPT], value_rows[:PROMPT], bias, distance >= 0)

    def one_branch(item):
        q_rows, k_rows, v_rows, start = item
        steps_in = jnp.arange(CONT_LEN, dtype=jnp.int32)
        query_pos = start + steps_in
        key_pos = jnp.concatenate([prompt_pos, query_pos])
        gap = query_pos[:, None] - key_pos[None, :]
        in_prompt = jnp.arange(PROMPT + CONT_LEN, dtype=jnp.int32) < PROMPT
        pair_mask = jnp.where(in_prompt[None, :], key_pos[None, :] < start, gap >= 0)
        branch_bias = jnp.take(per_distance, jnp.clip(gap, 0, dist_count - 1), axis=1)
        return attend(q_rows, jnp.concatenate([key_rows[:PROMPT], k_rows]), jnp.concatenate([value_rows[:PROMPT], v_rows]), branch_bias, pair_mask)
    shaped = (CONTS, CONT_LEN, D)
    mixed_branch = lax.map(jax.checkpoint(one_branch), (queries[PROMPT:].reshape(shaped), key_rows[PROMPT:].reshape(shaped), value_rows[PROMPT:].reshape(shaped), starts))
    mixed = jnp.concatenate([mixed_prompt, mixed_branch.reshape(-1, D)], axis=0)
    after_one = stream + low_back(matmul(mixed, w_comb[0]))
    input_two = low(norm_rows(after_one, norm_gains[1]))
    query_two = both_ways(matmul(input_two, w_proj[3]))
    cross_keys = both_ways(matmul(encoder, w_proj[4]))
    cross_values = both_ways(matmul(encoder, w_proj[5]))
    zero_bias = jnp.zeros((HEADS, 1, 1), jnp.float32)
    open_mask = jnp.ones((1, 1), bool)
    mixed_two = jax.checkpoint(attend)(query_two, cross_keys, cross_values, zero_bias, open_mask)
    after_two = after_one + low_back(matmul(mixed_two, w_comb[1]))
    input_three = low(norm_rows(after_two, norm_gains[2]))
    gate = low_back(matmul(input_three, w_exp[0]))
    up_value = low_back(matmul(input_three, w_exp[1]))
    hidden = low(gelu_mix(gate, up_value))
    return after_two + low_back(matmul(hidden, w_con))

def adam(weight, first, second, grad, rate):
    first_new = BETA_ONE * first + (1.0 - BETA_ONE) * grad
    second_new = BETA_TWO * second + (1.0 - BETA_TWO) * grad * grad
    mean_hat = first_new / (1.0 - BETA_ONE ** STEP)
    square_hat = second_new / (1.0 - BETA_TWO ** STEP)
    updated = weight - rate * (mean_hat / (jnp.sqrt(square_hat) + ADAM_EPS) + DECAY * weight)
    return (updated, first_new, second_new)

def reference(prompt_states, branch_states, encoder_states, branch_start, bucket_table, prompt_cotangent, branch_cotangent, projections, projections_first, projections_second, combiners, combiners_first, combiners_second, expansion, expansion_first, expansion_second, contraction, contraction_first, contraction_second, norm_gains, gains_first, gains_second, position_bias, bias_first, bias_second):
    params = (projections, combiners, expansion, contraction, norm_gains, position_bias)

    def group_step(running, item):
        prompt, branches, encoder, starts, prompt_cot, branch_cot = item

        def forward(weights, prompt_in, branch_in, encoder_in):
            result = layer(weights, prompt_in, branch_in, encoder_in, starts, bucket_table)
            return (result[:PROMPT], result[PROMPT:].reshape(branch_in.shape))
        outputs, pull = jax.vjp(forward, params, prompt.astype(jnp.float32), branches.astype(jnp.float32), encoder.astype(jnp.float32))
        grads, prompt_grad, branch_grad, encoder_grad = pull((prompt_cot.astype(jnp.float32), branch_cot.astype(jnp.float32)))
        running = jax.tree.map(jnp.add, running, grads)
        return (running, (outputs[0].astype(jnp.bfloat16), outputs[1].astype(jnp.bfloat16), prompt_grad, branch_grad, encoder_grad))
    zeros = jax.tree.map(jnp.zeros_like, params)
    grads, results = lax.scan(group_step, zeros, (prompt_states, branch_states, encoder_states, branch_start, prompt_cotangent, branch_cotangent))
    grad_norm = jnp.sqrt(sum((jnp.sum(grad * grad) for grad in grads)))
    factor = jnp.minimum(1.0, CLIP / (grad_norm + 1e-06))
    firsts = (projections_first, combiners_first, expansion_first, contraction_first, gains_first, bias_first)
    seconds = (projections_second, combiners_second, expansion_second, contraction_second, gains_second, bias_second)
    states = [adam(params[index], firsts[index], seconds[index], grads[index] * factor, RATES[index]) for index in range(6)]
    return (results[0], results[1], results[2], results[3], results[4], grad_norm, states[0][0], states[0][1], states[0][2], states[1][0], states[1][1], states[1][2], states[2][0], states[2][1], states[2][2], states[3][0], states[3][1], states[3][2], states[4][0], states[4][1], states[4][2], states[5][0], states[5][1], states[5][2], states[0][0].astype(jnp.bfloat16), states[1][0].astype(jnp.bfloat16), states[2][0].astype(jnp.bfloat16), states[3][0].astype(jnp.bfloat16))
```

```python
import functools

import jax
import jax.numpy as jnp
from jax import lax
from jax.experimental import pallas as pl
from jax.experimental.pallas import tpu as pltpu
from jax.sharding import PartitionSpec as P

D = 1024
FF = 2816
HEADS = 16
HD = 64
BUCKETS = 32
PROMPT = 1024
STEP = 10


EPS = 1e-06
CLIP = 1.0
BETA_ONE = 0.9
BETA_TWO = 0.999
ADAM_EPS = 1e-08
DECAY = 0.01
RATES = (0.05, 0.3, 0.05, 0.03, 1.0, 1.0)
MASKED = -1e30


def rms_forward(stream, gain):
    scale = lax.rsqrt(jnp.mean(stream * stream, axis=-1, keepdims=True) + EPS)
    return (stream * scale * gain, scale)


def rms_backward(stream, scale, gain, upstream):
    weighted = upstream * gain
    grad_in = scale * weighted - stream * scale**3 * jnp.mean(
        weighted * stream, axis=-1, keepdims=True
    )
    return (grad_in, jnp.sum(upstream * stream * scale, axis=0))


def gelu_mix(gate, up_value):
    inner = 0.7978845608028654 * (gate + 0.044715 * gate * gate * gate)
    return 0.5 * gate * (1.0 + jnp.tanh(inner)) * up_value


def raw_scores(queries, key_rows):
    qh = queries.reshape(queries.shape[0], HEADS, HD)
    kh = key_rows.reshape(key_rows.shape[0], HEADS, HD)
    return jnp.einsum("rhd,khd->hrk", qh, kh, preferred_element_type=jnp.float32) * HD ** (-0.5)


def softmax_forward(scores, value_rows):
    row_max = jnp.max(scores, axis=-1, keepdims=True)
    expo = jnp.exp(scores - row_max)
    total = jnp.sum(expo, axis=-1, keepdims=True)
    probs = (expo / total).astype(jnp.bfloat16)
    vh = value_rows.reshape(value_rows.shape[0], HEADS, HD)
    mixed = jnp.einsum("hrk,khd->rhd", probs, vh, preferred_element_type=jnp.float32)
    return (mixed.reshape(mixed.shape[0], D).astype(jnp.bfloat16), row_max + jnp.log(total))


def softmax_backward(scores, logsum, queries, key_rows, value_rows, grad_mixed):
    probs = jnp.exp(scores - logsum)
    grad_heads = grad_mixed.reshape(grad_mixed.shape[0], HEADS, HD)
    vh = value_rows.reshape(value_rows.shape[0], HEADS, HD)
    kh = key_rows.reshape(key_rows.shape[0], HEADS, HD)
    qh = queries.reshape(queries.shape[0], HEADS, HD)
    grad_values = jnp.einsum(
        "hrk,rhd->khd", probs.astype(jnp.bfloat16), grad_heads, preferred_element_type=jnp.float32
    )
    grad_probs = jnp.einsum("rhd,khd->hrk", grad_heads, vh, preferred_element_type=jnp.float32)
    grad_scores = probs * (grad_probs - jnp.sum(probs * grad_probs, axis=-1, keepdims=True))
    scaled = (grad_scores * HD ** (-0.5)).astype(jnp.bfloat16)
    grad_queries = jnp.einsum("hrk,khd->rhd", scaled, kh, preferred_element_type=jnp.float32)
    grad_keys = jnp.einsum("hrk,rhd->khd", scaled, qh, preferred_element_type=jnp.float32)
    return (
        grad_queries.reshape(-1, D),
        grad_keys.reshape(-1, D),
        grad_values.reshape(-1, D),
        grad_scores,
    )


def hankel_bias(per_distance, shift, rows, keys):
    heads = per_distance.shape[0]
    front = jnp.broadcast_to(per_distance[:, :1], (heads, keys - 1))
    padded = jnp.concatenate([front, per_distance], axis=1)
    width = rows + keys - 1
    window = lax.dynamic_slice_in_dim(padded, shift, width, 1)
    tiled = jnp.tile(window, (1, rows + 1))[:, : rows * (width + 1)]
    skewed = tiled.reshape(heads, rows, width + 1)[:, :, :keys]
    return jnp.flip(skewed, axis=2)


def distance_grads(grad_block, shift, dist_count):
    heads, rows, keys = grad_block.shape
    width = rows + keys - 1
    flipped = jnp.flip(grad_block, axis=2)
    widened = jnp.concatenate(
        [flipped, jnp.zeros((heads, rows, width + 1 - keys), jnp.float32)], axis=2
    )
    flat = jnp.concatenate(
        [widened.reshape(heads, rows * (width + 1)), jnp.zeros((heads, keys - 1), jnp.float32)],
        axis=1,
    )
    window = jnp.sum(flat.reshape(heads, rows + 1, width), axis=1)
    padded = lax.dynamic_update_slice_in_dim(
        jnp.zeros((heads, dist_count + keys - 1), jnp.float32), window, shift, 1
    )
    head_part = jnp.sum(padded[:, :keys], axis=1, keepdims=True)
    return jnp.concatenate([head_part, padded[:, keys:]], axis=1)


def adam(weight, first, second, grad, rate):
    first_new = BETA_ONE * first + (1.0 - BETA_ONE) * grad
    second_new = BETA_TWO * second + (1.0 - BETA_TWO) * grad * grad
    mean_hat = first_new / (1.0 - BETA_ONE**STEP)
    square_hat = second_new / (1.0 - BETA_TWO**STEP)
    updated = weight - rate * (mean_hat / (jnp.sqrt(square_hat) + ADAM_EPS) + DECAY * weight)
    return (updated, first_new, second_new)


def body(
    prompt_states,
    branch_states,
    encoder_states,
    branch_start,
    bucket_table,
    prompt_cotangent,
    branch_cotangent,
    projections,
    projections_first,
    projections_second,
    combiners,
    combiners_first,
    combiners_second,
    expansion,
    expansion_first,
    expansion_second,
    contraction,
    contraction_first,
    contraction_second,
    norm_gains,
    gains_first,
    gains_second,
    position_bias,
    bias_first,
    bias_second,
):
    rows_here = prompt_states.shape[1]
    branch_count = branch_states.shape[1]
    branch_size = branch_states.shape[2]
    branch_rows = branch_count * branch_size
    dist_count = bucket_table.shape[0]
    offset = lax.axis_index("fsdp") * rows_here
    local_rows = jnp.arange(rows_here, dtype=jnp.int32)
    steps_in = jnp.arange(branch_size, dtype=jnp.int32)
    bucket_ids = jnp.arange(BUCKETS, dtype=jnp.int32)
    bucket_onehot = (bucket_table[:, None] == bucket_ids[None, :]).astype(jnp.float32)
    per_distance = jnp.dot(bucket_onehot, position_bias, precision=lax.Precision.HIGHEST).T
    own_bias = hankel_bias(per_distance, 0, branch_size, branch_size)
    shards = (
        projections.astype(jnp.bfloat16),
        combiners.astype(jnp.bfloat16),
        expansion.astype(jnp.bfloat16),
        contraction.astype(jnp.bfloat16),
    )

    def layout(starts):
        branch_pos = (starts[:, None] + steps_in[None, :]).reshape(-1)
        branch_seg = jnp.arange(branch_rows, dtype=jnp.int32) // branch_size
        query_pos = jnp.concatenate([offset + local_rows, branch_pos])
        query_seg = jnp.concatenate([jnp.full((rows_here,), -1, jnp.int32), branch_seg])
        query_limit = jnp.concatenate(
            [
                jnp.zeros((rows_here,), jnp.int32),
                jnp.broadcast_to(starts[:, None], (branch_count, branch_size)).reshape(-1),
            ]
        )
        key_pos = jnp.concatenate([jnp.arange(PROMPT, dtype=jnp.int32), branch_pos])
        key_seg = jnp.concatenate([jnp.full((PROMPT,), -1, jnp.int32), branch_seg])
        same_seg = (key_seg[None, :] == query_seg[:, None]) & (
            key_pos[None, :] <= query_pos[:, None]
        )
        from_prompt = (key_seg[None, :] == -1) & (key_pos[None, :] < query_limit[:, None])
        return same_seg | from_prompt

    def build_bias(starts):
        prompt_block = hankel_bias(per_distance, offset, rows_here, PROMPT)
        upper = jnp.concatenate(
            [prompt_block, jnp.zeros((HEADS, rows_here, branch_rows), jnp.float32)], axis=2
        )

        def branch_block(start):
            return hankel_bias(per_distance, start, branch_size, PROMPT)

        cross_blocks = lax.map(branch_block, starts)
        cross_blocks = jnp.transpose(cross_blocks, (1, 0, 2, 3)).reshape(HEADS, branch_rows, PROMPT)
        lower = jnp.concatenate(
            [cross_blocks, jnp.tile(own_bias, (1, branch_count, branch_count))], axis=2
        )
        return jnp.concatenate([upper, lower], axis=1)

    def bias_gradient(grad_scores, starts):
        total = distance_grads(grad_scores[:, :rows_here, :PROMPT], offset, dist_count)

        def add_branch(index, running):
            begin = rows_here + index * branch_size
            rows_block = lax.dynamic_slice_in_dim(grad_scores, begin, branch_size, 1)
            running = running + distance_grads(rows_block[:, :, :PROMPT], starts[index], dist_count)
            own_block = lax.dynamic_slice_in_dim(
                rows_block, PROMPT + index * branch_size, branch_size, 2
            )
            return running + distance_grads(own_block, 0, dist_count)

        total = lax.fori_loop(0, branch_count, add_branch, total)
        return jnp.dot(total, bucket_onehot, precision=lax.Precision.HIGHEST).T

    def group_step(running, item):
        big_sum, gain_sum, bias_sum = running
        prompt, branches, encoder, starts, prompt_cot, branch_cot = item
        weights = (
            lax.all_gather(shards[0], ("dp", "fsdp"), axis=1, tiled=True),
            lax.all_gather(shards[1], ("dp", "fsdp"), axis=1, tiled=True),
            lax.all_gather(shards[2], ("dp", "fsdp"), axis=1, tiled=True),
            lax.all_gather(shards[3], ("dp", "fsdp"), axis=0, tiled=True),
        )
        w_proj, w_comb, w_exp, w_con = weights
        pair_mask = layout(starts)
        stream = jnp.concatenate(
            [prompt.astype(jnp.float32), branches.reshape(-1, D).astype(jnp.float32)], axis=0
        )
        normed_one, scale_one = rms_forward(stream, norm_gains[0])
        input_one = normed_one.astype(jnp.bfloat16)
        self_rows = jnp.einsum(
            "td,kde->kte", input_one, w_proj[:3], preferred_element_type=jnp.float32
        ).astype(jnp.bfloat16)
        prompt_keys, prompt_values = (
            lax.all_gather(self_rows[1, :rows_here], "fsdp", axis=0, tiled=True),
            lax.all_gather(self_rows[2, :rows_here], "fsdp", axis=0, tiled=True),
        )
        encoder_rows = jnp.einsum(
            "td,kde->kte", encoder, w_proj[4:], preferred_element_type=jnp.float32
        ).astype(jnp.bfloat16)
        cross_keys, cross_values = (
            lax.all_gather(encoder_rows[0], "fsdp", axis=0, tiled=True),
            lax.all_gather(encoder_rows[1], "fsdp", axis=0, tiled=True),
        )
        key_rows = jnp.concatenate([prompt_keys, self_rows[1, rows_here:]], axis=0)
        value_rows = jnp.concatenate([prompt_values, self_rows[2, rows_here:]], axis=0)
        pair_bias = build_bias(starts)
        scores_one = jnp.where(
            pair_mask[None], raw_scores(self_rows[0], key_rows) + pair_bias, MASKED
        )
        mixed_one, logsum_one = softmax_forward(scores_one, value_rows)
        after_one = stream + jnp.dot(mixed_one, w_comb[0], preferred_element_type=jnp.float32)
        normed_two, scale_two = rms_forward(after_one, norm_gains[1])
        input_two = normed_two.astype(jnp.bfloat16)
        query_two = jnp.dot(input_two, w_proj[3], preferred_element_type=jnp.float32).astype(
            jnp.bfloat16
        )
        scores_two = raw_scores(query_two, cross_keys)
        mixed_two, logsum_two = softmax_forward(scores_two, cross_values)
        after_two = after_one + jnp.dot(mixed_two, w_comb[1], preferred_element_type=jnp.float32)
        normed_three, scale_three = rms_forward(after_two, norm_gains[2])
        input_three = normed_three.astype(jnp.bfloat16)
        gate_up = jnp.einsum("td,kdf->ktf", input_three, w_exp, preferred_element_type=jnp.float32)
        hidden, mix_pull = jax.vjp(gelu_mix, gate_up[0], gate_up[1])
        hidden_low = hidden.astype(jnp.bfloat16)
        output = after_two + jnp.dot(hidden_low, w_con, preferred_element_type=jnp.float32)
        again = (
            lax.all_gather(shards[0], ("dp", "fsdp"), axis=1, tiled=True),
            lax.all_gather(shards[1], ("dp", "fsdp"), axis=1, tiled=True),
            lax.all_gather(shards[2], ("dp", "fsdp"), axis=1, tiled=True),
            lax.all_gather(shards[3], ("dp", "fsdp"), axis=0, tiled=True),
        )
        b_proj, b_comb, b_exp, b_con = again
        upstream = jnp.concatenate(
            [prompt_cot.astype(jnp.float32), branch_cot.reshape(-1, D).astype(jnp.float32)], axis=0
        )
        upstream_low = upstream.astype(jnp.bfloat16)
        grad_con = jnp.einsum(
            "tf,td->fd", hidden_low, upstream_low, preferred_element_type=jnp.float32
        )
        grad_hidden = jnp.einsum(
            "td,fd->tf", upstream_low, b_con, preferred_element_type=jnp.float32
        )
        grad_gate, grad_up = mix_pull(grad_hidden)
        gate_low = jnp.stack([grad_gate, grad_up]).astype(jnp.bfloat16)
        grad_exp = jnp.einsum(
            "td,ktf->kdf", input_three, gate_low, preferred_element_type=jnp.float32
        )
        grad_three = jnp.einsum("ktf,kdf->td", gate_low, b_exp, preferred_element_type=jnp.float32)
        back_three, gain_three = rms_backward(after_two, scale_three, norm_gains[2], grad_three)
        grad_after_two = upstream + back_three
        cross_low = grad_after_two.astype(jnp.bfloat16)
        grad_comb_two = jnp.einsum(
            "te,td->ed", mixed_two, cross_low, preferred_element_type=jnp.float32
        )
        grad_mixed_two = jnp.einsum(
            "td,ed->te", cross_low, b_comb[1], preferred_element_type=jnp.float32
        ).astype(jnp.bfloat16)
        grad_query_two, grad_keys_two, grad_values_two, unused_scores = softmax_backward(
            scores_two, logsum_two, query_two, cross_keys, cross_values, grad_mixed_two
        )
        own_keys, own_values = (
            lax.psum_scatter(
                grad_keys_two.astype(jnp.bfloat16), "fsdp", scatter_dimension=0, tiled=True
            ).astype(jnp.float32),
            lax.psum_scatter(
                grad_values_two.astype(jnp.bfloat16), "fsdp", scatter_dimension=0, tiled=True
            ).astype(jnp.float32),
        )
        encoder_low = jnp.stack([own_keys, own_values]).astype(jnp.bfloat16)
        grad_cross_proj = jnp.einsum(
            "td,kte->kde", encoder, encoder_low, preferred_element_type=jnp.float32
        )
        encoder_grad = jnp.einsum(
            "kte,kde->td", encoder_low, b_proj[4:], preferred_element_type=jnp.float32
        )
        query_two_low = grad_query_two.astype(jnp.bfloat16)
        grad_query_proj = jnp.einsum(
            "td,te->de", input_two, query_two_low, preferred_element_type=jnp.float32
        )
        grad_two = jnp.einsum(
            "te,de->td", query_two_low, b_proj[3], preferred_element_type=jnp.float32
        )
        back_two, gain_two = rms_backward(after_one, scale_two, norm_gains[1], grad_two)
        grad_after_one = grad_after_two + back_two
        self_low = grad_after_one.astype(jnp.bfloat16)
        grad_comb_one = jnp.einsum(
            "te,td->ed", mixed_one, self_low, preferred_element_type=jnp.float32
        )
        grad_mixed_one = jnp.einsum(
            "td,ed->te", self_low, b_comb[0], preferred_element_type=jnp.float32
        ).astype(jnp.bfloat16)
        grad_query, grad_keys, grad_values, grad_scores = softmax_backward(
            scores_one, logsum_one, self_rows[0], key_rows, value_rows, grad_mixed_one
        )
        prompt_key_grad, prompt_value_grad = (
            lax.psum_scatter(
                grad_keys[:PROMPT].astype(jnp.bfloat16), "fsdp", scatter_dimension=0, tiled=True
            ).astype(jnp.float32),
            lax.psum_scatter(
                grad_values[:PROMPT].astype(jnp.bfloat16), "fsdp", scatter_dimension=0, tiled=True
            ).astype(jnp.float32),
        )
        self_grad_low = jnp.stack(
            [
                grad_query,
                jnp.concatenate([prompt_key_grad, grad_keys[PROMPT:]], axis=0),
                jnp.concatenate([prompt_value_grad, grad_values[PROMPT:]], axis=0),
            ]
        ).astype(jnp.bfloat16)
        grad_self_proj = jnp.einsum(
            "td,kte->kde", input_one, self_grad_low, preferred_element_type=jnp.float32
        )
        grad_one = jnp.einsum(
            "kte,kde->td", self_grad_low, b_proj[:3], preferred_element_type=jnp.float32
        )
        back_one, gain_one = rms_backward(stream, scale_one, norm_gains[0], grad_one)
        stream_grad = grad_after_one + back_one
        grad_bias = bias_gradient(grad_scores, starts)
        group_big = (
            jnp.concatenate([grad_self_proj, grad_query_proj[None], grad_cross_proj], axis=0),
            jnp.stack([grad_comb_one, grad_comb_two]),
            grad_exp,
            grad_con,
        )
        big_sum = jax.tree.map(jnp.add, big_sum, group_big)
        gain_sum = gain_sum + jnp.stack([gain_one, gain_two, gain_three])
        bias_sum = bias_sum + grad_bias
        results = (
            output[:rows_here].astype(jnp.bfloat16),
            output[rows_here:].reshape(branch_count, branch_size, D).astype(jnp.bfloat16),
            stream_grad[:rows_here],
            stream_grad[rows_here:].reshape(branch_count, branch_size, D),
            encoder_grad,
        )
        return ((big_sum, gain_sum, bias_sum), results)

    big_start = (
        jnp.zeros((6, D, D), jnp.float32),
        jnp.zeros((2, D, D), jnp.float32),
        jnp.zeros((2, D, FF), jnp.float32),
        jnp.zeros((FF, D), jnp.float32),
    )
    start_state = (
        big_start,
        jnp.zeros(norm_gains.shape, jnp.float32),
        jnp.zeros(position_bias.shape, jnp.float32),
    )
    final_state, results = lax.scan(
        group_step,
        start_state,
        (
            prompt_states,
            branch_states,
            encoder_states,
            branch_start,
            prompt_cotangent,
            branch_cotangent,
        ),
    )
    big_sum, gain_sum, bias_sum = final_state
    owned = (
        lax.psum_scatter(big_sum[0], ("dp", "fsdp"), scatter_dimension=1, tiled=True),
        lax.psum_scatter(big_sum[1], ("dp", "fsdp"), scatter_dimension=1, tiled=True),
        lax.psum_scatter(big_sum[2], ("dp", "fsdp"), scatter_dimension=1, tiled=True),
        lax.psum_scatter(big_sum[3], ("dp", "fsdp"), scatter_dimension=0, tiled=True),
    )
    squares = sum((jnp.sum(grad * grad) for grad in owned))
    gain_total, bias_total, square_total = lax.psum((gain_sum, bias_sum, squares), ("dp", "fsdp"))
    grad_norm = jnp.sqrt(
        square_total + jnp.sum(gain_total * gain_total) + jnp.sum(bias_total * bias_total)
    )
    factor = jnp.minimum(1.0, CLIP / (grad_norm + 1e-06))
    params = (projections, combiners, expansion, contraction, norm_gains, position_bias)
    firsts = (
        projections_first,
        combiners_first,
        expansion_first,
        contraction_first,
        gains_first,
        bias_first,
    )
    seconds = (
        projections_second,
        combiners_second,
        expansion_second,
        contraction_second,
        gains_second,
        bias_second,
    )
    grads = (owned[0], owned[1], owned[2], owned[3], gain_total, bias_total)
    states = [
        adam(params[index], firsts[index], seconds[index], grads[index] * factor, RATES[index])
        for index in range(6)
    ]
    return (
        results[0],
        results[1],
        results[2],
        results[3],
        results[4],
        grad_norm,
        states[0][0],
        states[0][1],
        states[0][2],
        states[1][0],
        states[1][1],
        states[1][2],
        states[2][0],
        states[2][1],
        states[2][2],
        states[3][0],
        states[3][1],
        states[3][2],
        states[4][0],
        states[4][1],
        states[4][2],
        states[5][0],
        states[5][1],
        states[5][2],
        states[0][0].astype(jnp.bfloat16),
        states[1][0].astype(jnp.bfloat16),
        states[2][0].astype(jnp.bfloat16),
        states[3][0].astype(jnp.bfloat16),
    )


BF = jnp.bfloat16
F32 = jnp.float32
PAIR = 2 * HD
PAIRS = HEADS // 2
TILE = 256


def params(limit=60):
    return pltpu.CompilerParams(vmem_limit_bytes=limit * 1024 * 1024)


def dot(left, right, contract):
    return lax.dot_general(
        left, right, ((contract[:1], contract[1:]), ((), ())), preferred_element_type=F32
    )


def strip_kernel(prompt, size, starts_ref, base_ref, branch_ref, strip_ref, cross_ref):
    base = jnp.broadcast_to(base_ref[0], (TILE, prompt + TILE))
    strip_ref[0] = pltpu.roll(base, 0, 1, stride=1, stride_axis=0)[:, TILE:]
    place = lax.broadcasted_iota(jnp.int32, (size, prompt), 1)
    for index in range(2):
        row = jnp.broadcast_to(branch_ref[0, index], (size, prompt + size))
        skewed = pltpu.roll(row, 0, 1, stride=1, stride_axis=0)[:, size:]
        cross_ref[0, index * size:(index + 1) * size] = jnp.where(place < starts_ref[index], skewed, MASKED)


def bias_strips(per_distance, starts, prompt, size):
    far = jnp.arange(prompt + TILE)
    base = jnp.where(prompt - far >= 0, per_distance[:, jnp.maximum(prompt - far, 0)], MASKED)
    flipped = jnp.flip(per_distance, axis=1)
    count = per_distance.shape[1]
    padded = jnp.pad(flipped, ((0, 0), (1, prompt + size)))
    rows = [
        lax.dynamic_slice_in_dim(padded, count - size - starts[index], prompt + size, 1)
        for index in range(2)
    ]
    branch = jnp.stack(rows, axis=1)[:, :, None]
    return pl.pallas_call(
        functools.partial(strip_kernel, prompt, size),
        grid_spec=pltpu.PrefetchScalarGridSpec(
            num_scalar_prefetch=1,
            grid=(HEADS,),
            in_specs=[
                pl.BlockSpec((1, 1, prompt + TILE), lambda h, s: (h, 0, 0)),
                pl.BlockSpec((1, 2, 1, prompt + size), lambda h, s: (h, 0, 0, 0)),
            ],
            out_specs=[
                pl.BlockSpec((1, TILE, prompt), lambda h, s: (h, 0, 0)),
                pl.BlockSpec((1, 2 * size, prompt), lambda h, s: (h, 0, 0)),
            ],
        ),
        out_shape=[
            jax.ShapeDtypeStruct((HEADS, TILE, prompt), F32),
            jax.ShapeDtypeStruct((HEADS, 2 * size, prompt), F32),
        ],
        compiler_params=params(),
        name="bias_strips",
    )(starts, base[:, None], branch)


def lanes_of(value, half):
    lane = lax.broadcasted_iota(jnp.int32, value.shape, 1)
    return jnp.where((lane >= HD) if half else (lane < HD), value, jnp.zeros_like(value))


def self_kernel(prompt, size, q_ref, k_ref, v_ref, strip_ref, cross_ref, o_ref, p_ref):
    blocks = prompt // TILE
    begins = [TILE * i * (i + 1) // 2 for i in range(blocks + 1)]
    for half in range(2):
        def put(rows, value):
            if half == 0:
                o_ref[rows] = value.astype(BF)
            else:
                lane = lax.broadcasted_iota(jnp.int32, value.shape, 1)
                o_ref[rows] = jnp.where(lane >= HD, value.astype(BF), o_ref[rows])

        for i in range(blocks):
            rows = slice(i * TILE, (i + 1) * TILE)
            seen = (i + 1) * TILE
            q = lanes_of(q_ref[rows] * BF(HD ** -0.5), half)
            s = dot(q, k_ref[:seen], (1, 1)) + strip_ref[half, :, prompt - seen:]
            e = jnp.exp(s - jnp.max(s, axis=1, keepdims=True))
            p = (e * (1.0 / jnp.sum(e, axis=1, keepdims=True))).astype(BF)
            p_ref[half, :, begins[i]:begins[i + 1]] = p
            put(rows, dot(p, v_ref[:seen], (1, 0)))
        rows = slice(prompt, prompt + 2 * size)
        q = lanes_of(q_ref[rows] * BF(HD ** -0.5), half)
        s = dot(q, k_ref[:prompt], (1, 1)) + cross_ref[half]
        near = strip_ref[half, :size, prompt - TILE:prompt - TILE + size]
        own = jnp.concatenate(
            [
                dot(q[b * size:(b + 1) * size], k_ref[prompt + b * size:prompt + (b + 1) * size], (1, 1)) + near
                for b in range(2)
            ],
            axis=0,
        )
        top = jnp.maximum(jnp.max(s, axis=1, keepdims=True), jnp.max(own, axis=1, keepdims=True))
        e = jnp.exp(s - top)
        f = jnp.exp(own - top)
        inverse = 1.0 / (jnp.sum(e, axis=1, keepdims=True) + jnp.sum(f, axis=1, keepdims=True))
        p = (e * inverse).astype(BF)
        r = (f * inverse).astype(BF)
        p_ref[half, :, begins[blocks]:begins[blocks] + prompt] = p
        p_ref[half, :, begins[blocks] + prompt:] = r
        far = dot(p, v_ref[:prompt], (1, 0))
        mine = jnp.concatenate(
            [
                dot(r[b * size:(b + 1) * size], v_ref[prompt + b * size:prompt + (b + 1) * size], (1, 0))
                for b in range(2)
            ],
            axis=0,
        )
        put(rows, far + mine)


def probs_width(prompt, size):
    blocks = prompt // TILE
    return TILE * blocks * (blocks + 1) // 2 + prompt + size


def self_forward(qkv, strip, cross, prompt, size):
    count = prompt + 2 * size
    width = probs_width(prompt, size)
    column = lambda part: pl.BlockSpec((None, count, PAIR), lambda j, part=part: (part, 0, j))
    return pl.pallas_call(
        functools.partial(self_kernel, prompt, size),
        grid=(PAIRS,),
        in_specs=[
            column(0),
            column(1),
            column(2),
            pl.BlockSpec((2, TILE, prompt), lambda j: (j, 0, 0)),
            pl.BlockSpec((2, 2 * size, prompt), lambda j: (j, 0, 0)),
        ],
        out_specs=[
            pl.BlockSpec((count, PAIR), lambda j: (0, j)),
            pl.BlockSpec((2, TILE, width), lambda j: (j, 0, 0)),
        ],
        out_shape=[
            jax.ShapeDtypeStruct((count, D), BF),
            jax.ShapeDtypeStruct((HEADS, TILE, width), BF),
        ],
        compiler_params=params(),
        cost_estimate=pl.CostEstimate(flops=32_000_000_000, bytes_accessed=60_000_000, transcendentals=0),
        name="self_forward",
    )(qkv, qkv, qkv, strip, cross)


def fold(grid, stop=8):
    rows, width = grid.shape
    while rows > stop:
        rows //= 2
        grid = grid[:rows] + pltpu.roll(grid[rows:], width - rows, 1)
    return grid


def self_back_kernel(prompt, size, q_ref, k_ref, v_ref, do_ref, p_ref, dq_ref, dk_ref, dv_ref, strip_ref, cross_ref,
                     sums, dq_acc, dk_acc, dv_acc):
    blocks = prompt // TILE
    begins = [TILE * i * (i + 1) // 2 for i in range(blocks + 1)]
    scale = BF(HD ** -0.5)
    for half in range(2):
        sums[...] = jnp.zeros_like(sums)

        def add(ref, rows, value):
            if half == 0:
                ref[rows] = value
            else:
                ref[rows] += value

        for i in reversed(range(blocks)):
            rows = slice(i * TILE, (i + 1) * TILE)
            seen = (i + 1) * TILE
            do = lanes_of(do_ref[rows], half)
            q = lanes_of(q_ref[rows] * scale, half)
            low = p_ref[half, :, begins[i]:begins[i + 1]]
            p = low.astype(F32)
            pull = p * dot(do, v_ref[:seen], (1, 1))
            ds = pull - p * jnp.sum(pull, axis=1, keepdims=True)
            sums[:, TILE + prompt - seen:] += ds
            down = ds.astype(BF)
            add(dq_acc, rows, dot(down, lanes_of(k_ref[:seen] * scale, half), (1, 0)))
            if i == blocks - 1 and half == 0:
                dk_acc[:seen] = dot(down, q, (0, 0))
                dv_acc[:seen] = dot(low, do, (0, 0))
            else:
                dk_acc[:seen] += dot(down, q, (0, 0))
                dv_acc[:seen] += dot(low, do, (0, 0))
        rows = slice(prompt, prompt + 2 * size)
        do = lanes_of(do_ref[rows], half)
        q = lanes_of(q_ref[rows] * scale, half)
        low = p_ref[half, :, begins[blocks]:begins[blocks] + prompt]
        low_own = p_ref[half, :, begins[blocks] + prompt:]
        p = low.astype(F32)
        p_own = low_own.astype(F32)
        pull = p * dot(do, v_ref[:prompt], (1, 1))
        parts = [slice(b * size, (b + 1) * size) for b in range(2)]
        keys = [slice(prompt + b * size, prompt + (b + 1) * size) for b in range(2)]
        pull_own = p_own * jnp.concatenate(
            [dot(do[parts[b]], v_ref[keys[b]], (1, 1)) for b in range(2)], axis=0
        )
        total = jnp.sum(pull, axis=1, keepdims=True) + jnp.sum(pull_own, axis=1, keepdims=True)
        ds = pull - p * total
        ds_own = pull_own - p_own * total
        sums[:size, prompt:prompt + size] += ds_own[:size] + ds_own[size:]
        down = ds.astype(BF)
        down_own = ds_own.astype(BF)
        k_own = [lanes_of(k_ref[keys[b]] * scale, half) for b in range(2)]
        add(
            dq_acc,
            rows,
            dot(down, lanes_of(k_ref[:prompt] * scale, half), (1, 0))
            + jnp.concatenate([dot(down_own[parts[b]], k_own[b], (1, 0)) for b in range(2)], axis=0),
        )
        dk_acc[:prompt] += dot(down, q, (0, 0))
        dv_acc[:prompt] += dot(low, do, (0, 0))
        for b in range(2):
            add(dk_acc, keys[b], dot(down_own[parts[b]], q[parts[b]], (0, 0)))
            add(dv_acc, keys[b], dot(low_own[parts[b]], do[parts[b]], (0, 0)))
        strip_ref[half] = fold(sums[...])
        for b in range(2):
            wide = jnp.concatenate([jnp.zeros((size, size), F32), ds[parts[b]]], axis=1)
            cross_ref[half, b] = fold(wide)
    dq_ref[...] = dq_acc[...].astype(BF)
    dk_ref[...] = dk_acc[...].astype(BF)
    dv_ref[...] = dv_acc[...].astype(BF)


def self_backward(qkv, do, probs, prompt, size):
    count = prompt + 2 * size
    width = probs_width(prompt, size)
    column = lambda part: pl.BlockSpec((None, count, PAIR), lambda j, part=part: (part, 0, j))
    flat = pl.BlockSpec((count, PAIR), lambda j: (0, j))
    acc = pltpu.VMEM((count, PAIR), F32)
    return pl.pallas_call(
        functools.partial(self_back_kernel, prompt, size),
        grid=(PAIRS,),
        in_specs=[column(0), column(1), column(2), flat, pl.BlockSpec((2, TILE, width), lambda j: (j, 0, 0))],
        out_specs=[
            flat,
            flat,
            flat,
            pl.BlockSpec((2, 8, prompt + TILE), lambda j: (j, 0, 0)),
            pl.BlockSpec((2, 2, 8, prompt + size), lambda j: (j, 0, 0, 0)),
        ],
        out_shape=[
            jax.ShapeDtypeStruct((count, D), BF),
            jax.ShapeDtypeStruct((count, D), BF),
            jax.ShapeDtypeStruct((count, D), BF),
            jax.ShapeDtypeStruct((HEADS, 8, prompt + TILE), F32),
            jax.ShapeDtypeStruct((HEADS, 2, 8, prompt + size), F32),
        ],
        scratch_shapes=[pltpu.VMEM((TILE, prompt + TILE), F32), acc, acc, acc],
        compiler_params=params(),
        cost_estimate=pl.CostEstimate(flops=60_000_000_000, bytes_accessed=60_000_000, transcendentals=0),
        name="self_backward",
    )(qkv, qkv, qkv, do, probs)


def bias_gradient(strip, cross, starts, bucket_onehot, prompt, size):
    count = bucket_onehot.shape[0]
    near = sum(jnp.roll(strip[:, r], -r, axis=1) for r in range(8))
    per_distance = jnp.pad(jnp.flip(near[:, 1:prompt + 1], axis=1), ((0, 0), (0, count - prompt)))
    for index in range(2):
        far = sum(jnp.roll(cross[:, index, r], -r, axis=1) for r in range(8))
        wide = lax.dynamic_update_slice_in_dim(
            jnp.zeros((HEADS, 2 * prompt + 2 * size), F32), jnp.flip(far, axis=1), starts[index], 1
        )
        first = prompt - 1
        per_distance = per_distance + wide[:, first:first + count]
    return jnp.dot(per_distance, bucket_onehot, precision=lax.Precision.HIGHEST).T


def cross_kernel(q_ref, k_ref, v_ref, o_ref, p_ref):
    count = q_ref.shape[0]
    for i in range(count // TILE):
        rows = slice(i * TILE, (i + 1) * TILE)
        mixed = []
        for half in range(2):
            q = lanes_of(q_ref[rows] * BF(HD ** -0.5), half)
            s = dot(q, k_ref[...], (1, 1))
            e = jnp.exp(s - jnp.max(s, axis=1, keepdims=True))
            p = (e * (1.0 / jnp.sum(e, axis=1, keepdims=True))).astype(BF)
            p_ref[half, rows] = p
            mixed.append(dot(p, v_ref[...], (1, 0)))
        lane = lax.broadcasted_iota(jnp.int32, mixed[0].shape, 1)
        o_ref[rows] = jnp.where(lane < HD, mixed[0], mixed[1]).astype(BF)


def cross_forward(q, kv):
    count = q.shape[0]
    enc = kv.shape[1]
    column = lambda part: pl.BlockSpec((None, enc, PAIR), lambda j, part=part: (part, 0, j))
    flat = pl.BlockSpec((count, PAIR), lambda j: (0, j))
    return pl.pallas_call(
        cross_kernel,
        grid=(PAIRS,),
        in_specs=[flat, column(0), column(1)],
        out_specs=[flat, pl.BlockSpec((2, count, enc), lambda j: (j, 0, 0))],
        out_shape=[jax.ShapeDtypeStruct((count, D), BF), jax.ShapeDtypeStruct((HEADS, count, enc), BF)],
        compiler_params=params(),
        cost_estimate=pl.CostEstimate(flops=12_000_000_000, bytes_accessed=20_000_000, transcendentals=0),
        name="cross_forward",
    )(q, kv, kv)


def cross_back_kernel(q_ref, k_ref, v_ref, do_ref, p_ref, dq_ref, dkv_ref, dk_acc, dv_acc):
    count = q_ref.shape[0]
    scale = BF(HD ** -0.5)
    dk_acc[...] = jnp.zeros_like(dk_acc)
    dv_acc[...] = jnp.zeros_like(dv_acc)
    k_half = [lanes_of(k_ref[...] * scale, half) for half in range(2)]
    for i in range(count // TILE):
        rows = slice(i * TILE, (i + 1) * TILE)
        dq = None
        for half in range(2):
            do = lanes_of(do_ref[rows], half)
            q = lanes_of(q_ref[rows] * scale, half)
            low = p_ref[half, rows]
            p = low.astype(F32)
            pull = p * dot(do, v_ref[...], (1, 1))
            down = (pull - p * jnp.sum(pull, axis=1, keepdims=True)).astype(BF)
            part = dot(down, k_half[half], (1, 0))
            dq = part if dq is None else dq + part
            dk_acc[...] += dot(down, q, (0, 0))
            dv_acc[...] += dot(low, do, (0, 0))
        dq_ref[rows] = dq.astype(BF)
    dkv_ref[0] = dk_acc[...].astype(BF)
    dkv_ref[1] = dv_acc[...].astype(BF)


def cross_backward(q, kv, do, probs):
    count = q.shape[0]
    enc = kv.shape[1]
    column = lambda part: pl.BlockSpec((None, enc, PAIR), lambda j, part=part: (part, 0, j))
    flat = pl.BlockSpec((count, PAIR), lambda j: (0, j))
    acc = pltpu.VMEM((enc, PAIR), F32)
    return pl.pallas_call(
        cross_back_kernel,
        grid=(PAIRS,),
        in_specs=[flat, column(0), column(1), flat, pl.BlockSpec((2, count, enc), lambda j: (j, 0, 0))],
        out_specs=[flat, pl.BlockSpec((2, enc, PAIR), lambda j: (0, 0, j))],
        out_shape=[jax.ShapeDtypeStruct((count, D), BF), jax.ShapeDtypeStruct((2, enc, D), BF)],
        scratch_shapes=[acc, acc],
        compiler_params=params(),
        cost_estimate=pl.CostEstimate(flops=24_000_000_000, bytes_accessed=20_000_000, transcendentals=0),
        name="cross_backward",
    )(q, kv, kv, do, probs)


SIDE = 2
LINE = 4
AXES = ("dp", "fsdp")


def place_of(z, y, x, core):
    return ((z * SIDE + y) * SIDE + x) * 2 + core


def moves(rule):
    every = [(z, y, x, c) for z in range(LINE) for y in range(SIDE) for x in range(SIDE) for c in range(2)]
    return [(place_of(*here), place_of(*rule(*here))) for here in every]


def send(value, rule):
    return lax.ppermute(value, AXES, moves(rule))


def along_line(shift):
    return lambda z, y, x, c: ((z + shift) % LINE, y, x, c)


def first_flip(z, y, x, c):
    return (z, y, 1 - x, c) if c == 0 else (z, 1 - y, x, c)


def second_flip(z, y, x, c):
    return (z, 1 - y, x, c) if c == 0 else (z, y, 1 - x, c)


def core_flip(z, y, x, c):
    return (z, y, x, 1 - c)


def spots(y, x, core):
    here = y * SIDE + x
    along_x = y * SIDE + 1 - x
    along_y = (1 - y) * SIDE + x
    across = (1 - y) * SIDE + 1 - x
    near = jnp.where(core == 0, along_x, along_y)
    far = jnp.where(core == 0, along_y, along_x)
    return here, near, far, across


def put_kernel(leading, slots_ref, *refs):
    *pieces, out, sems = refs
    copies = []
    for index, piece in enumerate(pieces):
        where = (slice(None),) * leading + tuple(slots_ref[index, i] for i in range(slots_ref.shape[1]))
        copies.append(pltpu.make_async_copy(piece, out.at[where], sems.at[index]))
    for copy in copies:
        copy.start()
    for copy in copies:
        copy.wait()


def put_together(pieces, slots, leading, sizes):
    shape = pieces[0].shape
    return pl.pallas_call(
        functools.partial(put_kernel, leading),
        in_specs=[pl.BlockSpec(memory_space=pltpu.SMEM)] + [pl.BlockSpec(memory_space=pl.ANY)] * len(pieces),
        out_specs=pl.BlockSpec(memory_space=pltpu.VMEM),
        out_shape=jax.ShapeDtypeStruct(shape[:leading] + sizes + shape[leading:], pieces[0].dtype),
        scratch_shapes=[pltpu.SemaphoreType.DMA((len(pieces),))],
        compiler_params=params(40),
        name="put_together",
    )(slots, *pieces)


def gather_weight(shard, place):
    z, y, x, core = place
    line = [shard] + [send(shard, along_line(shift)) for shift in range(1, LINE)]
    slots = jnp.stack([(z - shift) % LINE for shift in range(LINE)])[:, None]
    own = put_together(line, slots, 1, (LINE,))
    near = send(own, first_flip)
    far = send(own, second_flip)
    across = send(near, second_flip)
    mine = [own, near, far, across]
    other = [send(piece, core_flip) for piece in mine]
    slots = jnp.stack(
        [jnp.stack([spot, core]) for spot in spots(y, x, core)]
        + [jnp.stack([spot, 1 - core]) for spot in spots(y, x, 1 - core)]
    )
    full = put_together(mine + other, slots, 2, (SIDE * SIDE, 2))
    count, rows, columns = shard.shape
    return full.reshape(count, LINE * SIDE * SIDE * 2 * rows, columns)


def reduce_weight(grad, place):
    z, y, x, core = place
    count, rows, columns = grad.shape
    m = rows // (LINE * SIDE * SIDE * 2)
    grid = grad.reshape(count, LINE, SIDE * SIDE, 2, m, columns)

    def part(spot, side):
        return lax.dynamic_slice(grid, (0, 0, spot, side, 0, 0), (count, LINE, 1, 1, m, columns)).reshape(
            count, LINE, m, columns
        )

    def plus(one, two):
        return (one.astype(F32) + two.astype(F32)).astype(BF)

    def paired_sum(spot):
        return plus(part(spot, core), send(part(spot, 1 - core), core_flip))

    here, near, far, across = spots(y, x, core)
    sum_here, sum_far, sum_near, sum_across = (
        paired_sum(y * SIDE + x),
        paired_sum((1 - y) * SIDE + x),
        paired_sum(y * SIDE + 1 - x),
        paired_sum((1 - y) * SIDE + 1 - x),
    )
    along_y, along_x = sum_far, sum_near
    near_sum = jnp.where(core == 0, along_x, along_y)
    far_sum = jnp.where(core == 0, along_y, along_x)
    here_sum = plus(sum_here, send(far_sum, second_flip))
    near_sum = plus(near_sum, send(sum_across, second_flip))
    line = plus(here_sum, send(near_sum, first_flip))

    def at(index):
        return lax.dynamic_index_in_dim(line, index, 1, keepdims=False)

    total = at(z).astype(F32)
    for shift in range(1, LINE):
        total = total + send(at((z + shift) % LINE), along_line(shift)).astype(F32)
    return total


def swap_halves(value, core):
    mine = lax.dynamic_index_in_dim(value, core, 0, keepdims=False)
    theirs = send(lax.dynamic_index_in_dim(value, 1 - core, 0, keepdims=False), core_flip)
    return jnp.concatenate([jnp.where(core == 0, mine, theirs), jnp.where(core == 0, theirs, mine)], axis=0)


def give_back(value, core):
    mine = lax.dynamic_index_in_dim(value, core, 0, keepdims=False)
    theirs = send(lax.dynamic_index_in_dim(value, 1 - core, 0, keepdims=False), core_flip)
    return jnp.stack([jnp.where(core == 0, mine, theirs), jnp.where(core == 0, theirs, mine)])


def matmul(left, right):
    return jnp.dot(left, right, preferred_element_type=F32)


def matmul_t(left, right):
    return lax.dot_general(left, right, (((1,), (1,)), ((), ())), preferred_element_type=F32)


def weight_grad(left, right):
    return lax.dot_general(left, right, (((0,), (0,)), ((), ())), preferred_element_type=F32).astype(BF)


def paired_body(
    prompt_states,
    branch_states,
    encoder_states,
    branch_start,
    bucket_table,
    prompt_cotangent,
    branch_cotangent,
    projections,
    projections_first,
    projections_second,
    combiners,
    combiners_first,
    combiners_second,
    expansion,
    expansion_first,
    expansion_second,
    contraction,
    contraction_first,
    contraction_second,
    norm_gains,
    gains_first,
    gains_second,
    position_bias,
    bias_first,
    bias_second,
):
    rows_here = prompt_states.shape[1]
    prompt = 2 * rows_here
    size = branch_states.shape[2]
    place_index = lax.axis_index("dp")
    core = lax.axis_index("fsdp")
    place = (place_index // (SIDE * SIDE), place_index // SIDE % SIDE, place_index % SIDE, core)

    w_qkv = gather_weight(projections[:3].astype(BF), place)
    w_mid = gather_weight(
        jnp.concatenate([combiners[:1], projections[3:], combiners[1:]], axis=0).astype(BF), place
    )
    w_exp = gather_weight(expansion.astype(BF), place)
    w_con = gather_weight(contraction[None].astype(BF), place)[0]

    starts = swap_halves(branch_start, core)
    prompt_rows = swap_halves(prompt_states, core)
    branch_rows = swap_halves(branch_states, core).reshape(2 * size, D)
    encoder = swap_halves(encoder_states, core)
    low_up = jnp.concatenate(
        [swap_halves(prompt_cotangent, core), swap_halves(branch_cotangent, core).reshape(2 * size, D)], axis=0
    )

    bucket_ids = jnp.arange(BUCKETS, dtype=jnp.int32)
    bucket_onehot = (bucket_table[:, None] == bucket_ids[None, :]).astype(F32)
    per_distance = jnp.dot(bucket_onehot, position_bias, precision=lax.Precision.HIGHEST).T
    strip, cross = bias_strips(per_distance, starts, prompt, size)

    stream = jnp.concatenate([prompt_rows, branch_rows], axis=0).astype(F32)
    normed_one, scale_one = rms_forward(stream, norm_gains[0])
    input_one = normed_one.astype(BF)
    qkv = jnp.einsum("td,kde->kte", input_one, w_qkv, preferred_element_type=F32).astype(BF)
    kv_two = jnp.einsum("td,kde->kte", encoder, w_mid[2:4], preferred_element_type=F32).astype(BF)
    mixed_one, probs_one = self_forward(qkv, strip, cross, prompt, size)
    after_one = stream + matmul(mixed_one, w_mid[0])
    normed_two, scale_two = rms_forward(after_one, norm_gains[1])
    input_two = normed_two.astype(BF)
    query_two = matmul(input_two, w_mid[1]).astype(BF)
    mixed_two, probs_two = cross_forward(query_two, kv_two)
    after_two = after_one + matmul(mixed_two, w_mid[4])
    normed_three, scale_three = rms_forward(after_two, norm_gains[2])
    input_three = normed_three.astype(BF)
    gate = matmul(input_three, w_exp[0])
    up_value = matmul(input_three, w_exp[1])
    hidden, mix_pull = jax.vjp(gelu_mix, gate, up_value)
    hidden_low = hidden.astype(BF)
    output = (after_two + matmul(hidden_low, w_con)).astype(BF)

    upstream = low_up.astype(F32)
    grad_con = weight_grad(hidden_low, low_up)
    grad_gate, grad_up = mix_pull(matmul_t(low_up, w_con))
    gate_low = grad_gate.astype(BF)
    up_low = grad_up.astype(BF)
    grad_exp = jnp.stack([weight_grad(input_three, gate_low), weight_grad(input_three, up_low)])
    grad_three = matmul_t(gate_low, w_exp[0]) + matmul_t(up_low, w_exp[1])
    back_three, gain_three = rms_backward(after_two, scale_three, norm_gains[2], grad_three)
    grad_after_two = upstream + back_three
    cross_low = grad_after_two.astype(BF)
    grad_comb_two = weight_grad(mixed_two, cross_low)
    grad_mixed_two = matmul_t(cross_low, w_mid[4]).astype(BF)
    query_two_low, kv_two_low = cross_backward(query_two, kv_two, grad_mixed_two, probs_two)
    grad_cross = jnp.stack([weight_grad(encoder, kv_two_low[0]), weight_grad(encoder, kv_two_low[1])])
    encoder_grad = matmul_t(kv_two_low[0], w_mid[2]) + matmul_t(kv_two_low[1], w_mid[3])
    grad_query = weight_grad(input_two, query_two_low)
    grad_two = matmul_t(query_two_low, w_mid[1])
    back_two, gain_two = rms_backward(after_one, scale_two, norm_gains[1], grad_two)
    grad_after_one = grad_after_two + back_two
    self_low = grad_after_one.astype(BF)
    grad_comb_one = weight_grad(mixed_one, self_low)
    grad_mixed_one = matmul_t(self_low, w_mid[0]).astype(BF)
    owned_con = reduce_weight(grad_con[None], place)[0]
    owned_exp = reduce_weight(grad_exp, place)
    grad_mixed_one, owned_con, owned_exp = lax.optimization_barrier((grad_mixed_one, owned_con, owned_exp))
    query_low, key_low, value_low, strip_sums, cross_sums = self_backward(
        qkv, grad_mixed_one, probs_one, prompt, size
    )
    grad_self = jnp.stack(
        [weight_grad(input_one, query_low), weight_grad(input_one, key_low), weight_grad(input_one, value_low)]
    )
    grad_one = matmul_t(query_low, w_qkv[0]) + matmul_t(key_low, w_qkv[1]) + matmul_t(value_low, w_qkv[2])
    back_one, gain_one = rms_backward(stream, scale_one, norm_gains[0], grad_one)
    stream_grad = grad_after_one + back_one
    grad_bias = bias_gradient(strip_sums, cross_sums, starts, bucket_onehot, prompt, size)

    owned_mid = reduce_weight(
        jnp.concatenate([grad_comb_one[None], grad_query[None], grad_cross, grad_comb_two[None]], axis=0), place
    )
    owned_self = reduce_weight(grad_self, place)
    owned = (
        jnp.concatenate([owned_self, owned_mid[1:4]], axis=0),
        jnp.stack([owned_mid[0], owned_mid[4]]),
        owned_exp,
        owned_con,
    )
    squares = sum((jnp.sum(grad * grad) for grad in owned))
    gain_total, bias_total, square_total = lax.psum(
        (jnp.stack([gain_one, gain_two, gain_three]), grad_bias, squares), AXES
    )
    grad_norm = jnp.sqrt(
        square_total + jnp.sum(gain_total * gain_total) + jnp.sum(bias_total * bias_total)
    )
    factor = jnp.minimum(1.0, CLIP / (grad_norm + 1e-06))
    weights = (projections, combiners, expansion, contraction, norm_gains, position_bias)
    firsts = (projections_first, combiners_first, expansion_first, contraction_first, gains_first, bias_first)
    seconds = (
        projections_second,
        combiners_second,
        expansion_second,
        contraction_second,
        gains_second,
        bias_second,
    )
    grads = owned + (gain_total, bias_total)
    states = [
        adam(weights[index], firsts[index], seconds[index], grads[index] * factor, RATES[index])
        for index in range(6)
    ]
    rows = (rows_here, D)
    return (
        give_back(output[:prompt].reshape((2,) + rows), core),
        give_back(output[prompt:].reshape(2, 1, size, D), core),
        give_back(stream_grad[:prompt].reshape((2,) + rows), core),
        give_back(stream_grad[prompt:].reshape(2, 1, size, D), core),
        give_back(encoder_grad.reshape(2, -1, D), core),
        grad_norm,
        *states[0],
        *states[1],
        *states[2],
        *states[3],
        *states[4],
        *states[5],
        states[0][0].astype(BF),
        states[1][0].astype(BF),
        states[2][0].astype(BF),
        states[3][0].astype(BF),
    )


def solution(mesh):
    paired = mesh.shape["dp"] == 4 * SIDE * SIDE and mesh.shape["fsdp"] == 2
    return jax.shard_map(
        paired_body if paired else body,
        mesh=mesh,
        in_specs=(
            P("dp", "fsdp", None),
            P("dp", "fsdp", None, None),
            P("dp", "fsdp", None),
            P("dp", "fsdp"),
            P(),
            P("dp", "fsdp", None),
            P("dp", "fsdp", None, None),
            P(None, ("dp", "fsdp"), None),
            P(None, ("dp", "fsdp"), None),
            P(None, ("dp", "fsdp"), None),
            P(None, ("dp", "fsdp"), None),
            P(None, ("dp", "fsdp"), None),
            P(None, ("dp", "fsdp"), None),
            P(None, ("dp", "fsdp"), None),
            P(None, ("dp", "fsdp"), None),
            P(None, ("dp", "fsdp"), None),
            P(("dp", "fsdp"), None),
            P(("dp", "fsdp"), None),
            P(("dp", "fsdp"), None),
            P(),
            P(),
            P(),
            P(),
            P(),
            P(),
        ),
        out_specs=(
            P("dp", "fsdp", None),
            P("dp", "fsdp", None, None),
            P("dp", "fsdp", None),
            P("dp", "fsdp", None, None),
            P("dp", "fsdp", None),
            P(),
            P(None, ("dp", "fsdp"), None),
            P(None, ("dp", "fsdp"), None),
            P(None, ("dp", "fsdp"), None),
            P(None, ("dp", "fsdp"), None),
            P(None, ("dp", "fsdp"), None),
            P(None, ("dp", "fsdp"), None),
            P(None, ("dp", "fsdp"), None),
            P(None, ("dp", "fsdp"), None),
            P(None, ("dp", "fsdp"), None),
            P(("dp", "fsdp"), None),
            P(("dp", "fsdp"), None),
            P(("dp", "fsdp"), None),
            P(),
            P(),
            P(),
            P(),
            P(),
            P(),
            P(None, ("dp", "fsdp"), None),
            P(None, ("dp", "fsdp"), None),
            P(None, ("dp", "fsdp"), None),
            P(("dp", "fsdp"), None),
        ),
        check_vma=False,
    )
```

```python
import functools

import jax
import jax.numpy as jnp
from jax import lax
from jax.experimental import pallas as pl
from jax.experimental.pallas import tpu as pltpu
from jax.sharding import PartitionSpec as P

D = 1024
FF = 2816
HEADS = 16
HD = 64
BUCKETS = 32
PROMPT = 1024
STEP = 10


EPS = 1e-06
CLIP = 1.0
BETA_ONE = 0.9
BETA_TWO = 0.999
ADAM_EPS = 1e-08
DECAY = 0.01
RATES = (0.05, 0.3, 0.05, 0.03, 1.0, 1.0)
MASKED = -1e30


def rms_forward(stream, gain):
    scale = lax.rsqrt(jnp.mean(stream * stream, axis=-1, keepdims=True) + EPS)
    return (stream * scale * gain, scale)


def rms_backward(stream, scale, gain, upstream):
    weighted = upstream * gain
    grad_in = scale * weighted - stream * scale**3 * jnp.mean(
        weighted * stream, axis=-1, keepdims=True
    )
    return (grad_in, jnp.sum(upstream * stream * scale, axis=0))


def gelu_mix(gate, up_value):
    inner = 0.7978845608028654 * (gate + 0.044715 * gate * gate * gate)
    return 0.5 * gate * (1.0 + jnp.tanh(inner)) * up_value


def raw_scores(queries, key_rows):
    qh = queries.reshape(queries.shape[0], HEADS, HD)
    kh = key_rows.reshape(key_rows.shape[0], HEADS, HD)
    return jnp.einsum("rhd,khd->hrk", qh, kh, preferred_element_type=jnp.float32) * HD ** (-0.5)


def softmax_forward(scores, value_rows):
    row_max = jnp.max(scores, axis=-1, keepdims=True)
    expo = jnp.exp(scores - row_max)
    total = jnp.sum(expo, axis=-1, keepdims=True)
    probs = (expo / total).astype(jnp.bfloat16)
    vh = value_rows.reshape(value_rows.shape[0], HEADS, HD)
    mixed = jnp.einsum("hrk,khd->rhd", probs, vh, preferred_element_type=jnp.float32)
    return (mixed.reshape(mixed.shape[0], D).astype(jnp.bfloat16), row_max + jnp.log(total))


def softmax_backward(scores, logsum, queries, key_rows, value_rows, grad_mixed):
    probs = jnp.exp(scores - logsum)
    grad_heads = grad_mixed.reshape(grad_mixed.shape[0], HEADS, HD)
    vh = value_rows.reshape(value_rows.shape[0], HEADS, HD)
    kh = key_rows.reshape(key_rows.shape[0], HEADS, HD)
    qh = queries.reshape(queries.shape[0], HEADS, HD)
    grad_values = jnp.einsum(
        "hrk,rhd->khd", probs.astype(jnp.bfloat16), grad_heads, preferred_element_type=jnp.float32
    )
    grad_probs = jnp.einsum("rhd,khd->hrk", grad_heads, vh, preferred_element_type=jnp.float32)
    grad_scores = probs * (grad_probs - jnp.sum(probs * grad_probs, axis=-1, keepdims=True))
    scaled = (grad_scores * HD ** (-0.5)).astype(jnp.bfloat16)
    grad_queries = jnp.einsum("hrk,khd->rhd", scaled, kh, preferred_element_type=jnp.float32)
    grad_keys = jnp.einsum("hrk,rhd->khd", scaled, qh, preferred_element_type=jnp.float32)
    return (
        grad_queries.reshape(-1, D),
        grad_keys.reshape(-1, D),
        grad_values.reshape(-1, D),
        grad_scores,
    )


def hankel_bias(per_distance, shift, rows, keys):
    heads = per_distance.shape[0]
    front = jnp.broadcast_to(per_distance[:, :1], (heads, keys - 1))
    padded = jnp.concatenate([front, per_distance], axis=1)
    width = rows + keys - 1
    window = lax.dynamic_slice_in_dim(padded, shift, width, 1)
    tiled = jnp.tile(window, (1, rows + 1))[:, : rows * (width + 1)]
    skewed = tiled.reshape(heads, rows, width + 1)[:, :, :keys]
    return jnp.flip(skewed, axis=2)


def distance_grads(grad_block, shift, dist_count):
    heads, rows, keys = grad_block.shape
    width = rows + keys - 1
    flipped = jnp.flip(grad_block, axis=2)
    widened = jnp.concatenate(
        [flipped, jnp.zeros((heads, rows, width + 1 - keys), jnp.float32)], axis=2
    )
    flat = jnp.concatenate(
        [widened.reshape(heads, rows * (width + 1)), jnp.zeros((heads, keys - 1), jnp.float32)],
        axis=1,
    )
    window = jnp.sum(flat.reshape(heads, rows + 1, width), axis=1)
    padded = lax.dynamic_update_slice_in_dim(
        jnp.zeros((heads, dist_count + keys - 1), jnp.float32), window, shift, 1
    )
    head_part = jnp.sum(padded[:, :keys], axis=1, keepdims=True)
    return jnp.concatenate([head_part, padded[:, keys:]], axis=1)


def adam(weight, first, second, grad, rate):
    first_new = BETA_ONE * first + (1.0 - BETA_ONE) * grad
    second_new = BETA_TWO * second + (1.0 - BETA_TWO) * grad * grad
    mean_hat = first_new / (1.0 - BETA_ONE**STEP)
    square_hat = second_new / (1.0 - BETA_TWO**STEP)
    updated = weight - rate * (mean_hat / (jnp.sqrt(square_hat) + ADAM_EPS) + DECAY * weight)
    return (updated, first_new, second_new)


def body(
    prompt_states,
    branch_states,
    encoder_states,
    branch_start,
    bucket_table,
    prompt_cotangent,
    branch_cotangent,
    projections,
    projections_first,
    projections_second,
    combiners,
    combiners_first,
    combiners_second,
    expansion,
    expansion_first,
    expansion_second,
    contraction,
    contraction_first,
    contraction_second,
    norm_gains,
    gains_first,
    gains_second,
    position_bias,
    bias_first,
    bias_second,
):
    rows_here = prompt_states.shape[1]
    branch_count = branch_states.shape[1]
    branch_size = branch_states.shape[2]
    branch_rows = branch_count * branch_size
    dist_count = bucket_table.shape[0]
    offset = lax.axis_index("fsdp") * rows_here
    local_rows = jnp.arange(rows_here, dtype=jnp.int32)
    steps_in = jnp.arange(branch_size, dtype=jnp.int32)
    bucket_ids = jnp.arange(BUCKETS, dtype=jnp.int32)
    bucket_onehot = (bucket_table[:, None] == bucket_ids[None, :]).astype(jnp.float32)
    per_distance = jnp.dot(bucket_onehot, position_bias, precision=lax.Precision.HIGHEST).T
    own_bias = hankel_bias(per_distance, 0, branch_size, branch_size)
    shards = (
        projections.astype(jnp.bfloat16),
        combiners.astype(jnp.bfloat16),
        expansion.astype(jnp.bfloat16),
        contraction.astype(jnp.bfloat16),
    )

    def layout(starts):
        branch_pos = (starts[:, None] + steps_in[None, :]).reshape(-1)
        branch_seg = jnp.arange(branch_rows, dtype=jnp.int32) // branch_size
        query_pos = jnp.concatenate([offset + local_rows, branch_pos])
        query_seg = jnp.concatenate([jnp.full((rows_here,), -1, jnp.int32), branch_seg])
        query_limit = jnp.concatenate(
            [
                jnp.zeros((rows_here,), jnp.int32),
                jnp.broadcast_to(starts[:, None], (branch_count, branch_size)).reshape(-1),
            ]
        )
        key_pos = jnp.concatenate([jnp.arange(PROMPT, dtype=jnp.int32), branch_pos])
        key_seg = jnp.concatenate([jnp.full((PROMPT,), -1, jnp.int32), branch_seg])
        same_seg = (key_seg[None, :] == query_seg[:, None]) & (
            key_pos[None, :] <= query_pos[:, None]
        )
        from_prompt = (key_seg[None, :] == -1) & (key_pos[None, :] < query_limit[:, None])
        return same_seg | from_prompt

    def build_bias(starts):
        prompt_block = hankel_bias(per_distance, offset, rows_here, PROMPT)
        upper = jnp.concatenate(
            [prompt_block, jnp.zeros((HEADS, rows_here, branch_rows), jnp.float32)], axis=2
        )

        def branch_block(start):
            return hankel_bias(per_distance, start, branch_size, PROMPT)

        cross_blocks = lax.map(branch_block, starts)
        cross_blocks = jnp.transpose(cross_blocks, (1, 0, 2, 3)).reshape(HEADS, branch_rows, PROMPT)
        lower = jnp.concatenate(
            [cross_blocks, jnp.tile(own_bias, (1, branch_count, branch_count))], axis=2
        )
        return jnp.concatenate([upper, lower], axis=1)

    def bias_gradient(grad_scores, starts):
        total = distance_grads(grad_scores[:, :rows_here, :PROMPT], offset, dist_count)

        def add_branch(index, running):
            begin = rows_here + index * branch_size
            rows_block = lax.dynamic_slice_in_dim(grad_scores, begin, branch_size, 1)
            running = running + distance_grads(rows_block[:, :, :PROMPT], starts[index], dist_count)
            own_block = lax.dynamic_slice_in_dim(
                rows_block, PROMPT + index * branch_size, branch_size, 2
            )
            return running + distance_grads(own_block, 0, dist_count)

        total = lax.fori_loop(0, branch_count, add_branch, total)
        return jnp.dot(total, bucket_onehot, precision=lax.Precision.HIGHEST).T

    def group_step(running, item):
        big_sum, gain_sum, bias_sum = running
        prompt, branches, encoder, starts, prompt_cot, branch_cot = item
        weights = (
            lax.all_gather(shards[0], ("dp", "fsdp"), axis=1, tiled=True),
            lax.all_gather(shards[1], ("dp", "fsdp"), axis=1, tiled=True),
            lax.all_gather(shards[2], ("dp", "fsdp"), axis=1, tiled=True),
            lax.all_gather(shards[3], ("dp", "fsdp"), axis=0, tiled=True),
        )
        w_proj, w_comb, w_exp, w_con = weights
        pair_mask = layout(starts)
        stream = jnp.concatenate(
            [prompt.astype(jnp.float32), branches.reshape(-1, D).astype(jnp.float32)], axis=0
        )
        normed_one, scale_one = rms_forward(stream, norm_gains[0])
        input_one = normed_one.astype(jnp.bfloat16)
        self_rows = jnp.einsum(
            "td,kde->kte", input_one, w_proj[:3], preferred_element_type=jnp.float32
        ).astype(jnp.bfloat16)
        prompt_keys, prompt_values = (
            lax.all_gather(self_rows[1, :rows_here], "fsdp", axis=0, tiled=True),
            lax.all_gather(self_rows[2, :rows_here], "fsdp", axis=0, tiled=True),
        )
        encoder_rows = jnp.einsum(
            "td,kde->kte", encoder, w_proj[4:], preferred_element_type=jnp.float32
        ).astype(jnp.bfloat16)
        cross_keys, cross_values = (
            lax.all_gather(encoder_rows[0], "fsdp", axis=0, tiled=True),
            lax.all_gather(encoder_rows[1], "fsdp", axis=0, tiled=True),
        )
        key_rows = jnp.concatenate([prompt_keys, self_rows[1, rows_here:]], axis=0)
        value_rows = jnp.concatenate([prompt_values, self_rows[2, rows_here:]], axis=0)
        pair_bias = build_bias(starts)
        scores_one = jnp.where(
            pair_mask[None], raw_scores(self_rows[0], key_rows) + pair_bias, MASKED
        )
        mixed_one, logsum_one = softmax_forward(scores_one, value_rows)
        after_one = stream + jnp.dot(mixed_one, w_comb[0], preferred_element_type=jnp.float32)
        normed_two, scale_two = rms_forward(after_one, norm_gains[1])
        input_two = normed_two.astype(jnp.bfloat16)
        query_two = jnp.dot(input_two, w_proj[3], preferred_element_type=jnp.float32).astype(
            jnp.bfloat16
        )
        scores_two = raw_scores(query_two, cross_keys)
        mixed_two, logsum_two = softmax_forward(scores_two, cross_values)
        after_two = after_one + jnp.dot(mixed_two, w_comb[1], preferred_element_type=jnp.float32)
        normed_three, scale_three = rms_forward(after_two, norm_gains[2])
        input_three = normed_three.astype(jnp.bfloat16)
        gate_up = jnp.einsum("td,kdf->ktf", input_three, w_exp, preferred_element_type=jnp.float32)
        hidden, mix_pull = jax.vjp(gelu_mix, gate_up[0], gate_up[1])
        hidden_low = hidden.astype(jnp.bfloat16)
        output = after_two + jnp.dot(hidden_low, w_con, preferred_element_type=jnp.float32)
        again = (
            lax.all_gather(shards[0], ("dp", "fsdp"), axis=1, tiled=True),
            lax.all_gather(shards[1], ("dp", "fsdp"), axis=1, tiled=True),
            lax.all_gather(shards[2], ("dp", "fsdp"), axis=1, tiled=True),
            lax.all_gather(shards[3], ("dp", "fsdp"), axis=0, tiled=True),
        )
        b_proj, b_comb, b_exp, b_con = again
        upstream = jnp.concatenate(
            [prompt_cot.astype(jnp.float32), branch_cot.reshape(-1, D).astype(jnp.float32)], axis=0
        )
        upstream_low = upstream.astype(jnp.bfloat16)
        grad_con = jnp.einsum(
            "tf,td->fd", hidden_low, upstream_low, preferred_element_type=jnp.float32
        )
        grad_hidden = jnp.einsum(
            "td,fd->tf", upstream_low, b_con, preferred_element_type=jnp.float32
        )
        grad_gate, grad_up = mix_pull(grad_hidden)
        gate_low = jnp.stack([grad_gate, grad_up]).astype(jnp.bfloat16)
        grad_exp = jnp.einsum(
            "td,ktf->kdf", input_three, gate_low, preferred_element_type=jnp.float32
        )
        grad_three = jnp.einsum("ktf,kdf->td", gate_low, b_exp, preferred_element_type=jnp.float32)
        back_three, gain_three = rms_backward(after_two, scale_three, norm_gains[2], grad_three)
        grad_after_two = upstream + back_three
        cross_low = grad_after_two.astype(jnp.bfloat16)
        grad_comb_two = jnp.einsum(
            "te,td->ed", mixed_two, cross_low, preferred_element_type=jnp.float32
        )
        grad_mixed_two = jnp.einsum(
            "td,ed->te", cross_low, b_comb[1], preferred_element_type=jnp.float32
        ).astype(jnp.bfloat16)
        grad_query_two, grad_keys_two, grad_values_two, unused_scores = softmax_backward(
            scores_two, logsum_two, query_two, cross_keys, cross_values, grad_mixed_two
        )
        own_keys, own_values = (
            lax.psum_scatter(
                grad_keys_two.astype(jnp.bfloat16), "fsdp", scatter_dimension=0, tiled=True
            ).astype(jnp.float32),
            lax.psum_scatter(
                grad_values_two.astype(jnp.bfloat16), "fsdp", scatter_dimension=0, tiled=True
            ).astype(jnp.float32),
        )
        encoder_low = jnp.stack([own_keys, own_values]).astype(jnp.bfloat16)
        grad_cross_proj = jnp.einsum(
            "td,kte->kde", encoder, encoder_low, preferred_element_type=jnp.float32
        )
        encoder_grad = jnp.einsum(
            "kte,kde->td", encoder_low, b_proj[4:], preferred_element_type=jnp.float32
        )
        query_two_low = grad_query_two.astype(jnp.bfloat16)
        grad_query_proj = jnp.einsum(
            "td,te->de", input_two, query_two_low, preferred_element_type=jnp.float32
        )
        grad_two = jnp.einsum(
            "te,de->td", query_two_low, b_proj[3], preferred_element_type=jnp.float32
        )
        back_two, gain_two = rms_backward(after_one, scale_two, norm_gains[1], grad_two)
        grad_after_one = grad_after_two + back_two
        self_low = grad_after_one.astype(jnp.bfloat16)
        grad_comb_one = jnp.einsum(
            "te,td->ed", mixed_one, self_low, preferred_element_type=jnp.float32
        )
        grad_mixed_one = jnp.einsum(
            "td,ed->te", self_low, b_comb[0], preferred_element_type=jnp.float32
        ).astype(jnp.bfloat16)
        grad_query, grad_keys, grad_values, grad_scores = softmax_backward(
            scores_one, logsum_one, self_rows[0], key_rows, value_rows, grad_mixed_one
        )
        prompt_key_grad, prompt_value_grad = (
            lax.psum_scatter(
                grad_keys[:PROMPT].astype(jnp.bfloat16), "fsdp", scatter_dimension=0, tiled=True
            ).astype(jnp.float32),
            lax.psum_scatter(
                grad_values[:PROMPT].astype(jnp.bfloat16), "fsdp", scatter_dimension=0, tiled=True
            ).astype(jnp.float32),
        )
        self_grad_low = jnp.stack(
            [
                grad_query,
                jnp.concatenate([prompt_key_grad, grad_keys[PROMPT:]], axis=0),
                jnp.concatenate([prompt_value_grad, grad_values[PROMPT:]], axis=0),
            ]
        ).astype(jnp.bfloat16)
        grad_self_proj = jnp.einsum(
            "td,kte->kde", input_one, self_grad_low, preferred_element_type=jnp.float32
        )
        grad_one = jnp.einsum(
            "kte,kde->td", self_grad_low, b_proj[:3], preferred_element_type=jnp.float32
        )
        back_one, gain_one = rms_backward(stream, scale_one, norm_gains[0], grad_one)
        stream_grad = grad_after_one + back_one
        grad_bias = bias_gradient(grad_scores, starts)
        group_big = (
            jnp.concatenate([grad_self_proj, grad_query_proj[None], grad_cross_proj], axis=0),
            jnp.stack([grad_comb_one, grad_comb_two]),
            grad_exp,
            grad_con,
        )
        big_sum = jax.tree.map(jnp.add, big_sum, group_big)
        gain_sum = gain_sum + jnp.stack([gain_one, gain_two, gain_three])
        bias_sum = bias_sum + grad_bias
        results = (
            output[:rows_here].astype(jnp.bfloat16),
            output[rows_here:].reshape(branch_count, branch_size, D).astype(jnp.bfloat16),
            stream_grad[:rows_here],
            stream_grad[rows_here:].reshape(branch_count, branch_size, D),
            encoder_grad,
        )
        return ((big_sum, gain_sum, bias_sum), results)

    big_start = (
        jnp.zeros((6, D, D), jnp.float32),
        jnp.zeros((2, D, D), jnp.float32),
        jnp.zeros((2, D, FF), jnp.float32),
        jnp.zeros((FF, D), jnp.float32),
    )
    start_state = (
        big_start,
        jnp.zeros(norm_gains.shape, jnp.float32),
        jnp.zeros(position_bias.shape, jnp.float32),
    )
    final_state, results = lax.scan(
        group_step,
        start_state,
        (
            prompt_states,
            branch_states,
            encoder_states,
            branch_start,
            prompt_cotangent,
            branch_cotangent,
        ),
    )
    big_sum, gain_sum, bias_sum = final_state
    owned = (
        lax.psum_scatter(big_sum[0], ("dp", "fsdp"), scatter_dimension=1, tiled=True),
        lax.psum_scatter(big_sum[1], ("dp", "fsdp"), scatter_dimension=1, tiled=True),
        lax.psum_scatter(big_sum[2], ("dp", "fsdp"), scatter_dimension=1, tiled=True),
        lax.psum_scatter(big_sum[3], ("dp", "fsdp"), scatter_dimension=0, tiled=True),
    )
    squares = sum((jnp.sum(grad * grad) for grad in owned))
    gain_total, bias_total, square_total = lax.psum((gain_sum, bias_sum, squares), ("dp", "fsdp"))
    grad_norm = jnp.sqrt(
        square_total + jnp.sum(gain_total * gain_total) + jnp.sum(bias_total * bias_total)
    )
    factor = jnp.minimum(1.0, CLIP / (grad_norm + 1e-06))
    params = (projections, combiners, expansion, contraction, norm_gains, position_bias)
    firsts = (
        projections_first,
        combiners_first,
        expansion_first,
        contraction_first,
        gains_first,
        bias_first,
    )
    seconds = (
        projections_second,
        combiners_second,
        expansion_second,
        contraction_second,
        gains_second,
        bias_second,
    )
    grads = (owned[0], owned[1], owned[2], owned[3], gain_total, bias_total)
    states = [
        adam(params[index], firsts[index], seconds[index], grads[index] * factor, RATES[index])
        for index in range(6)
    ]
    return (
        results[0],
        results[1],
        results[2],
        results[3],
        results[4],
        grad_norm,
        states[0][0],
        states[0][1],
        states[0][2],
        states[1][0],
        states[1][1],
        states[1][2],
        states[2][0],
        states[2][1],
        states[2][2],
        states[3][0],
        states[3][1],
        states[3][2],
        states[4][0],
        states[4][1],
        states[4][2],
        states[5][0],
        states[5][1],
        states[5][2],
        states[0][0].astype(jnp.bfloat16),
        states[1][0].astype(jnp.bfloat16),
        states[2][0].astype(jnp.bfloat16),
        states[3][0].astype(jnp.bfloat16),
    )


BF = jnp.bfloat16
F32 = jnp.float32
PAIR = 2 * HD
PAIRS = HEADS // 2
TILE = 256


def params(limit=60):
    return pltpu.CompilerParams(vmem_limit_bytes=limit * 1024 * 1024)


def cost(microseconds):
    return pl.CostEstimate(flops=int(microseconds), bytes_accessed=1, transcendentals=0)


def dot(left, right, contract):
    return lax.dot_general(
        left, right, ((contract[:1], contract[1:]), ((), ())), preferred_element_type=F32
    )


def bias_rows(flipped, starts, prompt, size):
    base = jnp.pad(flipped[:, size - 1:], ((0, 0), (0, TILE - 1)), constant_values=MASKED)
    padded = jnp.pad(flipped, ((0, 0), (1, prompt)))
    rows = [
        lax.dynamic_slice_in_dim(padded, prompt - starts[index], prompt + size, 1) for index in range(2)
    ]
    return base[:, None], jnp.stack(rows, axis=1)[:, :, None]


def fill_bias(prompt, size, starts_ref, base, branches, strip_ref, cross_ref):
    wide = jnp.broadcast_to(base, (TILE, prompt + TILE))
    strip_ref[...] = pltpu.roll(wide, 0, 1, stride=1, stride_axis=0)[:, TILE:]
    place = lax.broadcasted_iota(jnp.int32, (size, prompt), 1)
    for index, branch in enumerate(branches):
        row = jnp.broadcast_to(branch, (size, prompt + size))
        skewed = pltpu.roll(row, 0, 1, stride=1, stride_axis=0)[:, size:]
        cross_ref[index * size:(index + 1) * size] = jnp.where(place < starts_ref[index], skewed, MASKED)


def lanes_of(value, half):
    lane = lax.broadcasted_iota(jnp.int32, value.shape, 1)
    return jnp.where((lane >= HD) if half else (lane < HD), value, jnp.zeros_like(value))


def probs_width(prompt, size):
    blocks = prompt // TILE
    return TILE * blocks * (blocks + 1) // 2 + prompt + size


def fold(grid):
    rows, width = grid.shape
    while rows > 1:
        rows //= 2
        grid = grid[:rows] + pltpu.roll(grid[rows:], width - rows, 1)
    return grid


def self_kernel(prompt, size, more, starts_ref, q_ref, k_ref, v_ref, base_ref, branch_ref, *refs):
    o_ref, e_ref, inv_ref, s_ref, strips_ref, crosses_ref = refs[more:]
    blocks = prompt // TILE
    begins = [TILE * i * (i + 1) // 2 for i in range(blocks + 1)]
    lane = lax.broadcasted_iota(jnp.int32, (TILE, PAIR), 1)
    for half in range(2):
        strip_ref, cross_ref = strips_ref.at[half], crosses_ref.at[half]
        branches = [branch_ref[half, index] for index in range(2)]
        fill_bias(prompt, size, starts_ref, base_ref[half], branches, strip_ref, cross_ref)
        for i in range(blocks + 1):
            rows = slice(i * TILE, (i + 1) * TILE)
            q = lanes_of(q_ref[rows] * BF(HD ** -0.5), half)
            tiles = []
            for j in range(min(i + 1, blocks)):
                keys = slice(j * TILE, (j + 1) * TILE)
                begin = prompt - (i + 1 - j) * TILE
                bias = strip_ref.at[:, begin:begin + TILE] if i < blocks else cross_ref.at[:, keys]
                tiles.append((keys, bias))
            top = None
            for j, (keys, bias) in enumerate(tiles):
                s = dot(q, k_ref[keys], (1, 1)) + bias[...]
                s_ref[:, j * TILE:(j + 1) * TILE] = s
                high = jnp.maximum(s[:, :PAIR], s[:, PAIR:])
                top = high if top is None else jnp.maximum(top, high)
            if i == blocks:
                near = strip_ref[:size, prompt - TILE:prompt - TILE + size]
                own = jnp.concatenate(
                    [
                        dot(q[b * size:(b + 1) * size], k_ref[prompt + b * size:prompt + (b + 1) * size], (1, 1)) + near
                        for b in range(2)
                    ],
                    axis=0,
                )
                top = jnp.maximum(top, own)
            top = jnp.max(top, axis=1, keepdims=True)
            total = None
            out = None
            for j, (keys, _) in enumerate(tiles):
                e = jnp.exp(s_ref[:, j * TILE:(j + 1) * TILE] - top)
                part = e[:, :PAIR] + e[:, PAIR:]
                total = part if total is None else total + part
                low = e.astype(BF)
                e_ref[half, :, begins[i] + j * TILE:begins[i] + (j + 1) * TILE] = low
                part = dot(low, v_ref[keys], (1, 0))
                out = part if out is None else out + part
            if i == blocks:
                e = jnp.exp(own - top)
                total = total + e
                low = e.astype(BF)
                e_ref[half, :, begins[i] + prompt:] = low
                out = out + jnp.concatenate(
                    [
                        dot(low[b * size:(b + 1) * size], v_ref[prompt + b * size:prompt + (b + 1) * size], (1, 0))
                        for b in range(2)
                    ],
                    axis=0,
                )
            inverse = 1.0 / jnp.sum(total, axis=1, keepdims=True)
            out = out * inverse
            if half == 0:
                o_ref[rows] = out.astype(BF)
                inv_ref[rows] = jnp.broadcast_to(inverse, (TILE, PAIR))
            else:
                o_ref[rows] = jnp.where(lane >= HD, out.astype(BF), o_ref[rows])
                inv_ref[rows] = jnp.where(lane >= HD, inverse, inv_ref[rows])


def self_forward(qkv, base, branch, starts, prompt, size, first, pairs, before=None):
    count = prompt + 2 * size
    width = probs_width(prompt, size)
    column = lambda part: pl.BlockSpec((None, count, PAIR), lambda j, s, part=part: (part, 0, first + j))
    flat = pl.BlockSpec((count, PAIR), lambda j, s: (0, first + j))
    bias = pltpu.VMEM((2, TILE, prompt), F32)
    more = [] if before is None else list(before)
    return pl.pallas_call(
        functools.partial(self_kernel, prompt, size, len(more)),
        grid_spec=pltpu.PrefetchScalarGridSpec(
            num_scalar_prefetch=1,
            grid=(pairs,),
            in_specs=[
                column(0),
                column(1),
                column(2),
                pl.BlockSpec((2, 1, prompt + TILE), lambda j, s: (first + j, 0, 0)),
                pl.BlockSpec((2, 2, 1, prompt + size), lambda j, s: (first + j, 0, 0, 0)),
            ]
            + [pl.BlockSpec(memory_space=pl.ANY)] * len(more),
            out_specs=[flat, pl.BlockSpec((2, TILE, width), lambda j, s: (first + j, 0, 0)), flat],
            scratch_shapes=[pltpu.VMEM((TILE, prompt), F32), bias, bias],
        ),
        out_shape=[
            jax.ShapeDtypeStruct((count, D), BF),
            jax.ShapeDtypeStruct((HEADS, TILE, width), BF),
            jax.ShapeDtypeStruct((count, D), F32),
        ],
        input_output_aliases={6 + index: index for index in range(len(more))},
        compiler_params=params(),
        cost_estimate=cost(6 * pairs),
        name="self_forward",
    )(starts, qkv, qkv, qkv, base, branch, *more)


def self_back_kernel(prompt, size, q_ref, k_ref, v_ref, do_ref, o_ref, e_ref, inv_ref, dq_ref, dk_ref, dv_ref,
                     strip_ref, cross_ref, sums, far_sums, dk_acc, dv_acc):
    blocks = prompt // TILE
    begins = [TILE * i * (i + 1) // 2 for i in range(blocks + 1)]
    scale = BF(HD ** -0.5)
    lane = lax.broadcasted_iota(jnp.int32, (TILE, PAIR), 1)
    dk_acc[...] = jnp.zeros_like(dk_acc)
    dv_acc[...] = jnp.zeros_like(dv_acc)
    for half in range(2):
        sums[...] = jnp.zeros_like(sums)

        def gather(left, grads, keys, acc):
            acc[half * HD:(half + 1) * HD, keys] += dot(grads[half * HD:(half + 1) * HD], left, (1, 0))

        for i in range(blocks + 1):
            rows = slice(i * TILE, (i + 1) * TILE)
            scaled = do_ref[rows].astype(F32) * inv_ref[rows]
            do = lanes_of(scaled.astype(BF), half)
            part = lanes_of(do.astype(F32) * o_ref[rows].astype(F32), half)
            drop = jnp.sum(part, axis=1, keepdims=True)
            do_left, q_left = do.T, (q_ref[rows] * scale).T
            dq = None
            for j in range(min(i + 1, blocks)):
                keys = slice(j * TILE, (j + 1) * TILE)
                low = e_ref[half, :, begins[i] + j * TILE:begins[i] + (j + 1) * TILE]
                ds = low.astype(F32) * (dot(do, v_ref[keys], (1, 1)) - drop)
                if i < blocks:
                    begin = TILE + prompt - (i + 1 - j) * TILE
                    sums[:, begin:begin + TILE] += ds
                else:
                    far_sums[:, size + j * TILE:size + (j + 1) * TILE] = ds
                down = ds.astype(BF)
                part = dot(down, k_ref[keys], (1, 0))
                dq = part if dq is None else dq + part
                gather(down, q_left, keys, dk_acc)
                gather(low, do_left, keys, dv_acc)
            if i == blocks:
                low = e_ref[half, :, begins[i] + prompt:]
                parts = [slice(b * size, (b + 1) * size) for b in range(2)]
                keys = [slice(prompt + b * size, prompt + (b + 1) * size) for b in range(2)]
                own = jnp.concatenate([dot(do[parts[b]], v_ref[keys[b]], (1, 1)) for b in range(2)], axis=0)
                ds = low.astype(F32) * (own - drop)
                sums[:size, prompt:prompt + size] += ds[:size] + ds[size:]
                down = ds.astype(BF)
                dq = dq + jnp.concatenate(
                    [dot(down[parts[b]], k_ref[keys[b]], (1, 0)) for b in range(2)], axis=0
                )
                for b in range(2):
                    gather(down[parts[b]], q_left[:, parts[b]], keys[b], dk_acc)
                    gather(low[parts[b]], do_left[:, parts[b]], keys[b], dv_acc)
            dq = (dq * (HD ** -0.5)).astype(BF)
            dq_ref[rows] = dq if half == 0 else jnp.where(lane >= HD, dq, dq_ref[rows])
        strip_ref[half] = fold(sums[...])
        for b in range(2):
            wide = far_sums[b * size:(b + 1) * size]
            place = lax.broadcasted_iota(jnp.int32, wide.shape, 1)
            cross_ref[half, b] = fold(jnp.where(place < size, 0.0, wide))
    dk_ref[...] = dk_acc[...].T.astype(BF)
    dv_ref[...] = dv_acc[...].T.astype(BF)


def self_backward(qkv, do, mixed, expos, inverse, prompt, size, first, pairs):
    count = prompt + 2 * size
    width = probs_width(prompt, size)
    column = lambda part: pl.BlockSpec((None, count, PAIR), lambda j, part=part: (part, 0, first + j))
    flat = pl.BlockSpec((count, PAIR), lambda j: (0, j))
    given = pl.BlockSpec((count, PAIR), lambda j: (0, first + j))
    acc = pltpu.VMEM((PAIR, count), F32)
    return pl.pallas_call(
        functools.partial(self_back_kernel, prompt, size),
        grid=(pairs,),
        in_specs=[
            column(0),
            column(1),
            column(2),
            given,
            given,
            pl.BlockSpec((2, TILE, width), lambda j: (first + j, 0, 0)),
            given,
        ],
        out_specs=[
            flat,
            flat,
            flat,
            pl.BlockSpec((2, 1, prompt + TILE), lambda j: (j, 0, 0)),
            pl.BlockSpec((2, 2, 1, prompt + size), lambda j: (j, 0, 0, 0)),
        ],
        out_shape=[
            jax.ShapeDtypeStruct((count, pairs * PAIR), BF),
            jax.ShapeDtypeStruct((count, pairs * PAIR), BF),
            jax.ShapeDtypeStruct((count, pairs * PAIR), BF),
            jax.ShapeDtypeStruct((2 * pairs, 1, prompt + TILE), F32),
            jax.ShapeDtypeStruct((2 * pairs, 2, 1, prompt + size), F32),
        ],
        scratch_shapes=[pltpu.VMEM((TILE, prompt + TILE), F32), pltpu.VMEM((2 * size, prompt + size), F32), acc, acc],
        compiler_params=params(),
        cost_estimate=cost(8 * pairs),
        name="self_backward",
    )(qkv, qkv, qkv, do, mixed, expos, inverse)


def distance_buckets(flipped, starts, prompt, size):
    bucket_ids = jnp.arange(BUCKETS, dtype=jnp.int32)
    whole = jnp.pad(flipped[size - 1:], (0, TILE - 1), constant_values=-1)
    padded = jnp.pad(flipped, (1, prompt), constant_values=-1)
    rows = [lax.dynamic_slice_in_dim(padded, prompt - starts[index], prompt + size, 0) for index in range(2)]
    order = jnp.concatenate([whole] + rows)
    return (order[:, None] == bucket_ids[None, :]).astype(F32)


def bias_gradient(strip, cross, buckets):
    sums = jnp.concatenate([strip[:, 0], cross[:, 0, 0], cross[:, 1, 0]], axis=1)
    return jnp.dot(sums, buckets, precision=lax.Precision.HIGHEST).T


def mlp_kernel(core_ref, x_ref, a_ref, a_t, dy_ref, wg_ref, wu_ref, wd_ref, out_ref, da_ref, away_ref, keep_ref,
               away_con_ref, keep_con_ref, y_ref, hid, dgate, dup, dwd, sem):
    count = a_ref.shape[0]
    step = pl.program_id(0)

    @pl.when(step == 0)
    def _():
        copy = pltpu.make_async_copy(x_ref, y_ref, sem)
        copy.start()
        da_ref[...] = jnp.zeros_like(da_ref)
        copy.wait()

    slope = 0.7978845608028654
    for i in range(0, count, TILE):
        rows = slice(i, i + TILE)
        g = dot(a_ref[rows], wg_ref[...], (1, 0))
        u = dot(a_ref[rows], wu_ref[...], (1, 0))
        dh = dot(dy_ref[rows], wd_ref[...], (1, 1))
        square = g * g
        th = jnp.tanh(slope * g * (1.0 + 0.044715 * square))
        half = 0.5 + 0.5 * th
        gelu = g * half
        slant = half + (0.5 * slope) * g * (1.0 - th * th) * (1.0 + 0.134145 * square)
        low = (gelu * u).astype(BF)
        dg = (dh * u * slant).astype(BF)
        du = (dh * gelu).astype(BF)
        hid[rows] = low
        dgate[rows] = dg
        dup[rows] = du
        y_ref[rows] += dot(low, wd_ref[...], (1, 0))
        da_ref[rows] += dot(dg, wg_ref[...], (1, 1)) + dot(du, wu_ref[...], (1, 1))
    dwd[pl.ds(pl.multiple_of(step * TILE, TILE), TILE)] = dot(hid[...], dy_ref[...], (0, 0))
    core = core_ref[0]
    for index, grad in enumerate((dgate, dup)):
        blocks = dot(a_t[...], grad[...], (1, 0)).astype(BF).reshape(D // 64, 2, 32, TILE)
        away_ref[index] = jnp.where(core == 0, blocks[:, 1], blocks[:, 0])
        keep_ref[index] = jnp.where(core == 0, blocks[:, 0], blocks[:, 1])

    @pl.when(step == pl.num_programs(0) - 1)
    def _():
        for i in range(0, count, TILE):
            out_ref[i:i + TILE] = y_ref[i:i + TILE].astype(BF)
        pairs, m, _ = keep_con_ref.shape
        for index in range(pairs):
            even = dwd[2 * index * m:(2 * index + 1) * m].astype(BF)
            odd = dwd[(2 * index + 1) * m:(2 * index + 2) * m].astype(BF)
            away_con_ref[index] = jnp.where(core == 0, odd, even)
            keep_con_ref[index] = jnp.where(core == 0, even, odd)


def mlp(core, after_two, inputs, turned, low_up, w_gate, w_up, w_con, owners):
    count = inputs.shape[0]
    hidden = w_gate.shape[1]
    m = hidden // owners
    once = pl.Buffered(1)
    flat = pl.BlockSpec((count, D), lambda t, c: (0, 0), pipeline_mode=once)
    column = pl.BlockSpec((D, TILE), lambda t, c: (0, t))
    row = pl.BlockSpec((TILE, D), lambda t, c: (t, 0))
    shared = pl.BlockSpec((2, D // 64, 32, TILE), lambda t, c: (0, 0, 0, t))
    part = jax.ShapeDtypeStruct((2, D // 64, 32, hidden), BF)
    con = pl.BlockSpec((owners // 2, m, D), lambda t, c: (0, 0, 0), pipeline_mode=once)
    con_part = jax.ShapeDtypeStruct((owners // 2, m, D), BF)
    tile = pltpu.VMEM((count, TILE), BF)
    return pl.pallas_call(
        mlp_kernel,
        grid_spec=pltpu.PrefetchScalarGridSpec(
            num_scalar_prefetch=1,
            grid=(hidden // TILE,),
            in_specs=[pl.BlockSpec(memory_space=pl.ANY), flat, whole_block(turned), flat, column, column, row],
            out_specs=[flat, flat, shared, shared, con, con],
            scratch_shapes=[
                pltpu.VMEM((count, D), F32),
                tile,
                tile,
                tile,
                pltpu.VMEM((hidden, D), F32),
                pltpu.SemaphoreType.DMA,
            ],
        ),
        out_shape=[
            jax.ShapeDtypeStruct((count, D), BF),
            jax.ShapeDtypeStruct((count, D), F32),
            part,
            part,
            con_part,
            con_part,
        ],
        compiler_params=params(),
        cost_estimate=cost(85),
        name="mlp",
    )(core, after_two, inputs, turned, low_up, w_gate, w_up, w_con)


def part_kernel(jobs, counts, plan_ref, *refs):
    lefts = refs[:1 + max(jobs)]
    rights = refs[len(lefts):len(lefts) + sum(counts)]
    rest = refs[len(lefts) + len(rights):]

    def finish(index, value):
        if len(rest) == 1:
            rest[0][index] = value.astype(BF).reshape(rest[0].shape[1:])
        else:
            got, away, stay, held = rest
            held[...] = (value + got[index].astype(F32).reshape(value.shape)).astype(BF).reshape(held.shape)
            for slot in range(2):
                away[slot, :, index] = held[:, plan_ref[1 + slot]]
                stay[slot, :, index] = held[:, plan_ref[3 + slot]]

    first = 0
    for index, left in enumerate(jobs):
        if counts[index] == 1:
            finish(index, dot(lefts[left][...], rights[first][...], (1, 0)))
        else:
            for tile in range(counts[index]):
                @pl.when(pl.program_id(0) == tile)
                def _(index=index, left=left, right=rights[first + tile]):
                    finish(index, dot(lefts[left][...], right[...], (1, 0)))
        first += counts[index]


def weight_part(plan, lefts, jobs, got=None):
    rights = [right if isinstance(right, list) else [right] for _, right in jobs]
    columns = sum(right.shape[1] for right in rights[0])
    counts = [len(right) for right in rights]
    m = 32

    def side(left):
        return pl.BlockSpec((None,) + left.shape[1:], lambda t, p: (p[0], 0, 0), pipeline_mode=pl.Buffered(1))

    def tile(right):
        return pl.BlockSpec((right.shape[0], TILE), lambda t, p: (0, t) if right.shape[1] > TILE else (0, 0))

    shared = pl.BlockSpec((len(jobs), D // 64, m, TILE), lambda t, p: (0, 0, 0, t))
    part = jax.ShapeDtypeStruct((len(jobs), D // 64, m, columns), BF)
    split = pl.BlockSpec((2, LINE, len(jobs), m, TILE), lambda t, p: (0, 0, 0, 0, t))
    half = jax.ShapeDtypeStruct((2, LINE, len(jobs), m, columns), BF)
    return pl.pallas_call(
        functools.partial(part_kernel, [left for left, _ in jobs], counts),
        grid_spec=pltpu.PrefetchScalarGridSpec(
            num_scalar_prefetch=1,
            grid=(columns // TILE,),
            in_specs=[side(left) for left in lefts]
            + [tile(value) for right in rights for value in right]
            + ([] if got is None else [shared]),
            out_specs=shared if got is None else [split, split],
            scratch_shapes=[] if got is None else [pltpu.VMEM((LINE, SIDE * SIDE, m, TILE), BF)],
        ),
        out_shape=part if got is None else [half, half],
        compiler_params=params(),
        cost_estimate=cost(2),
        name="weight_part",
    )(plan, *lefts, *(value for right in rights for value in right), *([] if got is None else [got]))


def root(value):
    return lax.rsqrt(jnp.mean(value * value, axis=1, keepdims=True) + EPS)


def normed(value, gain):
    return (value * root(value) * gain).astype(BF)


def norm_back(value, gain, upstream):
    scale = root(value)
    weighted = upstream * gain
    grad = scale * weighted - value * (scale * scale * scale) * jnp.mean(weighted * value, axis=1, keepdims=True)
    terms = upstream * value * scale
    return grad, jnp.sum(terms.reshape(-1, 8, D), axis=0)


def whole_block(value):
    zeros = (0,) * len(value.shape)
    return pl.BlockSpec(value.shape, lambda *index: zeros, pipeline_mode=pl.Buffered(1))


def row_block(columns=D):
    return pl.BlockSpec((TILE, columns), lambda i: (i, 0))


def turned_block():
    return pl.BlockSpec((D, TILE), lambda i: (0, i))


def sided_block():
    return pl.BlockSpec((2, D // 2, TILE), lambda i: (0, 0, i))


def put_sides(ref, value):
    columns = value.T.reshape(D // 64, 2, 32, value.shape[0])
    for side in range(2):
        ref[side] = columns[:, side].reshape(D // 2, value.shape[0])


def fetch(slots_ref, sources, held, sems, index):
    copies = []
    for number, source in enumerate(sources):
        for half in range(2):
            spot = slots_ref[2 * number + half, 0]
            side = slots_ref[2 * number + half, 1]
            copies.append(
                pltpu.make_async_copy(
                    source.at[half, index], held.at[index, :, spot, side], sems.at[index, 2 * number + half]
                )
            )
    return copies


def held_weight(held, index):
    return held[index].reshape(D, D)


def arrive(slots_ref, sources, held, in_sems, count):
    @pl.when(pl.program_id(0) == 0)
    def _():
        for index in range(count):
            for copy in fetch(slots_ref, sources, held, in_sems, index):
                copy.start()


def ready(slots_ref, sources, held, outs, in_sems, out_sems, index):
    @pl.when(pl.program_id(0) == 0)
    def _():
        for copy in fetch(slots_ref, sources, held, in_sems, index):
            copy.wait()
        pltpu.make_async_copy(held.at[index], outs[index], out_sems.at[index]).start()


def settle(held, outs, out_sems):
    @pl.when(pl.program_id(0) == pl.num_programs(0) - 1)
    def _():
        for index, out in enumerate(outs):
            pltpu.make_async_copy(held.at[index], out, out_sems.at[index]).wait()


def weight_specs(sources):
    _, count, line, rows, columns = sources[0].shape
    shape = (line, SIDE * SIDE, 2, rows, columns)
    anywhere = pl.BlockSpec(memory_space=pl.ANY)
    return (
        [pl.BlockSpec(memory_space=pltpu.SMEM)] + [anywhere] * 4,
        [anywhere] * count,
        [jax.ShapeDtypeStruct(shape, BF)] * count,
        [
            pltpu.VMEM((count,) + shape, BF),
            pltpu.SemaphoreType.DMA((count, 8)),
            pltpu.SemaphoreType.DMA((count,)),
        ],
    )


def enter_kernel(slots_ref, *refs):
    sources = refs[:4]
    x_ref, gain_ref, a_ref, qkv_ref = refs[4:8]
    outs = refs[8:11]
    held, in_sems, out_sems = refs[11:]
    arrive(slots_ref, sources, held, in_sems, 3)
    a = normed(x_ref[...].astype(F32), gain_ref[...])
    put_sides(a_ref, a)
    for index in range(3):
        ready(slots_ref, sources, held, outs, in_sems, out_sems, index)
        qkv_ref[index] = dot(a, held_weight(held, index), (1, 0)).astype(BF)
    settle(held, outs, out_sems)


def enter(stream_low, gain, slots, sources):
    count = stream_low.shape[0]
    weight_ins, weight_outs, weight_shapes, scratch = weight_specs(sources)
    turned, qkv, *weights = pl.pallas_call(
        enter_kernel,
        grid=(count // TILE,),
        in_specs=weight_ins + [row_block(), whole_block(gain)],
        out_specs=[sided_block(), pl.BlockSpec((3, TILE, D), lambda i: (0, i, 0))] + weight_outs,
        out_shape=[jax.ShapeDtypeStruct((2, D // 2, count), BF), jax.ShapeDtypeStruct((3, count, D), BF)] + weight_shapes,
        scratch_shapes=scratch,
        compiler_params=params(),
        cost_estimate=cost(12),
        name="enter",
    )(slots, *sources, stream_low, gain)
    return turned, qkv, [weight.reshape(D, D) for weight in weights]


def middle_kernel(parts, slots_ref, *refs):
    sources = refs[:4]
    x_ref, *mixed_refs = refs[4:5 + parts]
    (gain_two_ref, gain_three_ref, e_ref, x1_ref, x2_ref, a2_ref, a3_ref, q_ref, o_ref, p_ref, kv_ref, a3_t_ref,
     mixed_t_ref, e_t_ref, *outs) = refs[5 + parts:24 + parts]
    held, in_sems, out_sems, o_scr = refs[24 + parts:]
    arrive(slots_ref, sources, held, in_sems, 5)

    def weight(index):
        ready(slots_ref, sources, held, outs, in_sems, out_sems, index)
        return held_weight(held, index)

    for index in range(2):
        w = weight(2 + index)

        @pl.when(pl.program_id(0) == 0)
        def _(index=index, w=w):
            kv_ref[index] = dot(e_ref[...], w, (1, 0)).astype(BF)

    @pl.when(pl.program_id(0) == 0)
    def _():
        put_sides(e_t_ref, e_ref[...])

    w_first = weight(0)
    (mixed_ref,) = mixed_refs
    x1 = x_ref[...].astype(F32) + dot(mixed_ref[...], w_first, (1, 0))
    x1_ref[...] = x1
    a2 = normed(x1, gain_two_ref[...])
    put_sides(mixed_t_ref, mixed_ref[...])
    put_sides(a2_ref, a2)
    q_ref[...] = dot(a2, weight(1), (1, 0)).astype(BF)
    for pair in range(PAIRS):
        columns = slice(pair * PAIR, (pair + 1) * PAIR)
        k = kv_ref[0, :, columns]
        v = kv_ref[1, :, columns]
        mixed = []
        for half in range(2):
            q = lanes_of(q_ref[:, columns] * BF(HD ** -0.5), half)
            s = dot(q, k, (1, 1))
            e = jnp.exp(s - jnp.max(s, axis=1, keepdims=True))
            p = (e * (1.0 / jnp.sum(e, axis=1, keepdims=True))).astype(BF)
            p_ref[2 * pair + half] = p
            mixed.append(dot(p, v, (1, 0)))
        lane = lax.broadcasted_iota(jnp.int32, mixed[0].shape, 1)
        o_scr[:, columns] = jnp.where(lane < HD, mixed[0], mixed[1]).astype(BF)
    put_sides(o_ref, o_scr[...])
    x2 = x1_ref[...] + dot(o_scr[...], weight(4), (1, 0))
    x2_ref[...] = x2
    a3 = normed(x2, gain_three_ref[...])
    a3_ref[...] = a3
    a3_t_ref[...] = a3.T
    settle(held, outs, out_sems)


def middle(stream_low, mixed, gain_two, gain_three, encoder, slots, sources):
    count = stream_low.shape[0]
    enc = encoder.shape[0]
    low = jax.ShapeDtypeStruct((count, D), BF)
    wide = jax.ShapeDtypeStruct((count, D), F32)
    turned = jax.ShapeDtypeStruct((D, count), BF)
    sided = jax.ShapeDtypeStruct((2, D // 2, count), BF)
    weight_ins, weight_outs, weight_shapes, scratch = weight_specs(sources)
    *results, w1, w2, w3, w4, w5 = pl.pallas_call(
        functools.partial(middle_kernel, len(mixed)),
        grid=(count // TILE,),
        in_specs=weight_ins
        + [row_block()]
        + [row_block(part.shape[1]) for part in mixed]
        + [whole_block(value) for value in (gain_two, gain_three, encoder)],
        out_specs=[row_block(), row_block(), sided_block(), row_block(), row_block(), sided_block()]
        + [
            pl.BlockSpec((HEADS, TILE, enc), lambda i: (0, i, 0)),
            pl.BlockSpec((2, enc, D), lambda i: (0, 0, 0)),
            turned_block(),
            sided_block(),
            pl.BlockSpec((2, D // 2, enc), lambda i: (0, 0, 0)),
        ]
        + weight_outs,
        out_shape=[
            wide,
            wide,
            sided,
            low,
            low,
            sided,
            jax.ShapeDtypeStruct((HEADS, count, enc), BF),
            jax.ShapeDtypeStruct((2, enc, D), BF),
            turned,
            sided,
            jax.ShapeDtypeStruct((2, D // 2, enc), BF),
        ]
        + weight_shapes,
        scratch_shapes=scratch + [pltpu.VMEM((TILE, D), BF)],
        compiler_params=params(),
        cost_estimate=cost(30),
        name="middle",
    )(slots, *sources, stream_low, *mixed, gain_two, gain_three, encoder)
    return results + [[weight.reshape(D, D) for weight in (w1, w2, w3, w4, w5)]]


def middle_back_kernel(dy_ref, da3_ref, x2_ref, x1_ref, q_ref, p_ref, kv_ref, gain_two_ref, gain_three_ref, wc_ref, wq_ref,
                       wo_ref, *refs):
    before = refs[:-9]
    low2_ref, dq_ref, dx1_ref, low1_ref, do1_ref, dkv_ref, sums_ref, gains_ref, do_ref = refs[-9:]
    dk_acc, dv_acc = sums_ref.at[0], sums_ref.at[1]
    step = pl.program_id(0)

    @pl.when(step == 0)
    def _():
        sums_ref[...] = before[-2][...] if before else jnp.zeros_like(sums_ref)
        gains_ref[...] = before[-1][...] if before else jnp.zeros_like(gains_ref)

    back, terms = norm_back(x2_ref[...], gain_three_ref[...], da3_ref[...])
    gains_ref[1] += terms
    dx2 = dy_ref[...].astype(F32) + back
    dx1_ref[...] = dx2
    low2 = dx2.astype(BF)
    low2_ref[...] = low2
    do_ref[...] = dot(low2, wo_ref[...], (1, 1)).astype(BF)
    scale = BF(HD ** -0.5)
    for pair in range(PAIRS):
        columns = slice(pair * PAIR, (pair + 1) * PAIR)
        k = kv_ref[0, :, columns] * scale
        v = kv_ref[1, :, columns]
        dq = None
        for half in range(2):
            do = lanes_of(do_ref[:, columns], half)
            q = lanes_of(q_ref[:, columns] * scale, half)
            low = p_ref[2 * pair + half]
            p = low.astype(F32)
            pull = p * dot(do, v, (1, 1))
            down = (pull - p * jnp.sum(pull, axis=1, keepdims=True)).astype(BF)
            part = dot(down, lanes_of(k, half), (1, 0))
            dq = part if dq is None else dq + part
            dk_acc[:, columns] += dot(down, q, (0, 0))
            dv_acc[:, columns] += dot(low, do, (0, 0))
        dq_ref[:, columns] = dq.astype(BF)
    da2 = dot(dq_ref[...], wq_ref[...], (1, 1))
    back, terms = norm_back(x1_ref[...], gain_two_ref[...], da2)
    gains_ref[0] += terms
    dx1 = dx1_ref[...] + back
    dx1_ref[...] = dx1
    low1 = dx1.astype(BF)
    low1_ref[...] = low1
    do1_ref[...] = dot(low1, wc_ref[...], (1, 1)).astype(BF)

    @pl.when(step == pl.num_programs(0) - 1)
    def _():
        dkv_ref[0] = dk_acc[...].astype(BF)
        dkv_ref[1] = dv_acc[...].astype(BF)


def middle_back(first, blocks, low_up, grad_three, after_two, after_one, query_two, probs_two, kv_two, gain_two, gain_three,
                w_comb_one, w_query_two, w_comb_two, before=None):
    count = low_up.shape[0]
    enc = kv_two.shape[1]
    low = jax.ShapeDtypeStruct((count, D), BF)
    wide = jax.ShapeDtypeStruct((count, D), F32)
    rows = pl.BlockSpec((TILE, D), lambda i: (first + i, 0))
    sums = jax.ShapeDtypeStruct((2, enc, D), F32)
    gains = jax.ShapeDtypeStruct((2, 8, D), F32)
    whole = (kv_two, gain_two, gain_three, w_comb_one, w_query_two, w_comb_two)
    operands = (low_up, grad_three, after_two, after_one, query_two, probs_two) + whole
    more = [] if before is None else list(before[:5]) + list(before[6:])
    aliases = {} if before is None else {len(operands) + index: index for index in range(5)}
    return pl.pallas_call(
        middle_back_kernel,
        grid=(blocks,),
        in_specs=[rows] * 5
        + [pl.BlockSpec((HEADS, TILE, enc), lambda i: (0, first + i, 0))]
        + [whole_block(value) for value in whole]
        + ([] if before is None else [pl.BlockSpec(memory_space=pl.ANY)] * 5 + [whole_block(sums), whole_block(gains)]),
        out_specs=[rows] * 5
        + [
            pl.BlockSpec((2, enc, D), lambda i: (0, 0, 0)),
            pl.BlockSpec((2, enc, D), lambda i: (0, 0, 0)),
            pl.BlockSpec((2, 8, D), lambda i: (0, 0, 0)),
        ],
        out_shape=[low, low, wide, low, low, jax.ShapeDtypeStruct((2, enc, D), BF), sums, gains],
        scratch_shapes=[pltpu.VMEM((TILE, D), BF)],
        input_output_aliases=aliases,
        compiler_params=params(),
        cost_estimate=cost(45),
        name="middle_back",
    )(*operands, *more)


def leave_kernel(parts, plan_ref, x_ref, dx1_ref, *refs):
    grads = refs[:3 * parts]
    gain_ref, wq_ref, wk_ref, wv_ref, out_ref, gains_ref = refs[3 * parts:]
    width = D // parts

    @pl.when(pl.program_id(0) == 0)
    def _():
        gains_ref[...] = jnp.zeros_like(gains_ref)

    da = None
    for index in range(parts):
        columns = slice(index * width, (index + 1) * width)
        for which, w_ref in enumerate((wq_ref, wk_ref, wv_ref)):
            part = dot(grads[3 * index + which][...], w_ref[:, columns], (1, 1))
            da = part if da is None else da + part
    back, terms = norm_back(x_ref[...].astype(F32), gain_ref[...], da)
    gains_ref[...] += terms
    out_ref[...] = dx1_ref[...] + back


def leave(plan, blocks, stream_low, grad_after_one, parts, gain, w_query, w_key, w_value):
    weights = (w_query, w_key, w_value)
    flat = [value for part in parts for value in part]

    def rows(value):
        return pl.BlockSpec((TILE, value.shape[1]), lambda i, p: (p[i], 0))

    return pl.pallas_call(
        functools.partial(leave_kernel, len(parts)),
        grid_spec=pltpu.PrefetchScalarGridSpec(
            num_scalar_prefetch=1,
            grid=(blocks,),
            in_specs=[rows(stream_low), rows(grad_after_one)]
            + [rows(value) for value in flat]
            + [whole_block(value) for value in (gain,) + weights],
            out_specs=[pl.BlockSpec((TILE, D), lambda i, p: (i, 0)), pl.BlockSpec((8, D), lambda i, p: (0, 0))],
        ),
        out_shape=[jax.ShapeDtypeStruct((blocks * TILE, D), F32), jax.ShapeDtypeStruct((8, D), F32)],
        compiler_params=params(),
        cost_estimate=cost(2),
        name="leave",
    )(plan, stream_low, grad_after_one, *flat, gain, *weights)


SIDE = 2
LINE = 4
AXES = ("dp", "fsdp")


def place_of(z, y, x, core):
    return ((z * SIDE + y) * SIDE + x) * 2 + core


def moves(rule):
    every = [(z, y, x, c) for z in range(LINE) for y in range(SIDE) for x in range(SIDE) for c in range(2)]
    return [(place_of(*here), place_of(*rule(*here))) for here in every]


def send(value, rule):
    return lax.ppermute(value, AXES, moves(rule))


def along_line(shift):
    return lambda z, y, x, c: ((z + shift) % LINE, y, x, c)


def line_far(z, y, x, c):
    return (z ^ 2, y, x, c)


def line_near(z, y, x, c):
    return (z ^ 1, y, x, c)


def first_flip(z, y, x, c):
    return (z, y, 1 - x, c) if c == 0 else (z, 1 - y, x, c)


def second_flip(z, y, x, c):
    return (z, 1 - y, x, c) if c == 0 else (z, y, 1 - x, c)


def core_flip(z, y, x, c):
    return (z, y, x, 1 - c)


def spots(y, x, core):
    here = y * SIDE + x
    along_x = y * SIDE + 1 - x
    along_y = (1 - y) * SIDE + x
    across = (1 - y) * SIDE + 1 - x
    near = jnp.where(core == 0, along_x, along_y)
    far = jnp.where(core == 0, along_y, along_x)
    return here, near, far, across


def put_kernel(z_ref, shard, far, near, out, sems):
    z = z_ref[0]
    sources = [(shard, z), (far, z ^ 2), (near.at[0], z ^ 1), (near.at[1], z ^ 3)]
    copies = [
        pltpu.make_async_copy(source, out.at[:, slot], sems.at[index])
        for index, (source, slot) in enumerate(sources)
    ]
    for copy in copies:
        copy.start()
    for copy in copies:
        copy.wait()


def put_in_line(shard, far, near, z):
    count, rows, columns = shard.shape
    return pl.pallas_call(
        put_kernel,
        in_specs=[pl.BlockSpec(memory_space=pltpu.SMEM)] + [pl.BlockSpec(memory_space=pl.ANY)] * 3,
        out_specs=pl.BlockSpec(memory_space=pltpu.VMEM),
        out_shape=jax.ShapeDtypeStruct((count, LINE, rows, columns), shard.dtype),
        scratch_shapes=[pltpu.SemaphoreType.DMA((LINE,))],
        compiler_params=params(40),
        cost_estimate=cost(1),
        name="put_in_line",
    )(z[None], shard, far, near)


def assemble_kernel(slots_ref, *refs):
    sources = refs[:4]
    outs, sems = refs[4:-1], refs[-1]
    copies = []
    for index, source in enumerate(sources):
        for half in range(2):
            spot = slots_ref[2 * index + half, 0]
            side = slots_ref[2 * index + half, 1]
            for k, out in enumerate(outs):
                copies.append(
                    pltpu.make_async_copy(source.at[half, k], out.at[:, spot, side], sems.at[len(copies)])
                )
    for copy in copies:
        copy.start()
    for copy in copies:
        copy.wait()


def assemble(sources, slots):
    _, count, line, rows, columns = sources[0].shape
    shape = (line, SIDE * SIDE, 2, rows, columns)
    outs = pl.pallas_call(
        assemble_kernel,
        in_specs=[pl.BlockSpec(memory_space=pltpu.SMEM)] + [pl.BlockSpec(memory_space=pl.ANY)] * 4,
        out_specs=[pl.BlockSpec(memory_space=pltpu.VMEM)] * count,
        out_shape=[jax.ShapeDtypeStruct(shape, sources[0].dtype)] * count,
        scratch_shapes=[pltpu.SemaphoreType.DMA((8 * count,))],
        compiler_params=params(40),
        cost_estimate=cost(2 * count),
        name="assemble",
    )(slots, *sources)
    return [out.reshape(line * SIDE * SIDE * 2 * rows, columns) for out in outs]


def tie(*values):
    return lax.optimization_barrier(values)


def line_stage(shard):
    return [send(shard, along_line(shift)) for shift in range(1, LINE)]


def piece_slots(place):
    _, y, x, core = place
    mine = spots(y, x, core)
    theirs = spots(y, x, 1 - core)
    order = [(mine[0], core), (mine[1], core), (theirs[0], 1 - core), (theirs[1], 1 - core)]
    order += [(mine[2], core), (mine[3], core), (theirs[2], 1 - core), (theirs[3], 1 - core)]
    return jnp.stack([jnp.stack(pair) for pair in order])


def add_split_kernel(spots_ref, one_ref, two_ref, away_ref, stay_ref):
    slot = pl.program_id(0)
    value = one_ref[...] + two_ref[...]

    for out_ref, here in ((away_ref, slot < 2), (stay_ref, slot >= 2)):
        @pl.when(here)
        def _(out_ref=out_ref):
            for index in range(value.shape[0]):
                out_ref[0, :, index] = value[index, :, 0]


def add_split(keep, received, place):
    _, y, x, core = place
    here, near, far, across = spots(y, x, core)
    count, _, rows, columns = keep.shape
    grid = (count, LINE, SIDE * SIDE, rows, columns)
    wide = columns // 2
    source = pl.BlockSpec((count, LINE, 1, rows, wide), lambda j, t, s: (0, 0, s[j], 0, t))
    out = jax.ShapeDtypeStruct((2, LINE, count, rows, columns), BF)
    block = (1, LINE, count, rows, wide)
    return pl.pallas_call(
        add_split_kernel,
        grid_spec=pltpu.PrefetchScalarGridSpec(
            num_scalar_prefetch=1,
            grid=(4, 2),
            in_specs=[source, source],
            out_specs=[
                pl.BlockSpec(block, lambda j, t, s: (jnp.minimum(j, 1), 0, 0, 0, jnp.where(j < 2, t, 1))),
                pl.BlockSpec(block, lambda j, t, s: (jnp.maximum(j - 2, 0), 0, 0, 0, jnp.where(j < 2, 0, t))),
            ],
        ),
        out_shape=[out, out],
        compiler_params=params(),
        cost_estimate=cost(1),
        name="add_split",
    )(jnp.stack([far, across, here, near]), keep.reshape(grid), received.reshape(grid))


def plus(one, two):
    return (one.astype(F32) + two.astype(F32)).astype(BF)


def line_split(line, place):
    z = place[0]

    def at(index):
        return lax.dynamic_index_in_dim(line, index, 0, keepdims=False)

    return (at(z), at(z ^ 2)), jnp.stack([at(z ^ 1), at(z ^ 3)])


def add_in_order(value, received, own, owners):
    total = None
    for index in range(4):
        term = jnp.where(own == index, value, 0.0)
        for part, owner in zip(received, owners):
            term = term + jnp.where(owner == index, part, 0.0)
        total = term if total is None else total + term
    return total


def sum_everywhere(value, place):
    z, y, x, core = place
    parts = [send(value, along_line(shift)) for shift in range(1, LINE)]
    value = add_in_order(value, parts, z, [(z - shift) % LINE for shift in range(1, LINE)])
    flips = [(0, 1), (1, 0), (1, 1)]
    parts = [send(value, lambda z, y, x, c, dy=dy, dx=dx: (z, y ^ dy, x ^ dx, c)) for dy, dx in flips]
    value = add_in_order(
        value, parts, y * SIDE + x, [jnp.bitwise_xor(y, dy) * SIDE + jnp.bitwise_xor(x, dx) for dy, dx in flips]
    )
    return value + send(value, core_flip)


def swap_halves(parts, core):
    def block(index):
        return jnp.concatenate(
            [lax.dynamic_index_in_dim(part, index, 0, keepdims=False).reshape(-1, D) for part in parts], axis=0
        )

    mine = block(core)
    theirs = send(block(1 - core), core_flip)
    first = jnp.where(core == 0, mine, theirs)
    second = jnp.where(core == 0, theirs, mine)
    whole, begin = [], 0
    for part in parts:
        end = begin + part.size // 2 // D
        whole.append(jnp.concatenate([first[begin:end], second[begin:end]], axis=0))
        begin = end
    return whole


def hand_over(parts, core):
    halves = [part.reshape((2, -1, D)) for part in parts]

    def block(index):
        return jnp.concatenate([lax.dynamic_index_in_dim(part, index, 0, keepdims=False) for part in halves], axis=0)

    return block(core), send(block(1 - core), core_flip)


def both_groups(mine, other, core):
    return jnp.stack([jnp.where(core == 0, mine, other), jnp.where(core == 0, other, mine)])


def matmul(left, right):
    return jnp.dot(left, right, preferred_element_type=F32)


def matmul_t(left, right):
    return lax.dot_general(left, right, (((1,), (1,)), ((), ())), preferred_element_type=F32)


def paired_body(
    prompt_states,
    branch_states,
    encoder_states,
    branch_start,
    bucket_table,
    prompt_cotangent,
    branch_cotangent,
    projections,
    projections_first,
    projections_second,
    combiners,
    combiners_first,
    combiners_second,
    expansion,
    expansion_first,
    expansion_second,
    contraction,
    contraction_first,
    contraction_second,
    norm_gains,
    gains_first,
    gains_second,
    position_bias,
    bias_first,
    bias_second,
):
    rows_here = prompt_states.shape[1]
    prompt = 2 * rows_here
    size = branch_states.shape[2]
    place_index = lax.axis_index("dp")
    core = lax.axis_index("fsdp")
    place = (place_index // (SIDE * SIDE), place_index // SIDE % SIDE, place_index % SIDE, core)

    z = place[0]
    core_ref = core[None]

    shard_qkv = projections[:3].astype(BF)
    shard_mid = jnp.concatenate([combiners[:1], projections[3:], combiners[1:]], axis=0).astype(BF)
    shard_exp = expansion.astype(BF)
    shard_con = contraction[None].astype(BF)
    far_line_qkv = send(shard_qkv, line_far)

    other_start = send(lax.dynamic_index_in_dim(branch_start, 1 - core, 0, keepdims=False), core_flip)
    own_start = lax.dynamic_index_in_dim(branch_start, core, 0, keepdims=False)
    starts = jnp.concatenate(
        [jnp.where(core == 0, own_start, other_start), jnp.where(core == 0, other_start, own_start)]
    )
    gain_rows = [norm_gains[index:index + 1] for index in range(3)]

    bucket_ids = jnp.arange(BUCKETS, dtype=jnp.int32)
    flipped_table = jnp.flip(bucket_table)
    flipped_onehot = (flipped_table[:, None] == bucket_ids[None, :]).astype(F32)
    flipped_bias = jnp.dot(flipped_onehot, position_bias, precision=lax.Precision.HIGHEST).T
    buckets = distance_buckets(flipped_table, starts, prompt, size)
    slots = piece_slots(place)

    shard_mid, far_line_qkv, prompt_states, starts = tie(shard_mid, far_line_qkv, prompt_states, starts)
    near_line_qkv = send(jnp.stack([shard_qkv, far_line_qkv]), line_near)
    far_line_mid = send(shard_mid, line_far)
    prompt_rows, branch_rows, prompt_up, branch_up, encoder = swap_halves(
        [prompt_states, branch_states, prompt_cotangent, branch_cotangent, encoder_states], core
    )
    own_qkv = put_in_line(shard_qkv, far_line_qkv, near_line_qkv, z)
    near_qkv = send(own_qkv, first_flip)
    near_qkv, own_qkv, far_line_mid = tie(near_qkv, own_qkv, far_line_mid)
    close_qkv = jnp.stack([own_qkv, near_qkv])
    far_qkv = send(close_qkv, second_flip)
    near_line_mid = send(jnp.stack([shard_mid, far_line_mid]), line_near)
    close_qkv_two = send(close_qkv, core_flip)
    base, branch = bias_rows(flipped_bias, starts, prompt, size)
    stream_low = jnp.concatenate([prompt_rows, branch_rows], axis=0)
    low_up = jnp.concatenate([prompt_up, branch_up], axis=0)
    far_qkv, near_line_mid, close_qkv_two, stream_low, low_up, encoder, base, branch, shard_exp, shard_con = tie(
        far_qkv, near_line_mid, close_qkv_two, stream_low, low_up, encoder, base, branch, shard_exp, shard_con
    )
    far_qkv_two = send(far_qkv, core_flip)
    own_mid = put_in_line(shard_mid, far_line_mid, near_line_mid, z)
    near_mid = send(own_mid, first_flip)
    far_line_exp = send(shard_exp, line_far)
    stream_low, own_mid, far_qkv_two = tie(stream_low, own_mid, far_qkv_two)

    turned_one, qkv, (w_query, w_key, w_value) = enter(
        stream_low, gain_rows[0], slots, [close_qkv, close_qkv_two, far_qkv, far_qkv_two]
    )
    qkv, near_mid, far_line_exp, shard_con = tie(qkv, near_mid, far_line_exp, shard_con)
    close_mid = jnp.stack([own_mid, near_mid])
    far_mid = send(close_mid, second_flip)
    near_line_exp = send(jnp.stack([shard_exp, far_line_exp]), line_near)
    far_line_con = send(shard_con, line_far)
    close_mid_two = send(close_mid, core_flip)
    qkv, close_mid = tie(qkv, close_mid)
    most = 5 * PAIRS // 8
    heads = self_forward(qkv, base, branch, starts, prompt, size, 0, most)
    *heads, qkv, far_mid, close_mid_two, near_line_exp, far_line_con = tie(
        *heads, qkv, far_mid, close_mid_two, near_line_exp, far_line_con
    )
    own_exp = put_in_line(shard_exp, far_line_exp, near_line_exp, z)
    near_exp = send(own_exp, first_flip)
    far_mid_two = send(far_mid, core_flip)
    near_line_con = send(jnp.stack([shard_con, far_line_con]), line_near)
    qkv, own_exp, far_mid = tie(qkv, own_exp, far_mid)
    heads = self_forward(qkv, base, branch, starts, prompt, size, most, PAIRS - most, heads)
    *heads, far_mid_two, near_exp, near_line_con = tie(*heads, far_mid_two, near_exp, near_line_con)
    mixed_one, expos, inverse = heads
    close_exp = jnp.stack([own_exp, near_exp])
    far_exp = send(close_exp, second_flip)
    close_exp_two = send(close_exp, core_flip)
    own_con = put_in_line(shard_con, far_line_con, near_line_con, z)
    near_con = send(own_con, first_flip)
    mixed_one, close_exp, own_con = tie(mixed_one, close_exp, own_con)
    (after_one, after_two, turned_two, input_three, query_two, turned_mixed_two, probs_two, kv_two, turned_three,
     turned_mixed_one, turned_encoder, weights_mid) = middle(
        stream_low,
        [mixed_one],
        gain_rows[1],
        gain_rows[2],
        encoder,
        slots,
        [close_mid, close_mid_two, far_mid, far_mid_two],
    )
    w_comb_one, w_query_two, w_key_two, w_value_two, w_comb_two = weights_mid
    input_three, far_exp, near_con, close_exp_two = tie(input_three, far_exp, near_con, close_exp_two)
    far_exp_two = send(far_exp, core_flip)
    close_con = jnp.stack([own_con, near_con])
    far_con = send(close_con, second_flip)
    close_con_two = send(close_con, core_flip)
    w_gate, w_up = assemble([close_exp, close_exp_two, far_exp, far_exp_two], slots)
    w_gate, w_up, far_con, close_con_two = tie(w_gate, w_up, far_con, close_con_two)
    far_con_two = send(far_con, core_flip)
    w_con = assemble([close_con, close_con_two, far_con, far_con_two], slots)[0]

    owners = LINE * SIDE * SIDE * 2
    output, grad_three, away_exp, keep_exp, away_con, keep_con = mlp(
        core_ref, after_two, input_three, turned_three, low_up, w_gate, w_up, w_con, owners
    )
    got_exp = send(away_exp, core_flip)
    got_con = send(away_con[None], core_flip)
    low_up, away_exp, away_con, grad_three, output = tie(low_up, away_exp, away_con, grad_three, output)
    own_output, other_output = hand_over([output[:prompt], output[prompt:]], core)
    low_up, own_output = tie(low_up, own_output)

    def middle_part(first, blocks, before=None):
        return middle_back(
            first,
            blocks,
            low_up,
            grad_three,
            after_two,
            after_one,
            query_two,
            probs_two,
            kv_two,
            gain_rows[1],
            gain_rows[2],
            w_comb_one,
            w_query_two,
            w_comb_two,
            before,
        )

    before = middle_part(0, 1)
    *before, got_exp, got_con = tie(*before, got_exp, got_con)
    away_con, stay_con = add_split(keep_con[None], got_con, place)
    got_con = send(away_con, second_flip)
    away_exp, stay_exp = add_split(keep_exp, got_exp, place)
    got_exp = send(away_exp, second_flip)
    *before, away_exp, away_con = tie(*before, away_exp, away_con)
    (cross_low, query_two_low, grad_after_one, self_low, grad_mixed_one, kv_two_low, _, gain_back) = middle_part(
        1, prompt // TILE + 2 * size // TILE - 1, before
    )
    _, y, x, _ = place
    here, near, far, across = spots(y, x, core)
    keep_plan = jnp.stack([core, far, across, here, near])
    away_plan = jnp.stack([1 - core, far, across, here, near])
    lefts_mid = [turned_mixed_one, turned_two, turned_encoder, turned_mixed_two]
    jobs_mid = [(0, self_low), (1, query_two_low), (2, kv_two_low[0]), (2, kv_two_low[1]), (3, cross_low)]
    away_mid = weight_part(away_plan, lefts_mid, jobs_mid)
    encoder_grad = matmul_t(kv_two_low[0], w_key_two) + matmul_t(kv_two_low[1], w_value_two)
    away_mid, encoder_grad, other_output, got_exp, got_con = tie(away_mid, encoder_grad, other_output, got_exp, got_con)
    got_mid = send(away_mid, core_flip)
    near_con = plus(stay_con[1], got_con[1])
    got_near_con = send(near_con, first_flip)
    near_exp = plus(stay_exp[1], got_exp[1])
    got_near_exp = send(near_exp, first_flip)
    own_encoder, other_encoder = hand_over([encoder_grad], core)
    grad_mixed_one, away_mid, near_exp, near_con, own_encoder = tie(
        grad_mixed_one, away_mid, near_exp, near_con, own_encoder
    )

    half = PAIRS // 2

    def attend_back(index, *values):
        part = self_backward(
            qkv, grad_mixed_one, mixed_one, expos, inverse, prompt, size, index * half, half
        )
        first, *rest = tie(part[0], grad_mixed_one, *values)
        return ((first,) + tuple(part[1:]), *rest)

    def jobs_of(part):
        return [(0, part[i]) for i in range(3)]

    part_one, grad_mixed_one, got_mid, other_encoder, got_near_con, got_near_exp = attend_back(
        0, got_mid, other_encoder, got_near_con, got_near_exp
    )
    line_exp, away_exp = line_split(plus(plus(stay_exp[0], got_exp[0]), got_near_exp), place)
    got_line_exp = send(away_exp, line_near)
    away_mid, stay_mid = weight_part(keep_plan, lefts_mid, jobs_mid, got_mid)
    got_mid = send(away_mid, second_flip)
    line_con, away_con = line_split(plus(plus(stay_con[0], got_con[0]), got_near_con), place)
    got_line_con = send(away_con, line_near)
    away_plan, away_exp, away_con, away_mid = tie(away_plan, away_exp, away_con, away_mid)
    away_one = weight_part(away_plan, [turned_one], jobs_of(part_one))
    got_one = send(away_one, core_flip)
    grad_mixed_one, away_one = tie(grad_mixed_one, away_one)

    part_two, grad_mixed_one, got_one, got_mid, got_line_exp, got_line_con, away_plan = attend_back(
        1, got_one, got_mid, got_line_exp, got_line_con, away_plan
    )
    away_two = weight_part(away_plan, [turned_one], jobs_of(part_two))
    got_two = send(away_two, core_flip)
    near_mid = plus(stay_mid[1], got_mid[1])
    got_near_mid = send(near_mid, first_flip)
    last_exp = plus(line_exp[1], got_line_exp[1])
    got_last_exp = send(last_exp, line_far)
    keep_plan, away_two, near_mid, last_exp = tie(keep_plan, away_two, near_mid, last_exp)
    away_one, stay_one = weight_part(keep_plan, [turned_one], jobs_of(part_one), got_one)
    got_one = send(away_one, second_flip)
    leave_values = (
        stream_low,
        grad_after_one,
        [part_one[:3], part_two[:3]],
        gain_rows[0],
        w_query,
        w_key,
        w_value,
    )
    blocks = prompt // TILE // 2
    steps = jnp.arange(blocks, dtype=jnp.int32)
    theirs_plan = jnp.concatenate([(1 - core) * blocks + steps, jnp.full((1,), 2 * blocks, jnp.int32)])
    ours_plan = core * blocks + steps

    theirs_plan, away_one, got_two = tie(theirs_plan, away_one, got_two)
    theirs_grad, gain_one = leave(theirs_plan, blocks + 1, *leave_values)
    theirs_grad, got_one, got_near_mid, got_last_exp, keep_plan = tie(
        theirs_grad, got_one, got_near_mid, got_last_exp, keep_plan
    )
    near_one = plus(stay_one[1], got_one[1])
    got_near_one = send(near_one, first_flip)
    line_mid, away_mid = line_split(plus(plus(stay_mid[0], got_mid[0]), got_near_mid), place)
    got_line_mid = send(away_mid, line_near)
    last_con = plus(line_con[1], got_line_con[1])
    got_last_con = send(last_con, line_far)
    keep_plan, near_one, away_mid, last_con = tie(keep_plan, near_one, away_mid, last_con)
    away_two, stay_two = weight_part(keep_plan, [turned_one], jobs_of(part_two), got_two)
    got_two = send(away_two, second_flip)
    got_grad = send(theirs_grad, core_flip)
    ours_plan, away_two, got_near_one, got_line_mid, got_last_con = tie(
        ours_plan, away_two, got_near_one, got_line_mid, got_last_con
    )
    line_one, away_one = line_split(plus(plus(stay_one[0], got_one[0]), got_near_one), place)
    got_line_one = send(away_one, line_near)
    last_mid = plus(line_mid[1], got_line_mid[1])
    got_last_mid = send(last_mid, line_far)
    ours_plan, away_one, last_mid = tie(ours_plan, away_one, last_mid)
    ours_grad, gain_more = leave(ours_plan, blocks, *leave_values)
    ours_grad, got_two, got_line_one, got_grad = tie(ours_grad, got_two, got_line_one, got_grad)
    near_two = plus(stay_two[1], got_two[1])
    got_near_two = send(near_two, first_flip)
    last_one = plus(line_one[1], got_line_one[1])
    got_last_one = send(last_one, line_far)

    def owned_part(line, got_line, got_last):
        return line[0].astype(F32) + got_line[0].astype(F32) + got_last.astype(F32)

    def square(value):
        return jnp.sum(value * value)

    owned_exp = owned_part(line_exp, got_line_exp, got_last_exp)
    owned_con = owned_part(line_con, got_line_con, got_last_con)[0]
    squares = square(owned_exp) + square(owned_con)
    half_rows = prompt // 2
    prompt_grad = both_groups(ours_grad, got_grad[:half_rows], core)
    own_branch = lax.dynamic_slice_in_dim(theirs_grad, half_rows + core * size, size, 0)
    other_branch = lax.dynamic_slice_in_dim(got_grad, half_rows + core * size, size, 0)
    branch_grad = both_groups(own_branch, other_branch, core)
    squares, got_near_two, prompt_grad, branch_grad = tie(squares, got_near_two, prompt_grad, branch_grad)
    line_two, away_two = line_split(plus(plus(stay_two[0], got_two[0]), got_near_two), place)
    got_line_two = send(away_two, line_near)
    whole_output = both_groups(own_output, other_output, core)
    prompt_output, branch_output = whole_output[:, :half_rows], whole_output[:, half_rows:]
    encoder_out = both_groups(own_encoder, other_encoder, core)
    owned_mid = owned_part(line_mid, got_line_mid, got_last_mid)
    squares = squares + square(owned_mid)
    squares, got_line_two, prompt_output, branch_output, encoder_out = tie(
        squares, got_line_two, prompt_output, branch_output, encoder_out
    )
    got_last_two = send(plus(line_two[1], got_line_two[1]), line_far)
    grad_bias = bias_gradient(
        jnp.concatenate([part_one[3], part_two[3]]), jnp.concatenate([part_one[4], part_two[4]]), buckets
    )
    owned_one = owned_part(line_one, got_line_one, got_last_one)
    squares = squares + square(owned_one)
    squares, grad_bias, got_last_two = tie(squares, grad_bias, got_last_two)
    owned_two = owned_part(line_two, got_line_two, got_last_two)
    squares = squares + square(owned_two)
    owned_self = jnp.concatenate([owned_one, owned_two], axis=2)

    owned = (
        jnp.concatenate([owned_self, owned_mid[1:4]], axis=0),
        jnp.stack([owned_mid[0], owned_mid[4]]),
        owned_exp,
        owned_con,
    )
    gain_back = jnp.sum(jnp.concatenate([(gain_one + gain_more)[None], gain_back]), axis=1)
    rest = jnp.concatenate([grad_bias.reshape(-1), squares[None]])
    shared = sum_everywhere(
        jnp.concatenate([gain_back, jnp.pad(rest, (0, D - rest.size))[None]]), place
    )
    gain_total = shared[:3]
    bias_total = shared[3, :grad_bias.size].reshape(grad_bias.shape)
    square_total = shared[3, grad_bias.size]
    grad_norm = jnp.sqrt(
        square_total + jnp.sum(gain_total * gain_total) + jnp.sum(bias_total * bias_total)
    )
    factor = jnp.minimum(1.0, CLIP / (grad_norm + 1e-06))
    weights = (projections, combiners, expansion, contraction, norm_gains, position_bias)
    firsts = (projections_first, combiners_first, expansion_first, contraction_first, gains_first, bias_first)
    seconds = (
        projections_second,
        combiners_second,
        expansion_second,
        contraction_second,
        gains_second,
        bias_second,
    )
    grads = owned + (gain_total, bias_total)
    states = [
        adam(weights[index], firsts[index], seconds[index], grads[index] * factor, RATES[index])
        for index in range(6)
    ]
    branch_shape = (2, 1, size, D)
    return (
        prompt_output,
        branch_output.reshape(branch_shape),
        prompt_grad,
        branch_grad.reshape(branch_shape),
        encoder_out,
        grad_norm,
        *states[0],
        *states[1],
        *states[2],
        *states[3],
        *states[4],
        *states[5],
        states[0][0].astype(BF),
        states[1][0].astype(BF),
        states[2][0].astype(BF),
        states[3][0].astype(BF),
    )


def solution(mesh):
    paired = mesh.shape["dp"] == 4 * SIDE * SIDE and mesh.shape["fsdp"] == 2
    return jax.shard_map(
        paired_body if paired else body,
        mesh=mesh,
        in_specs=(
            P("dp", "fsdp", None),
            P("dp", "fsdp", None, None),
            P("dp", "fsdp", None),
            P("dp", "fsdp"),
            P(),
            P("dp", "fsdp", None),
            P("dp", "fsdp", None, None),
            P(None, ("dp", "fsdp"), None),
            P(None, ("dp", "fsdp"), None),
            P(None, ("dp", "fsdp"), None),
            P(None, ("dp", "fsdp"), None),
            P(None, ("dp", "fsdp"), None),
            P(None, ("dp", "fsdp"), None),
            P(None, ("dp", "fsdp"), None),
            P(None, ("dp", "fsdp"), None),
            P(None, ("dp", "fsdp"), None),
            P(("dp", "fsdp"), None),
            P(("dp", "fsdp"), None),
            P(("dp", "fsdp"), None),
            P(),
            P(),
            P(),
            P(),
            P(),
            P(),
        ),
        out_specs=(
            P("dp", "fsdp", None),
            P("dp", "fsdp", None, None),
            P("dp", "fsdp", None),
            P("dp", "fsdp", None, None),
            P("dp", "fsdp", None),
            P(),
            P(None, ("dp", "fsdp"), None),
            P(None, ("dp", "fsdp"), None),
            P(None, ("dp", "fsdp"), None),
            P(None, ("dp", "fsdp"), None),
            P(None, ("dp", "fsdp"), None),
            P(None, ("dp", "fsdp"), None),
            P(None, ("dp", "fsdp"), None),
            P(None, ("dp", "fsdp"), None),
            P(None, ("dp", "fsdp"), None),
            P(("dp", "fsdp"), None),
            P(("dp", "fsdp"), None),
            P(("dp", "fsdp"), None),
            P(),
            P(),
            P(),
            P(),
            P(),
            P(),
            P(None, ("dp", "fsdp"), None),
            P(None, ("dp", "fsdp"), None),
            P(None, ("dp", "fsdp"), None),
            P(("dp", "fsdp"), None),
        ),
        check_vma=False,
    )
```

```python
import functools

import jax
import jax.numpy as jnp
from jax import lax
from jax.experimental import pallas as pl
from jax.experimental.pallas import tpu as pltpu
from jax.sharding import PartitionSpec as P

D = 1024
FF = 2816
HEADS = 16
HD = 64
BUCKETS = 32
PROMPT = 1024
STEP = 10


EPS = 1e-06
CLIP = 1.0
BETA_ONE = 0.9
BETA_TWO = 0.999
ADAM_EPS = 1e-08
DECAY = 0.01
RATES = (0.05, 0.3, 0.05, 0.03, 1.0, 1.0)
MASKED = -1e30


def rms_forward(stream, gain):
    scale = lax.rsqrt(jnp.mean(stream * stream, axis=-1, keepdims=True) + EPS)
    return (stream * scale * gain, scale)


def rms_backward(stream, scale, gain, upstream):
    weighted = upstream * gain
    grad_in = scale * weighted - stream * scale**3 * jnp.mean(
        weighted * stream, axis=-1, keepdims=True
    )
    return (grad_in, jnp.sum(upstream * stream * scale, axis=0))


def gelu_mix(gate, up_value):
    inner = 0.7978845608028654 * (gate + 0.044715 * gate * gate * gate)
    return 0.5 * gate * (1.0 + jnp.tanh(inner)) * up_value


def raw_scores(queries, key_rows):
    qh = queries.reshape(queries.shape[0], HEADS, HD)
    kh = key_rows.reshape(key_rows.shape[0], HEADS, HD)
    return jnp.einsum("rhd,khd->hrk", qh, kh, preferred_element_type=jnp.float32) * HD ** (-0.5)


def softmax_forward(scores, value_rows):
    row_max = jnp.max(scores, axis=-1, keepdims=True)
    expo = jnp.exp(scores - row_max)
    total = jnp.sum(expo, axis=-1, keepdims=True)
    probs = (expo / total).astype(jnp.bfloat16)
    vh = value_rows.reshape(value_rows.shape[0], HEADS, HD)
    mixed = jnp.einsum("hrk,khd->rhd", probs, vh, preferred_element_type=jnp.float32)
    return (mixed.reshape(mixed.shape[0], D).astype(jnp.bfloat16), row_max + jnp.log(total))


def softmax_backward(scores, logsum, queries, key_rows, value_rows, grad_mixed):
    probs = jnp.exp(scores - logsum)
    grad_heads = grad_mixed.reshape(grad_mixed.shape[0], HEADS, HD)
    vh = value_rows.reshape(value_rows.shape[0], HEADS, HD)
    kh = key_rows.reshape(key_rows.shape[0], HEADS, HD)
    qh = queries.reshape(queries.shape[0], HEADS, HD)
    grad_values = jnp.einsum(
        "hrk,rhd->khd", probs.astype(jnp.bfloat16), grad_heads, preferred_element_type=jnp.float32
    )
    grad_probs = jnp.einsum("rhd,khd->hrk", grad_heads, vh, preferred_element_type=jnp.float32)
    grad_scores = probs * (grad_probs - jnp.sum(probs * grad_probs, axis=-1, keepdims=True))
    scaled = (grad_scores * HD ** (-0.5)).astype(jnp.bfloat16)
    grad_queries = jnp.einsum("hrk,khd->rhd", scaled, kh, preferred_element_type=jnp.float32)
    grad_keys = jnp.einsum("hrk,rhd->khd", scaled, qh, preferred_element_type=jnp.float32)
    return (
        grad_queries.reshape(-1, D),
        grad_keys.reshape(-1, D),
        grad_values.reshape(-1, D),
        grad_scores,
    )


def hankel_bias(per_distance, shift, rows, keys):
    heads = per_distance.shape[0]
    front = jnp.broadcast_to(per_distance[:, :1], (heads, keys - 1))
    padded = jnp.concatenate([front, per_distance], axis=1)
    width = rows + keys - 1
    window = lax.dynamic_slice_in_dim(padded, shift, width, 1)
    tiled = jnp.tile(window, (1, rows + 1))[:, : rows * (width + 1)]
    skewed = tiled.reshape(heads, rows, width + 1)[:, :, :keys]
    return jnp.flip(skewed, axis=2)


def distance_grads(grad_block, shift, dist_count):
    heads, rows, keys = grad_block.shape
    width = rows + keys - 1
    flipped = jnp.flip(grad_block, axis=2)
    widened = jnp.concatenate(
        [flipped, jnp.zeros((heads, rows, width + 1 - keys), jnp.float32)], axis=2
    )
    flat = jnp.concatenate(
        [widened.reshape(heads, rows * (width + 1)), jnp.zeros((heads, keys - 1), jnp.float32)],
        axis=1,
    )
    window = jnp.sum(flat.reshape(heads, rows + 1, width), axis=1)
    padded = lax.dynamic_update_slice_in_dim(
        jnp.zeros((heads, dist_count + keys - 1), jnp.float32), window, shift, 1
    )
    head_part = jnp.sum(padded[:, :keys], axis=1, keepdims=True)
    return jnp.concatenate([head_part, padded[:, keys:]], axis=1)


def adam(weight, first, second, grad, rate):
    first_new = BETA_ONE * first + (1.0 - BETA_ONE) * grad
    second_new = BETA_TWO * second + (1.0 - BETA_TWO) * grad * grad
    mean_hat = first_new / (1.0 - BETA_ONE**STEP)
    square_hat = second_new / (1.0 - BETA_TWO**STEP)
    updated = weight - rate * (mean_hat / (jnp.sqrt(square_hat) + ADAM_EPS) + DECAY * weight)
    return (updated, first_new, second_new)


def body(
    prompt_states,
    branch_states,
    encoder_states,
    branch_start,
    bucket_table,
    prompt_cotangent,
    branch_cotangent,
    projections,
    projections_first,
    projections_second,
    combiners,
    combiners_first,
    combiners_second,
    expansion,
    expansion_first,
    expansion_second,
    contraction,
    contraction_first,
    contraction_second,
    norm_gains,
    gains_first,
    gains_second,
    position_bias,
    bias_first,
    bias_second,
):
    rows_here = prompt_states.shape[1]
    branch_count = branch_states.shape[1]
    branch_size = branch_states.shape[2]
    branch_rows = branch_count * branch_size
    dist_count = bucket_table.shape[0]
    offset = lax.axis_index("fsdp") * rows_here
    local_rows = jnp.arange(rows_here, dtype=jnp.int32)
    steps_in = jnp.arange(branch_size, dtype=jnp.int32)
    bucket_ids = jnp.arange(BUCKETS, dtype=jnp.int32)
    bucket_onehot = (bucket_table[:, None] == bucket_ids[None, :]).astype(jnp.float32)
    per_distance = jnp.dot(bucket_onehot, position_bias, precision=lax.Precision.HIGHEST).T
    own_bias = hankel_bias(per_distance, 0, branch_size, branch_size)
    shards = (
        projections.astype(jnp.bfloat16),
        combiners.astype(jnp.bfloat16),
        expansion.astype(jnp.bfloat16),
        contraction.astype(jnp.bfloat16),
    )

    def layout(starts):
        branch_pos = (starts[:, None] + steps_in[None, :]).reshape(-1)
        branch_seg = jnp.arange(branch_rows, dtype=jnp.int32) // branch_size
        query_pos = jnp.concatenate([offset + local_rows, branch_pos])
        query_seg = jnp.concatenate([jnp.full((rows_here,), -1, jnp.int32), branch_seg])
        query_limit = jnp.concatenate(
            [
                jnp.zeros((rows_here,), jnp.int32),
                jnp.broadcast_to(starts[:, None], (branch_count, branch_size)).reshape(-1),
            ]
        )
        key_pos = jnp.concatenate([jnp.arange(PROMPT, dtype=jnp.int32), branch_pos])
        key_seg = jnp.concatenate([jnp.full((PROMPT,), -1, jnp.int32), branch_seg])
        same_seg = (key_seg[None, :] == query_seg[:, None]) & (
            key_pos[None, :] <= query_pos[:, None]
        )
        from_prompt = (key_seg[None, :] == -1) & (key_pos[None, :] < query_limit[:, None])
        return same_seg | from_prompt

    def build_bias(starts):
        prompt_block = hankel_bias(per_distance, offset, rows_here, PROMPT)
        upper = jnp.concatenate(
            [prompt_block, jnp.zeros((HEADS, rows_here, branch_rows), jnp.float32)], axis=2
        )

        def branch_block(start):
            return hankel_bias(per_distance, start, branch_size, PROMPT)

        cross_blocks = lax.map(branch_block, starts)
        cross_blocks = jnp.transpose(cross_blocks, (1, 0, 2, 3)).reshape(HEADS, branch_rows, PROMPT)
        lower = jnp.concatenate(
            [cross_blocks, jnp.tile(own_bias, (1, branch_count, branch_count))], axis=2
        )
        return jnp.concatenate([upper, lower], axis=1)

    def bias_gradient(grad_scores, starts):
        total = distance_grads(grad_scores[:, :rows_here, :PROMPT], offset, dist_count)

        def add_branch(index, running):
            begin = rows_here + index * branch_size
            rows_block = lax.dynamic_slice_in_dim(grad_scores, begin, branch_size, 1)
            running = running + distance_grads(rows_block[:, :, :PROMPT], starts[index], dist_count)
            own_block = lax.dynamic_slice_in_dim(
                rows_block, PROMPT + index * branch_size, branch_size, 2
            )
            return running + distance_grads(own_block, 0, dist_count)

        total = lax.fori_loop(0, branch_count, add_branch, total)
        return jnp.dot(total, bucket_onehot, precision=lax.Precision.HIGHEST).T

    def group_step(running, item):
        big_sum, gain_sum, bias_sum = running
        prompt, branches, encoder, starts, prompt_cot, branch_cot = item
        weights = (
            lax.all_gather(shards[0], ("dp", "fsdp"), axis=1, tiled=True),
            lax.all_gather(shards[1], ("dp", "fsdp"), axis=1, tiled=True),
            lax.all_gather(shards[2], ("dp", "fsdp"), axis=1, tiled=True),
            lax.all_gather(shards[3], ("dp", "fsdp"), axis=0, tiled=True),
        )
        w_proj, w_comb, w_exp, w_con = weights
        pair_mask = layout(starts)
        stream = jnp.concatenate(
            [prompt.astype(jnp.float32), branches.reshape(-1, D).astype(jnp.float32)], axis=0
        )
        normed_one, scale_one = rms_forward(stream, norm_gains[0])
        input_one = normed_one.astype(jnp.bfloat16)
        self_rows = jnp.einsum(
            "td,kde->kte", input_one, w_proj[:3], preferred_element_type=jnp.float32
        ).astype(jnp.bfloat16)
        prompt_keys, prompt_values = (
            lax.all_gather(self_rows[1, :rows_here], "fsdp", axis=0, tiled=True),
            lax.all_gather(self_rows[2, :rows_here], "fsdp", axis=0, tiled=True),
        )
        encoder_rows = jnp.einsum(
            "td,kde->kte", encoder, w_proj[4:], preferred_element_type=jnp.float32
        ).astype(jnp.bfloat16)
        cross_keys, cross_values = (
            lax.all_gather(encoder_rows[0], "fsdp", axis=0, tiled=True),
            lax.all_gather(encoder_rows[1], "fsdp", axis=0, tiled=True),
        )
        key_rows = jnp.concatenate([prompt_keys, self_rows[1, rows_here:]], axis=0)
        value_rows = jnp.concatenate([prompt_values, self_rows[2, rows_here:]], axis=0)
        pair_bias = build_bias(starts)
        scores_one = jnp.where(
            pair_mask[None], raw_scores(self_rows[0], key_rows) + pair_bias, MASKED
        )
        mixed_one, logsum_one = softmax_forward(scores_one, value_rows)
        after_one = stream + jnp.dot(mixed_one, w_comb[0], preferred_element_type=jnp.float32)
        normed_two, scale_two = rms_forward(after_one, norm_gains[1])
        input_two = normed_two.astype(jnp.bfloat16)
        query_two = jnp.dot(input_two, w_proj[3], preferred_element_type=jnp.float32).astype(
            jnp.bfloat16
        )
        scores_two = raw_scores(query_two, cross_keys)
        mixed_two, logsum_two = softmax_forward(scores_two, cross_values)
        after_two = after_one + jnp.dot(mixed_two, w_comb[1], preferred_element_type=jnp.float32)
        normed_three, scale_three = rms_forward(after_two, norm_gains[2])
        input_three = normed_three.astype(jnp.bfloat16)
        gate_up = jnp.einsum("td,kdf->ktf", input_three, w_exp, preferred_element_type=jnp.float32)
        hidden, mix_pull = jax.vjp(gelu_mix, gate_up[0], gate_up[1])
        hidden_low = hidden.astype(jnp.bfloat16)
        output = after_two + jnp.dot(hidden_low, w_con, preferred_element_type=jnp.float32)
        again = (
            lax.all_gather(shards[0], ("dp", "fsdp"), axis=1, tiled=True),
            lax.all_gather(shards[1], ("dp", "fsdp"), axis=1, tiled=True),
            lax.all_gather(shards[2], ("dp", "fsdp"), axis=1, tiled=True),
            lax.all_gather(shards[3], ("dp", "fsdp"), axis=0, tiled=True),
        )
        b_proj, b_comb, b_exp, b_con = again
        upstream = jnp.concatenate(
            [prompt_cot.astype(jnp.float32), branch_cot.reshape(-1, D).astype(jnp.float32)], axis=0
        )
        upstream_low = upstream.astype(jnp.bfloat16)
        grad_con = jnp.einsum(
            "tf,td->fd", hidden_low, upstream_low, preferred_element_type=jnp.float32
        )
        grad_hidden = jnp.einsum(
            "td,fd->tf", upstream_low, b_con, preferred_element_type=jnp.float32
        )
        grad_gate, grad_up = mix_pull(grad_hidden)
        gate_low = jnp.stack([grad_gate, grad_up]).astype(jnp.bfloat16)
        grad_exp = jnp.einsum(
            "td,ktf->kdf", input_three, gate_low, preferred_element_type=jnp.float32
        )
        grad_three = jnp.einsum("ktf,kdf->td", gate_low, b_exp, preferred_element_type=jnp.float32)
        back_three, gain_three = rms_backward(after_two, scale_three, norm_gains[2], grad_three)
        grad_after_two = upstream + back_three
        cross_low = grad_after_two.astype(jnp.bfloat16)
        grad_comb_two = jnp.einsum(
            "te,td->ed", mixed_two, cross_low, preferred_element_type=jnp.float32
        )
        grad_mixed_two = jnp.einsum(
            "td,ed->te", cross_low, b_comb[1], preferred_element_type=jnp.float32
        ).astype(jnp.bfloat16)
        grad_query_two, grad_keys_two, grad_values_two, unused_scores = softmax_backward(
            scores_two, logsum_two, query_two, cross_keys, cross_values, grad_mixed_two
        )
        own_keys, own_values = (
            lax.psum_scatter(
                grad_keys_two.astype(jnp.bfloat16), "fsdp", scatter_dimension=0, tiled=True
            ).astype(jnp.float32),
            lax.psum_scatter(
                grad_values_two.astype(jnp.bfloat16), "fsdp", scatter_dimension=0, tiled=True
            ).astype(jnp.float32),
        )
        encoder_low = jnp.stack([own_keys, own_values]).astype(jnp.bfloat16)
        grad_cross_proj = jnp.einsum(
            "td,kte->kde", encoder, encoder_low, preferred_element_type=jnp.float32
        )
        encoder_grad = jnp.einsum(
            "kte,kde->td", encoder_low, b_proj[4:], preferred_element_type=jnp.float32
        )
        query_two_low = grad_query_two.astype(jnp.bfloat16)
        grad_query_proj = jnp.einsum(
            "td,te->de", input_two, query_two_low, preferred_element_type=jnp.float32
        )
        grad_two = jnp.einsum(
            "te,de->td", query_two_low, b_proj[3], preferred_element_type=jnp.float32
        )
        back_two, gain_two = rms_backward(after_one, scale_two, norm_gains[1], grad_two)
        grad_after_one = grad_after_two + back_two
        self_low = grad_after_one.astype(jnp.bfloat16)
        grad_comb_one = jnp.einsum(
            "te,td->ed", mixed_one, self_low, preferred_element_type=jnp.float32
        )
        grad_mixed_one = jnp.einsum(
            "td,ed->te", self_low, b_comb[0], preferred_element_type=jnp.float32
        ).astype(jnp.bfloat16)
        grad_query, grad_keys, grad_values, grad_scores = softmax_backward(
            scores_one, logsum_one, self_rows[0], key_rows, value_rows, grad_mixed_one
        )
        prompt_key_grad, prompt_value_grad = (
            lax.psum_scatter(
                grad_keys[:PROMPT].astype(jnp.bfloat16), "fsdp", scatter_dimension=0, tiled=True
            ).astype(jnp.float32),
            lax.psum_scatter(
                grad_values[:PROMPT].astype(jnp.bfloat16), "fsdp", scatter_dimension=0, tiled=True
            ).astype(jnp.float32),
        )
        self_grad_low = jnp.stack(
            [
                grad_query,
                jnp.concatenate([prompt_key_grad, grad_keys[PROMPT:]], axis=0),
                jnp.concatenate([prompt_value_grad, grad_values[PROMPT:]], axis=0),
            ]
        ).astype(jnp.bfloat16)
        grad_self_proj = jnp.einsum(
            "td,kte->kde", input_one, self_grad_low, preferred_element_type=jnp.float32
        )
        grad_one = jnp.einsum(
            "kte,kde->td", self_grad_low, b_proj[:3], preferred_element_type=jnp.float32
        )
        back_one, gain_one = rms_backward(stream, scale_one, norm_gains[0], grad_one)
        stream_grad = grad_after_one + back_one
        grad_bias = bias_gradient(grad_scores, starts)
        group_big = (
            jnp.concatenate([grad_self_proj, grad_query_proj[None], grad_cross_proj], axis=0),
            jnp.stack([grad_comb_one, grad_comb_two]),
            grad_exp,
            grad_con,
        )
        big_sum = jax.tree.map(jnp.add, big_sum, group_big)
        gain_sum = gain_sum + jnp.stack([gain_one, gain_two, gain_three])
        bias_sum = bias_sum + grad_bias
        results = (
            output[:rows_here].astype(jnp.bfloat16),
            output[rows_here:].reshape(branch_count, branch_size, D).astype(jnp.bfloat16),
            stream_grad[:rows_here],
            stream_grad[rows_here:].reshape(branch_count, branch_size, D),
            encoder_grad,
        )
        return ((big_sum, gain_sum, bias_sum), results)

    big_start = (
        jnp.zeros((6, D, D), jnp.float32),
        jnp.zeros((2, D, D), jnp.float32),
        jnp.zeros((2, D, FF), jnp.float32),
        jnp.zeros((FF, D), jnp.float32),
    )
    start_state = (
        big_start,
        jnp.zeros(norm_gains.shape, jnp.float32),
        jnp.zeros(position_bias.shape, jnp.float32),
    )
    final_state, results = lax.scan(
        group_step,
        start_state,
        (
            prompt_states,
            branch_states,
            encoder_states,
            branch_start,
            prompt_cotangent,
            branch_cotangent,
        ),
    )
    big_sum, gain_sum, bias_sum = final_state
    owned = (
        lax.psum_scatter(big_sum[0], ("dp", "fsdp"), scatter_dimension=1, tiled=True),
        lax.psum_scatter(big_sum[1], ("dp", "fsdp"), scatter_dimension=1, tiled=True),
        lax.psum_scatter(big_sum[2], ("dp", "fsdp"), scatter_dimension=1, tiled=True),
        lax.psum_scatter(big_sum[3], ("dp", "fsdp"), scatter_dimension=0, tiled=True),
    )
    squares = sum((jnp.sum(grad * grad) for grad in owned))
    gain_total, bias_total, square_total = lax.psum((gain_sum, bias_sum, squares), ("dp", "fsdp"))
    grad_norm = jnp.sqrt(
        square_total + jnp.sum(gain_total * gain_total) + jnp.sum(bias_total * bias_total)
    )
    factor = jnp.minimum(1.0, CLIP / (grad_norm + 1e-06))
    params = (projections, combiners, expansion, contraction, norm_gains, position_bias)
    firsts = (
        projections_first,
        combiners_first,
        expansion_first,
        contraction_first,
        gains_first,
        bias_first,
    )
    seconds = (
        projections_second,
        combiners_second,
        expansion_second,
        contraction_second,
        gains_second,
        bias_second,
    )
    grads = (owned[0], owned[1], owned[2], owned[3], gain_total, bias_total)
    states = [
        adam(params[index], firsts[index], seconds[index], grads[index] * factor, RATES[index])
        for index in range(6)
    ]
    return (
        results[0],
        results[1],
        results[2],
        results[3],
        results[4],
        grad_norm,
        states[0][0],
        states[0][1],
        states[0][2],
        states[1][0],
        states[1][1],
        states[1][2],
        states[2][0],
        states[2][1],
        states[2][2],
        states[3][0],
        states[3][1],
        states[3][2],
        states[4][0],
        states[4][1],
        states[4][2],
        states[5][0],
        states[5][1],
        states[5][2],
        states[0][0].astype(jnp.bfloat16),
        states[1][0].astype(jnp.bfloat16),
        states[2][0].astype(jnp.bfloat16),
        states[3][0].astype(jnp.bfloat16),
    )


BF = jnp.bfloat16
F32 = jnp.float32
PAIR = 2 * HD
PAIRS = HEADS // 2
TILE = 256


def params(limit=60):
    return pltpu.CompilerParams(vmem_limit_bytes=limit * 1024 * 1024)


def cost(microseconds):
    return pl.CostEstimate(flops=int(microseconds), bytes_accessed=1, transcendentals=0)


def dot(left, right, contract):
    return lax.dot_general(
        left, right, ((contract[:1], contract[1:]), ((), ())), preferred_element_type=F32
    )


def bias_rows(flipped, starts, prompt, size):
    base = jnp.pad(flipped[:, size - 1:], ((0, 0), (0, TILE - 1)), constant_values=MASKED)
    padded = jnp.pad(flipped, ((0, 0), (1, prompt)))
    rows = [
        lax.dynamic_slice_in_dim(padded, prompt - starts[index], prompt + size, 1) for index in range(2)
    ]
    return base[:, None], jnp.stack(rows, axis=1)[:, :, None]


def fill_bias(prompt, size, starts_ref, base, branches, strip_ref, cross_ref):
    wide = jnp.broadcast_to(base, (TILE, prompt + TILE))
    strip_ref[...] = pltpu.roll(wide, 0, 1, stride=1, stride_axis=0)[:, TILE:]
    place = lax.broadcasted_iota(jnp.int32, (size, prompt), 1)
    for index, branch in enumerate(branches):
        row = jnp.broadcast_to(branch, (size, prompt + size))
        skewed = pltpu.roll(row, 0, 1, stride=1, stride_axis=0)[:, size:]
        cross_ref[index * size:(index + 1) * size] = jnp.where(place < starts_ref[index], skewed, MASKED)


def lanes_of(value, half):
    lane = lax.broadcasted_iota(jnp.int32, value.shape, 1)
    return jnp.where((lane >= HD) if half else (lane < HD), value, jnp.zeros_like(value))


def probs_width(prompt, size):
    blocks = prompt // TILE
    return TILE * blocks * (blocks + 1) // 2 + prompt + size


def fold(grid):
    rows, width = grid.shape
    while rows > 1:
        rows //= 2
        grid = grid[:rows] + pltpu.roll(grid[rows:], width - rows, 1)
    return grid


def self_kernel(prompt, size, more, starts_ref, q_ref, k_ref, v_ref, base_ref, branch_ref, *refs):
    o_ref, e_ref, inv_ref, s_ref, strips_ref, crosses_ref = refs[more:]
    blocks = prompt // TILE
    begins = [TILE * i * (i + 1) // 2 for i in range(blocks + 1)]
    lane = lax.broadcasted_iota(jnp.int32, (TILE, PAIR), 1)
    for half in range(2):
        strip_ref, cross_ref = strips_ref.at[half], crosses_ref.at[half]
        branches = [branch_ref[half, index] for index in range(2)]
        fill_bias(prompt, size, starts_ref, base_ref[half], branches, strip_ref, cross_ref)
        for i in range(blocks + 1):
            rows = slice(i * TILE, (i + 1) * TILE)
            q = lanes_of(q_ref[rows] * BF(HD ** -0.5), half)
            tiles = []
            for j in range(min(i + 1, blocks)):
                keys = slice(j * TILE, (j + 1) * TILE)
                begin = prompt - (i + 1 - j) * TILE
                bias = strip_ref.at[:, begin:begin + TILE] if i < blocks else cross_ref.at[:, keys]
                tiles.append((keys, bias))
            top = None
            for j, (keys, bias) in enumerate(tiles):
                s = dot(q, k_ref[keys], (1, 1)) + bias[...]
                s_ref[:, j * TILE:(j + 1) * TILE] = s
                high = jnp.maximum(s[:, :PAIR], s[:, PAIR:])
                top = high if top is None else jnp.maximum(top, high)
            if i == blocks:
                near = strip_ref[:size, prompt - TILE:prompt - TILE + size]
                own = jnp.concatenate(
                    [
                        dot(q[b * size:(b + 1) * size], k_ref[prompt + b * size:prompt + (b + 1) * size], (1, 1)) + near
                        for b in range(2)
                    ],
                    axis=0,
                )
                top = jnp.maximum(top, own)
            top = jnp.max(top, axis=1, keepdims=True)
            total = None
            out = None
            for j, (keys, _) in enumerate(tiles):
                e = jnp.exp(s_ref[:, j * TILE:(j + 1) * TILE] - top)
                part = e[:, :PAIR] + e[:, PAIR:]
                total = part if total is None else total + part
                low = e.astype(BF)
                e_ref[half, :, begins[i] + j * TILE:begins[i] + (j + 1) * TILE] = low
                part = dot(low, v_ref[keys], (1, 0))
                out = part if out is None else out + part
            if i == blocks:
                e = jnp.exp(own - top)
                total = total + e
                low = e.astype(BF)
                e_ref[half, :, begins[i] + prompt:] = low
                out = out + jnp.concatenate(
                    [
                        dot(low[b * size:(b + 1) * size], v_ref[prompt + b * size:prompt + (b + 1) * size], (1, 0))
                        for b in range(2)
                    ],
                    axis=0,
                )
            inverse = 1.0 / jnp.sum(total, axis=1, keepdims=True)
            out = out * inverse
            if half == 0:
                o_ref[rows] = out.astype(BF)
                inv_ref[rows] = jnp.broadcast_to(inverse, (TILE, PAIR))
            else:
                o_ref[rows] = jnp.where(lane >= HD, out.astype(BF), o_ref[rows])
                inv_ref[rows] = jnp.where(lane >= HD, inverse, inv_ref[rows])


def self_forward(qkv, base, branch, starts, prompt, size, first, pairs, before=None):
    count = prompt + 2 * size
    width = probs_width(prompt, size)
    column = lambda part: pl.BlockSpec((None, count, PAIR), lambda j, s, part=part: (part, 0, first + j))
    flat = pl.BlockSpec((count, PAIR), lambda j, s: (0, first + j))
    bias = pltpu.VMEM((2, TILE, prompt), F32)
    more = [] if before is None else list(before)
    return pl.pallas_call(
        functools.partial(self_kernel, prompt, size, len(more)),
        grid_spec=pltpu.PrefetchScalarGridSpec(
            num_scalar_prefetch=1,
            grid=(pairs,),
            in_specs=[
                column(0),
                column(1),
                column(2),
                pl.BlockSpec((2, 1, prompt + TILE), lambda j, s: (first + j, 0, 0)),
                pl.BlockSpec((2, 2, 1, prompt + size), lambda j, s: (first + j, 0, 0, 0)),
            ]
            + [pl.BlockSpec(memory_space=pl.ANY)] * len(more),
            out_specs=[flat, pl.BlockSpec((2, TILE, width), lambda j, s: (first + j, 0, 0)), flat],
            scratch_shapes=[pltpu.VMEM((TILE, prompt), F32), bias, bias],
        ),
        out_shape=[
            jax.ShapeDtypeStruct((count, D), BF),
            jax.ShapeDtypeStruct((HEADS, TILE, width), BF),
            jax.ShapeDtypeStruct((count, D), F32),
        ],
        input_output_aliases={6 + index: index for index in range(len(more))},
        compiler_params=params(),
        cost_estimate=cost(6 * pairs),
        name="self_forward",
    )(starts, qkv, qkv, qkv, base, branch, *more)


def self_back_kernel(prompt, size, q_ref, k_ref, v_ref, do_ref, o_ref, e_ref, inv_ref, dq_ref, dk_ref, dv_ref,
                     strip_ref, cross_ref, sums, far_sums, dk_acc, dv_acc):
    blocks = prompt // TILE
    begins = [TILE * i * (i + 1) // 2 for i in range(blocks + 1)]
    scale = BF(HD ** -0.5)
    lane = lax.broadcasted_iota(jnp.int32, (TILE, PAIR), 1)
    dk_acc[...] = jnp.zeros_like(dk_acc)
    dv_acc[...] = jnp.zeros_like(dv_acc)
    for half in range(2):
        sums[...] = jnp.zeros_like(sums)

        def gather(left, grads, keys, acc):
            acc[half * HD:(half + 1) * HD, keys] += dot(grads[half * HD:(half + 1) * HD], left, (1, 0))

        for i in range(blocks + 1):
            rows = slice(i * TILE, (i + 1) * TILE)
            scaled = do_ref[rows].astype(F32) * inv_ref[rows]
            do = lanes_of(scaled.astype(BF), half)
            part = lanes_of(do.astype(F32) * o_ref[rows].astype(F32), half)
            drop = jnp.sum(part, axis=1, keepdims=True)
            do_left, q_left = do.T, (q_ref[rows] * scale).T
            dq = None
            for j in range(min(i + 1, blocks)):
                keys = slice(j * TILE, (j + 1) * TILE)
                low = e_ref[half, :, begins[i] + j * TILE:begins[i] + (j + 1) * TILE]
                ds = low.astype(F32) * (dot(do, v_ref[keys], (1, 1)) - drop)
                if i < blocks:
                    begin = TILE + prompt - (i + 1 - j) * TILE
                    sums[:, begin:begin + TILE] += ds
                else:
                    far_sums[:, size + j * TILE:size + (j + 1) * TILE] = ds
                down = ds.astype(BF)
                part = dot(down, k_ref[keys], (1, 0))
                dq = part if dq is None else dq + part
                gather(down, q_left, keys, dk_acc)
                gather(low, do_left, keys, dv_acc)
            if i == blocks:
                low = e_ref[half, :, begins[i] + prompt:]
                parts = [slice(b * size, (b + 1) * size) for b in range(2)]
                keys = [slice(prompt + b * size, prompt + (b + 1) * size) for b in range(2)]
                own = jnp.concatenate([dot(do[parts[b]], v_ref[keys[b]], (1, 1)) for b in range(2)], axis=0)
                ds = low.astype(F32) * (own - drop)
                sums[:size, prompt:prompt + size] += ds[:size] + ds[size:]
                down = ds.astype(BF)
                dq = dq + jnp.concatenate(
                    [dot(down[parts[b]], k_ref[keys[b]], (1, 0)) for b in range(2)], axis=0
                )
                for b in range(2):
                    gather(down[parts[b]], q_left[:, parts[b]], keys[b], dk_acc)
                    gather(low[parts[b]], do_left[:, parts[b]], keys[b], dv_acc)
            dq = (dq * (HD ** -0.5)).astype(BF)
            dq_ref[rows] = dq if half == 0 else jnp.where(lane >= HD, dq, dq_ref[rows])
        strip_ref[half] = fold(sums[...])
        for b in range(2):
            wide = far_sums[b * size:(b + 1) * size]
            place = lax.broadcasted_iota(jnp.int32, wide.shape, 1)
            cross_ref[half, b] = fold(jnp.where(place < size, 0.0, wide))
    dk_ref[...] = dk_acc[...].T.astype(BF)
    dv_ref[...] = dv_acc[...].T.astype(BF)


def self_backward(qkv, do, mixed, expos, inverse, prompt, size, first, pairs):
    count = prompt + 2 * size
    width = probs_width(prompt, size)
    column = lambda part: pl.BlockSpec((None, count, PAIR), lambda j, part=part: (part, 0, first + j))
    flat = pl.BlockSpec((count, PAIR), lambda j: (0, j))
    given = pl.BlockSpec((count, PAIR), lambda j: (0, first + j))
    acc = pltpu.VMEM((PAIR, count), F32)
    return pl.pallas_call(
        functools.partial(self_back_kernel, prompt, size),
        grid=(pairs,),
        in_specs=[
            column(0),
            column(1),
            column(2),
            given,
            given,
            pl.BlockSpec((2, TILE, width), lambda j: (first + j, 0, 0)),
            given,
        ],
        out_specs=[
            flat,
            flat,
            flat,
            pl.BlockSpec((2, 1, prompt + TILE), lambda j: (j, 0, 0)),
            pl.BlockSpec((2, 2, 1, prompt + size), lambda j: (j, 0, 0, 0)),
        ],
        out_shape=[
            jax.ShapeDtypeStruct((count, pairs * PAIR), BF),
            jax.ShapeDtypeStruct((count, pairs * PAIR), BF),
            jax.ShapeDtypeStruct((count, pairs * PAIR), BF),
            jax.ShapeDtypeStruct((2 * pairs, 1, prompt + TILE), F32),
            jax.ShapeDtypeStruct((2 * pairs, 2, 1, prompt + size), F32),
        ],
        scratch_shapes=[pltpu.VMEM((TILE, prompt + TILE), F32), pltpu.VMEM((2 * size, prompt + size), F32), acc, acc],
        compiler_params=params(),
        cost_estimate=cost(8 * pairs),
        name="self_backward",
    )(qkv, qkv, qkv, do, mixed, expos, inverse)


def distance_buckets(flipped, starts, prompt, size):
    bucket_ids = jnp.arange(BUCKETS, dtype=jnp.int32)
    whole = jnp.pad(flipped[size - 1:], (0, TILE - 1), constant_values=-1)
    padded = jnp.pad(flipped, (1, prompt), constant_values=-1)
    rows = [lax.dynamic_slice_in_dim(padded, prompt - starts[index], prompt + size, 0) for index in range(2)]
    order = jnp.concatenate([whole] + rows)
    return (order[:, None] == bucket_ids[None, :]).astype(F32)


def bias_gradient(strip, cross, buckets):
    sums = jnp.concatenate([strip[:, 0], cross[:, 0, 0], cross[:, 1, 0]], axis=1)
    return jnp.dot(sums, buckets, precision=lax.Precision.HIGHEST).T


def mlp_kernel(core_ref, x_ref, a_ref, a_t, dy_ref, wg_ref, wu_ref, wd_ref, out_ref, da_ref, away_ref, keep_ref,
               away_con_ref, keep_con_ref, y_ref, hid, dgate, dup, dwd, sem):
    count = a_ref.shape[0]
    step = pl.program_id(0)

    @pl.when(step == 0)
    def _():
        copy = pltpu.make_async_copy(x_ref, y_ref, sem)
        copy.start()
        da_ref[...] = jnp.zeros_like(da_ref)
        copy.wait()

    slope = 0.7978845608028654
    for i in range(0, count, TILE):
        rows = slice(i, i + TILE)
        g = dot(a_ref[rows], wg_ref[...], (1, 0))
        u = dot(a_ref[rows], wu_ref[...], (1, 0))
        dh = dot(dy_ref[rows], wd_ref[...], (1, 1))
        square = g * g
        th = jnp.tanh(slope * g * (1.0 + 0.044715 * square))
        half = 0.5 + 0.5 * th
        gelu = g * half
        slant = half + (0.5 * slope) * g * (1.0 - th * th) * (1.0 + 0.134145 * square)
        low = (gelu * u).astype(BF)
        dg = (dh * u * slant).astype(BF)
        du = (dh * gelu).astype(BF)
        hid[rows] = low
        dgate[rows] = dg
        dup[rows] = du
        y_ref[rows] += dot(low, wd_ref[...], (1, 0))
        da_ref[rows] += dot(dg, wg_ref[...], (1, 1)) + dot(du, wu_ref[...], (1, 1))
    dwd[pl.ds(pl.multiple_of(step * TILE, TILE), TILE)] = dot(hid[...], dy_ref[...], (0, 0))
    core = core_ref[0]
    for index, grad in enumerate((dgate, dup)):
        blocks = dot(a_t[...], grad[...], (1, 0)).astype(BF).reshape(D // 64, 2, 32, TILE)
        away_ref[index] = jnp.where(core == 0, blocks[:, 1], blocks[:, 0])
        keep_ref[index] = jnp.where(core == 0, blocks[:, 0], blocks[:, 1])

    @pl.when(step == pl.num_programs(0) - 1)
    def _():
        for i in range(0, count, TILE):
            out_ref[i:i + TILE] = y_ref[i:i + TILE].astype(BF)
        pairs, m, _ = keep_con_ref.shape
        for index in range(pairs):
            even = dwd[2 * index * m:(2 * index + 1) * m].astype(BF)
            odd = dwd[(2 * index + 1) * m:(2 * index + 2) * m].astype(BF)
            away_con_ref[index] = jnp.where(core == 0, odd, even)
            keep_con_ref[index] = jnp.where(core == 0, even, odd)


def mlp(core, after_two, inputs, turned, low_up, w_gate, w_up, w_con, owners):
    count = inputs.shape[0]
    hidden = w_gate.shape[1]
    m = hidden // owners
    once = pl.Buffered(1)
    flat = pl.BlockSpec((count, D), lambda t, c: (0, 0), pipeline_mode=once)
    column = pl.BlockSpec((D, TILE), lambda t, c: (0, t))
    row = pl.BlockSpec((TILE, D), lambda t, c: (t, 0))
    shared = pl.BlockSpec((2, D // 64, 32, TILE), lambda t, c: (0, 0, 0, t))
    part = jax.ShapeDtypeStruct((2, D // 64, 32, hidden), BF)
    con = pl.BlockSpec((owners // 2, m, D), lambda t, c: (0, 0, 0), pipeline_mode=once)
    con_part = jax.ShapeDtypeStruct((owners // 2, m, D), BF)
    tile = pltpu.VMEM((count, TILE), BF)
    return pl.pallas_call(
        mlp_kernel,
        grid_spec=pltpu.PrefetchScalarGridSpec(
            num_scalar_prefetch=1,
            grid=(hidden // TILE,),
            in_specs=[pl.BlockSpec(memory_space=pl.ANY), flat, whole_block(turned), flat, column, column, row],
            out_specs=[flat, flat, shared, shared, con, con],
            scratch_shapes=[
                pltpu.VMEM((count, D), F32),
                tile,
                tile,
                tile,
                pltpu.VMEM((hidden, D), F32),
                pltpu.SemaphoreType.DMA,
            ],
        ),
        out_shape=[
            jax.ShapeDtypeStruct((count, D), BF),
            jax.ShapeDtypeStruct((count, D), F32),
            part,
            part,
            con_part,
            con_part,
        ],
        compiler_params=params(),
        cost_estimate=cost(85),
        name="mlp",
    )(core, after_two, inputs, turned, low_up, w_gate, w_up, w_con)


def part_kernel(jobs, counts, plan_ref, *refs):
    lefts = refs[:1 + max(jobs)]
    rights = refs[len(lefts):len(lefts) + sum(counts)]
    rest = refs[len(lefts) + len(rights):]

    def finish(index, value):
        if len(rest) == 1:
            rest[0][index] = value.astype(BF).reshape(rest[0].shape[1:])
        else:
            got, away, stay, held = rest
            held[...] = (value + got[index].astype(F32).reshape(value.shape)).astype(BF).reshape(held.shape)
            for slot in range(2):
                away[slot, :, index] = held[:, plan_ref[1 + slot]]
                stay[slot, :, index] = held[:, plan_ref[3 + slot]]

    first = 0
    for index, left in enumerate(jobs):
        if counts[index] == 1:
            finish(index, dot(lefts[left][...], rights[first][...], (1, 0)))
        else:
            for tile in range(counts[index]):
                @pl.when(pl.program_id(0) == tile)
                def _(index=index, left=left, right=rights[first + tile]):
                    finish(index, dot(lefts[left][...], right[...], (1, 0)))
        first += counts[index]


def weight_part(plan, lefts, jobs, got=None):
    rights = [right if isinstance(right, list) else [right] for _, right in jobs]
    columns = sum(right.shape[1] for right in rights[0])
    counts = [len(right) for right in rights]
    m = 32

    def side(left):
        return pl.BlockSpec((None,) + left.shape[1:], lambda t, p: (p[0], 0, 0), pipeline_mode=pl.Buffered(1))

    def tile(right):
        return pl.BlockSpec((right.shape[0], TILE), lambda t, p: (0, t) if right.shape[1] > TILE else (0, 0))

    shared = pl.BlockSpec((len(jobs), D // 64, m, TILE), lambda t, p: (0, 0, 0, t))
    part = jax.ShapeDtypeStruct((len(jobs), D // 64, m, columns), BF)
    split = pl.BlockSpec((2, LINE, len(jobs), m, TILE), lambda t, p: (0, 0, 0, 0, t))
    half = jax.ShapeDtypeStruct((2, LINE, len(jobs), m, columns), BF)
    return pl.pallas_call(
        functools.partial(part_kernel, [left for left, _ in jobs], counts),
        grid_spec=pltpu.PrefetchScalarGridSpec(
            num_scalar_prefetch=1,
            grid=(columns // TILE,),
            in_specs=[side(left) for left in lefts]
            + [tile(value) for right in rights for value in right]
            + ([] if got is None else [shared]),
            out_specs=shared if got is None else [split, split],
            scratch_shapes=[] if got is None else [pltpu.VMEM((LINE, SIDE * SIDE, m, TILE), BF)],
        ),
        out_shape=part if got is None else [half, half],
        compiler_params=params(),
        cost_estimate=cost(2),
        name="weight_part",
    )(plan, *lefts, *(value for right in rights for value in right), *([] if got is None else [got]))


def root(value):
    return lax.rsqrt(jnp.mean(value * value, axis=1, keepdims=True) + EPS)


def normed(value, gain):
    return (value * root(value) * gain).astype(BF)


def norm_back(value, gain, upstream):
    scale = root(value)
    weighted = upstream * gain
    grad = scale * weighted - value * (scale * scale * scale) * jnp.mean(weighted * value, axis=1, keepdims=True)
    terms = upstream * value * scale
    return grad, jnp.sum(terms.reshape(-1, 8, D), axis=0)


def whole_block(value):
    zeros = (0,) * len(value.shape)
    return pl.BlockSpec(value.shape, lambda *index: zeros, pipeline_mode=pl.Buffered(1))


def row_block(columns=D):
    return pl.BlockSpec((TILE, columns), lambda i: (i, 0))


def turned_block():
    return pl.BlockSpec((D, TILE), lambda i: (0, i))


def sided_block():
    return pl.BlockSpec((2, D // 2, TILE), lambda i: (0, 0, i))


def put_sides(ref, value):
    columns = value.T.reshape(D // 64, 2, 32, value.shape[0])
    for side in range(2):
        ref[side] = columns[:, side].reshape(D // 2, value.shape[0])


def fetch(slots_ref, sources, held, sems, index):
    copies = []
    for number, source in enumerate(sources):
        for half in range(2):
            spot = slots_ref[2 * number + half, 0]
            side = slots_ref[2 * number + half, 1]
            copies.append(
                pltpu.make_async_copy(
                    source.at[half, index], held.at[index, :, spot, side], sems.at[index, 2 * number + half]
                )
            )
    return copies


def held_weight(held, index):
    return held[index].reshape(D, D)


def arrive(slots_ref, sources, held, in_sems, count):
    @pl.when(pl.program_id(0) == 0)
    def _():
        for index in range(count):
            for copy in fetch(slots_ref, sources, held, in_sems, index):
                copy.start()


def ready(slots_ref, sources, held, outs, in_sems, out_sems, index):
    @pl.when(pl.program_id(0) == 0)
    def _():
        for copy in fetch(slots_ref, sources, held, in_sems, index):
            copy.wait()
        pltpu.make_async_copy(held.at[index], outs[index], out_sems.at[index]).start()


def settle(held, outs, out_sems):
    @pl.when(pl.program_id(0) == pl.num_programs(0) - 1)
    def _():
        for index, out in enumerate(outs):
            pltpu.make_async_copy(held.at[index], out, out_sems.at[index]).wait()


def weight_specs(sources):
    _, count, line, rows, columns = sources[0].shape
    shape = (line, SIDE * SIDE, 2, rows, columns)
    anywhere = pl.BlockSpec(memory_space=pl.ANY)
    return (
        [pl.BlockSpec(memory_space=pltpu.SMEM)] + [anywhere] * 4,
        [anywhere] * count,
        [jax.ShapeDtypeStruct(shape, BF)] * count,
        [
            pltpu.VMEM((count,) + shape, BF),
            pltpu.SemaphoreType.DMA((count, 8)),
            pltpu.SemaphoreType.DMA((count,)),
        ],
    )


def enter_kernel(slots_ref, *refs):
    sources = refs[:4]
    x_ref, gain_ref, a_ref, qkv_ref = refs[4:8]
    outs = refs[8:11]
    held, in_sems, out_sems = refs[11:]
    arrive(slots_ref, sources, held, in_sems, 3)
    a = normed(x_ref[...].astype(F32), gain_ref[...])
    put_sides(a_ref, a)
    for index in range(3):
        ready(slots_ref, sources, held, outs, in_sems, out_sems, index)
        qkv_ref[index] = dot(a, held_weight(held, index), (1, 0)).astype(BF)
    settle(held, outs, out_sems)


def enter(stream_low, gain, slots, sources):
    count = stream_low.shape[0]
    weight_ins, weight_outs, weight_shapes, scratch = weight_specs(sources)
    turned, qkv, *weights = pl.pallas_call(
        enter_kernel,
        grid=(count // TILE,),
        in_specs=weight_ins + [row_block(), whole_block(gain)],
        out_specs=[sided_block(), pl.BlockSpec((3, TILE, D), lambda i: (0, i, 0))] + weight_outs,
        out_shape=[jax.ShapeDtypeStruct((2, D // 2, count), BF), jax.ShapeDtypeStruct((3, count, D), BF)] + weight_shapes,
        scratch_shapes=scratch,
        compiler_params=params(),
        cost_estimate=cost(12),
        name="enter",
    )(slots, *sources, stream_low, gain)
    return turned, qkv, [weight.reshape(D, D) for weight in weights]


def middle_kernel(parts, slots_ref, *refs):
    sources = refs[:4]
    x_ref, *mixed_refs = refs[4:5 + parts]
    (gain_two_ref, gain_three_ref, e_ref, x1_ref, x2_ref, a2_ref, a3_ref, q_ref, o_ref, p_ref, kv_ref, a3_t_ref,
     mixed_t_ref, e_t_ref, o_scr, inv_ref, *outs) = refs[5 + parts:26 + parts]
    held, in_sems, out_sems = refs[26 + parts:]
    arrive(slots_ref, sources, held, in_sems, 5)

    def weight(index):
        ready(slots_ref, sources, held, outs, in_sems, out_sems, index)
        return held_weight(held, index)

    for index in range(2):
        w = weight(2 + index)

        @pl.when(pl.program_id(0) == 0)
        def _(index=index, w=w):
            kv_ref[index] = dot(e_ref[...], w, (1, 0)).astype(BF)

    @pl.when(pl.program_id(0) == 0)
    def _():
        put_sides(e_t_ref, e_ref[...])

    w_first = weight(0)
    (mixed_ref,) = mixed_refs
    x1 = x_ref[...].astype(F32) + dot(mixed_ref[...], w_first, (1, 0))
    x1_ref[...] = x1
    a2 = normed(x1, gain_two_ref[...])
    put_sides(mixed_t_ref, mixed_ref[...])
    put_sides(a2_ref, a2)
    q_ref[...] = dot(a2, weight(1), (1, 0)).astype(BF)
    lane = lax.broadcasted_iota(jnp.int32, (TILE, PAIR), 1)
    inverses = jnp.zeros((TILE, PAIR), F32)
    for pair in range(PAIRS):
        columns = slice(pair * PAIR, (pair + 1) * PAIR)
        k = kv_ref[0, :, columns]
        v = kv_ref[1, :, columns]
        mixed = []
        for half in range(2):
            q = lanes_of(q_ref[:, columns] * BF(HD ** -0.5), half)
            s = dot(q, k, (1, 1))
            e = jnp.exp(s - jnp.max(s, axis=1, keepdims=True))
            inverse = 1.0 / jnp.sum(e, axis=1, keepdims=True)
            low = e.astype(BF)
            p_ref[2 * pair + half] = low
            inverses = jnp.where(lane == 2 * pair + half, inverse, inverses)
            mixed.append(dot(low, v, (1, 0)) * inverse)
        o_scr[:, columns] = jnp.where(lane < HD, mixed[0], mixed[1]).astype(BF)
    inv_ref[...] = inverses
    put_sides(o_ref, o_scr[...])
    x2 = x1_ref[...] + dot(o_scr[...], weight(4), (1, 0))
    x2_ref[...] = x2
    a3 = normed(x2, gain_three_ref[...])
    a3_ref[...] = a3
    a3_t_ref[...] = a3.T
    settle(held, outs, out_sems)


def middle(stream_low, mixed, gain_two, gain_three, encoder, slots, sources):
    count = stream_low.shape[0]
    enc = encoder.shape[0]
    low = jax.ShapeDtypeStruct((count, D), BF)
    wide = jax.ShapeDtypeStruct((count, D), F32)
    turned = jax.ShapeDtypeStruct((D, count), BF)
    sided = jax.ShapeDtypeStruct((2, D // 2, count), BF)
    weight_ins, weight_outs, weight_shapes, scratch = weight_specs(sources)
    *results, w1, w2, w3, w4, w5 = pl.pallas_call(
        functools.partial(middle_kernel, len(mixed)),
        grid=(count // TILE,),
        in_specs=weight_ins
        + [row_block()]
        + [row_block(part.shape[1]) for part in mixed]
        + [whole_block(value) for value in (gain_two, gain_three, encoder)],
        out_specs=[row_block(), row_block(), sided_block(), row_block(), row_block(), sided_block()]
        + [
            pl.BlockSpec((HEADS, TILE, enc), lambda i: (0, i, 0)),
            pl.BlockSpec((2, enc, D), lambda i: (0, 0, 0)),
            turned_block(),
            sided_block(),
            pl.BlockSpec((2, D // 2, enc), lambda i: (0, 0, 0)),
            row_block(),
            row_block(PAIR),
        ]
        + weight_outs,
        out_shape=[
            wide,
            wide,
            sided,
            low,
            low,
            sided,
            jax.ShapeDtypeStruct((HEADS, count, enc), BF),
            jax.ShapeDtypeStruct((2, enc, D), BF),
            turned,
            sided,
            jax.ShapeDtypeStruct((2, D // 2, enc), BF),
            low,
            jax.ShapeDtypeStruct((count, PAIR), F32),
        ]
        + weight_shapes,
        scratch_shapes=scratch,
        compiler_params=params(),
        cost_estimate=cost(30),
        name="middle",
    )(slots, *sources, stream_low, *mixed, gain_two, gain_three, encoder)
    return results + [[weight.reshape(D, D) for weight in (w1, w2, w3, w4, w5)]]


def middle_back_kernel(dy_ref, da3_ref, x2_ref, x1_ref, q_ref, o_ref, inv_ref, p_ref, kv_ref, gain_two_ref, gain_three_ref, wc_ref, wq_ref,
                       wo_ref, *refs):
    before = refs[:-9]
    low2_ref, dq_ref, dx1_ref, low1_ref, do1_ref, dkv_ref, sums_ref, gains_ref, do_ref = refs[-9:]
    dk_acc, dv_acc = sums_ref.at[0], sums_ref.at[1]
    step = pl.program_id(0)

    @pl.when(step == 0)
    def _():
        sums_ref[...] = before[-2][...] if before else jnp.zeros_like(sums_ref)
        gains_ref[...] = before[-1][...] if before else jnp.zeros_like(gains_ref)

    back, terms = norm_back(x2_ref[...], gain_three_ref[...], da3_ref[...])
    gains_ref[1] += terms
    dx2 = dy_ref[...].astype(F32) + back
    dx1_ref[...] = dx2
    low2 = dx2.astype(BF)
    low2_ref[...] = low2
    do_ref[...] = dot(low2, wo_ref[...], (1, 1)).astype(BF)
    lane = lax.broadcasted_iota(jnp.int32, (TILE, PAIR), 1)
    for pair in range(PAIRS):
        columns = slice(pair * PAIR, (pair + 1) * PAIR)
        k = kv_ref[0, :, columns]
        v = kv_ref[1, :, columns]
        inverse = jnp.where(lane < HD, inv_ref[:, 2 * pair:2 * pair + 1], inv_ref[:, 2 * pair + 1:2 * pair + 2])
        do = (do_ref[:, columns].astype(F32) * inverse).astype(BF)
        drops = do.astype(F32) * o_ref[:, columns].astype(F32)
        q_left, do_left = (q_ref[:, columns] * BF(HD ** -0.5)).T, do.T
        parts = []
        for half in range(2):
            rows = slice(half * HD, (half + 1) * HD)
            places = slice(pair * PAIR + half * HD, pair * PAIR + (half + 1) * HD)
            low = p_ref[2 * pair + half]
            drop = jnp.sum(lanes_of(drops, half), axis=1, keepdims=True)
            down = (low.astype(F32) * (dot(lanes_of(do, half), v, (1, 1)) - drop)).astype(BF)
            parts.append(dot(down, k, (1, 0)))
            dk_acc[places] += dot(q_left[rows], down, (1, 0))
            dv_acc[places] += dot(do_left[rows], low, (1, 0))
        dq_ref[:, columns] = (jnp.where(lane < HD, parts[0], parts[1]) * (HD ** -0.5)).astype(BF)
    da2 = dot(dq_ref[...], wq_ref[...], (1, 1))
    back, terms = norm_back(x1_ref[...], gain_two_ref[...], da2)
    gains_ref[0] += terms
    dx1 = dx1_ref[...] + back
    dx1_ref[...] = dx1
    low1 = dx1.astype(BF)
    low1_ref[...] = low1
    do1_ref[...] = dot(low1, wc_ref[...], (1, 1)).astype(BF)

    @pl.when(step == pl.num_programs(0) - 1)
    def _():
        dkv_ref[0] = dk_acc[...].T.astype(BF)
        dkv_ref[1] = dv_acc[...].T.astype(BF)


def middle_back(first, blocks, low_up, grad_three, after_two, after_one, query_two, mixed_two, inverse_two, expos_two,
                kv_two, gain_two, gain_three, w_comb_one, w_query_two, w_comb_two, before=None):
    count = low_up.shape[0]
    enc = kv_two.shape[1]
    low = jax.ShapeDtypeStruct((count, D), BF)
    wide = jax.ShapeDtypeStruct((count, D), F32)
    rows = pl.BlockSpec((TILE, D), lambda i: (first + i, 0))
    sums = jax.ShapeDtypeStruct((2, D, enc), F32)
    gains = jax.ShapeDtypeStruct((2, 8, D), F32)
    whole = (kv_two, gain_two, gain_three, w_comb_one, w_query_two, w_comb_two)
    operands = (low_up, grad_three, after_two, after_one, query_two, mixed_two, inverse_two, expos_two) + whole
    more = [] if before is None else list(before[:5]) + list(before[6:])
    aliases = {} if before is None else {len(operands) + index: index for index in range(5)}
    return pl.pallas_call(
        middle_back_kernel,
        grid=(blocks,),
        in_specs=[rows] * 6
        + [
            pl.BlockSpec((TILE, PAIR), lambda i: (first + i, 0)),
            pl.BlockSpec((HEADS, TILE, enc), lambda i: (0, first + i, 0)),
        ]
        + [whole_block(value) for value in whole]
        + ([] if before is None else [pl.BlockSpec(memory_space=pl.ANY)] * 5 + [whole_block(sums), whole_block(gains)]),
        out_specs=[rows] * 5
        + [
            pl.BlockSpec((2, enc, D), lambda i: (0, 0, 0)),
            pl.BlockSpec((2, D, enc), lambda i: (0, 0, 0)),
            pl.BlockSpec((2, 8, D), lambda i: (0, 0, 0)),
        ],
        out_shape=[low, low, wide, low, low, jax.ShapeDtypeStruct((2, enc, D), BF), sums, gains],
        scratch_shapes=[pltpu.VMEM((TILE, D), BF)],
        input_output_aliases=aliases,
        compiler_params=params(),
        cost_estimate=cost(45),
        name="middle_back",
    )(*operands, *more)


def leave_kernel(parts, plan_ref, x_ref, dx1_ref, *refs):
    grads = refs[:3 * parts]
    gain_ref, wq_ref, wk_ref, wv_ref, out_ref, gains_ref = refs[3 * parts:]

    @pl.when(pl.program_id(0) == 0)
    def _():
        gains_ref[...] = jnp.zeros_like(gains_ref)

    da = None
    end = 0
    for index in range(parts):
        columns = slice(end, end + grads[3 * index].shape[1])
        end = columns.stop
        for which, w_ref in enumerate((wq_ref, wk_ref, wv_ref)):
            part = dot(grads[3 * index + which][...], w_ref[:, columns], (1, 1))
            da = part if da is None else da + part
    back, terms = norm_back(x_ref[...].astype(F32), gain_ref[...], da)
    gains_ref[...] += terms
    out_ref[...] = dx1_ref[...] + back


def leave(plan, blocks, stream_low, grad_after_one, parts, gain, w_query, w_key, w_value):
    weights = (w_query, w_key, w_value)
    flat = [value for part in parts for value in part]

    def rows(value):
        return pl.BlockSpec((TILE, value.shape[1]), lambda i, p: (p[i], 0))

    return pl.pallas_call(
        functools.partial(leave_kernel, len(parts)),
        grid_spec=pltpu.PrefetchScalarGridSpec(
            num_scalar_prefetch=1,
            grid=(blocks,),
            in_specs=[rows(stream_low), rows(grad_after_one)]
            + [rows(value) for value in flat]
            + [whole_block(value) for value in (gain,) + weights],
            out_specs=[pl.BlockSpec((TILE, D), lambda i, p: (i, 0)), pl.BlockSpec((8, D), lambda i, p: (0, 0))],
        ),
        out_shape=[jax.ShapeDtypeStruct((blocks * TILE, D), F32), jax.ShapeDtypeStruct((8, D), F32)],
        compiler_params=params(),
        cost_estimate=cost(2),
        name="leave",
    )(plan, stream_low, grad_after_one, *flat, gain, *weights)


def update_kernel(count, lows, factor_ref, *refs):
    ins = refs[:4 * count]
    outs = refs[4 * count:7 * count + lows]
    held = refs[7 * count + lows:11 * count + lows]
    ready = refs[11 * count + lows:14 * count + 2 * lows]
    in_sems, out_sems = refs[14 * count + 2 * lows:]
    arrivals = [pltpu.make_async_copy(ref, kept, in_sems.at[n]) for n, (ref, kept) in enumerate(zip(ins, held))]
    departures = [pltpu.make_async_copy(kept, ref, out_sems.at[n]) for n, (ref, kept) in enumerate(zip(outs, ready))]
    for index in range(count):
        for group in range(4):
            arrivals[group * count + index].start()
    factor = factor_ref[0]
    for index in range(count):
        for group in range(4):
            arrivals[group * count + index].wait()
        weight, first, second, grad = (held[group * count + index] for group in range(4))
        states = adam(weight[...], first[...], second[...], grad[...] * factor, RATES[index])
        for place, value in enumerate(states):
            ready[3 * index + place][...] = value
            departures[3 * index + place].start()
        if index < lows:
            ready[3 * count + index][...] = states[0].astype(BF)
            departures[3 * count + index].start()
    for copy in departures:
        copy.wait()


def update(factor, weights, firsts, seconds, grads, lows=4):
    count = len(weights)
    operands = tuple(weights) + tuple(firsts) + tuple(seconds) + tuple(grads)
    shapes = [jax.ShapeDtypeStruct(weight.shape, F32) for weight in weights for _ in range(3)]
    shapes += [jax.ShapeDtypeStruct(weight.shape, BF) for weight in weights[:lows]]
    anywhere = pl.BlockSpec(memory_space=pl.ANY)
    outs = pl.pallas_call(
        functools.partial(update_kernel, count, lows),
        in_specs=[pl.BlockSpec(memory_space=pltpu.SMEM)] + [anywhere] * len(operands),
        out_specs=[anywhere] * len(shapes),
        out_shape=shapes,
        scratch_shapes=[pltpu.VMEM(value.shape, F32) for value in operands]
        + [pltpu.VMEM(shape.shape, shape.dtype) for shape in shapes]
        + [pltpu.SemaphoreType.DMA((len(operands),)), pltpu.SemaphoreType.DMA((len(shapes),))],
        compiler_params=params(),
        cost_estimate=cost(5),
        name="update",
    )(factor.reshape(1), *operands)
    return [outs[3 * index:3 * index + 3] for index in range(count)], outs[3 * count:]


SIDE = 2
LINE = 4
AXES = ("dp", "fsdp")


def place_of(z, y, x, core):
    return ((z * SIDE + y) * SIDE + x) * 2 + core


def moves(rule):
    every = [(z, y, x, c) for z in range(LINE) for y in range(SIDE) for x in range(SIDE) for c in range(2)]
    return [(place_of(*here), place_of(*rule(*here))) for here in every]


def send(value, rule):
    return lax.ppermute(value, AXES, moves(rule))


def along_line(shift):
    return lambda z, y, x, c: ((z + shift) % LINE, y, x, c)


def line_far(z, y, x, c):
    return (z ^ 2, y, x, c)


def line_near(z, y, x, c):
    return (z ^ 1, y, x, c)


def first_flip(z, y, x, c):
    return (z, y, 1 - x, c) if c == 0 else (z, 1 - y, x, c)


def second_flip(z, y, x, c):
    return (z, 1 - y, x, c) if c == 0 else (z, y, 1 - x, c)


def core_flip(z, y, x, c):
    return (z, y, x, 1 - c)


def spots(y, x, core):
    here = y * SIDE + x
    along_x = y * SIDE + 1 - x
    along_y = (1 - y) * SIDE + x
    across = (1 - y) * SIDE + 1 - x
    near = jnp.where(core == 0, along_x, along_y)
    far = jnp.where(core == 0, along_y, along_x)
    return here, near, far, across


def put_kernel(z_ref, shard, far, near, out, sems):
    z = z_ref[0]
    sources = [(shard, z), (far, z ^ 2), (near.at[0], z ^ 1), (near.at[1], z ^ 3)]
    copies = [
        pltpu.make_async_copy(source, out.at[:, slot], sems.at[index])
        for index, (source, slot) in enumerate(sources)
    ]
    for copy in copies:
        copy.start()
    for copy in copies:
        copy.wait()


def put_in_line(shard, far, near, z):
    count, rows, columns = shard.shape
    return pl.pallas_call(
        put_kernel,
        in_specs=[pl.BlockSpec(memory_space=pltpu.SMEM)] + [pl.BlockSpec(memory_space=pl.ANY)] * 3,
        out_specs=pl.BlockSpec(memory_space=pltpu.VMEM),
        out_shape=jax.ShapeDtypeStruct((count, LINE, rows, columns), shard.dtype),
        scratch_shapes=[pltpu.SemaphoreType.DMA((LINE,))],
        compiler_params=params(40),
        cost_estimate=cost(1),
        name="put_in_line",
    )(z[None], shard, far, near)


def assemble_kernel(slots_ref, *refs):
    sources = refs[:4]
    outs, sems = refs[4:-1], refs[-1]
    copies = []
    for index, source in enumerate(sources):
        for half in range(2):
            spot = slots_ref[2 * index + half, 0]
            side = slots_ref[2 * index + half, 1]
            for k, out in enumerate(outs):
                copies.append(
                    pltpu.make_async_copy(source.at[half, k], out.at[:, spot, side], sems.at[len(copies)])
                )
    for copy in copies:
        copy.start()
    for copy in copies:
        copy.wait()


def assemble(sources, slots):
    _, count, line, rows, columns = sources[0].shape
    shape = (line, SIDE * SIDE, 2, rows, columns)
    outs = pl.pallas_call(
        assemble_kernel,
        in_specs=[pl.BlockSpec(memory_space=pltpu.SMEM)] + [pl.BlockSpec(memory_space=pl.ANY)] * 4,
        out_specs=[pl.BlockSpec(memory_space=pltpu.VMEM)] * count,
        out_shape=[jax.ShapeDtypeStruct(shape, sources[0].dtype)] * count,
        scratch_shapes=[pltpu.SemaphoreType.DMA((8 * count,))],
        compiler_params=params(40),
        cost_estimate=cost(2 * count),
        name="assemble",
    )(slots, *sources)
    return [out.reshape(line * SIDE * SIDE * 2 * rows, columns) for out in outs]


def tie(*values):
    return lax.optimization_barrier(values)


def line_stage(shard):
    return [send(shard, along_line(shift)) for shift in range(1, LINE)]


def piece_slots(place):
    _, y, x, core = place
    mine = spots(y, x, core)
    theirs = spots(y, x, 1 - core)
    order = [(mine[0], core), (mine[1], core), (theirs[0], 1 - core), (theirs[1], 1 - core)]
    order += [(mine[2], core), (mine[3], core), (theirs[2], 1 - core), (theirs[3], 1 - core)]
    return jnp.stack([jnp.stack(pair) for pair in order])


def add_split_kernel(spots_ref, one_ref, two_ref, away_ref, stay_ref):
    slot = pl.program_id(0)
    value = one_ref[...] + two_ref[...]

    for out_ref, here in ((away_ref, slot < 2), (stay_ref, slot >= 2)):
        @pl.when(here)
        def _(out_ref=out_ref):
            for index in range(value.shape[0]):
                out_ref[0, :, index] = value[index, :, 0]


def add_split(keep, received, place):
    _, y, x, core = place
    here, near, far, across = spots(y, x, core)
    count, _, rows, columns = keep.shape
    grid = (count, LINE, SIDE * SIDE, rows, columns)
    wide = columns // 2
    source = pl.BlockSpec((count, LINE, 1, rows, wide), lambda j, t, s: (0, 0, s[j], 0, t))
    out = jax.ShapeDtypeStruct((2, LINE, count, rows, columns), BF)
    block = (1, LINE, count, rows, wide)
    return pl.pallas_call(
        add_split_kernel,
        grid_spec=pltpu.PrefetchScalarGridSpec(
            num_scalar_prefetch=1,
            grid=(4, 2),
            in_specs=[source, source],
            out_specs=[
                pl.BlockSpec(block, lambda j, t, s: (jnp.minimum(j, 1), 0, 0, 0, jnp.where(j < 2, t, 1))),
                pl.BlockSpec(block, lambda j, t, s: (jnp.maximum(j - 2, 0), 0, 0, 0, jnp.where(j < 2, 0, t))),
            ],
        ),
        out_shape=[out, out],
        compiler_params=params(),
        cost_estimate=cost(1),
        name="add_split",
    )(jnp.stack([far, across, here, near]), keep.reshape(grid), received.reshape(grid))


def plus(one, two):
    return (one.astype(F32) + two.astype(F32)).astype(BF)


def line_split(line, place):
    z = place[0]

    def at(index):
        return lax.dynamic_index_in_dim(line, index, 0, keepdims=False)

    return (at(z), at(z ^ 2)), jnp.stack([at(z ^ 1), at(z ^ 3)])


def add_in_order(value, received, own, owners):
    total = None
    for index in range(4):
        term = jnp.where(own == index, value, 0.0)
        for part, owner in zip(received, owners):
            term = term + jnp.where(owner == index, part, 0.0)
        total = term if total is None else total + term
    return total


def sum_everywhere(value, place):
    z, y, x, core = place
    parts = [send(value, along_line(shift)) for shift in range(1, LINE)]
    value = add_in_order(value, parts, z, [(z - shift) % LINE for shift in range(1, LINE)])
    flips = [(0, 1), (1, 0), (1, 1)]
    parts = [send(value, lambda z, y, x, c, dy=dy, dx=dx: (z, y ^ dy, x ^ dx, c)) for dy, dx in flips]
    value = add_in_order(
        value, parts, y * SIDE + x, [jnp.bitwise_xor(y, dy) * SIDE + jnp.bitwise_xor(x, dx) for dy, dx in flips]
    )
    return value + send(value, core_flip)


def swap_halves(parts, core):
    def block(index):
        return jnp.concatenate(
            [lax.dynamic_index_in_dim(part, index, 0, keepdims=False).reshape(-1, D) for part in parts], axis=0
        )

    mine = block(core)
    theirs = send(block(1 - core), core_flip)
    first = jnp.where(core == 0, mine, theirs)
    second = jnp.where(core == 0, theirs, mine)
    whole, begin = [], 0
    for part in parts:
        end = begin + part.size // 2 // D
        whole.append(jnp.concatenate([first[begin:end], second[begin:end]], axis=0))
        begin = end
    return whole


def hand_over(parts, core):
    halves = [part.reshape((2, -1, D)) for part in parts]

    def block(index):
        return jnp.concatenate([lax.dynamic_index_in_dim(part, index, 0, keepdims=False) for part in halves], axis=0)

    return block(core), send(block(1 - core), core_flip)


def both_groups(mine, other, core):
    return jnp.stack([jnp.where(core == 0, mine, other), jnp.where(core == 0, other, mine)])


def matmul(left, right):
    return jnp.dot(left, right, preferred_element_type=F32)


def matmul_t(left, right):
    return lax.dot_general(left, right, (((1,), (1,)), ((), ())), preferred_element_type=F32)


def paired_body(
    prompt_states,
    branch_states,
    encoder_states,
    branch_start,
    bucket_table,
    prompt_cotangent,
    branch_cotangent,
    projections,
    projections_first,
    projections_second,
    combiners,
    combiners_first,
    combiners_second,
    expansion,
    expansion_first,
    expansion_second,
    contraction,
    contraction_first,
    contraction_second,
    norm_gains,
    gains_first,
    gains_second,
    position_bias,
    bias_first,
    bias_second,
):
    rows_here = prompt_states.shape[1]
    prompt = 2 * rows_here
    size = branch_states.shape[2]
    place_index = lax.axis_index("dp")
    core = lax.axis_index("fsdp")
    place = (place_index // (SIDE * SIDE), place_index // SIDE % SIDE, place_index % SIDE, core)

    z = place[0]
    core_ref = core[None]

    shard_qkv = projections[:3].astype(BF)
    shard_mid = jnp.concatenate([combiners[:1], projections[3:], combiners[1:]], axis=0).astype(BF)
    shard_exp = expansion.astype(BF)
    shard_con = contraction[None].astype(BF)
    far_line_qkv = send(shard_qkv, line_far)

    other_start = send(lax.dynamic_index_in_dim(branch_start, 1 - core, 0, keepdims=False), core_flip)
    own_start = lax.dynamic_index_in_dim(branch_start, core, 0, keepdims=False)
    starts = jnp.concatenate(
        [jnp.where(core == 0, own_start, other_start), jnp.where(core == 0, other_start, own_start)]
    )
    gain_rows = [norm_gains[index:index + 1] for index in range(3)]

    bucket_ids = jnp.arange(BUCKETS, dtype=jnp.int32)
    flipped_table = jnp.flip(bucket_table)
    flipped_onehot = (flipped_table[:, None] == bucket_ids[None, :]).astype(F32)
    flipped_bias = jnp.dot(flipped_onehot, position_bias, precision=lax.Precision.HIGHEST).T
    buckets = distance_buckets(flipped_table, starts, prompt, size)
    slots = piece_slots(place)

    far_line_qkv, starts = tie(far_line_qkv, starts)
    near_line_qkv = send(jnp.stack([shard_qkv, far_line_qkv]), line_near)
    near_line_qkv, prompt_states, shard_mid = tie(near_line_qkv, prompt_states, shard_mid)
    far_line_mid = send(shard_mid, line_far)
    prompt_rows, branch_rows, prompt_up, branch_up, encoder = swap_halves(
        [prompt_states, branch_states, prompt_cotangent, branch_cotangent, encoder_states], core
    )
    own_qkv = put_in_line(shard_qkv, far_line_qkv, near_line_qkv, z)
    near_qkv = send(own_qkv, first_flip)
    near_qkv, own_qkv = tie(near_qkv, own_qkv)
    close_qkv = jnp.stack([own_qkv, near_qkv])
    far_qkv = send(close_qkv, second_flip)
    close_qkv, far_line_mid = tie(close_qkv, far_line_mid)
    near_line_mid = send(jnp.stack([shard_mid, far_line_mid]), line_near)
    close_qkv_two = send(close_qkv, core_flip)
    base, branch = bias_rows(flipped_bias, starts, prompt, size)
    stream_low = jnp.concatenate([prompt_rows, branch_rows], axis=0)
    low_up = jnp.concatenate([prompt_up, branch_up], axis=0)
    far_qkv, near_line_mid, close_qkv_two, stream_low, low_up, encoder, base, branch, shard_exp, shard_con = tie(
        far_qkv, near_line_mid, close_qkv_two, stream_low, low_up, encoder, base, branch, shard_exp, shard_con
    )
    far_qkv_two = send(far_qkv, core_flip)
    own_mid = put_in_line(shard_mid, far_line_mid, near_line_mid, z)
    near_mid = send(own_mid, first_flip)
    far_line_exp = send(shard_exp, line_far)
    stream_low, own_mid, far_qkv_two = tie(stream_low, own_mid, far_qkv_two)

    turned_one, qkv, (w_query, w_key, w_value) = enter(
        stream_low, gain_rows[0], slots, [close_qkv, close_qkv_two, far_qkv, far_qkv_two]
    )
    qkv, near_mid, far_line_exp, shard_con = tie(qkv, near_mid, far_line_exp, shard_con)
    close_mid = jnp.stack([own_mid, near_mid])
    far_mid = send(close_mid, second_flip)
    near_line_exp = send(jnp.stack([shard_exp, far_line_exp]), line_near)
    far_line_con = send(shard_con, line_far)
    close_mid_two = send(close_mid, core_flip)
    qkv, close_mid = tie(qkv, close_mid)
    most = PAIRS // 2
    heads = self_forward(qkv, base, branch, starts, prompt, size, 0, most)
    *heads, qkv, far_mid, close_mid_two, near_line_exp, far_line_con = tie(
        *heads, qkv, far_mid, close_mid_two, near_line_exp, far_line_con
    )
    own_exp = put_in_line(shard_exp, far_line_exp, near_line_exp, z)
    near_exp = send(own_exp, first_flip)
    far_mid_two = send(far_mid, core_flip)
    near_line_con = send(jnp.stack([shard_con, far_line_con]), line_near)
    qkv, own_exp, far_mid = tie(qkv, own_exp, far_mid)
    heads = self_forward(qkv, base, branch, starts, prompt, size, most, PAIRS - most, heads)
    *heads, far_mid_two, near_exp, near_line_con = tie(*heads, far_mid_two, near_exp, near_line_con)
    mixed_one, expos, inverse = heads
    close_exp = jnp.stack([own_exp, near_exp])
    far_exp = send(close_exp, second_flip)
    close_exp_two = send(close_exp, core_flip)
    own_con = put_in_line(shard_con, far_line_con, near_line_con, z)
    near_con = send(own_con, first_flip)
    mixed_one, close_exp, own_con = tie(mixed_one, close_exp, own_con)
    (after_one, after_two, turned_two, input_three, query_two, turned_mixed_two, expos_two, kv_two, turned_three,
     turned_mixed_one, turned_encoder, mixed_two, inverse_two, weights_mid) = middle(
        stream_low,
        [mixed_one],
        gain_rows[1],
        gain_rows[2],
        encoder,
        slots,
        [close_mid, close_mid_two, far_mid, far_mid_two],
    )
    w_comb_one, w_query_two, w_key_two, w_value_two, w_comb_two = weights_mid
    input_three, far_exp, near_con, close_exp_two = tie(input_three, far_exp, near_con, close_exp_two)
    far_exp_two = send(far_exp, core_flip)
    close_con = jnp.stack([own_con, near_con])
    far_con = send(close_con, second_flip)
    close_con_two = send(close_con, core_flip)
    w_gate, w_up = assemble([close_exp, close_exp_two, far_exp, far_exp_two], slots)
    w_gate, w_up, far_con, close_con_two = tie(w_gate, w_up, far_con, close_con_two)
    far_con_two = send(far_con, core_flip)
    w_con = assemble([close_con, close_con_two, far_con, far_con_two], slots)[0]

    owners = LINE * SIDE * SIDE * 2
    output, grad_three, away_exp, keep_exp, away_con, keep_con = mlp(
        core_ref, after_two, input_three, turned_three, low_up, w_gate, w_up, w_con, owners
    )
    got_exp = send(away_exp, core_flip)
    got_con = send(away_con[None], core_flip)
    low_up, away_exp, away_con, grad_three, output = tie(low_up, away_exp, away_con, grad_three, output)
    own_output, other_output = hand_over([output[:prompt], output[prompt:]], core)
    low_up, own_output = tie(low_up, own_output)

    def middle_part(first, blocks, before=None):
        return middle_back(
            first,
            blocks,
            low_up,
            grad_three,
            after_two,
            after_one,
            query_two,
            mixed_two,
            inverse_two,
            expos_two,
            kv_two,
            gain_rows[1],
            gain_rows[2],
            w_comb_one,
            w_query_two,
            w_comb_two,
            before,
        )

    before = middle_part(0, 1)
    *before, got_exp, got_con = tie(*before, got_exp, got_con)
    away_con, stay_con = add_split(keep_con[None], got_con, place)
    got_con = send(away_con, second_flip)
    away_exp, stay_exp = add_split(keep_exp, got_exp, place)
    got_exp = send(away_exp, second_flip)
    *before, away_exp, away_con = tie(*before, away_exp, away_con)
    (cross_low, query_two_low, grad_after_one, self_low, grad_mixed_one, kv_two_low, _, gain_back) = middle_part(
        1, prompt // TILE + 2 * size // TILE - 1, before
    )
    _, y, x, _ = place
    here, near, far, across = spots(y, x, core)
    keep_plan = jnp.stack([core, far, across, here, near])
    away_plan = jnp.stack([1 - core, far, across, here, near])
    lefts_mid = [turned_mixed_one, turned_two, turned_encoder, turned_mixed_two]
    jobs_mid = [(0, self_low), (1, query_two_low), (2, kv_two_low[0]), (2, kv_two_low[1]), (3, cross_low)]
    away_mid = weight_part(away_plan, lefts_mid, jobs_mid)
    encoder_grad = matmul_t(kv_two_low[0], w_key_two) + matmul_t(kv_two_low[1], w_value_two)
    away_mid, encoder_grad, other_output, got_exp, got_con = tie(away_mid, encoder_grad, other_output, got_exp, got_con)
    got_mid = send(away_mid, core_flip)
    near_con = plus(stay_con[1], got_con[1])
    got_near_con = send(near_con, first_flip)
    near_exp = plus(stay_exp[1], got_exp[1])
    got_near_exp = send(near_exp, first_flip)
    own_encoder, other_encoder = hand_over([encoder_grad], core)
    grad_mixed_one, away_mid, near_exp, near_con, own_encoder = tie(
        grad_mixed_one, away_mid, near_exp, near_con, own_encoder
    )

    half = PAIRS // 2

    def attend_back(first, pairs, *values):
        part = self_backward(qkv, grad_mixed_one, mixed_one, expos, inverse, prompt, size, first, pairs)
        first, *rest = tie(part[0], grad_mixed_one, *values)
        return ((first,) + tuple(part[1:]), *rest)

    def jobs_of(*parts):
        return [(0, [part[i] for part in parts] if len(parts) > 1 else parts[0][i]) for i in range(3)]

    part_one, grad_mixed_one, got_mid, other_encoder, got_near_con, got_near_exp = attend_back(
        0, half, got_mid, other_encoder, got_near_con, got_near_exp
    )
    line_exp, away_exp = line_split(plus(plus(stay_exp[0], got_exp[0]), got_near_exp), place)
    got_line_exp = send(away_exp, line_near)
    away_mid, stay_mid = weight_part(keep_plan, lefts_mid, jobs_mid, got_mid)
    got_mid = send(away_mid, second_flip)
    line_con, away_con = line_split(plus(plus(stay_con[0], got_con[0]), got_near_con), place)
    got_line_con = send(away_con, line_near)
    away_plan, away_exp, away_con, away_mid = tie(away_plan, away_exp, away_con, away_mid)
    away_one = weight_part(away_plan, [turned_one], jobs_of(part_one))
    got_one = send(away_one, core_flip)
    grad_mixed_one, away_one = tie(grad_mixed_one, away_one)

    part_two, grad_mixed_one, got_one, got_mid, got_line_exp, got_line_con = attend_back(
        half, half // 2, got_one, got_mid, got_line_exp, got_line_con
    )
    near_mid = plus(stay_mid[1], got_mid[1])
    got_near_mid = send(near_mid, first_flip)
    last_exp = plus(line_exp[1], got_line_exp[1])
    got_last_exp = send(last_exp, line_far)
    grad_mixed_one, near_mid, last_exp = tie(grad_mixed_one, near_mid, last_exp)

    part_three, grad_mixed_one, got_near_mid, got_last_exp, away_plan = attend_back(
        half + half // 2, half // 2, got_near_mid, got_last_exp, away_plan
    )
    away_two = weight_part(away_plan, [turned_one], jobs_of(part_two, part_three))
    got_two = send(away_two, core_flip)
    line_mid, away_mid = line_split(plus(plus(stay_mid[0], got_mid[0]), got_near_mid), place)
    got_line_mid = send(away_mid, line_near)
    keep_plan, away_two, away_mid = tie(keep_plan, away_two, away_mid)
    away_one, stay_one = weight_part(keep_plan, [turned_one], jobs_of(part_one), got_one)
    got_one = send(away_one, second_flip)
    leave_values = (
        stream_low,
        grad_after_one,
        [part_one[:3], part_two[:3], part_three[:3]],
        gain_rows[0],
        w_query,
        w_key,
        w_value,
    )
    blocks = prompt // TILE // 2
    steps = jnp.arange(blocks, dtype=jnp.int32)
    theirs_plan = jnp.concatenate([(1 - core) * blocks + steps, jnp.full((1,), 2 * blocks, jnp.int32)])
    ours_plan = core * blocks + steps

    theirs_plan, away_one, got_two = tie(theirs_plan, away_one, got_two)
    theirs_grad, gain_one = leave(theirs_plan, blocks + 1, *leave_values)
    theirs_grad, got_one, got_line_mid, keep_plan = tie(theirs_grad, got_one, got_line_mid, keep_plan)
    away_two, stay_two = weight_part(keep_plan, [turned_one], jobs_of(part_two, part_three), got_two)
    got_two = send(away_two, second_flip)
    away_two, stay_one, stay_mid, theirs_grad = tie(away_two, stay_one, stay_mid, theirs_grad)
    near_one = plus(stay_one[1], got_one[1])
    got_near_one = send(near_one, first_flip)
    last_mid = plus(line_mid[1], got_line_mid[1])
    got_last_mid = send(last_mid, line_far)
    last_con = plus(line_con[1], got_line_con[1])
    got_last_con = send(last_con, line_far)
    ours_plan, near_one, last_mid, last_con = tie(ours_plan, near_one, last_mid, last_con)
    ours_grad, gain_more = leave(ours_plan, blocks, *leave_values)
    ours_grad, got_two, got_near_one = tie(ours_grad, got_two, got_near_one)
    near_two = plus(stay_two[1], got_two[1])
    got_near_two = send(near_two, first_flip)
    line_one, away_one = line_split(plus(plus(stay_one[0], got_one[0]), got_near_one), place)
    got_line_one = send(away_one, line_near)
    got_grad = send(theirs_grad, core_flip)
    half_rows = prompt // 2
    whole_output = both_groups(own_output, other_output, core)
    prompt_output, branch_output = whole_output[:, :half_rows], whole_output[:, half_rows:]
    encoder_out = both_groups(own_encoder, other_encoder, core)
    got_near_two, got_line_one, got_last_mid, got_last_con, prompt_output, branch_output, encoder_out = tie(
        got_near_two, got_line_one, got_last_mid, got_last_con, prompt_output, branch_output, encoder_out
    )
    line_two, away_two = line_split(plus(plus(stay_two[0], got_two[0]), got_near_two), place)
    got_line_two = send(away_two, line_near)
    got_last_one = send(plus(line_one[1], got_line_one[1]), line_far)

    def owned_part(line, got_line, got_last):
        return line[0].astype(F32) + got_line[0].astype(F32) + got_last.astype(F32)

    def square(value):
        return jnp.sum(value * value)

    owned_exp = owned_part(line_exp, got_line_exp, got_last_exp)
    owned_con = owned_part(line_con, got_line_con, got_last_con)[0]
    squares = square(owned_exp) + square(owned_con)
    prompt_grad = both_groups(ours_grad, got_grad[:half_rows], core)
    squares, got_line_two, got_last_one, prompt_grad = tie(squares, got_line_two, got_last_one, prompt_grad)
    got_last_two = send(plus(line_two[1], got_line_two[1]), line_far)
    owned_mid = owned_part(line_mid, got_line_mid, got_last_mid)
    owned_one = owned_part(line_one, got_line_one, got_last_one)
    squares = squares + square(owned_mid) + square(owned_one)
    grad_bias = bias_gradient(
        jnp.concatenate([part_one[3], part_two[3], part_three[3]]),
        jnp.concatenate([part_one[4], part_two[4], part_three[4]]),
        buckets,
    )
    own_branch = lax.dynamic_slice_in_dim(theirs_grad, half_rows + core * size, size, 0)
    other_branch = lax.dynamic_slice_in_dim(got_grad, half_rows + core * size, size, 0)
    branch_grad = both_groups(own_branch, other_branch, core)
    squares, grad_bias, got_last_two, branch_grad = tie(squares, grad_bias, got_last_two, branch_grad)
    owned_two = owned_part(line_two, got_line_two, got_last_two)
    squares = squares + square(owned_two)
    owned_self = jnp.concatenate([owned_one, owned_two], axis=2)

    owned = (
        jnp.concatenate([owned_self, owned_mid[1:4]], axis=0),
        jnp.stack([owned_mid[0], owned_mid[4]]),
        owned_exp,
        owned_con,
    )
    gain_back = jnp.sum(jnp.concatenate([(gain_one + gain_more)[None], gain_back]), axis=1)
    rest = jnp.concatenate([grad_bias.reshape(-1), squares[None]])
    shared = sum_everywhere(
        jnp.concatenate([gain_back, jnp.pad(rest, (0, D - rest.size))[None]]), place
    )
    gain_total = shared[:3]
    bias_total = shared[3, :grad_bias.size].reshape(grad_bias.shape)
    square_total = shared[3, grad_bias.size]
    grad_norm = jnp.sqrt(
        square_total + jnp.sum(gain_total * gain_total) + jnp.sum(bias_total * bias_total)
    )
    factor = jnp.minimum(1.0, CLIP / (grad_norm + 1e-06))
    weights = (projections, combiners, expansion, contraction, norm_gains, position_bias)
    firsts = (projections_first, combiners_first, expansion_first, contraction_first, gains_first, bias_first)
    seconds = (
        projections_second,
        combiners_second,
        expansion_second,
        contraction_second,
        gains_second,
        bias_second,
    )
    states, copies = update(factor, weights[:5], firsts[:5], seconds[:5], owned + (gain_total,))
    states.append(adam(weights[5], firsts[5], seconds[5], bias_total * factor, RATES[5]))
    branch_shape = (2, 1, size, D)
    return (
        prompt_output,
        branch_output.reshape(branch_shape),
        prompt_grad,
        branch_grad.reshape(branch_shape),
        encoder_out,
        grad_norm,
        *states[0],
        *states[1],
        *states[2],
        *states[3],
        *states[4],
        *states[5],
        copies[0],
        copies[1],
        copies[2],
        copies[3],
    )


def solution(mesh):
    paired = mesh.shape["dp"] == 4 * SIDE * SIDE and mesh.shape["fsdp"] == 2
    return jax.shard_map(
        paired_body if paired else body,
        mesh=mesh,
        in_specs=(
            P("dp", "fsdp", None),
            P("dp", "fsdp", None, None),
            P("dp", "fsdp", None),
            P("dp", "fsdp"),
            P(),
            P("dp", "fsdp", None),
            P("dp", "fsdp", None, None),
            P(None, ("dp", "fsdp"), None),
            P(None, ("dp", "fsdp"), None),
            P(None, ("dp", "fsdp"), None),
            P(None, ("dp", "fsdp"), None),
            P(None, ("dp", "fsdp"), None),
            P(None, ("dp", "fsdp"), None),
            P(None, ("dp", "fsdp"), None),
            P(None, ("dp", "fsdp"), None),
            P(None, ("dp", "fsdp"), None),
            P(("dp", "fsdp"), None),
            P(("dp", "fsdp"), None),
            P(("dp", "fsdp"), None),
            P(),
            P(),
            P(),
            P(),
            P(),
            P(),
        ),
        out_specs=(
            P("dp", "fsdp", None),
            P("dp", "fsdp", None, None),
            P("dp", "fsdp", None),
            P("dp", "fsdp", None, None),
            P("dp", "fsdp", None),
            P(),
            P(None, ("dp", "fsdp"), None),
            P(None, ("dp", "fsdp"), None),
            P(None, ("dp", "fsdp"), None),
            P(None, ("dp", "fsdp"), None),
            P(None, ("dp", "fsdp"), None),
            P(None, ("dp", "fsdp"), None),
            P(None, ("dp", "fsdp"), None),
            P(None, ("dp", "fsdp"), None),
            P(None, ("dp", "fsdp"), None),
            P(("dp", "fsdp"), None),
            P(("dp", "fsdp"), None),
            P(("dp", "fsdp"), None),
            P(),
            P(),
            P(),
            P(),
            P(),
            P(),
            P(None, ("dp", "fsdp"), None),
            P(None, ("dp", "fsdp"), None),
            P(None, ("dp", "fsdp"), None),
            P(("dp", "fsdp"), None),
        ),
        check_vma=False,
    )
```

```python
import functools

import jax
import jax.numpy as jnp
from jax import lax
from jax.experimental import pallas as pl
from jax.experimental.pallas import tpu as pltpu
from jax.sharding import PartitionSpec as P

D = 1024
FF = 2816
HEADS = 16
HD = 64
BUCKETS = 32
PROMPT = 1024
STEP = 10


EPS = 1e-06
CLIP = 1.0
BETA_ONE = 0.9
BETA_TWO = 0.999
ADAM_EPS = 1e-08
DECAY = 0.01
RATES = (0.05, 0.3, 0.05, 0.03, 1.0, 1.0)
MASKED = -1e30


def rms_forward(stream, gain):
    scale = lax.rsqrt(jnp.mean(stream * stream, axis=-1, keepdims=True) + EPS)
    return (stream * scale * gain, scale)


def rms_backward(stream, scale, gain, upstream):
    weighted = upstream * gain
    grad_in = scale * weighted - stream * scale**3 * jnp.mean(
        weighted * stream, axis=-1, keepdims=True
    )
    return (grad_in, jnp.sum(upstream * stream * scale, axis=0))


def gelu_mix(gate, up_value):
    inner = 0.7978845608028654 * (gate + 0.044715 * gate * gate * gate)
    return 0.5 * gate * (1.0 + jnp.tanh(inner)) * up_value


def raw_scores(queries, key_rows):
    qh = queries.reshape(queries.shape[0], HEADS, HD)
    kh = key_rows.reshape(key_rows.shape[0], HEADS, HD)
    return jnp.einsum("rhd,khd->hrk", qh, kh, preferred_element_type=jnp.float32) * HD ** (-0.5)


def softmax_forward(scores, value_rows):
    row_max = jnp.max(scores, axis=-1, keepdims=True)
    expo = jnp.exp(scores - row_max)
    total = jnp.sum(expo, axis=-1, keepdims=True)
    probs = (expo / total).astype(jnp.bfloat16)
    vh = value_rows.reshape(value_rows.shape[0], HEADS, HD)
    mixed = jnp.einsum("hrk,khd->rhd", probs, vh, preferred_element_type=jnp.float32)
    return (mixed.reshape(mixed.shape[0], D).astype(jnp.bfloat16), row_max + jnp.log(total))


def softmax_backward(scores, logsum, queries, key_rows, value_rows, grad_mixed):
    probs = jnp.exp(scores - logsum)
    grad_heads = grad_mixed.reshape(grad_mixed.shape[0], HEADS, HD)
    vh = value_rows.reshape(value_rows.shape[0], HEADS, HD)
    kh = key_rows.reshape(key_rows.shape[0], HEADS, HD)
    qh = queries.reshape(queries.shape[0], HEADS, HD)
    grad_values = jnp.einsum(
        "hrk,rhd->khd", probs.astype(jnp.bfloat16), grad_heads, preferred_element_type=jnp.float32
    )
    grad_probs = jnp.einsum("rhd,khd->hrk", grad_heads, vh, preferred_element_type=jnp.float32)
    grad_scores = probs * (grad_probs - jnp.sum(probs * grad_probs, axis=-1, keepdims=True))
    scaled = (grad_scores * HD ** (-0.5)).astype(jnp.bfloat16)
    grad_queries = jnp.einsum("hrk,khd->rhd", scaled, kh, preferred_element_type=jnp.float32)
    grad_keys = jnp.einsum("hrk,rhd->khd", scaled, qh, preferred_element_type=jnp.float32)
    return (
        grad_queries.reshape(-1, D),
        grad_keys.reshape(-1, D),
        grad_values.reshape(-1, D),
        grad_scores,
    )


def hankel_bias(per_distance, shift, rows, keys):
    heads = per_distance.shape[0]
    front = jnp.broadcast_to(per_distance[:, :1], (heads, keys - 1))
    padded = jnp.concatenate([front, per_distance], axis=1)
    width = rows + keys - 1
    window = lax.dynamic_slice_in_dim(padded, shift, width, 1)
    tiled = jnp.tile(window, (1, rows + 1))[:, : rows * (width + 1)]
    skewed = tiled.reshape(heads, rows, width + 1)[:, :, :keys]
    return jnp.flip(skewed, axis=2)


def distance_grads(grad_block, shift, dist_count):
    heads, rows, keys = grad_block.shape
    width = rows + keys - 1
    flipped = jnp.flip(grad_block, axis=2)
    widened = jnp.concatenate(
        [flipped, jnp.zeros((heads, rows, width + 1 - keys), jnp.float32)], axis=2
    )
    flat = jnp.concatenate(
        [widened.reshape(heads, rows * (width + 1)), jnp.zeros((heads, keys - 1), jnp.float32)],
        axis=1,
    )
    window = jnp.sum(flat.reshape(heads, rows + 1, width), axis=1)
    padded = lax.dynamic_update_slice_in_dim(
        jnp.zeros((heads, dist_count + keys - 1), jnp.float32), window, shift, 1
    )
    head_part = jnp.sum(padded[:, :keys], axis=1, keepdims=True)
    return jnp.concatenate([head_part, padded[:, keys:]], axis=1)


def adam(weight, first, second, grad, rate):
    first_new = BETA_ONE * first + (1.0 - BETA_ONE) * grad
    second_new = BETA_TWO * second + (1.0 - BETA_TWO) * grad * grad
    mean_hat = first_new / (1.0 - BETA_ONE**STEP)
    square_hat = second_new / (1.0 - BETA_TWO**STEP)
    updated = weight - rate * (mean_hat / (jnp.sqrt(square_hat) + ADAM_EPS) + DECAY * weight)
    return (updated, first_new, second_new)


def body(
    prompt_states,
    branch_states,
    encoder_states,
    branch_start,
    bucket_table,
    prompt_cotangent,
    branch_cotangent,
    projections,
    projections_first,
    projections_second,
    combiners,
    combiners_first,
    combiners_second,
    expansion,
    expansion_first,
    expansion_second,
    contraction,
    contraction_first,
    contraction_second,
    norm_gains,
    gains_first,
    gains_second,
    position_bias,
    bias_first,
    bias_second,
):
    rows_here = prompt_states.shape[1]
    branch_count = branch_states.shape[1]
    branch_size = branch_states.shape[2]
    branch_rows = branch_count * branch_size
    dist_count = bucket_table.shape[0]
    offset = lax.axis_index("fsdp") * rows_here
    local_rows = jnp.arange(rows_here, dtype=jnp.int32)
    steps_in = jnp.arange(branch_size, dtype=jnp.int32)
    bucket_ids = jnp.arange(BUCKETS, dtype=jnp.int32)
    bucket_onehot = (bucket_table[:, None] == bucket_ids[None, :]).astype(jnp.float32)
    per_distance = jnp.dot(bucket_onehot, position_bias, precision=lax.Precision.HIGHEST).T
    own_bias = hankel_bias(per_distance, 0, branch_size, branch_size)
    shards = (
        projections.astype(jnp.bfloat16),
        combiners.astype(jnp.bfloat16),
        expansion.astype(jnp.bfloat16),
        contraction.astype(jnp.bfloat16),
    )

    def layout(starts):
        branch_pos = (starts[:, None] + steps_in[None, :]).reshape(-1)
        branch_seg = jnp.arange(branch_rows, dtype=jnp.int32) // branch_size
        query_pos = jnp.concatenate([offset + local_rows, branch_pos])
        query_seg = jnp.concatenate([jnp.full((rows_here,), -1, jnp.int32), branch_seg])
        query_limit = jnp.concatenate(
            [
                jnp.zeros((rows_here,), jnp.int32),
                jnp.broadcast_to(starts[:, None], (branch_count, branch_size)).reshape(-1),
            ]
        )
        key_pos = jnp.concatenate([jnp.arange(PROMPT, dtype=jnp.int32), branch_pos])
        key_seg = jnp.concatenate([jnp.full((PROMPT,), -1, jnp.int32), branch_seg])
        same_seg = (key_seg[None, :] == query_seg[:, None]) & (
            key_pos[None, :] <= query_pos[:, None]
        )
        from_prompt = (key_seg[None, :] == -1) & (key_pos[None, :] < query_limit[:, None])
        return same_seg | from_prompt

    def build_bias(starts):
        prompt_block = hankel_bias(per_distance, offset, rows_here, PROMPT)
        upper = jnp.concatenate(
            [prompt_block, jnp.zeros((HEADS, rows_here, branch_rows), jnp.float32)], axis=2
        )

        def branch_block(start):
            return hankel_bias(per_distance, start, branch_size, PROMPT)

        cross_blocks = lax.map(branch_block, starts)
        cross_blocks = jnp.transpose(cross_blocks, (1, 0, 2, 3)).reshape(HEADS, branch_rows, PROMPT)
        lower = jnp.concatenate(
            [cross_blocks, jnp.tile(own_bias, (1, branch_count, branch_count))], axis=2
        )
        return jnp.concatenate([upper, lower], axis=1)

    def bias_gradient(grad_scores, starts):
        total = distance_grads(grad_scores[:, :rows_here, :PROMPT], offset, dist_count)

        def add_branch(index, running):
            begin = rows_here + index * branch_size
            rows_block = lax.dynamic_slice_in_dim(grad_scores, begin, branch_size, 1)
            running = running + distance_grads(rows_block[:, :, :PROMPT], starts[index], dist_count)
            own_block = lax.dynamic_slice_in_dim(
                rows_block, PROMPT + index * branch_size, branch_size, 2
            )
            return running + distance_grads(own_block, 0, dist_count)

        total = lax.fori_loop(0, branch_count, add_branch, total)
        return jnp.dot(total, bucket_onehot, precision=lax.Precision.HIGHEST).T

    def group_step(running, item):
        big_sum, gain_sum, bias_sum = running
        prompt, branches, encoder, starts, prompt_cot, branch_cot = item
        weights = (
            lax.all_gather(shards[0], ("dp", "fsdp"), axis=1, tiled=True),
            lax.all_gather(shards[1], ("dp", "fsdp"), axis=1, tiled=True),
            lax.all_gather(shards[2], ("dp", "fsdp"), axis=1, tiled=True),
            lax.all_gather(shards[3], ("dp", "fsdp"), axis=0, tiled=True),
        )
        w_proj, w_comb, w_exp, w_con = weights
        pair_mask = layout(starts)
        stream = jnp.concatenate(
            [prompt.astype(jnp.float32), branches.reshape(-1, D).astype(jnp.float32)], axis=0
        )
        normed_one, scale_one = rms_forward(stream, norm_gains[0])
        input_one = normed_one.astype(jnp.bfloat16)
        self_rows = jnp.einsum(
            "td,kde->kte", input_one, w_proj[:3], preferred_element_type=jnp.float32
        ).astype(jnp.bfloat16)
        prompt_keys, prompt_values = (
            lax.all_gather(self_rows[1, :rows_here], "fsdp", axis=0, tiled=True),
            lax.all_gather(self_rows[2, :rows_here], "fsdp", axis=0, tiled=True),
        )
        encoder_rows = jnp.einsum(
            "td,kde->kte", encoder, w_proj[4:], preferred_element_type=jnp.float32
        ).astype(jnp.bfloat16)
        cross_keys, cross_values = (
            lax.all_gather(encoder_rows[0], "fsdp", axis=0, tiled=True),
            lax.all_gather(encoder_rows[1], "fsdp", axis=0, tiled=True),
        )
        key_rows = jnp.concatenate([prompt_keys, self_rows[1, rows_here:]], axis=0)
        value_rows = jnp.concatenate([prompt_values, self_rows[2, rows_here:]], axis=0)
        pair_bias = build_bias(starts)
        scores_one = jnp.where(
            pair_mask[None], raw_scores(self_rows[0], key_rows) + pair_bias, MASKED
        )
        mixed_one, logsum_one = softmax_forward(scores_one, value_rows)
        after_one = stream + jnp.dot(mixed_one, w_comb[0], preferred_element_type=jnp.float32)
        normed_two, scale_two = rms_forward(after_one, norm_gains[1])
        input_two = normed_two.astype(jnp.bfloat16)
        query_two = jnp.dot(input_two, w_proj[3], preferred_element_type=jnp.float32).astype(
            jnp.bfloat16
        )
        scores_two = raw_scores(query_two, cross_keys)
        mixed_two, logsum_two = softmax_forward(scores_two, cross_values)
        after_two = after_one + jnp.dot(mixed_two, w_comb[1], preferred_element_type=jnp.float32)
        normed_three, scale_three = rms_forward(after_two, norm_gains[2])
        input_three = normed_three.astype(jnp.bfloat16)
        gate_up = jnp.einsum("td,kdf->ktf", input_three, w_exp, preferred_element_type=jnp.float32)
        hidden, mix_pull = jax.vjp(gelu_mix, gate_up[0], gate_up[1])
        hidden_low = hidden.astype(jnp.bfloat16)
        output = after_two + jnp.dot(hidden_low, w_con, preferred_element_type=jnp.float32)
        again = (
            lax.all_gather(shards[0], ("dp", "fsdp"), axis=1, tiled=True),
            lax.all_gather(shards[1], ("dp", "fsdp"), axis=1, tiled=True),
            lax.all_gather(shards[2], ("dp", "fsdp"), axis=1, tiled=True),
            lax.all_gather(shards[3], ("dp", "fsdp"), axis=0, tiled=True),
        )
        b_proj, b_comb, b_exp, b_con = again
        upstream = jnp.concatenate(
            [prompt_cot.astype(jnp.float32), branch_cot.reshape(-1, D).astype(jnp.float32)], axis=0
        )
        upstream_low = upstream.astype(jnp.bfloat16)
        grad_con = jnp.einsum(
            "tf,td->fd", hidden_low, upstream_low, preferred_element_type=jnp.float32
        )
        grad_hidden = jnp.einsum(
            "td,fd->tf", upstream_low, b_con, preferred_element_type=jnp.float32
        )
        grad_gate, grad_up = mix_pull(grad_hidden)
        gate_low = jnp.stack([grad_gate, grad_up]).astype(jnp.bfloat16)
        grad_exp = jnp.einsum(
            "td,ktf->kdf", input_three, gate_low, preferred_element_type=jnp.float32
        )
        grad_three = jnp.einsum("ktf,kdf->td", gate_low, b_exp, preferred_element_type=jnp.float32)
        back_three, gain_three = rms_backward(after_two, scale_three, norm_gains[2], grad_three)
        grad_after_two = upstream + back_three
        cross_low = grad_after_two.astype(jnp.bfloat16)
        grad_comb_two = jnp.einsum(
            "te,td->ed", mixed_two, cross_low, preferred_element_type=jnp.float32
        )
        grad_mixed_two = jnp.einsum(
            "td,ed->te", cross_low, b_comb[1], preferred_element_type=jnp.float32
        ).astype(jnp.bfloat16)
        grad_query_two, grad_keys_two, grad_values_two, unused_scores = softmax_backward(
            scores_two, logsum_two, query_two, cross_keys, cross_values, grad_mixed_two
        )
        own_keys, own_values = (
            lax.psum_scatter(
                grad_keys_two.astype(jnp.bfloat16), "fsdp", scatter_dimension=0, tiled=True
            ).astype(jnp.float32),
            lax.psum_scatter(
                grad_values_two.astype(jnp.bfloat16), "fsdp", scatter_dimension=0, tiled=True
            ).astype(jnp.float32),
        )
        encoder_low = jnp.stack([own_keys, own_values]).astype(jnp.bfloat16)
        grad_cross_proj = jnp.einsum(
            "td,kte->kde", encoder, encoder_low, preferred_element_type=jnp.float32
        )
        encoder_grad = jnp.einsum(
            "kte,kde->td", encoder_low, b_proj[4:], preferred_element_type=jnp.float32
        )
        query_two_low = grad_query_two.astype(jnp.bfloat16)
        grad_query_proj = jnp.einsum(
            "td,te->de", input_two, query_two_low, preferred_element_type=jnp.float32
        )
        grad_two = jnp.einsum(
            "te,de->td", query_two_low, b_proj[3], preferred_element_type=jnp.float32
        )
        back_two, gain_two = rms_backward(after_one, scale_two, norm_gains[1], grad_two)
        grad_after_one = grad_after_two + back_two
        self_low = grad_after_one.astype(jnp.bfloat16)
        grad_comb_one = jnp.einsum(
            "te,td->ed", mixed_one, self_low, preferred_element_type=jnp.float32
        )
        grad_mixed_one = jnp.einsum(
            "td,ed->te", self_low, b_comb[0], preferred_element_type=jnp.float32
        ).astype(jnp.bfloat16)
        grad_query, grad_keys, grad_values, grad_scores = softmax_backward(
            scores_one, logsum_one, self_rows[0], key_rows, value_rows, grad_mixed_one
        )
        prompt_key_grad, prompt_value_grad = (
            lax.psum_scatter(
                grad_keys[:PROMPT].astype(jnp.bfloat16), "fsdp", scatter_dimension=0, tiled=True
            ).astype(jnp.float32),
            lax.psum_scatter(
                grad_values[:PROMPT].astype(jnp.bfloat16), "fsdp", scatter_dimension=0, tiled=True
            ).astype(jnp.float32),
        )
        self_grad_low = jnp.stack(
            [
                grad_query,
                jnp.concatenate([prompt_key_grad, grad_keys[PROMPT:]], axis=0),
                jnp.concatenate([prompt_value_grad, grad_values[PROMPT:]], axis=0),
            ]
        ).astype(jnp.bfloat16)
        grad_self_proj = jnp.einsum(
            "td,kte->kde", input_one, self_grad_low, preferred_element_type=jnp.float32
        )
        grad_one = jnp.einsum(
            "kte,kde->td", self_grad_low, b_proj[:3], preferred_element_type=jnp.float32
        )
        back_one, gain_one = rms_backward(stream, scale_one, norm_gains[0], grad_one)
        stream_grad = grad_after_one + back_one
        grad_bias = bias_gradient(grad_scores, starts)
        group_big = (
            jnp.concatenate([grad_self_proj, grad_query_proj[None], grad_cross_proj], axis=0),
            jnp.stack([grad_comb_one, grad_comb_two]),
            grad_exp,
            grad_con,
        )
        big_sum = jax.tree.map(jnp.add, big_sum, group_big)
        gain_sum = gain_sum + jnp.stack([gain_one, gain_two, gain_three])
        bias_sum = bias_sum + grad_bias
        results = (
            output[:rows_here].astype(jnp.bfloat16),
            output[rows_here:].reshape(branch_count, branch_size, D).astype(jnp.bfloat16),
            stream_grad[:rows_here],
            stream_grad[rows_here:].reshape(branch_count, branch_size, D),
            encoder_grad,
        )
        return ((big_sum, gain_sum, bias_sum), results)

    big_start = (
        jnp.zeros((6, D, D), jnp.float32),
        jnp.zeros((2, D, D), jnp.float32),
        jnp.zeros((2, D, FF), jnp.float32),
        jnp.zeros((FF, D), jnp.float32),
    )
    start_state = (
        big_start,
        jnp.zeros(norm_gains.shape, jnp.float32),
        jnp.zeros(position_bias.shape, jnp.float32),
    )
    final_state, results = lax.scan(
        group_step,
        start_state,
        (
            prompt_states,
            branch_states,
            encoder_states,
            branch_start,
            prompt_cotangent,
            branch_cotangent,
        ),
    )
    big_sum, gain_sum, bias_sum = final_state
    owned = (
        lax.psum_scatter(big_sum[0], ("dp", "fsdp"), scatter_dimension=1, tiled=True),
        lax.psum_scatter(big_sum[1], ("dp", "fsdp"), scatter_dimension=1, tiled=True),
        lax.psum_scatter(big_sum[2], ("dp", "fsdp"), scatter_dimension=1, tiled=True),
        lax.psum_scatter(big_sum[3], ("dp", "fsdp"), scatter_dimension=0, tiled=True),
    )
    squares = sum((jnp.sum(grad * grad) for grad in owned))
    gain_total, bias_total, square_total = lax.psum((gain_sum, bias_sum, squares), ("dp", "fsdp"))
    grad_norm = jnp.sqrt(
        square_total + jnp.sum(gain_total * gain_total) + jnp.sum(bias_total * bias_total)
    )
    factor = jnp.minimum(1.0, CLIP / (grad_norm + 1e-06))
    params = (projections, combiners, expansion, contraction, norm_gains, position_bias)
    firsts = (
        projections_first,
        combiners_first,
        expansion_first,
        contraction_first,
        gains_first,
        bias_first,
    )
    seconds = (
        projections_second,
        combiners_second,
        expansion_second,
        contraction_second,
        gains_second,
        bias_second,
    )
    grads = (owned[0], owned[1], owned[2], owned[3], gain_total, bias_total)
    states = [
        adam(params[index], firsts[index], seconds[index], grads[index] * factor, RATES[index])
        for index in range(6)
    ]
    return (
        results[0],
        results[1],
        results[2],
        results[3],
        results[4],
        grad_norm,
        states[0][0],
        states[0][1],
        states[0][2],
        states[1][0],
        states[1][1],
        states[1][2],
        states[2][0],
        states[2][1],
        states[2][2],
        states[3][0],
        states[3][1],
        states[3][2],
        states[4][0],
        states[4][1],
        states[4][2],
        states[5][0],
        states[5][1],
        states[5][2],
        states[0][0].astype(jnp.bfloat16),
        states[1][0].astype(jnp.bfloat16),
        states[2][0].astype(jnp.bfloat16),
        states[3][0].astype(jnp.bfloat16),
    )


BF = jnp.bfloat16
F32 = jnp.float32
PAIR = 2 * HD
PAIRS = HEADS // 2
TILE = 256


def params(limit=60):
    return pltpu.CompilerParams(vmem_limit_bytes=limit * 1024 * 1024)


def cost(microseconds):
    return pl.CostEstimate(flops=int(microseconds), bytes_accessed=1, transcendentals=0)


def dot(left, right, contract):
    return lax.dot_general(
        left, right, ((contract[:1], contract[1:]), ((), ())), preferred_element_type=F32
    )


def bias_rows(flipped, starts, prompt, size):
    base = jnp.pad(flipped[:, size - 1:], ((0, 0), (0, TILE - 1)), constant_values=MASKED)
    padded = jnp.pad(flipped, ((0, 0), (1, prompt)))
    rows = [
        lax.dynamic_slice_in_dim(padded, prompt - starts[index], prompt + size, 1) for index in range(2)
    ]
    return base[:, None], jnp.stack(rows, axis=1)[:, :, None]


def fill_bias(prompt, size, starts_ref, base, branches, strip_ref, cross_ref):
    wide = jnp.broadcast_to(base, (TILE, prompt + TILE))
    strip_ref[...] = pltpu.roll(wide, 0, 1, stride=1, stride_axis=0)[:, TILE:]
    place = lax.broadcasted_iota(jnp.int32, (size, prompt), 1)
    for index, branch in enumerate(branches):
        row = jnp.broadcast_to(branch, (size, prompt + size))
        skewed = pltpu.roll(row, 0, 1, stride=1, stride_axis=0)[:, size:]
        cross_ref[index * size:(index + 1) * size] = jnp.where(place < starts_ref[index], skewed, MASKED)


def lanes_of(value, half):
    lane = lax.broadcasted_iota(jnp.int32, value.shape, 1)
    return jnp.where((lane >= HD) if half else (lane < HD), value, jnp.zeros_like(value))


def both_halves(value):
    return jnp.concatenate([lanes_of(value, 0), lanes_of(value, 1)], axis=0)


def probs_width(prompt, size):
    blocks = prompt // TILE
    return TILE * blocks * (blocks + 1) // 2 + prompt + size


def fold(grid):
    rows, width = grid.shape
    while rows > 1:
        rows //= 2
        grid = grid[:rows] + pltpu.roll(grid[rows:], width - rows, 1)
    return grid


def self_kernel(prompt, size, more, starts_ref, q_ref, k_ref, v_ref, base_ref, branch_ref, *refs):
    o_ref, e_ref, inv_ref, s_ref, strips_ref, crosses_ref = refs[more:]
    blocks = prompt // TILE
    begins = [TILE * i * (i + 1) // 2 for i in range(blocks + 1)]
    lane = lax.broadcasted_iota(jnp.int32, (TILE, PAIR), 1)
    for half in range(2):
        strip_ref, cross_ref = strips_ref.at[half], crosses_ref.at[half]
        branches = [branch_ref[half, index] for index in range(2)]
        fill_bias(prompt, size, starts_ref, base_ref[half], branches, strip_ref, cross_ref)
        for i in range(blocks + 1):
            rows = slice(i * TILE, (i + 1) * TILE)
            q = lanes_of(q_ref[rows] * BF(HD ** -0.5), half)
            tiles = []
            for j in range(min(i + 1, blocks)):
                keys = slice(j * TILE, (j + 1) * TILE)
                begin = prompt - (i + 1 - j) * TILE
                bias = strip_ref.at[:, begin:begin + TILE] if i < blocks else cross_ref.at[:, keys]
                tiles.append((keys, bias))
            top = None
            for j, (keys, bias) in enumerate(tiles):
                s = dot(q, k_ref[keys], (1, 1)) + bias[...]
                s_ref[:, j * TILE:(j + 1) * TILE] = s
                high = jnp.maximum(s[:, :PAIR], s[:, PAIR:])
                top = high if top is None else jnp.maximum(top, high)
            if i == blocks:
                near = strip_ref[:size, prompt - TILE:prompt - TILE + size]
                own = jnp.concatenate(
                    [
                        dot(q[b * size:(b + 1) * size], k_ref[prompt + b * size:prompt + (b + 1) * size], (1, 1)) + near
                        for b in range(2)
                    ],
                    axis=0,
                )
                top = jnp.maximum(top, own)
            top = jnp.max(top, axis=1, keepdims=True)
            total = None
            for j, (keys, _) in enumerate(tiles):
                e = jnp.exp(s_ref[:, j * TILE:(j + 1) * TILE] - top)
                part = e[:, :PAIR] + e[:, PAIR:]
                total = part if total is None else total + part
                low = e.astype(BF)
                e_ref[half, :, begins[i] + j * TILE:begins[i] + (j + 1) * TILE] = low
            seen = len(tiles) * TILE
            out = dot(e_ref[half, :, begins[i]:begins[i] + seen], v_ref[:seen], (1, 0))
            if i == blocks:
                e = jnp.exp(own - top)
                total = total + e
                low = e.astype(BF)
                e_ref[half, :, begins[i] + prompt:] = low
                out = out + jnp.concatenate(
                    [
                        dot(low[b * size:(b + 1) * size], v_ref[prompt + b * size:prompt + (b + 1) * size], (1, 0))
                        for b in range(2)
                    ],
                    axis=0,
                )
            inverse = 1.0 / jnp.sum(total, axis=1, keepdims=True)
            out = out * inverse
            if half == 0:
                o_ref[rows] = out.astype(BF)
                inv_ref[rows] = jnp.broadcast_to(inverse, (TILE, PAIR))
            else:
                o_ref[rows] = jnp.where(lane >= HD, out.astype(BF), o_ref[rows])
                inv_ref[rows] = jnp.where(lane >= HD, inverse, inv_ref[rows])


def self_forward(qkv, base, branch, starts, prompt, size, first, pairs, before=None):
    count = prompt + 2 * size
    width = probs_width(prompt, size)
    column = lambda part: pl.BlockSpec((None, count, PAIR), lambda j, s, part=part: (part, 0, first + j))
    flat = pl.BlockSpec((count, PAIR), lambda j, s: (0, first + j))
    bias = pltpu.VMEM((2, TILE, prompt), F32)
    more = [] if before is None else list(before)
    return pl.pallas_call(
        functools.partial(self_kernel, prompt, size, len(more)),
        grid_spec=pltpu.PrefetchScalarGridSpec(
            num_scalar_prefetch=1,
            grid=(pairs,),
            in_specs=[
                column(0),
                column(1),
                column(2),
                pl.BlockSpec((2, 1, prompt + TILE), lambda j, s: (first + j, 0, 0)),
                pl.BlockSpec((2, 2, 1, prompt + size), lambda j, s: (first + j, 0, 0, 0)),
            ]
            + [pl.BlockSpec(memory_space=pl.ANY)] * len(more),
            out_specs=[flat, pl.BlockSpec((2, TILE, width), lambda j, s: (first + j, 0, 0)), flat],
            scratch_shapes=[pltpu.VMEM((TILE, prompt), F32), bias, bias],
        ),
        out_shape=[
            jax.ShapeDtypeStruct((count, D), BF),
            jax.ShapeDtypeStruct((HEADS, TILE, width), BF),
            jax.ShapeDtypeStruct((count, D), F32),
        ],
        input_output_aliases={6 + index: index for index in range(len(more))},
        compiler_params=params(),
        cost_estimate=cost(6 * pairs),
        name="self_forward",
    )(starts, qkv, qkv, qkv, base, branch, *more)


def self_back_kernel(prompt, size, q_ref, k_ref, v_ref, do_ref, o_ref, e_ref, inv_ref, dq_ref, dk_ref, dv_ref,
                     strip_ref, cross_ref, sums, far_sums, dk_acc, dv_acc, down_ref, low_ref, q_left, do_left):
    blocks = prompt // TILE
    count = prompt + 2 * size
    begins = [TILE * i * (i + 1) // 2 for i in range(blocks + 1)]
    scale = BF(HD ** -0.5)
    lane = lax.broadcasted_iota(jnp.int32, (TILE, PAIR), 1)
    parts = [slice(b * size, (b + 1) * size) for b in range(2)]
    branches = [slice(prompt + b * size, prompt + (b + 1) * size) for b in range(2)]
    for i in range(blocks + 1):
        rows = slice(i * TILE, (i + 1) * TILE)
        q_left[:, rows] = (q_ref[rows] * scale).T
        do_left[:, rows] = (do_ref[rows].astype(F32) * inv_ref[rows]).astype(BF).T
    sums[...] = jnp.zeros_like(sums)
    for i in range(blocks + 1):
        rows = slice(i * TILE, (i + 1) * TILE)
        tiles = min(i + 1, blocks)
        seen = tiles * TILE
        scaled = (do_ref[rows].astype(F32) * inv_ref[rows]).astype(BF)
        do = both_halves(scaled)
        drops = scaled.astype(F32) * o_ref[rows].astype(F32)
        drop = [jnp.sum(lanes_of(drops, half), axis=1, keepdims=True) for half in range(2)]
        for j in range(tiles):
            keys = slice(j * TILE, (j + 1) * TILE)
            both = dot(do, v_ref[keys], (1, 1))
            for half in range(2):
                low = e_ref[half, :, begins[i] + j * TILE:begins[i] + (j + 1) * TILE]
                ds = low.astype(F32) * (both[half * TILE:(half + 1) * TILE] - drop[half])
                if i < blocks:
                    begin = TILE + prompt - (i + 1 - j) * TILE
                    sums[half, :, begin:begin + TILE] += ds
                else:
                    far_sums[half, :, size + j * TILE:size + (j + 1) * TILE] = ds
                down_ref[half, rows, keys] = ds.astype(BF)
                low_ref[half, rows, keys] = low
        down = jnp.concatenate([down_ref[half, rows, :seen] for half in range(2)], axis=0)
        dq = dot(down, k_ref[:seen], (1, 0))
        if i == blocks:
            more = []
            for half in range(2):
                lanes = slice(half * HD, (half + 1) * HD)
                low = e_ref[half, :, begins[i] + prompt:]
                own = jnp.concatenate(
                    [
                        dot(do[half * TILE + b * size:half * TILE + (b + 1) * size], v_ref[branches[b]], (1, 1))
                        for b in range(2)
                    ],
                    axis=0,
                )
                ds = low.astype(F32) * (own - drop[half])
                sums[half, :size, prompt:prompt + size] += ds[:size] + ds[size:]
                down = ds.astype(BF)
                more += [dot(down[parts[b]], k_ref[branches[b]], (1, 0)) for b in range(2)]
                for b in range(2):
                    dk_acc[lanes, branches[b]] = dot(q_left[lanes, branches[b]], down[parts[b]], (1, 0))
                    dv_acc[lanes, branches[b]] = dot(do_left[lanes, branches[b]], low[parts[b]], (1, 0))
            dq = dq + jnp.concatenate(more, axis=0)
        dq_ref[rows] = (jnp.where(lane < HD, dq[:TILE], dq[TILE:]) * (HD ** -0.5)).astype(BF)
    for half in range(2):
        lanes = slice(half * HD, (half + 1) * HD)
        for j in range(blocks):
            keys = slice(j * TILE, (j + 1) * TILE)
            rows = slice(j * TILE, count)
            dk_acc[lanes, keys] = dot(q_left[lanes, rows], down_ref[half, rows, keys], (1, 0))
            dv_acc[lanes, keys] = dot(do_left[lanes, rows], low_ref[half, rows, keys], (1, 0))
        strip_ref[half] = fold(sums[half])
        for b in range(2):
            wide = far_sums[half, b * size:(b + 1) * size]
            place = lax.broadcasted_iota(jnp.int32, wide.shape, 1)
            cross_ref[half, b] = fold(jnp.where(place < size, 0.0, wide))
    dk_ref[...] = dk_acc[...].T.astype(BF)
    dv_ref[...] = dv_acc[...].T.astype(BF)


def self_backward(qkv, do, mixed, expos, inverse, prompt, size, first, pairs):
    count = prompt + 2 * size
    width = probs_width(prompt, size)
    column = lambda part: pl.BlockSpec((None, count, PAIR), lambda j, part=part: (part, 0, first + j))
    flat = pl.BlockSpec((count, PAIR), lambda j: (0, j))
    given = pl.BlockSpec((count, PAIR), lambda j: (0, first + j))
    acc = pltpu.VMEM((PAIR, count), F32)
    return pl.pallas_call(
        functools.partial(self_back_kernel, prompt, size),
        grid=(pairs,),
        in_specs=[
            column(0),
            column(1),
            column(2),
            given,
            given,
            pl.BlockSpec((2, TILE, width), lambda j: (first + j, 0, 0)),
            given,
        ],
        out_specs=[
            flat,
            flat,
            flat,
            pl.BlockSpec((2, 1, prompt + TILE), lambda j: (j, 0, 0)),
            pl.BlockSpec((2, 2, 1, prompt + size), lambda j: (j, 0, 0, 0)),
        ],
        out_shape=[
            jax.ShapeDtypeStruct((count, pairs * PAIR), BF),
            jax.ShapeDtypeStruct((count, pairs * PAIR), BF),
            jax.ShapeDtypeStruct((count, pairs * PAIR), BF),
            jax.ShapeDtypeStruct((2 * pairs, 1, prompt + TILE), F32),
            jax.ShapeDtypeStruct((2 * pairs, 2, 1, prompt + size), F32),
        ],
        scratch_shapes=[
            pltpu.VMEM((2, TILE, prompt + TILE), F32),
            pltpu.VMEM((2, 2 * size, prompt + size), F32),
            acc,
            acc,
            pltpu.VMEM((2, count, prompt), BF),
            pltpu.VMEM((2, count, prompt), BF),
            pltpu.VMEM((PAIR, count), BF),
            pltpu.VMEM((PAIR, count), BF),
        ],
        compiler_params=params(),
        cost_estimate=cost(8 * pairs),
        name="self_backward",
    )(qkv, qkv, qkv, do, mixed, expos, inverse)


def distance_buckets(flipped, starts, prompt, size):
    bucket_ids = jnp.arange(BUCKETS, dtype=jnp.int32)
    whole = jnp.pad(flipped[size - 1:], (0, TILE - 1), constant_values=-1)
    padded = jnp.pad(flipped, (1, prompt), constant_values=-1)
    rows = [lax.dynamic_slice_in_dim(padded, prompt - starts[index], prompt + size, 0) for index in range(2)]
    order = jnp.concatenate([whole] + rows)
    return (order[:, None] == bucket_ids[None, :]).astype(F32)


def bias_gradient(strip, cross, buckets):
    sums = jnp.concatenate([strip[:, 0], cross[:, 0, 0], cross[:, 1, 0]], axis=1)
    return jnp.dot(sums, buckets, precision=lax.Precision.HIGHEST).T


def mlp_kernel(core_ref, x_ref, a_ref, a_t, dy_ref, wg_ref, wu_ref, wd_ref, out_ref, da_ref, away_ref, keep_ref,
               away_con_ref, keep_con_ref, y_ref, hid, dgate, dup, dwd, sem):
    count = a_ref.shape[0]
    step = pl.program_id(0)

    @pl.when(step == 0)
    def _():
        copy = pltpu.make_async_copy(x_ref, y_ref, sem)
        copy.start()
        da_ref[...] = jnp.zeros_like(da_ref)
        copy.wait()

    slope = 0.7978845608028654
    for i in range(0, count, TILE):
        rows = slice(i, i + TILE)
        g = dot(a_ref[rows], wg_ref[...], (1, 0))
        u = dot(a_ref[rows], wu_ref[...], (1, 0))
        dh = dot(dy_ref[rows], wd_ref[...], (1, 1))
        square = g * g
        th = jnp.tanh(slope * g * (1.0 + 0.044715 * square))
        half = 0.5 + 0.5 * th
        gelu = g * half
        slant = half + (0.5 * slope) * g * (1.0 - th * th) * (1.0 + 0.134145 * square)
        low = (gelu * u).astype(BF)
        dg = (dh * u * slant).astype(BF)
        du = (dh * gelu).astype(BF)
        hid[rows] = low
        dgate[rows] = dg
        dup[rows] = du
        y_ref[rows] += dot(low, wd_ref[...], (1, 0))
        da_ref[rows] += dot(dg, wg_ref[...], (1, 1)) + dot(du, wu_ref[...], (1, 1))
    dwd[pl.ds(pl.multiple_of(step * TILE, TILE), TILE)] = dot(hid[...], dy_ref[...], (0, 0))
    core = core_ref[0]
    for index, grad in enumerate((dgate, dup)):
        blocks = dot(a_t[...], grad[...], (1, 0)).astype(BF).reshape(D // 64, 2, 32, TILE)
        away_ref[index] = jnp.where(core == 0, blocks[:, 1], blocks[:, 0])
        keep_ref[index] = jnp.where(core == 0, blocks[:, 0], blocks[:, 1])

    @pl.when(step == pl.num_programs(0) - 1)
    def _():
        for i in range(0, count, TILE):
            out_ref[i:i + TILE] = y_ref[i:i + TILE].astype(BF)
        pairs, m, _ = keep_con_ref.shape
        for index in range(pairs):
            even = dwd[2 * index * m:(2 * index + 1) * m].astype(BF)
            odd = dwd[(2 * index + 1) * m:(2 * index + 2) * m].astype(BF)
            away_con_ref[index] = jnp.where(core == 0, odd, even)
            keep_con_ref[index] = jnp.where(core == 0, even, odd)


def mlp(core, after_two, inputs, turned, low_up, w_gate, w_up, w_con, owners):
    count = inputs.shape[0]
    hidden = w_gate.shape[1]
    m = hidden // owners
    once = pl.Buffered(1)
    flat = pl.BlockSpec((count, D), lambda t, c: (0, 0), pipeline_mode=once)
    column = pl.BlockSpec((D, TILE), lambda t, c: (0, t))
    row = pl.BlockSpec((TILE, D), lambda t, c: (t, 0))
    shared = pl.BlockSpec((2, D // 64, 32, TILE), lambda t, c: (0, 0, 0, t))
    part = jax.ShapeDtypeStruct((2, D // 64, 32, hidden), BF)
    con = pl.BlockSpec((owners // 2, m, D), lambda t, c: (0, 0, 0), pipeline_mode=once)
    con_part = jax.ShapeDtypeStruct((owners // 2, m, D), BF)
    tile = pltpu.VMEM((count, TILE), BF)
    return pl.pallas_call(
        mlp_kernel,
        grid_spec=pltpu.PrefetchScalarGridSpec(
            num_scalar_prefetch=1,
            grid=(hidden // TILE,),
            in_specs=[pl.BlockSpec(memory_space=pl.ANY), flat, whole_block(turned), flat, column, column, row],
            out_specs=[flat, flat, shared, shared, con, con],
            scratch_shapes=[
                pltpu.VMEM((count, D), F32),
                tile,
                tile,
                tile,
                pltpu.VMEM((hidden, D), F32),
                pltpu.SemaphoreType.DMA,
            ],
        ),
        out_shape=[
            jax.ShapeDtypeStruct((count, D), BF),
            jax.ShapeDtypeStruct((count, D), F32),
            part,
            part,
            con_part,
            con_part,
        ],
        compiler_params=params(),
        cost_estimate=cost(85),
        name="mlp",
    )(core, after_two, inputs, turned, low_up, w_gate, w_up, w_con)


def part_kernel(jobs, counts, plan_ref, *refs):
    lefts = refs[:1 + max(jobs)]
    rights = refs[len(lefts):len(lefts) + sum(counts)]
    rest = refs[len(lefts) + len(rights):]

    def finish(index, value):
        if len(rest) == 1:
            rest[0][index] = value.astype(BF).reshape(rest[0].shape[1:])
        else:
            got, away, stay, held = rest
            held[...] = (value + got[index].astype(F32).reshape(value.shape)).astype(BF).reshape(held.shape)
            for slot in range(2):
                away[slot, :, index] = held[:, plan_ref[1 + slot]]
                stay[slot, :, index] = held[:, plan_ref[3 + slot]]

    first = 0
    for index, left in enumerate(jobs):
        if counts[index] == 1:
            finish(index, dot(lefts[left][...], rights[first][...], (1, 0)))
        else:
            for tile in range(counts[index]):
                @pl.when(pl.program_id(0) == tile)
                def _(index=index, left=left, right=rights[first + tile]):
                    finish(index, dot(lefts[left][...], right[...], (1, 0)))
        first += counts[index]


def weight_part(plan, lefts, jobs, got=None):
    rights = [right if isinstance(right, list) else [right] for _, right in jobs]
    columns = sum(right.shape[1] for right in rights[0])
    counts = [len(right) for right in rights]
    m = 32

    def side(left):
        return pl.BlockSpec((None,) + left.shape[1:], lambda t, p: (p[0], 0, 0), pipeline_mode=pl.Buffered(1))

    def tile(right):
        return pl.BlockSpec((right.shape[0], TILE), lambda t, p: (0, t) if right.shape[1] > TILE else (0, 0))

    shared = pl.BlockSpec((len(jobs), D // 64, m, TILE), lambda t, p: (0, 0, 0, t))
    part = jax.ShapeDtypeStruct((len(jobs), D // 64, m, columns), BF)
    split = pl.BlockSpec((2, LINE, len(jobs), m, TILE), lambda t, p: (0, 0, 0, 0, t))
    half = jax.ShapeDtypeStruct((2, LINE, len(jobs), m, columns), BF)
    return pl.pallas_call(
        functools.partial(part_kernel, [left for left, _ in jobs], counts),
        grid_spec=pltpu.PrefetchScalarGridSpec(
            num_scalar_prefetch=1,
            grid=(columns // TILE,),
            in_specs=[side(left) for left in lefts]
            + [tile(value) for right in rights for value in right]
            + ([] if got is None else [shared]),
            out_specs=shared if got is None else [split, split],
            scratch_shapes=[] if got is None else [pltpu.VMEM((LINE, SIDE * SIDE, m, TILE), BF)],
        ),
        out_shape=part if got is None else [half, half],
        compiler_params=params(),
        cost_estimate=cost(2),
        name="weight_part",
    )(plan, *lefts, *(value for right in rights for value in right), *([] if got is None else [got]))


def root(value):
    return lax.rsqrt(jnp.mean(value * value, axis=1, keepdims=True) + EPS)


def normed(value, gain):
    return (value * root(value) * gain).astype(BF)


def norm_back(value, gain, upstream):
    scale = root(value)
    weighted = upstream * gain
    grad = scale * weighted - value * (scale * scale * scale) * jnp.mean(weighted * value, axis=1, keepdims=True)
    terms = upstream * value * scale
    return grad, jnp.sum(terms.reshape(-1, 8, D), axis=0)


def whole_block(value):
    zeros = (0,) * len(value.shape)
    return pl.BlockSpec(value.shape, lambda *index: zeros, pipeline_mode=pl.Buffered(1))


def row_block(columns=D):
    return pl.BlockSpec((TILE, columns), lambda i: (i, 0))


def turned_block():
    return pl.BlockSpec((D, TILE), lambda i: (0, i))


def sided_block():
    return pl.BlockSpec((2, D // 2, TILE), lambda i: (0, 0, i))


def put_sides(ref, value):
    columns = value.T.reshape(D // 64, 2, 32, value.shape[0])
    for side in range(2):
        ref[side] = columns[:, side].reshape(D // 2, value.shape[0])


def fetch(slots_ref, sources, held, sems, index):
    copies = []
    for number, source in enumerate(sources):
        for half in range(2):
            spot = slots_ref[2 * number + half, 0]
            side = slots_ref[2 * number + half, 1]
            copies.append(
                pltpu.make_async_copy(
                    source.at[half, index], held.at[index, :, spot, side], sems.at[index, 2 * number + half]
                )
            )
    return copies


def held_weight(held, index):
    return held[index].reshape(D, D)


def arrive(slots_ref, sources, held, in_sems, count):
    @pl.when(pl.program_id(0) == 0)
    def _():
        for index in range(count):
            for copy in fetch(slots_ref, sources, held, in_sems, index):
                copy.start()


def ready(slots_ref, sources, held, outs, in_sems, out_sems, index):
    @pl.when(pl.program_id(0) == 0)
    def _():
        for copy in fetch(slots_ref, sources, held, in_sems, index):
            copy.wait()
        pltpu.make_async_copy(held.at[index], outs[index], out_sems.at[index]).start()


def settle(held, outs, out_sems):
    @pl.when(pl.program_id(0) == pl.num_programs(0) - 1)
    def _():
        for index, out in enumerate(outs):
            pltpu.make_async_copy(held.at[index], out, out_sems.at[index]).wait()


def weight_specs(sources):
    _, count, line, rows, columns = sources[0].shape
    shape = (line, SIDE * SIDE, 2, rows, columns)
    anywhere = pl.BlockSpec(memory_space=pl.ANY)
    return (
        [pl.BlockSpec(memory_space=pltpu.SMEM)] + [anywhere] * 4,
        [anywhere] * count,
        [jax.ShapeDtypeStruct(shape, BF)] * count,
        [
            pltpu.VMEM((count,) + shape, BF),
            pltpu.SemaphoreType.DMA((count, 8)),
            pltpu.SemaphoreType.DMA((count,)),
        ],
    )


def enter_kernel(slots_ref, *refs):
    sources = refs[:4]
    x_ref, gain_ref, a_ref, qkv_ref = refs[4:8]
    outs = refs[8:11]
    held, in_sems, out_sems = refs[11:]
    arrive(slots_ref, sources, held, in_sems, 3)
    a = normed(x_ref[...].astype(F32), gain_ref[...])
    put_sides(a_ref, a)
    for index in range(3):
        ready(slots_ref, sources, held, outs, in_sems, out_sems, index)
        qkv_ref[index] = dot(a, held_weight(held, index), (1, 0)).astype(BF)
    settle(held, outs, out_sems)


def enter(stream_low, gain, slots, sources):
    count = stream_low.shape[0]
    weight_ins, weight_outs, weight_shapes, scratch = weight_specs(sources)
    turned, qkv, *weights = pl.pallas_call(
        enter_kernel,
        grid=(count // TILE,),
        in_specs=weight_ins + [row_block(), whole_block(gain)],
        out_specs=[sided_block(), pl.BlockSpec((3, TILE, D), lambda i: (0, i, 0))] + weight_outs,
        out_shape=[jax.ShapeDtypeStruct((2, D // 2, count), BF), jax.ShapeDtypeStruct((3, count, D), BF)] + weight_shapes,
        scratch_shapes=scratch,
        compiler_params=params(),
        cost_estimate=cost(12),
        name="enter",
    )(slots, *sources, stream_low, gain)
    return turned, qkv, [weight.reshape(D, D) for weight in weights]


def middle_kernel(parts, slots_ref, *refs):
    sources = refs[:4]
    x_ref, *mixed_refs = refs[4:5 + parts]
    (gain_two_ref, gain_three_ref, e_ref, x1_ref, x2_ref, a2_ref, a3_ref, q_ref, o_ref, p_ref, kv_ref, a3_t_ref,
     mixed_t_ref, e_t_ref, o_scr, inv_ref, *outs) = refs[5 + parts:26 + parts]
    held, in_sems, out_sems = refs[26 + parts:]
    arrive(slots_ref, sources, held, in_sems, 5)

    def weight(index):
        ready(slots_ref, sources, held, outs, in_sems, out_sems, index)
        return held_weight(held, index)

    for index in range(2):
        w = weight(2 + index)

        @pl.when(pl.program_id(0) == 0)
        def _(index=index, w=w):
            kv_ref[index] = dot(e_ref[...], w, (1, 0)).astype(BF)

    @pl.when(pl.program_id(0) == 0)
    def _():
        put_sides(e_t_ref, e_ref[...])

    w_first = weight(0)
    (mixed_ref,) = mixed_refs
    x1 = x_ref[...].astype(F32) + dot(mixed_ref[...], w_first, (1, 0))
    x1_ref[...] = x1
    a2 = normed(x1, gain_two_ref[...])
    put_sides(mixed_t_ref, mixed_ref[...])
    put_sides(a2_ref, a2)
    q_ref[...] = dot(a2, weight(1), (1, 0)).astype(BF)
    lane = lax.broadcasted_iota(jnp.int32, (TILE, PAIR), 1)
    inverses = jnp.zeros((TILE, PAIR), F32)
    for pair in range(PAIRS):
        columns = slice(pair * PAIR, (pair + 1) * PAIR)
        k = kv_ref[0, :, columns]
        v = kv_ref[1, :, columns]
        s = dot(both_halves(q_ref[:, columns] * BF(HD ** -0.5)), k, (1, 1))
        e = jnp.exp(s - jnp.max(s, axis=1, keepdims=True))
        inverse = 1.0 / jnp.sum(e, axis=1, keepdims=True)
        low = e.astype(BF)
        mixed = dot(low, v, (1, 0)) * inverse
        for half in range(2):
            rows = slice(half * TILE, (half + 1) * TILE)
            p_ref[2 * pair + half] = low[rows]
            inverses = jnp.where(lane == 2 * pair + half, inverse[rows], inverses)
        o_scr[:, columns] = jnp.where(lane < HD, mixed[:TILE], mixed[TILE:]).astype(BF)
    inv_ref[...] = inverses
    put_sides(o_ref, o_scr[...])
    x2 = x1_ref[...] + dot(o_scr[...], weight(4), (1, 0))
    x2_ref[...] = x2
    a3 = normed(x2, gain_three_ref[...])
    a3_ref[...] = a3
    a3_t_ref[...] = a3.T
    settle(held, outs, out_sems)


def middle(stream_low, mixed, gain_two, gain_three, encoder, slots, sources):
    count = stream_low.shape[0]
    enc = encoder.shape[0]
    low = jax.ShapeDtypeStruct((count, D), BF)
    wide = jax.ShapeDtypeStruct((count, D), F32)
    turned = jax.ShapeDtypeStruct((D, count), BF)
    sided = jax.ShapeDtypeStruct((2, D // 2, count), BF)
    weight_ins, weight_outs, weight_shapes, scratch = weight_specs(sources)
    *results, w1, w2, w3, w4, w5 = pl.pallas_call(
        functools.partial(middle_kernel, len(mixed)),
        grid=(count // TILE,),
        in_specs=weight_ins
        + [row_block()]
        + [row_block(part.shape[1]) for part in mixed]
        + [whole_block(value) for value in (gain_two, gain_three, encoder)],
        out_specs=[row_block(), row_block(), sided_block(), row_block(), row_block(), sided_block()]
        + [
            pl.BlockSpec((HEADS, TILE, enc), lambda i: (0, i, 0)),
            pl.BlockSpec((2, enc, D), lambda i: (0, 0, 0)),
            turned_block(),
            sided_block(),
            pl.BlockSpec((2, D // 2, enc), lambda i: (0, 0, 0)),
            row_block(),
            row_block(PAIR),
        ]
        + weight_outs,
        out_shape=[
            wide,
            wide,
            sided,
            low,
            low,
            sided,
            jax.ShapeDtypeStruct((HEADS, count, enc), BF),
            jax.ShapeDtypeStruct((2, enc, D), BF),
            turned,
            sided,
            jax.ShapeDtypeStruct((2, D // 2, enc), BF),
            low,
            jax.ShapeDtypeStruct((count, PAIR), F32),
        ]
        + weight_shapes,
        scratch_shapes=scratch,
        compiler_params=params(),
        cost_estimate=cost(30),
        name="middle",
    )(slots, *sources, stream_low, *mixed, gain_two, gain_three, encoder)
    return results + [[weight.reshape(D, D) for weight in (w1, w2, w3, w4, w5)]]


def middle_back_kernel(dy_ref, da3_ref, x2_ref, x1_ref, q_ref, o_ref, inv_ref, p_ref, kv_ref, gain_two_ref, gain_three_ref, wc_ref, wq_ref,
                       wo_ref, *refs):
    before = refs[:-9]
    low2_ref, dq_ref, dx1_ref, low1_ref, do1_ref, dkv_ref, sums_ref, gains_ref, do_ref = refs[-9:]
    dk_acc, dv_acc = sums_ref.at[0], sums_ref.at[1]
    step = pl.program_id(0)

    @pl.when(step == 0)
    def _():
        sums_ref[...] = before[-2][...] if before else jnp.zeros_like(sums_ref)
        gains_ref[...] = before[-1][...] if before else jnp.zeros_like(gains_ref)

    back, terms = norm_back(x2_ref[...], gain_three_ref[...], da3_ref[...])
    gains_ref[1] += terms
    dx2 = dy_ref[...].astype(F32) + back
    dx1_ref[...] = dx2
    low2 = dx2.astype(BF)
    low2_ref[...] = low2
    do_ref[...] = dot(low2, wo_ref[...], (1, 1)).astype(BF)
    lane = lax.broadcasted_iota(jnp.int32, (TILE, PAIR), 1)
    for pair in range(PAIRS):
        columns = slice(pair * PAIR, (pair + 1) * PAIR)
        k = kv_ref[0, :, columns]
        v = kv_ref[1, :, columns]
        inverse = jnp.where(lane < HD, inv_ref[:, 2 * pair:2 * pair + 1], inv_ref[:, 2 * pair + 1:2 * pair + 2])
        do = (do_ref[:, columns].astype(F32) * inverse).astype(BF)
        drops = do.astype(F32) * o_ref[:, columns].astype(F32)
        q_left, do_left = (q_ref[:, columns] * BF(HD ** -0.5)).T, do.T
        drop = jnp.sum(both_halves(drops), axis=1, keepdims=True)
        low = jnp.concatenate([p_ref[2 * pair], p_ref[2 * pair + 1]], axis=0)
        down = (low.astype(F32) * (dot(both_halves(do), v, (1, 1)) - drop)).astype(BF)
        dq = dot(down, k, (1, 0))
        for half in range(2):
            rows = slice(half * HD, (half + 1) * HD)
            tile = slice(half * TILE, (half + 1) * TILE)
            places = slice(pair * PAIR + half * HD, pair * PAIR + (half + 1) * HD)
            dk_acc[places] += dot(q_left[rows], down[tile], (1, 0))
            dv_acc[places] += dot(do_left[rows], low[tile], (1, 0))
        dq_ref[:, columns] = (jnp.where(lane < HD, dq[:TILE], dq[TILE:]) * (HD ** -0.5)).astype(BF)
    da2 = dot(dq_ref[...], wq_ref[...], (1, 1))
    back, terms = norm_back(x1_ref[...], gain_two_ref[...], da2)
    gains_ref[0] += terms
    dx1 = dx1_ref[...] + back
    dx1_ref[...] = dx1
    low1 = dx1.astype(BF)
    low1_ref[...] = low1
    do1_ref[...] = dot(low1, wc_ref[...], (1, 1)).astype(BF)

    @pl.when(step == pl.num_programs(0) - 1)
    def _():
        dkv_ref[0] = dk_acc[...].T.astype(BF)
        dkv_ref[1] = dv_acc[...].T.astype(BF)


def middle_back(first, blocks, low_up, grad_three, after_two, after_one, query_two, mixed_two, inverse_two, expos_two,
                kv_two, gain_two, gain_three, w_comb_one, w_query_two, w_comb_two, before=None):
    count = low_up.shape[0]
    enc = kv_two.shape[1]
    low = jax.ShapeDtypeStruct((count, D), BF)
    wide = jax.ShapeDtypeStruct((count, D), F32)
    rows = pl.BlockSpec((TILE, D), lambda i: (first + i, 0))
    sums = jax.ShapeDtypeStruct((2, D, enc), F32)
    gains = jax.ShapeDtypeStruct((2, 8, D), F32)
    whole = (kv_two, gain_two, gain_three, w_comb_one, w_query_two, w_comb_two)
    operands = (low_up, grad_three, after_two, after_one, query_two, mixed_two, inverse_two, expos_two) + whole
    more = [] if before is None else list(before[:5]) + list(before[6:])
    aliases = {} if before is None else {len(operands) + index: index for index in range(5)}
    return pl.pallas_call(
        middle_back_kernel,
        grid=(blocks,),
        in_specs=[rows] * 6
        + [
            pl.BlockSpec((TILE, PAIR), lambda i: (first + i, 0)),
            pl.BlockSpec((HEADS, TILE, enc), lambda i: (0, first + i, 0)),
        ]
        + [whole_block(value) for value in whole]
        + ([] if before is None else [pl.BlockSpec(memory_space=pl.ANY)] * 5 + [whole_block(sums), whole_block(gains)]),
        out_specs=[rows] * 5
        + [
            pl.BlockSpec((2, enc, D), lambda i: (0, 0, 0)),
            pl.BlockSpec((2, D, enc), lambda i: (0, 0, 0)),
            pl.BlockSpec((2, 8, D), lambda i: (0, 0, 0)),
        ],
        out_shape=[low, low, wide, low, low, jax.ShapeDtypeStruct((2, enc, D), BF), sums, gains],
        scratch_shapes=[pltpu.VMEM((TILE, D), BF)],
        input_output_aliases=aliases,
        compiler_params=params(),
        cost_estimate=cost(45),
        name="middle_back",
    )(*operands, *more)


def leave_kernel(parts, plan_ref, x_ref, dx1_ref, *refs):
    grads = refs[:3 * parts]
    gain_ref, wq_ref, wk_ref, wv_ref, out_ref, gains_ref = refs[3 * parts:]

    @pl.when(pl.program_id(0) == 0)
    def _():
        gains_ref[...] = jnp.zeros_like(gains_ref)

    da = None
    end = 0
    for index in range(parts):
        columns = slice(end, end + grads[3 * index].shape[1])
        end = columns.stop
        for which, w_ref in enumerate((wq_ref, wk_ref, wv_ref)):
            part = dot(grads[3 * index + which][...], w_ref[:, columns], (1, 1))
            da = part if da is None else da + part
    back, terms = norm_back(x_ref[...].astype(F32), gain_ref[...], da)
    gains_ref[...] += terms
    out_ref[...] = dx1_ref[...] + back


def leave(plan, blocks, stream_low, grad_after_one, parts, gain, w_query, w_key, w_value):
    weights = (w_query, w_key, w_value)
    flat = [value for part in parts for value in part]

    def rows(value):
        return pl.BlockSpec((TILE, value.shape[1]), lambda i, p: (p[i], 0))

    return pl.pallas_call(
        functools.partial(leave_kernel, len(parts)),
        grid_spec=pltpu.PrefetchScalarGridSpec(
            num_scalar_prefetch=1,
            grid=(blocks,),
            in_specs=[rows(stream_low), rows(grad_after_one)]
            + [rows(value) for value in flat]
            + [whole_block(value) for value in (gain,) + weights],
            out_specs=[pl.BlockSpec((TILE, D), lambda i, p: (i, 0)), pl.BlockSpec((8, D), lambda i, p: (0, 0))],
        ),
        out_shape=[jax.ShapeDtypeStruct((blocks * TILE, D), F32), jax.ShapeDtypeStruct((8, D), F32)],
        compiler_params=params(),
        cost_estimate=cost(2),
        name="leave",
    )(plan, stream_low, grad_after_one, *flat, gain, *weights)


def update_kernel(count, lows, factor_ref, *refs):
    ins = refs[:4 * count]
    outs = refs[4 * count:7 * count + lows]
    held = refs[7 * count + lows:11 * count + lows]
    ready = refs[11 * count + lows:14 * count + 2 * lows]
    in_sems, out_sems = refs[14 * count + 2 * lows:]
    arrivals = [pltpu.make_async_copy(ref, kept, in_sems.at[n]) for n, (ref, kept) in enumerate(zip(ins, held))]
    departures = [pltpu.make_async_copy(kept, ref, out_sems.at[n]) for n, (ref, kept) in enumerate(zip(outs, ready))]
    for index in range(count):
        for group in range(4):
            arrivals[group * count + index].start()
    factor = factor_ref[0]
    for index in range(count):
        for group in range(4):
            arrivals[group * count + index].wait()
        weight, first, second, grad = (held[group * count + index] for group in range(4))
        states = adam(weight[...], first[...], second[...], grad[...] * factor, RATES[index])
        for place, value in enumerate(states):
            ready[3 * index + place][...] = value
            departures[3 * index + place].start()
        if index < lows:
            ready[3 * count + index][...] = states[0].astype(BF)
            departures[3 * count + index].start()
    for copy in departures:
        copy.wait()


def update(factor, weights, firsts, seconds, grads, lows=4):
    count = len(weights)
    operands = tuple(weights) + tuple(firsts) + tuple(seconds) + tuple(grads)
    shapes = [jax.ShapeDtypeStruct(weight.shape, F32) for weight in weights for _ in range(3)]
    shapes += [jax.ShapeDtypeStruct(weight.shape, BF) for weight in weights[:lows]]
    anywhere = pl.BlockSpec(memory_space=pl.ANY)
    outs = pl.pallas_call(
        functools.partial(update_kernel, count, lows),
        in_specs=[pl.BlockSpec(memory_space=pltpu.SMEM)] + [anywhere] * len(operands),
        out_specs=[anywhere] * len(shapes),
        out_shape=shapes,
        scratch_shapes=[pltpu.VMEM(value.shape, F32) for value in operands]
        + [pltpu.VMEM(shape.shape, shape.dtype) for shape in shapes]
        + [pltpu.SemaphoreType.DMA((len(operands),)), pltpu.SemaphoreType.DMA((len(shapes),))],
        compiler_params=params(),
        cost_estimate=cost(5),
        name="update",
    )(factor.reshape(1), *operands)
    return [outs[3 * index:3 * index + 3] for index in range(count)], outs[3 * count:]


SIDE = 2
LINE = 4
AXES = ("dp", "fsdp")


def place_of(z, y, x, core):
    return ((z * SIDE + y) * SIDE + x) * 2 + core


def moves(rule):
    every = [(z, y, x, c) for z in range(LINE) for y in range(SIDE) for x in range(SIDE) for c in range(2)]
    return [(place_of(*here), place_of(*rule(*here))) for here in every]


def send(value, rule):
    return lax.ppermute(value, AXES, moves(rule))


def along_line(shift):
    return lambda z, y, x, c: ((z + shift) % LINE, y, x, c)


def line_far(z, y, x, c):
    return (z ^ 2, y, x, c)


def line_near(z, y, x, c):
    return (z ^ 1, y, x, c)


def first_flip(z, y, x, c):
    return (z, y, 1 - x, c) if c == 0 else (z, 1 - y, x, c)


def second_flip(z, y, x, c):
    return (z, 1 - y, x, c) if c == 0 else (z, y, 1 - x, c)


def core_flip(z, y, x, c):
    return (z, y, x, 1 - c)


def spots(y, x, core):
    here = y * SIDE + x
    along_x = y * SIDE + 1 - x
    along_y = (1 - y) * SIDE + x
    across = (1 - y) * SIDE + 1 - x
    near = jnp.where(core == 0, along_x, along_y)
    far = jnp.where(core == 0, along_y, along_x)
    return here, near, far, across


def put_kernel(z_ref, shard, far, near, out, sems):
    z = z_ref[0]
    sources = [(shard, z), (far, z ^ 2), (near.at[0], z ^ 1), (near.at[1], z ^ 3)]
    copies = [
        pltpu.make_async_copy(source, out.at[:, slot], sems.at[index])
        for index, (source, slot) in enumerate(sources)
    ]
    for copy in copies:
        copy.start()
    for copy in copies:
        copy.wait()


def put_in_line(shard, far, near, z):
    count, rows, columns = shard.shape
    return pl.pallas_call(
        put_kernel,
        in_specs=[pl.BlockSpec(memory_space=pltpu.SMEM)] + [pl.BlockSpec(memory_space=pl.ANY)] * 3,
        out_specs=pl.BlockSpec(memory_space=pltpu.VMEM),
        out_shape=jax.ShapeDtypeStruct((count, LINE, rows, columns), shard.dtype),
        scratch_shapes=[pltpu.SemaphoreType.DMA((LINE,))],
        compiler_params=params(40),
        cost_estimate=cost(1),
        name="put_in_line",
    )(z[None], shard, far, near)


def assemble_kernel(slots_ref, *refs):
    sources = refs[:4]
    outs, sems = refs[4:-1], refs[-1]
    copies = []
    for index, source in enumerate(sources):
        for half in range(2):
            spot = slots_ref[2 * index + half, 0]
            side = slots_ref[2 * index + half, 1]
            for k, out in enumerate(outs):
                copies.append(
                    pltpu.make_async_copy(source.at[half, k], out.at[:, spot, side], sems.at[len(copies)])
                )
    for copy in copies:
        copy.start()
    for copy in copies:
        copy.wait()


def assemble(sources, slots):
    _, count, line, rows, columns = sources[0].shape
    shape = (line, SIDE * SIDE, 2, rows, columns)
    outs = pl.pallas_call(
        assemble_kernel,
        in_specs=[pl.BlockSpec(memory_space=pltpu.SMEM)] + [pl.BlockSpec(memory_space=pl.ANY)] * 4,
        out_specs=[pl.BlockSpec(memory_space=pltpu.VMEM)] * count,
        out_shape=[jax.ShapeDtypeStruct(shape, sources[0].dtype)] * count,
        scratch_shapes=[pltpu.SemaphoreType.DMA((8 * count,))],
        compiler_params=params(40),
        cost_estimate=cost(2 * count),
        name="assemble",
    )(slots, *sources)
    return [out.reshape(line * SIDE * SIDE * 2 * rows, columns) for out in outs]


def tie(*values):
    return lax.optimization_barrier(values)


def line_stage(shard):
    return [send(shard, along_line(shift)) for shift in range(1, LINE)]


def piece_slots(place):
    _, y, x, core = place
    mine = spots(y, x, core)
    theirs = spots(y, x, 1 - core)
    order = [(mine[0], core), (mine[1], core), (theirs[0], 1 - core), (theirs[1], 1 - core)]
    order += [(mine[2], core), (mine[3], core), (theirs[2], 1 - core), (theirs[3], 1 - core)]
    return jnp.stack([jnp.stack(pair) for pair in order])


def add_split_kernel(spots_ref, one_ref, two_ref, away_ref, stay_ref):
    slot = pl.program_id(0)
    value = one_ref[...] + two_ref[...]

    for out_ref, here in ((away_ref, slot < 2), (stay_ref, slot >= 2)):
        @pl.when(here)
        def _(out_ref=out_ref):
            for index in range(value.shape[0]):
                out_ref[0, :, index] = value[index, :, 0]


def add_split(keep, received, place):
    _, y, x, core = place
    here, near, far, across = spots(y, x, core)
    count, _, rows, columns = keep.shape
    grid = (count, LINE, SIDE * SIDE, rows, columns)
    wide = columns if columns <= D else columns // 2
    source = pl.BlockSpec((count, LINE, 1, rows, wide), lambda j, t, s: (0, 0, s[j], 0, t))
    out = jax.ShapeDtypeStruct((2, LINE, count, rows, columns), BF)
    block = (1, LINE, count, rows, wide)
    return pl.pallas_call(
        add_split_kernel,
        grid_spec=pltpu.PrefetchScalarGridSpec(
            num_scalar_prefetch=1,
            grid=(4, columns // wide),
            in_specs=[source, source],
            out_specs=[
                pl.BlockSpec(
                    block, lambda j, t, s: (jnp.minimum(j, 1), 0, 0, 0, jnp.where(j < 2, t, columns // wide - 1))
                ),
                pl.BlockSpec(block, lambda j, t, s: (jnp.maximum(j - 2, 0), 0, 0, 0, jnp.where(j < 2, 0, t))),
            ],
        ),
        out_shape=[out, out],
        compiler_params=params(),
        cost_estimate=cost(1),
        name="add_split",
    )(jnp.stack([far, across, here, near]), keep.reshape(grid), received.reshape(grid))


def plus(one, two):
    return (one.astype(F32) + two.astype(F32)).astype(BF)


def line_split(line, place):
    z = place[0]

    def at(index):
        return lax.dynamic_index_in_dim(line, index, 0, keepdims=False)

    return (at(z), at(z ^ 2)), jnp.stack([at(z ^ 1), at(z ^ 3)])


def add_in_order(value, received, own, owners):
    total = None
    for index in range(4):
        term = jnp.where(own == index, value, 0.0)
        for part, owner in zip(received, owners):
            term = term + jnp.where(owner == index, part, 0.0)
        total = term if total is None else total + term
    return total


def sum_everywhere(value, place):
    z, y, x, core = place
    parts = [send(value, along_line(shift)) for shift in range(1, LINE)]
    value = add_in_order(value, parts, z, [(z - shift) % LINE for shift in range(1, LINE)])
    flips = [(0, 1), (1, 0), (1, 1)]
    parts = [send(value, lambda z, y, x, c, dy=dy, dx=dx: (z, y ^ dy, x ^ dx, c)) for dy, dx in flips]
    value = add_in_order(
        value, parts, y * SIDE + x, [jnp.bitwise_xor(y, dy) * SIDE + jnp.bitwise_xor(x, dx) for dy, dx in flips]
    )
    return value + send(value, core_flip)


def swap_halves(parts, core):
    def block(index):
        return jnp.concatenate(
            [lax.dynamic_index_in_dim(part, index, 0, keepdims=False).reshape(-1, D) for part in parts], axis=0
        )

    mine = block(core)
    theirs = send(block(1 - core), core_flip)
    first = jnp.where(core == 0, mine, theirs)
    second = jnp.where(core == 0, theirs, mine)
    whole, begin = [], 0
    for part in parts:
        end = begin + part.size // 2 // D
        whole.append(jnp.concatenate([first[begin:end], second[begin:end]], axis=0))
        begin = end
    return whole


def hand_over(parts, core):
    halves = [part.reshape((2, -1, D)) for part in parts]

    def block(index):
        return jnp.concatenate([lax.dynamic_index_in_dim(part, index, 0, keepdims=False) for part in halves], axis=0)

    return block(core), send(block(1 - core), core_flip)


def both_groups(mine, other, core):
    return jnp.stack([jnp.where(core == 0, mine, other), jnp.where(core == 0, other, mine)])


def matmul(left, right):
    return jnp.dot(left, right, preferred_element_type=F32)


def matmul_t(left, right):
    return lax.dot_general(left, right, (((1,), (1,)), ((), ())), preferred_element_type=F32)


def paired_body(
    prompt_states,
    branch_states,
    encoder_states,
    branch_start,
    bucket_table,
    prompt_cotangent,
    branch_cotangent,
    projections,
    projections_first,
    projections_second,
    combiners,
    combiners_first,
    combiners_second,
    expansion,
    expansion_first,
    expansion_second,
    contraction,
    contraction_first,
    contraction_second,
    norm_gains,
    gains_first,
    gains_second,
    position_bias,
    bias_first,
    bias_second,
):
    rows_here = prompt_states.shape[1]
    prompt = 2 * rows_here
    size = branch_states.shape[2]
    place_index = lax.axis_index("dp")
    core = lax.axis_index("fsdp")
    place = (place_index // (SIDE * SIDE), place_index // SIDE % SIDE, place_index % SIDE, core)

    z = place[0]
    core_ref = core[None]

    shard_qkv = projections[:3].astype(BF)
    shard_mid = jnp.concatenate([combiners[:1], projections[3:], combiners[1:]], axis=0).astype(BF)
    shard_exp = expansion.astype(BF)
    shard_con = contraction[None].astype(BF)
    far_line_qkv = send(shard_qkv, line_far)

    other_start = send(lax.dynamic_index_in_dim(branch_start, 1 - core, 0, keepdims=False), core_flip)
    own_start = lax.dynamic_index_in_dim(branch_start, core, 0, keepdims=False)
    starts = jnp.concatenate(
        [jnp.where(core == 0, own_start, other_start), jnp.where(core == 0, other_start, own_start)]
    )
    gain_rows = [norm_gains[index:index + 1] for index in range(3)]

    bucket_ids = jnp.arange(BUCKETS, dtype=jnp.int32)
    flipped_table = jnp.flip(bucket_table)
    flipped_onehot = (flipped_table[:, None] == bucket_ids[None, :]).astype(F32)
    flipped_bias = jnp.dot(flipped_onehot, position_bias, precision=lax.Precision.HIGHEST).T
    buckets = distance_buckets(flipped_table, starts, prompt, size)
    slots = piece_slots(place)

    far_line_qkv, starts = tie(far_line_qkv, starts)
    near_line_qkv = send(jnp.stack([shard_qkv, far_line_qkv]), line_near)
    near_line_qkv, prompt_states, shard_mid = tie(near_line_qkv, prompt_states, shard_mid)
    far_line_mid = send(shard_mid, line_far)
    prompt_rows, branch_rows, prompt_up, branch_up, encoder = swap_halves(
        [prompt_states, branch_states, prompt_cotangent, branch_cotangent, encoder_states], core
    )
    own_qkv = put_in_line(shard_qkv, far_line_qkv, near_line_qkv, z)
    near_qkv = send(own_qkv, first_flip)
    near_qkv, own_qkv = tie(near_qkv, own_qkv)
    close_qkv = jnp.stack([own_qkv, near_qkv])
    far_qkv = send(close_qkv, second_flip)
    close_qkv, far_line_mid = tie(close_qkv, far_line_mid)
    near_line_mid = send(jnp.stack([shard_mid, far_line_mid]), line_near)
    close_qkv_two = send(close_qkv, core_flip)
    base, branch = bias_rows(flipped_bias, starts, prompt, size)
    stream_low = jnp.concatenate([prompt_rows, branch_rows], axis=0)
    low_up = jnp.concatenate([prompt_up, branch_up], axis=0)
    far_qkv, near_line_mid, close_qkv_two, stream_low, low_up, encoder, base, branch, shard_exp, shard_con = tie(
        far_qkv, near_line_mid, close_qkv_two, stream_low, low_up, encoder, base, branch, shard_exp, shard_con
    )
    far_qkv_two = send(far_qkv, core_flip)
    own_mid = put_in_line(shard_mid, far_line_mid, near_line_mid, z)
    near_mid = send(own_mid, first_flip)
    far_line_exp = send(shard_exp, line_far)
    stream_low, own_mid, far_qkv_two = tie(stream_low, own_mid, far_qkv_two)

    turned_one, qkv, (w_query, w_key, w_value) = enter(
        stream_low, gain_rows[0], slots, [close_qkv, close_qkv_two, far_qkv, far_qkv_two]
    )
    qkv, near_mid, far_line_exp, shard_con = tie(qkv, near_mid, far_line_exp, shard_con)
    close_mid = jnp.stack([own_mid, near_mid])
    far_mid = send(close_mid, second_flip)
    near_line_exp = send(jnp.stack([shard_exp, far_line_exp]), line_near)
    far_line_con = send(shard_con, line_far)
    close_mid_two = send(close_mid, core_flip)
    qkv, close_mid = tie(qkv, close_mid)
    most = PAIRS // 2
    heads = self_forward(qkv, base, branch, starts, prompt, size, 0, most)
    *heads, qkv, far_mid, close_mid_two, near_line_exp, far_line_con = tie(
        *heads, qkv, far_mid, close_mid_two, near_line_exp, far_line_con
    )
    own_exp = put_in_line(shard_exp, far_line_exp, near_line_exp, z)
    near_exp = send(own_exp, first_flip)
    far_mid_two = send(far_mid, core_flip)
    near_line_con = send(jnp.stack([shard_con, far_line_con]), line_near)
    qkv, own_exp, far_mid = tie(qkv, own_exp, far_mid)
    heads = self_forward(qkv, base, branch, starts, prompt, size, most, PAIRS - most, heads)
    *heads, far_mid_two, near_exp, near_line_con = tie(*heads, far_mid_two, near_exp, near_line_con)
    mixed_one, expos, inverse = heads
    close_exp = jnp.stack([own_exp, near_exp])
    far_exp = send(close_exp, second_flip)
    close_exp_two = send(close_exp, core_flip)
    own_con = put_in_line(shard_con, far_line_con, near_line_con, z)
    near_con = send(own_con, first_flip)
    mixed_one, close_exp, own_con = tie(mixed_one, close_exp, own_con)
    (after_one, after_two, turned_two, input_three, query_two, turned_mixed_two, expos_two, kv_two, turned_three,
     turned_mixed_one, turned_encoder, mixed_two, inverse_two, weights_mid) = middle(
        stream_low,
        [mixed_one],
        gain_rows[1],
        gain_rows[2],
        encoder,
        slots,
        [close_mid, close_mid_two, far_mid, far_mid_two],
    )
    w_comb_one, w_query_two, w_key_two, w_value_two, w_comb_two = weights_mid
    input_three, far_exp, near_con, close_exp_two = tie(input_three, far_exp, near_con, close_exp_two)
    far_exp_two = send(far_exp, core_flip)
    close_con = jnp.stack([own_con, near_con])
    far_con = send(close_con, second_flip)
    close_con_two = send(close_con, core_flip)
    w_gate, w_up = assemble([close_exp, close_exp_two, far_exp, far_exp_two], slots)
    w_gate, w_up, far_con, close_con_two = tie(w_gate, w_up, far_con, close_con_two)
    far_con_two = send(far_con, core_flip)
    w_con = assemble([close_con, close_con_two, far_con, far_con_two], slots)[0]

    owners = LINE * SIDE * SIDE * 2
    output, grad_three, away_exp, keep_exp, away_con, keep_con = mlp(
        core_ref, after_two, input_three, turned_three, low_up, w_gate, w_up, w_con, owners
    )
    got_exp = send(away_exp, core_flip)
    got_con = send(away_con[None], core_flip)
    low_up, away_exp, away_con, grad_three, output = tie(low_up, away_exp, away_con, grad_three, output)
    own_output, other_output = hand_over([output[:prompt], output[prompt:]], core)
    low_up, own_output = tie(low_up, own_output)

    def middle_part(first, blocks, before=None):
        return middle_back(
            first,
            blocks,
            low_up,
            grad_three,
            after_two,
            after_one,
            query_two,
            mixed_two,
            inverse_two,
            expos_two,
            kv_two,
            gain_rows[1],
            gain_rows[2],
            w_comb_one,
            w_query_two,
            w_comb_two,
            before,
        )

    before = middle_part(0, 1)
    *before, got_exp, got_con = tie(*before, got_exp, got_con)
    away_con, stay_con = add_split(keep_con[None], got_con, place)
    got_con = send(away_con, second_flip)
    away_exp, stay_exp = add_split(keep_exp, got_exp, place)
    got_exp = send(away_exp, second_flip)
    *before, away_exp, away_con = tie(*before, away_exp, away_con)
    (cross_low, query_two_low, grad_after_one, self_low, grad_mixed_one, kv_two_low, _, gain_back) = middle_part(
        1, prompt // TILE + 2 * size // TILE - 1, before
    )
    _, y, x, _ = place
    here, near, far, across = spots(y, x, core)
    keep_plan = jnp.stack([core, far, across, here, near])
    away_plan = jnp.stack([1 - core, far, across, here, near])
    lefts_mid = [turned_mixed_one, turned_two, turned_encoder, turned_mixed_two]
    jobs_mid = [(0, self_low), (1, query_two_low), (2, kv_two_low[0]), (2, kv_two_low[1]), (3, cross_low)]
    away_mid = weight_part(away_plan, lefts_mid, jobs_mid)
    encoder_grad = matmul_t(kv_two_low[0], w_key_two) + matmul_t(kv_two_low[1], w_value_two)
    away_mid, encoder_grad, other_output, got_exp, got_con = tie(away_mid, encoder_grad, other_output, got_exp, got_con)
    got_mid = send(away_mid, core_flip)
    near_con = plus(stay_con[1], got_con[1])
    got_near_con = send(near_con, first_flip)
    near_exp = plus(stay_exp[1], got_exp[1])
    got_near_exp = send(near_exp, first_flip)
    own_encoder, other_encoder = hand_over([encoder_grad], core)
    grad_mixed_one, away_mid, near_exp, near_con, own_encoder = tie(
        grad_mixed_one, away_mid, near_exp, near_con, own_encoder
    )

    half = PAIRS // 2

    def attend_back(first, pairs, *values):
        part = self_backward(qkv, grad_mixed_one, mixed_one, expos, inverse, prompt, size, first, pairs)
        first, *rest = tie(part[0], grad_mixed_one, *values)
        return ((first,) + tuple(part[1:]), *rest)

    def jobs_of(*parts):
        return [(0, [part[i] for part in parts] if len(parts) > 1 else parts[0][i]) for i in range(3)]

    part_one, grad_mixed_one, got_mid, other_encoder, got_near_con, got_near_exp = attend_back(
        0, half, got_mid, other_encoder, got_near_con, got_near_exp
    )
    line_exp, away_exp = line_split(plus(plus(stay_exp[0], got_exp[0]), got_near_exp), place)
    got_line_exp = send(away_exp, line_near)
    away_mid, stay_mid = weight_part(keep_plan, lefts_mid, jobs_mid, got_mid)
    got_mid = send(away_mid, second_flip)
    line_con, away_con = line_split(plus(plus(stay_con[0], got_con[0]), got_near_con), place)
    got_line_con = send(away_con, line_near)
    away_plan, away_exp, away_con, away_mid = tie(away_plan, away_exp, away_con, away_mid)
    away_one = weight_part(away_plan, [turned_one], jobs_of(part_one))
    got_one = send(away_one, core_flip)
    grad_mixed_one, away_one = tie(grad_mixed_one, away_one)

    part_two, grad_mixed_one, got_one, got_mid, got_line_exp, away_plan = attend_back(
        half, half, got_one, got_mid, got_line_exp, away_plan
    )
    near_mid = plus(stay_mid[1], got_mid[1])
    got_near_mid = send(near_mid, first_flip)
    away_plan, near_mid = tie(away_plan, near_mid)
    away_two = weight_part(away_plan, [turned_one], jobs_of(part_two))
    got_two = send(away_two, core_flip)
    last_exp = plus(line_exp[1], got_line_exp[1])
    got_last_exp = send(last_exp, line_far)
    keep_plan, away_two, last_exp = tie(keep_plan, away_two, last_exp)
    away_one, stay_one = weight_part(keep_plan, [turned_one], jobs_of(part_one), got_one)
    got_one = send(away_one, second_flip)
    leave_values = (
        stream_low,
        grad_after_one,
        [part_one[:3], part_two[:3]],
        gain_rows[0],
        w_query,
        w_key,
        w_value,
    )
    blocks = prompt // TILE // 2
    steps = jnp.arange(blocks, dtype=jnp.int32)
    theirs_plan = jnp.concatenate([(1 - core) * blocks + steps, jnp.full((1,), 2 * blocks, jnp.int32)])
    ours_plan = core * blocks + steps

    theirs_plan, away_one, got_two = tie(theirs_plan, away_one, got_two)
    theirs_grad, gain_one = leave(theirs_plan, blocks + 1, *leave_values)
    theirs_grad, got_one, got_near_mid, keep_plan, got_line_con = tie(
        theirs_grad, got_one, got_near_mid, keep_plan, got_line_con
    )
    away_two, stay_two = weight_part(keep_plan, [turned_one], jobs_of(part_two), got_two)
    got_two = send(away_two, second_flip)
    away_two, stay_one, stay_mid, theirs_grad = tie(away_two, stay_one, stay_mid, theirs_grad)
    near_one = plus(stay_one[1], got_one[1])
    got_near_one = send(near_one, first_flip)
    line_mid, away_mid = line_split(plus(plus(stay_mid[0], got_mid[0]), got_near_mid), place)
    got_line_mid = send(away_mid, line_near)
    last_con = plus(line_con[1], got_line_con[1])
    got_last_con = send(last_con, line_far)
    ours_plan, near_one, away_mid, last_con = tie(ours_plan, near_one, away_mid, last_con)
    ours_grad, gain_more = leave(ours_plan, blocks, *leave_values)
    ours_grad, got_two, got_near_one, got_line_mid = tie(ours_grad, got_two, got_near_one, got_line_mid)
    near_two = plus(stay_two[1], got_two[1])
    got_near_two = send(near_two, first_flip)
    line_one, away_one = line_split(plus(plus(stay_one[0], got_one[0]), got_near_one), place)
    got_line_one = send(away_one, line_near)
    last_mid = plus(line_mid[1], got_line_mid[1])
    got_last_mid = send(last_mid, line_far)
    got_grad = send(theirs_grad, core_flip)
    half_rows = prompt // 2
    whole_output = both_groups(own_output, other_output, core)
    prompt_output, branch_output = whole_output[:, :half_rows], whole_output[:, half_rows:]
    encoder_out = both_groups(own_encoder, other_encoder, core)
    got_near_two, got_line_one, got_last_con, got_last_exp, prompt_output, branch_output, encoder_out = tie(
        got_near_two, got_line_one, got_last_con, got_last_exp, prompt_output, branch_output, encoder_out
    )
    line_two, away_two = line_split(plus(plus(stay_two[0], got_two[0]), got_near_two), place)
    got_line_two = send(away_two, line_near)
    got_last_one = send(plus(line_one[1], got_line_one[1]), line_far)

    def owned_part(line, got_line, got_last):
        return line[0].astype(F32) + got_line[0].astype(F32) + got_last.astype(F32)

    def square(value):
        return jnp.sum(value * value)

    owned_exp = owned_part(line_exp, got_line_exp, got_last_exp)
    owned_con = owned_part(line_con, got_line_con, got_last_con)[0]
    squares = square(owned_exp) + square(owned_con)
    prompt_grad = both_groups(ours_grad, got_grad[:half_rows], core)
    squares, got_line_two, got_last_one, got_last_mid, prompt_grad = tie(
        squares, got_line_two, got_last_one, got_last_mid, prompt_grad
    )
    got_last_two = send(plus(line_two[1], got_line_two[1]), line_far)
    owned_mid = owned_part(line_mid, got_line_mid, got_last_mid)
    owned_one = owned_part(line_one, got_line_one, got_last_one)
    squares = squares + square(owned_mid) + square(owned_one)
    grad_bias = bias_gradient(
        jnp.concatenate([part_one[3], part_two[3]]),
        jnp.concatenate([part_one[4], part_two[4]]),
        buckets,
    )
    own_branch = lax.dynamic_slice_in_dim(theirs_grad, half_rows + core * size, size, 0)
    other_branch = lax.dynamic_slice_in_dim(got_grad, half_rows + core * size, size, 0)
    branch_grad = both_groups(own_branch, other_branch, core)
    squares, grad_bias, got_last_two, branch_grad = tie(squares, grad_bias, got_last_two, branch_grad)
    owned_two = owned_part(line_two, got_line_two, got_last_two)
    squares = squares + square(owned_two)
    owned_self = jnp.concatenate([owned_one, owned_two], axis=2)

    owned = (
        jnp.concatenate([owned_self, owned_mid[1:4]], axis=0),
        jnp.stack([owned_mid[0], owned_mid[4]]),
        owned_exp,
        owned_con,
    )
    gain_back = jnp.sum(jnp.concatenate([(gain_one + gain_more)[None], gain_back]), axis=1)
    rest = jnp.concatenate([grad_bias.reshape(-1), squares[None]])
    shared = sum_everywhere(
        jnp.concatenate([gain_back, jnp.pad(rest, (0, D - rest.size))[None]]), place
    )
    gain_total = shared[:3]
    bias_total = shared[3, :grad_bias.size].reshape(grad_bias.shape)
    square_total = shared[3, grad_bias.size]
    grad_norm = jnp.sqrt(
        square_total + jnp.sum(gain_total * gain_total) + jnp.sum(bias_total * bias_total)
    )
    factor = jnp.minimum(1.0, CLIP / (grad_norm + 1e-06))
    weights = (projections, combiners, expansion, contraction, norm_gains, position_bias)
    firsts = (projections_first, combiners_first, expansion_first, contraction_first, gains_first, bias_first)
    seconds = (
        projections_second,
        combiners_second,
        expansion_second,
        contraction_second,
        gains_second,
        bias_second,
    )
    states, copies = update(factor, weights[:5], firsts[:5], seconds[:5], owned + (gain_total,))
    states.append(adam(weights[5], firsts[5], seconds[5], bias_total * factor, RATES[5]))
    branch_shape = (2, 1, size, D)
    return (
        prompt_output,
        branch_output.reshape(branch_shape),
        prompt_grad,
        branch_grad.reshape(branch_shape),
        encoder_out,
        grad_norm,
        *states[0],
        *states[1],
        *states[2],
        *states[3],
        *states[4],
        *states[5],
        copies[0],
        copies[1],
        copies[2],
        copies[3],
    )


def solution(mesh):
    paired = mesh.shape["dp"] == 4 * SIDE * SIDE and mesh.shape["fsdp"] == 2
    return jax.shard_map(
        paired_body if paired else body,
        mesh=mesh,
        in_specs=(
            P("dp", "fsdp", None),
            P("dp", "fsdp", None, None),
            P("dp", "fsdp", None),
            P("dp", "fsdp"),
            P(),
            P("dp", "fsdp", None),
            P("dp", "fsdp", None, None),
            P(None, ("dp", "fsdp"), None),
            P(None, ("dp", "fsdp"), None),
            P(None, ("dp", "fsdp"), None),
            P(None, ("dp", "fsdp"), None),
            P(None, ("dp", "fsdp"), None),
            P(None, ("dp", "fsdp"), None),
            P(None, ("dp", "fsdp"), None),
            P(None, ("dp", "fsdp"), None),
            P(None, ("dp", "fsdp"), None),
            P(("dp", "fsdp"), None),
            P(("dp", "fsdp"), None),
            P(("dp", "fsdp"), None),
            P(),
            P(),
            P(),
            P(),
            P(),
            P(),
        ),
        out_specs=(
            P("dp", "fsdp", None),
            P("dp", "fsdp", None, None),
            P("dp", "fsdp", None),
            P("dp", "fsdp", None, None),
            P("dp", "fsdp", None),
            P(),
            P(None, ("dp", "fsdp"), None),
            P(None, ("dp", "fsdp"), None),
            P(None, ("dp", "fsdp"), None),
            P(None, ("dp", "fsdp"), None),
            P(None, ("dp", "fsdp"), None),
            P(None, ("dp", "fsdp"), None),
            P(None, ("dp", "fsdp"), None),
            P(None, ("dp", "fsdp"), None),
            P(None, ("dp", "fsdp"), None),
            P(("dp", "fsdp"), None),
            P(("dp", "fsdp"), None),
            P(("dp", "fsdp"), None),
            P(),
            P(),
            P(),
            P(),
            P(),
            P(),
            P(None, ("dp", "fsdp"), None),
            P(None, ("dp", "fsdp"), None),
            P(None, ("dp", "fsdp"), None),
            P(("dp", "fsdp"), None),
        ),
        check_vma=False,
    )
```

```python
import functools

import jax
import jax.numpy as jnp
from jax import lax
from jax.experimental import pallas as pl
from jax.experimental.pallas import tpu as pltpu
from jax.sharding import PartitionSpec as P

D = 1024
FF = 2816
HEADS = 16
HD = 64
BUCKETS = 32
PROMPT = 1024
STEP = 10


EPS = 1e-06
CLIP = 1.0
BETA_ONE = 0.9
BETA_TWO = 0.999
ADAM_EPS = 1e-08
DECAY = 0.01
RATES = (0.05, 0.3, 0.05, 0.03, 1.0, 1.0)
MASKED = -1e30


def rms_forward(stream, gain):
    scale = lax.rsqrt(jnp.mean(stream * stream, axis=-1, keepdims=True) + EPS)
    return (stream * scale * gain, scale)


def rms_backward(stream, scale, gain, upstream):
    weighted = upstream * gain
    grad_in = scale * weighted - stream * scale**3 * jnp.mean(
        weighted * stream, axis=-1, keepdims=True
    )
    return (grad_in, jnp.sum(upstream * stream * scale, axis=0))


def gelu_mix(gate, up_value):
    inner = 0.7978845608028654 * (gate + 0.044715 * gate * gate * gate)
    return 0.5 * gate * (1.0 + jnp.tanh(inner)) * up_value


def raw_scores(queries, key_rows):
    qh = queries.reshape(queries.shape[0], HEADS, HD)
    kh = key_rows.reshape(key_rows.shape[0], HEADS, HD)
    return jnp.einsum("rhd,khd->hrk", qh, kh, preferred_element_type=jnp.float32) * HD ** (-0.5)


def softmax_forward(scores, value_rows):
    row_max = jnp.max(scores, axis=-1, keepdims=True)
    expo = jnp.exp(scores - row_max)
    total = jnp.sum(expo, axis=-1, keepdims=True)
    probs = (expo / total).astype(jnp.bfloat16)
    vh = value_rows.reshape(value_rows.shape[0], HEADS, HD)
    mixed = jnp.einsum("hrk,khd->rhd", probs, vh, preferred_element_type=jnp.float32)
    return (mixed.reshape(mixed.shape[0], D).astype(jnp.bfloat16), row_max + jnp.log(total))


def softmax_backward(scores, logsum, queries, key_rows, value_rows, grad_mixed):
    probs = jnp.exp(scores - logsum)
    grad_heads = grad_mixed.reshape(grad_mixed.shape[0], HEADS, HD)
    vh = value_rows.reshape(value_rows.shape[0], HEADS, HD)
    kh = key_rows.reshape(key_rows.shape[0], HEADS, HD)
    qh = queries.reshape(queries.shape[0], HEADS, HD)
    grad_values = jnp.einsum(
        "hrk,rhd->khd", probs.astype(jnp.bfloat16), grad_heads, preferred_element_type=jnp.float32
    )
    grad_probs = jnp.einsum("rhd,khd->hrk", grad_heads, vh, preferred_element_type=jnp.float32)
    grad_scores = probs * (grad_probs - jnp.sum(probs * grad_probs, axis=-1, keepdims=True))
    scaled = (grad_scores * HD ** (-0.5)).astype(jnp.bfloat16)
    grad_queries = jnp.einsum("hrk,khd->rhd", scaled, kh, preferred_element_type=jnp.float32)
    grad_keys = jnp.einsum("hrk,rhd->khd", scaled, qh, preferred_element_type=jnp.float32)
    return (
        grad_queries.reshape(-1, D),
        grad_keys.reshape(-1, D),
        grad_values.reshape(-1, D),
        grad_scores,
    )


def hankel_bias(per_distance, shift, rows, keys):
    heads = per_distance.shape[0]
    front = jnp.broadcast_to(per_distance[:, :1], (heads, keys - 1))
    padded = jnp.concatenate([front, per_distance], axis=1)
    width = rows + keys - 1
    window = lax.dynamic_slice_in_dim(padded, shift, width, 1)
    tiled = jnp.tile(window, (1, rows + 1))[:, : rows * (width + 1)]
    skewed = tiled.reshape(heads, rows, width + 1)[:, :, :keys]
    return jnp.flip(skewed, axis=2)


def distance_grads(grad_block, shift, dist_count):
    heads, rows, keys = grad_block.shape
    width = rows + keys - 1
    flipped = jnp.flip(grad_block, axis=2)
    widened = jnp.concatenate(
        [flipped, jnp.zeros((heads, rows, width + 1 - keys), jnp.float32)], axis=2
    )
    flat = jnp.concatenate(
        [widened.reshape(heads, rows * (width + 1)), jnp.zeros((heads, keys - 1), jnp.float32)],
        axis=1,
    )
    window = jnp.sum(flat.reshape(heads, rows + 1, width), axis=1)
    padded = lax.dynamic_update_slice_in_dim(
        jnp.zeros((heads, dist_count + keys - 1), jnp.float32), window, shift, 1
    )
    head_part = jnp.sum(padded[:, :keys], axis=1, keepdims=True)
    return jnp.concatenate([head_part, padded[:, keys:]], axis=1)


def adam(weight, first, second, grad, rate):
    first_new = BETA_ONE * first + (1.0 - BETA_ONE) * grad
    second_new = BETA_TWO * second + (1.0 - BETA_TWO) * grad * grad
    mean_hat = first_new / (1.0 - BETA_ONE**STEP)
    square_hat = second_new / (1.0 - BETA_TWO**STEP)
    updated = weight - rate * (mean_hat / (jnp.sqrt(square_hat) + ADAM_EPS) + DECAY * weight)
    return (updated, first_new, second_new)


def body(
    prompt_states,
    branch_states,
    encoder_states,
    branch_start,
    bucket_table,
    prompt_cotangent,
    branch_cotangent,
    projections,
    projections_first,
    projections_second,
    combiners,
    combiners_first,
    combiners_second,
    expansion,
    expansion_first,
    expansion_second,
    contraction,
    contraction_first,
    contraction_second,
    norm_gains,
    gains_first,
    gains_second,
    position_bias,
    bias_first,
    bias_second,
):
    rows_here = prompt_states.shape[1]
    branch_count = branch_states.shape[1]
    branch_size = branch_states.shape[2]
    branch_rows = branch_count * branch_size
    dist_count = bucket_table.shape[0]
    offset = lax.axis_index("fsdp") * rows_here
    local_rows = jnp.arange(rows_here, dtype=jnp.int32)
    steps_in = jnp.arange(branch_size, dtype=jnp.int32)
    bucket_ids = jnp.arange(BUCKETS, dtype=jnp.int32)
    bucket_onehot = (bucket_table[:, None] == bucket_ids[None, :]).astype(jnp.float32)
    per_distance = jnp.dot(bucket_onehot, position_bias, precision=lax.Precision.HIGHEST).T
    own_bias = hankel_bias(per_distance, 0, branch_size, branch_size)
    shards = (
        projections.astype(jnp.bfloat16),
        combiners.astype(jnp.bfloat16),
        expansion.astype(jnp.bfloat16),
        contraction.astype(jnp.bfloat16),
    )

    def layout(starts):
        branch_pos = (starts[:, None] + steps_in[None, :]).reshape(-1)
        branch_seg = jnp.arange(branch_rows, dtype=jnp.int32) // branch_size
        query_pos = jnp.concatenate([offset + local_rows, branch_pos])
        query_seg = jnp.concatenate([jnp.full((rows_here,), -1, jnp.int32), branch_seg])
        query_limit = jnp.concatenate(
            [
                jnp.zeros((rows_here,), jnp.int32),
                jnp.broadcast_to(starts[:, None], (branch_count, branch_size)).reshape(-1),
            ]
        )
        key_pos = jnp.concatenate([jnp.arange(PROMPT, dtype=jnp.int32), branch_pos])
        key_seg = jnp.concatenate([jnp.full((PROMPT,), -1, jnp.int32), branch_seg])
        same_seg = (key_seg[None, :] == query_seg[:, None]) & (
            key_pos[None, :] <= query_pos[:, None]
        )
        from_prompt = (key_seg[None, :] == -1) & (key_pos[None, :] < query_limit[:, None])
        return same_seg | from_prompt

    def build_bias(starts):
        prompt_block = hankel_bias(per_distance, offset, rows_here, PROMPT)
        upper = jnp.concatenate(
            [prompt_block, jnp.zeros((HEADS, rows_here, branch_rows), jnp.float32)], axis=2
        )

        def branch_block(start):
            return hankel_bias(per_distance, start, branch_size, PROMPT)

        cross_blocks = lax.map(branch_block, starts)
        cross_blocks = jnp.transpose(cross_blocks, (1, 0, 2, 3)).reshape(HEADS, branch_rows, PROMPT)
        lower = jnp.concatenate(
            [cross_blocks, jnp.tile(own_bias, (1, branch_count, branch_count))], axis=2
        )
        return jnp.concatenate([upper, lower], axis=1)

    def bias_gradient(grad_scores, starts):
        total = distance_grads(grad_scores[:, :rows_here, :PROMPT], offset, dist_count)

        def add_branch(index, running):
            begin = rows_here + index * branch_size
            rows_block = lax.dynamic_slice_in_dim(grad_scores, begin, branch_size, 1)
            running = running + distance_grads(rows_block[:, :, :PROMPT], starts[index], dist_count)
            own_block = lax.dynamic_slice_in_dim(
                rows_block, PROMPT + index * branch_size, branch_size, 2
            )
            return running + distance_grads(own_block, 0, dist_count)

        total = lax.fori_loop(0, branch_count, add_branch, total)
        return jnp.dot(total, bucket_onehot, precision=lax.Precision.HIGHEST).T

    def group_step(running, item):
        big_sum, gain_sum, bias_sum = running
        prompt, branches, encoder, starts, prompt_cot, branch_cot = item
        weights = (
            lax.all_gather(shards[0], ("dp", "fsdp"), axis=1, tiled=True),
            lax.all_gather(shards[1], ("dp", "fsdp"), axis=1, tiled=True),
            lax.all_gather(shards[2], ("dp", "fsdp"), axis=1, tiled=True),
            lax.all_gather(shards[3], ("dp", "fsdp"), axis=0, tiled=True),
        )
        w_proj, w_comb, w_exp, w_con = weights
        pair_mask = layout(starts)
        stream = jnp.concatenate(
            [prompt.astype(jnp.float32), branches.reshape(-1, D).astype(jnp.float32)], axis=0
        )
        normed_one, scale_one = rms_forward(stream, norm_gains[0])
        input_one = normed_one.astype(jnp.bfloat16)
        self_rows = jnp.einsum(
            "td,kde->kte", input_one, w_proj[:3], preferred_element_type=jnp.float32
        ).astype(jnp.bfloat16)
        prompt_keys, prompt_values = (
            lax.all_gather(self_rows[1, :rows_here], "fsdp", axis=0, tiled=True),
            lax.all_gather(self_rows[2, :rows_here], "fsdp", axis=0, tiled=True),
        )
        encoder_rows = jnp.einsum(
            "td,kde->kte", encoder, w_proj[4:], preferred_element_type=jnp.float32
        ).astype(jnp.bfloat16)
        cross_keys, cross_values = (
            lax.all_gather(encoder_rows[0], "fsdp", axis=0, tiled=True),
            lax.all_gather(encoder_rows[1], "fsdp", axis=0, tiled=True),
        )
        key_rows = jnp.concatenate([prompt_keys, self_rows[1, rows_here:]], axis=0)
        value_rows = jnp.concatenate([prompt_values, self_rows[2, rows_here:]], axis=0)
        pair_bias = build_bias(starts)
        scores_one = jnp.where(
            pair_mask[None], raw_scores(self_rows[0], key_rows) + pair_bias, MASKED
        )
        mixed_one, logsum_one = softmax_forward(scores_one, value_rows)
        after_one = stream + jnp.dot(mixed_one, w_comb[0], preferred_element_type=jnp.float32)
        normed_two, scale_two = rms_forward(after_one, norm_gains[1])
        input_two = normed_two.astype(jnp.bfloat16)
        query_two = jnp.dot(input_two, w_proj[3], preferred_element_type=jnp.float32).astype(
            jnp.bfloat16
        )
        scores_two = raw_scores(query_two, cross_keys)
        mixed_two, logsum_two = softmax_forward(scores_two, cross_values)
        after_two = after_one + jnp.dot(mixed_two, w_comb[1], preferred_element_type=jnp.float32)
        normed_three, scale_three = rms_forward(after_two, norm_gains[2])
        input_three = normed_three.astype(jnp.bfloat16)
        gate_up = jnp.einsum("td,kdf->ktf", input_three, w_exp, preferred_element_type=jnp.float32)
        hidden, mix_pull = jax.vjp(gelu_mix, gate_up[0], gate_up[1])
        hidden_low = hidden.astype(jnp.bfloat16)
        output = after_two + jnp.dot(hidden_low, w_con, preferred_element_type=jnp.float32)
        again = (
            lax.all_gather(shards[0], ("dp", "fsdp"), axis=1, tiled=True),
            lax.all_gather(shards[1], ("dp", "fsdp"), axis=1, tiled=True),
            lax.all_gather(shards[2], ("dp", "fsdp"), axis=1, tiled=True),
            lax.all_gather(shards[3], ("dp", "fsdp"), axis=0, tiled=True),
        )
        b_proj, b_comb, b_exp, b_con = again
        upstream = jnp.concatenate(
            [prompt_cot.astype(jnp.float32), branch_cot.reshape(-1, D).astype(jnp.float32)], axis=0
        )
        upstream_low = upstream.astype(jnp.bfloat16)
        grad_con = jnp.einsum(
            "tf,td->fd", hidden_low, upstream_low, preferred_element_type=jnp.float32
        )
        grad_hidden = jnp.einsum(
            "td,fd->tf", upstream_low, b_con, preferred_element_type=jnp.float32
        )
        grad_gate, grad_up = mix_pull(grad_hidden)
        gate_low = jnp.stack([grad_gate, grad_up]).astype(jnp.bfloat16)
        grad_exp = jnp.einsum(
            "td,ktf->kdf", input_three, gate_low, preferred_element_type=jnp.float32
        )
        grad_three = jnp.einsum("ktf,kdf->td", gate_low, b_exp, preferred_element_type=jnp.float32)
        back_three, gain_three = rms_backward(after_two, scale_three, norm_gains[2], grad_three)
        grad_after_two = upstream + back_three
        cross_low = grad_after_two.astype(jnp.bfloat16)
        grad_comb_two = jnp.einsum(
            "te,td->ed", mixed_two, cross_low, preferred_element_type=jnp.float32
        )
        grad_mixed_two = jnp.einsum(
            "td,ed->te", cross_low, b_comb[1], preferred_element_type=jnp.float32
        ).astype(jnp.bfloat16)
        grad_query_two, grad_keys_two, grad_values_two, unused_scores = softmax_backward(
            scores_two, logsum_two, query_two, cross_keys, cross_values, grad_mixed_two
        )
        own_keys, own_values = (
            lax.psum_scatter(
                grad_keys_two.astype(jnp.bfloat16), "fsdp", scatter_dimension=0, tiled=True
            ).astype(jnp.float32),
            lax.psum_scatter(
                grad_values_two.astype(jnp.bfloat16), "fsdp", scatter_dimension=0, tiled=True
            ).astype(jnp.float32),
        )
        encoder_low = jnp.stack([own_keys, own_values]).astype(jnp.bfloat16)
        grad_cross_proj = jnp.einsum(
            "td,kte->kde", encoder, encoder_low, preferred_element_type=jnp.float32
        )
        encoder_grad = jnp.einsum(
            "kte,kde->td", encoder_low, b_proj[4:], preferred_element_type=jnp.float32
        )
        query_two_low = grad_query_two.astype(jnp.bfloat16)
        grad_query_proj = jnp.einsum(
            "td,te->de", input_two, query_two_low, preferred_element_type=jnp.float32
        )
        grad_two = jnp.einsum(
            "te,de->td", query_two_low, b_proj[3], preferred_element_type=jnp.float32
        )
        back_two, gain_two = rms_backward(after_one, scale_two, norm_gains[1], grad_two)
        grad_after_one = grad_after_two + back_two
        self_low = grad_after_one.astype(jnp.bfloat16)
        grad_comb_one = jnp.einsum(
            "te,td->ed", mixed_one, self_low, preferred_element_type=jnp.float32
        )
        grad_mixed_one = jnp.einsum(
            "td,ed->te", self_low, b_comb[0], preferred_element_type=jnp.float32
        ).astype(jnp.bfloat16)
        grad_query, grad_keys, grad_values, grad_scores = softmax_backward(
            scores_one, logsum_one, self_rows[0], key_rows, value_rows, grad_mixed_one
        )
        prompt_key_grad, prompt_value_grad = (
            lax.psum_scatter(
                grad_keys[:PROMPT].astype(jnp.bfloat16), "fsdp", scatter_dimension=0, tiled=True
            ).astype(jnp.float32),
            lax.psum_scatter(
                grad_values[:PROMPT].astype(jnp.bfloat16), "fsdp", scatter_dimension=0, tiled=True
            ).astype(jnp.float32),
        )
        self_grad_low = jnp.stack(
            [
                grad_query,
                jnp.concatenate([prompt_key_grad, grad_keys[PROMPT:]], axis=0),
                jnp.concatenate([prompt_value_grad, grad_values[PROMPT:]], axis=0),
            ]
        ).astype(jnp.bfloat16)
        grad_self_proj = jnp.einsum(
            "td,kte->kde", input_one, self_grad_low, preferred_element_type=jnp.float32
        )
        grad_one = jnp.einsum(
            "kte,kde->td", self_grad_low, b_proj[:3], preferred_element_type=jnp.float32
        )
        back_one, gain_one = rms_backward(stream, scale_one, norm_gains[0], grad_one)
        stream_grad = grad_after_one + back_one
        grad_bias = bias_gradient(grad_scores, starts)
        group_big = (
            jnp.concatenate([grad_self_proj, grad_query_proj[None], grad_cross_proj], axis=0),
            jnp.stack([grad_comb_one, grad_comb_two]),
            grad_exp,
            grad_con,
        )
        big_sum = jax.tree.map(jnp.add, big_sum, group_big)
        gain_sum = gain_sum + jnp.stack([gain_one, gain_two, gain_three])
        bias_sum = bias_sum + grad_bias
        results = (
            output[:rows_here].astype(jnp.bfloat16),
            output[rows_here:].reshape(branch_count, branch_size, D).astype(jnp.bfloat16),
            stream_grad[:rows_here],
            stream_grad[rows_here:].reshape(branch_count, branch_size, D),
            encoder_grad,
        )
        return ((big_sum, gain_sum, bias_sum), results)

    big_start = (
        jnp.zeros((6, D, D), jnp.float32),
        jnp.zeros((2, D, D), jnp.float32),
        jnp.zeros((2, D, FF), jnp.float32),
        jnp.zeros((FF, D), jnp.float32),
    )
    start_state = (
        big_start,
        jnp.zeros(norm_gains.shape, jnp.float32),
        jnp.zeros(position_bias.shape, jnp.float32),
    )
    final_state, results = lax.scan(
        group_step,
        start_state,
        (
            prompt_states,
            branch_states,
            encoder_states,
            branch_start,
            prompt_cotangent,
            branch_cotangent,
        ),
    )
    big_sum, gain_sum, bias_sum = final_state
    owned = (
        lax.psum_scatter(big_sum[0], ("dp", "fsdp"), scatter_dimension=1, tiled=True),
        lax.psum_scatter(big_sum[1], ("dp", "fsdp"), scatter_dimension=1, tiled=True),
        lax.psum_scatter(big_sum[2], ("dp", "fsdp"), scatter_dimension=1, tiled=True),
        lax.psum_scatter(big_sum[3], ("dp", "fsdp"), scatter_dimension=0, tiled=True),
    )
    squares = sum((jnp.sum(grad * grad) for grad in owned))
    gain_total, bias_total, square_total = lax.psum((gain_sum, bias_sum, squares), ("dp", "fsdp"))
    grad_norm = jnp.sqrt(
        square_total + jnp.sum(gain_total * gain_total) + jnp.sum(bias_total * bias_total)
    )
    factor = jnp.minimum(1.0, CLIP / (grad_norm + 1e-06))
    params = (projections, combiners, expansion, contraction, norm_gains, position_bias)
    firsts = (
        projections_first,
        combiners_first,
        expansion_first,
        contraction_first,
        gains_first,
        bias_first,
    )
    seconds = (
        projections_second,
        combiners_second,
        expansion_second,
        contraction_second,
        gains_second,
        bias_second,
    )
    grads = (owned[0], owned[1], owned[2], owned[3], gain_total, bias_total)
    states = [
        adam(params[index], firsts[index], seconds[index], grads[index] * factor, RATES[index])
        for index in range(6)
    ]
    return (
        results[0],
        results[1],
        results[2],
        results[3],
        results[4],
        grad_norm,
        states[0][0],
        states[0][1],
        states[0][2],
        states[1][0],
        states[1][1],
        states[1][2],
        states[2][0],
        states[2][1],
        states[2][2],
        states[3][0],
        states[3][1],
        states[3][2],
        states[4][0],
        states[4][1],
        states[4][2],
        states[5][0],
        states[5][1],
        states[5][2],
        states[0][0].astype(jnp.bfloat16),
        states[1][0].astype(jnp.bfloat16),
        states[2][0].astype(jnp.bfloat16),
        states[3][0].astype(jnp.bfloat16),
    )


BF = jnp.bfloat16
F32 = jnp.float32
PAIR = 2 * HD
PAIRS = HEADS // 2
TILE = 256


def params(limit=60):
    return pltpu.CompilerParams(vmem_limit_bytes=limit * 1024 * 1024)


def cost(microseconds):
    return pl.CostEstimate(flops=int(microseconds), bytes_accessed=1, transcendentals=0)


def dot(left, right, contract):
    return lax.dot_general(
        left, right, ((contract[:1], contract[1:]), ((), ())), preferred_element_type=F32
    )


def bias_rows(flipped, starts, prompt, size):
    base = jnp.pad(flipped[:, size - 1:], ((0, 0), (0, TILE - 1)), constant_values=MASKED)
    padded = jnp.pad(flipped, ((0, 0), (1, prompt)))
    rows = [
        lax.dynamic_slice_in_dim(padded, prompt - starts[index], prompt + size, 1) for index in range(2)
    ]
    return base[:, None], jnp.stack(rows, axis=1)[:, :, None]


def fill_bias(prompt, size, starts_ref, base, branches, strip_ref, cross_ref):
    wide = jnp.broadcast_to(base, (TILE, prompt + TILE))
    strip_ref[...] = pltpu.roll(wide, 0, 1, stride=1, stride_axis=0)[:, TILE:]
    place = lax.broadcasted_iota(jnp.int32, (size, prompt), 1)
    for index, branch in enumerate(branches):
        row = jnp.broadcast_to(branch, (size, prompt + size))
        skewed = pltpu.roll(row, 0, 1, stride=1, stride_axis=0)[:, size:]
        cross_ref[index * size:(index + 1) * size] = jnp.where(place < starts_ref[index], skewed, MASKED)


def lanes_of(value, half):
    lane = lax.broadcasted_iota(jnp.int32, value.shape, 1)
    return jnp.where((lane >= HD) if half else (lane < HD), value, jnp.zeros_like(value))


def both_halves(value):
    return jnp.concatenate([lanes_of(value, 0), lanes_of(value, 1)], axis=0)


def probs_width(prompt, size):
    blocks = prompt // TILE
    return TILE * blocks * (blocks + 1) // 2 + prompt + size


def fold(grid):
    rows, width = grid.shape
    while rows > 1:
        rows //= 2
        grid = grid[:rows] + pltpu.roll(grid[rows:], width - rows, 1)
    return grid


def self_kernel(prompt, size, more, starts_ref, q_ref, k_ref, v_ref, base_ref, branch_ref, *refs):
    o_ref, e_ref, inv_ref, s_ref, strips_ref, crosses_ref = refs[more:]
    blocks = prompt // TILE
    begins = [TILE * i * (i + 1) // 2 for i in range(blocks + 1)]
    lane = lax.broadcasted_iota(jnp.int32, (TILE, PAIR), 1)
    for half in range(2):
        strip_ref, cross_ref = strips_ref.at[half], crosses_ref.at[half]
        branches = [branch_ref[half, index] for index in range(2)]
        fill_bias(prompt, size, starts_ref, base_ref[half], branches, strip_ref, cross_ref)
        for i in range(blocks + 1):
            rows = slice(i * TILE, (i + 1) * TILE)
            q = lanes_of(q_ref[rows] * BF(HD ** -0.5), half)
            tiles = []
            for j in range(min(i + 1, blocks)):
                keys = slice(j * TILE, (j + 1) * TILE)
                begin = prompt - (i + 1 - j) * TILE
                bias = strip_ref.at[:, begin:begin + TILE] if i < blocks else cross_ref.at[:, keys]
                tiles.append((keys, bias))
            top = None
            for j, (keys, bias) in enumerate(tiles):
                s = dot(q, k_ref[keys], (1, 1)) + bias[...]
                s_ref[:, j * TILE:(j + 1) * TILE] = s
                high = jnp.maximum(s[:, :PAIR], s[:, PAIR:])
                top = high if top is None else jnp.maximum(top, high)
            if i == blocks:
                near = strip_ref[:size, prompt - TILE:prompt - TILE + size]
                own = jnp.concatenate(
                    [
                        dot(q[b * size:(b + 1) * size], k_ref[prompt + b * size:prompt + (b + 1) * size], (1, 1)) + near
                        for b in range(2)
                    ],
                    axis=0,
                )
                top = jnp.maximum(top, own)
            top = jnp.max(top, axis=1, keepdims=True)
            total = None
            for j, (keys, _) in enumerate(tiles):
                e = jnp.exp(s_ref[:, j * TILE:(j + 1) * TILE] - top)
                part = e[:, :PAIR] + e[:, PAIR:]
                total = part if total is None else total + part
                low = e.astype(BF)
                e_ref[half, :, begins[i] + j * TILE:begins[i] + (j + 1) * TILE] = low
            seen = len(tiles) * TILE
            out = dot(e_ref[half, :, begins[i]:begins[i] + seen], v_ref[:seen], (1, 0))
            if i == blocks:
                e = jnp.exp(own - top)
                total = total + e
                low = e.astype(BF)
                e_ref[half, :, begins[i] + prompt:] = low
                out = out + jnp.concatenate(
                    [
                        dot(low[b * size:(b + 1) * size], v_ref[prompt + b * size:prompt + (b + 1) * size], (1, 0))
                        for b in range(2)
                    ],
                    axis=0,
                )
            inverse = 1.0 / jnp.sum(total, axis=1, keepdims=True)
            out = out * inverse
            if half == 0:
                o_ref[rows] = out.astype(BF)
                inv_ref[rows] = jnp.broadcast_to(inverse, (TILE, PAIR))
            else:
                o_ref[rows] = jnp.where(lane >= HD, out.astype(BF), o_ref[rows])
                inv_ref[rows] = jnp.where(lane >= HD, inverse, inv_ref[rows])


def self_forward(qkv, base, branch, starts, prompt, size, first, pairs, before=None):
    count = prompt + 2 * size
    width = probs_width(prompt, size)
    column = lambda part: pl.BlockSpec((None, count, PAIR), lambda j, s, part=part: (part, 0, first + j))
    flat = pl.BlockSpec((count, PAIR), lambda j, s: (0, first + j))
    bias = pltpu.VMEM((2, TILE, prompt), F32)
    more = [] if before is None else list(before)
    return pl.pallas_call(
        functools.partial(self_kernel, prompt, size, len(more)),
        grid_spec=pltpu.PrefetchScalarGridSpec(
            num_scalar_prefetch=1,
            grid=(pairs,),
            in_specs=[
                column(0),
                column(1),
                column(2),
                pl.BlockSpec((2, 1, prompt + TILE), lambda j, s: (first + j, 0, 0)),
                pl.BlockSpec((2, 2, 1, prompt + size), lambda j, s: (first + j, 0, 0, 0)),
            ]
            + [pl.BlockSpec(memory_space=pl.ANY)] * len(more),
            out_specs=[flat, pl.BlockSpec((2, TILE, width), lambda j, s: (first + j, 0, 0)), flat],
            scratch_shapes=[pltpu.VMEM((TILE, prompt), F32), bias, bias],
        ),
        out_shape=[
            jax.ShapeDtypeStruct((count, D), BF),
            jax.ShapeDtypeStruct((HEADS, TILE, width), BF),
            jax.ShapeDtypeStruct((count, D), F32),
        ],
        input_output_aliases={6 + index: index for index in range(len(more))},
        compiler_params=params(),
        cost_estimate=cost(6 * pairs),
        name="self_forward",
    )(starts, qkv, qkv, qkv, base, branch, *more)


def self_back_kernel(prompt, size, q_ref, k_ref, v_ref, do_ref, o_ref, e_ref, inv_ref, dq_ref, dk_ref, dv_ref,
                     strip_ref, cross_ref, sums, far_sums, dk_acc, dv_acc, down_ref, low_ref, q_left, do_left):
    blocks = prompt // TILE
    count = prompt + 2 * size
    begins = [TILE * i * (i + 1) // 2 for i in range(blocks + 1)]
    scale = BF(HD ** -0.5)
    lane = lax.broadcasted_iota(jnp.int32, (TILE, PAIR), 1)
    parts = [slice(b * size, (b + 1) * size) for b in range(2)]
    branches = [slice(prompt + b * size, prompt + (b + 1) * size) for b in range(2)]
    for i in range(blocks + 1):
        rows = slice(i * TILE, (i + 1) * TILE)
        q_left[:, rows] = (q_ref[rows] * scale).T
        do_left[:, rows] = (do_ref[rows].astype(F32) * inv_ref[rows]).astype(BF).T
    sums[...] = jnp.zeros_like(sums)
    for i in range(blocks + 1):
        rows = slice(i * TILE, (i + 1) * TILE)
        tiles = min(i + 1, blocks)
        seen = tiles * TILE
        scaled = (do_ref[rows].astype(F32) * inv_ref[rows]).astype(BF)
        do = both_halves(scaled)
        drops = scaled.astype(F32) * o_ref[rows].astype(F32)
        drop = [jnp.sum(lanes_of(drops, half), axis=1, keepdims=True) for half in range(2)]
        for j in range(tiles):
            keys = slice(j * TILE, (j + 1) * TILE)
            both = dot(do, v_ref[keys], (1, 1))
            for half in range(2):
                low = e_ref[half, :, begins[i] + j * TILE:begins[i] + (j + 1) * TILE]
                ds = low.astype(F32) * (both[half * TILE:(half + 1) * TILE] - drop[half])
                if i < blocks:
                    begin = TILE + prompt - (i + 1 - j) * TILE
                    sums[half, :, begin:begin + TILE] += ds
                else:
                    far_sums[half, :, size + j * TILE:size + (j + 1) * TILE] = ds
                down_ref[half, rows, keys] = ds.astype(BF)
                low_ref[half, rows, keys] = low
        down = jnp.concatenate([down_ref[half, rows, :seen] for half in range(2)], axis=0)
        dq = dot(down, k_ref[:seen], (1, 0))
        if i == blocks:
            more = []
            for half in range(2):
                lanes = slice(half * HD, (half + 1) * HD)
                low = e_ref[half, :, begins[i] + prompt:]
                own = jnp.concatenate(
                    [
                        dot(do[half * TILE + b * size:half * TILE + (b + 1) * size], v_ref[branches[b]], (1, 1))
                        for b in range(2)
                    ],
                    axis=0,
                )
                ds = low.astype(F32) * (own - drop[half])
                sums[half, :size, prompt:prompt + size] += ds[:size] + ds[size:]
                down = ds.astype(BF)
                more += [dot(down[parts[b]], k_ref[branches[b]], (1, 0)) for b in range(2)]
                for b in range(2):
                    dk_acc[lanes, branches[b]] = dot(q_left[lanes, branches[b]], down[parts[b]], (1, 0))
                    dv_acc[lanes, branches[b]] = dot(do_left[lanes, branches[b]], low[parts[b]], (1, 0))
            dq = dq + jnp.concatenate(more, axis=0)
        dq_ref[rows] = (jnp.where(lane < HD, dq[:TILE], dq[TILE:]) * (HD ** -0.5)).astype(BF)
    for half in range(2):
        lanes = slice(half * HD, (half + 1) * HD)
        for j in range(blocks):
            keys = slice(j * TILE, (j + 1) * TILE)
            rows = slice(j * TILE, count)
            dk_acc[lanes, keys] = dot(q_left[lanes, rows], down_ref[half, rows, keys], (1, 0))
            dv_acc[lanes, keys] = dot(do_left[lanes, rows], low_ref[half, rows, keys], (1, 0))
        strip_ref[half] = fold(sums[half])
        for b in range(2):
            wide = far_sums[half, b * size:(b + 1) * size]
            place = lax.broadcasted_iota(jnp.int32, wide.shape, 1)
            cross_ref[half, b] = fold(jnp.where(place < size, 0.0, wide))
    dk_ref[...] = dk_acc[...].T.astype(BF)
    dv_ref[...] = dv_acc[...].T.astype(BF)


def self_backward(qkv, do, mixed, expos, inverse, prompt, size, first, pairs):
    count = prompt + 2 * size
    width = probs_width(prompt, size)
    column = lambda part: pl.BlockSpec((None, count, PAIR), lambda j, part=part: (part, 0, first + j))
    flat = pl.BlockSpec((count, PAIR), lambda j: (0, j))
    given = pl.BlockSpec((count, PAIR), lambda j: (0, first + j))
    acc = pltpu.VMEM((PAIR, count), F32)
    return pl.pallas_call(
        functools.partial(self_back_kernel, prompt, size),
        grid=(pairs,),
        in_specs=[
            column(0),
            column(1),
            column(2),
            given,
            given,
            pl.BlockSpec((2, TILE, width), lambda j: (first + j, 0, 0)),
            given,
        ],
        out_specs=[
            flat,
            flat,
            flat,
            pl.BlockSpec((2, 1, prompt + TILE), lambda j: (j, 0, 0)),
            pl.BlockSpec((2, 2, 1, prompt + size), lambda j: (j, 0, 0, 0)),
        ],
        out_shape=[
            jax.ShapeDtypeStruct((count, pairs * PAIR), BF),
            jax.ShapeDtypeStruct((count, pairs * PAIR), BF),
            jax.ShapeDtypeStruct((count, pairs * PAIR), BF),
            jax.ShapeDtypeStruct((2 * pairs, 1, prompt + TILE), F32),
            jax.ShapeDtypeStruct((2 * pairs, 2, 1, prompt + size), F32),
        ],
        scratch_shapes=[
            pltpu.VMEM((2, TILE, prompt + TILE), F32),
            pltpu.VMEM((2, 2 * size, prompt + size), F32),
            acc,
            acc,
            pltpu.VMEM((2, count, prompt), BF),
            pltpu.VMEM((2, count, prompt), BF),
            pltpu.VMEM((PAIR, count), BF),
            pltpu.VMEM((PAIR, count), BF),
        ],
        compiler_params=params(),
        cost_estimate=cost(8 * pairs),
        name="self_backward",
    )(qkv, qkv, qkv, do, mixed, expos, inverse)


def distance_buckets(flipped, starts, prompt, size):
    bucket_ids = jnp.arange(BUCKETS, dtype=jnp.int32)
    whole = jnp.pad(flipped[size - 1:], (0, TILE - 1), constant_values=-1)
    padded = jnp.pad(flipped, (1, prompt), constant_values=-1)
    rows = [lax.dynamic_slice_in_dim(padded, prompt - starts[index], prompt + size, 0) for index in range(2)]
    order = jnp.concatenate([whole] + rows)
    return (order[:, None] == bucket_ids[None, :]).astype(F32)


def bias_gradient(strip, cross, buckets):
    sums = jnp.concatenate([strip[:, 0], cross[:, 0, 0], cross[:, 1, 0]], axis=1)
    return jnp.dot(sums, buckets, precision=lax.Precision.HIGHEST).T


def mlp_kernel(branch_rows, core_ref, x_ref, a_ref, a_t, dy_ref, wg_ref, wu_ref, wd_ref, out_ref_own, out_ref_other, da_ref, away_ref, keep_ref,
               away_con_ref, keep_con_ref, y_ref, hid, dboth, dwd, sem):
    count = a_ref.shape[0]
    step = pl.program_id(0)

    @pl.when(step == 0)
    def _():
        copy = pltpu.make_async_copy(x_ref, y_ref, sem)
        copy.start()
        da_ref[...] = jnp.zeros_like(da_ref)
        copy.wait()

    slope = 0.7978845608028654
    w_both = jnp.concatenate([wg_ref[...], wu_ref[...]], axis=1)
    for i in range(0, count, TILE):
        rows = slice(i, i + TILE)
        both = dot(a_ref[rows], w_both, (1, 0))
        g, u = both[:, :TILE], both[:, TILE:]
        dh = dot(dy_ref[rows], wd_ref[...], (1, 1))
        square = g * g
        th = jnp.tanh(slope * g * (1.0 + 0.044715 * square))
        half = 0.5 + 0.5 * th
        gelu = g * half
        slant = half + (0.5 * slope) * g * (1.0 - th * th) * (1.0 + 0.134145 * square)
        low = (gelu * u).astype(BF)
        dg = (dh * u * slant).astype(BF)
        du = (dh * gelu).astype(BF)
        hid[rows] = low
        dboth[rows, :TILE] = dg
        dboth[rows, TILE:] = du
        y_ref[rows] += dot(low, wd_ref[...], (1, 0))
        da_ref[rows] += dot(dboth[rows], w_both, (1, 1))
    dwd[pl.ds(pl.multiple_of(step * TILE, TILE), TILE)] = dot(hid[...], dy_ref[...], (0, 0))
    core = core_ref[0]
    grads = dot(a_t[...], dboth[...], (1, 0)).astype(BF)
    for index in range(2):
        blocks = grads[:, index * TILE:(index + 1) * TILE].reshape(D // 64, 2, 32, TILE)
        away_ref[index] = jnp.where(core == 0, blocks[:, 1], blocks[:, 0])
        keep_ref[index] = jnp.where(core == 0, blocks[:, 0], blocks[:, 1])

    @pl.when(step == pl.num_programs(0) - 1)
    def _():
        half = (count - branch_rows) // 2
        part = branch_rows // 2
        for out_ref, side in ((out_ref_own, core), (out_ref_other, 1 - core)):
            for i in range(0, half, TILE):
                begin = pl.multiple_of(side * half + i, TILE)
                out_ref[i:i + TILE] = y_ref[pl.ds(begin, TILE)].astype(BF)
            begin = pl.multiple_of(2 * half + side * part, part)
            out_ref[half:] = y_ref[pl.ds(begin, part)].astype(BF)
        pairs, m, _ = keep_con_ref.shape
        for index in range(pairs):
            even = dwd[2 * index * m:(2 * index + 1) * m].astype(BF)
            odd = dwd[(2 * index + 1) * m:(2 * index + 2) * m].astype(BF)
            away_con_ref[index] = jnp.where(core == 0, odd, even)
            keep_con_ref[index] = jnp.where(core == 0, even, odd)


def mlp(core, after_two, inputs, turned, low_up, w_gate, w_up, w_con, owners, branch_rows):
    count = inputs.shape[0]
    hidden = w_gate.shape[1]
    m = hidden // owners
    once = pl.Buffered(1)
    flat = pl.BlockSpec((count, D), lambda t, c: (0, 0), pipeline_mode=once)
    column = pl.BlockSpec((D, TILE), lambda t, c: (0, t))
    row = pl.BlockSpec((TILE, D), lambda t, c: (t, 0))
    shared = pl.BlockSpec((2, D // 64, 32, TILE), lambda t, c: (0, 0, 0, t))
    part = jax.ShapeDtypeStruct((2, D // 64, 32, hidden), BF)
    half_rows = pl.BlockSpec((count // 2, D), lambda t, c: (0, 0), pipeline_mode=once)
    con = pl.BlockSpec((owners // 2, m, D), lambda t, c: (0, 0, 0), pipeline_mode=once)
    con_part = jax.ShapeDtypeStruct((owners // 2, m, D), BF)
    tile = pltpu.VMEM((count, TILE), BF)
    return pl.pallas_call(
        functools.partial(mlp_kernel, branch_rows),
        grid_spec=pltpu.PrefetchScalarGridSpec(
            num_scalar_prefetch=1,
            grid=(hidden // TILE,),
            in_specs=[pl.BlockSpec(memory_space=pl.ANY), flat, whole_block(turned), flat, column, column, row],
            out_specs=[half_rows, half_rows, flat, shared, shared, con, con],
            scratch_shapes=[
                pltpu.VMEM((count, D), F32),
                tile,
                pltpu.VMEM((count, 2 * TILE), BF),
                pltpu.VMEM((hidden, D), F32),
                pltpu.SemaphoreType.DMA,
            ],
        ),
        out_shape=[
            jax.ShapeDtypeStruct((count // 2, D), BF),
            jax.ShapeDtypeStruct((count // 2, D), BF),
            jax.ShapeDtypeStruct((count, D), F32),
            part,
            part,
            con_part,
            con_part,
        ],
        compiler_params=params(),
        cost_estimate=cost(85),
        name="mlp",
    )(core, after_two, inputs, turned, low_up, w_gate, w_up, w_con)


def part_kernel(jobs, counts, plan_ref, *refs):
    lefts = refs[:1 + max(jobs)]
    rights = refs[len(lefts):len(lefts) + sum(counts)]
    rest = refs[len(lefts) + len(rights):]

    def finish(index, value):
        if len(rest) == 1:
            rest[0][index] = value.astype(BF).reshape(rest[0].shape[1:])
        else:
            got, away, stay, held = rest
            held[...] = (value + got[index].astype(F32).reshape(value.shape)).astype(BF).reshape(held.shape)
            for slot in range(2):
                away[slot, :, index] = held[:, plan_ref[1 + slot]]
                stay[slot, :, index] = held[:, plan_ref[3 + slot]]

    first = 0
    for index, left in enumerate(jobs):
        if counts[index] == 1:
            finish(index, dot(lefts[left][...], rights[first][...], (1, 0)))
        else:
            for tile in range(counts[index]):
                @pl.when(pl.program_id(0) == tile)
                def _(index=index, left=left, right=rights[first + tile]):
                    finish(index, dot(lefts[left][...], right[...], (1, 0)))
        first += counts[index]


def weight_part(plan, lefts, jobs, got=None):
    rights = [right if isinstance(right, list) else [right] for _, right in jobs]
    columns = sum(right.shape[1] for right in rights[0])
    counts = [len(right) for right in rights]
    m = 32

    def side(left):
        return pl.BlockSpec((None,) + left.shape[1:], lambda t, p: (p[0], 0, 0), pipeline_mode=pl.Buffered(1))

    def tile(right):
        return pl.BlockSpec((right.shape[0], TILE), lambda t, p: (0, t) if right.shape[1] > TILE else (0, 0))

    shared = pl.BlockSpec((len(jobs), D // 64, m, TILE), lambda t, p: (0, 0, 0, t))
    part = jax.ShapeDtypeStruct((len(jobs), D // 64, m, columns), BF)
    split = pl.BlockSpec((2, LINE, len(jobs), m, TILE), lambda t, p: (0, 0, 0, 0, t))
    half = jax.ShapeDtypeStruct((2, LINE, len(jobs), m, columns), BF)
    return pl.pallas_call(
        functools.partial(part_kernel, [left for left, _ in jobs], counts),
        grid_spec=pltpu.PrefetchScalarGridSpec(
            num_scalar_prefetch=1,
            grid=(columns // TILE,),
            in_specs=[side(left) for left in lefts]
            + [tile(value) for right in rights for value in right]
            + ([] if got is None else [shared]),
            out_specs=shared if got is None else [split, split],
            scratch_shapes=[] if got is None else [pltpu.VMEM((LINE, SIDE * SIDE, m, TILE), BF)],
        ),
        out_shape=part if got is None else [half, half],
        compiler_params=params(),
        cost_estimate=cost(2),
        name="weight_part",
    )(plan, *lefts, *(value for right in rights for value in right), *([] if got is None else [got]))


def root(value):
    return lax.rsqrt(jnp.mean(value * value, axis=1, keepdims=True) + EPS)


def normed(value, gain):
    return (value * root(value) * gain).astype(BF)


def norm_back(value, gain, upstream):
    scale = root(value)
    weighted = upstream * gain
    grad = scale * weighted - value * (scale * scale * scale) * jnp.mean(weighted * value, axis=1, keepdims=True)
    terms = upstream * value * scale
    return grad, jnp.sum(terms.reshape(-1, 8, D), axis=0)


def whole_block(value):
    zeros = (0,) * len(value.shape)
    return pl.BlockSpec(value.shape, lambda *index: zeros, pipeline_mode=pl.Buffered(1))


def row_block(columns=D):
    return pl.BlockSpec((TILE, columns), lambda i: (i, 0))


def turned_block():
    return pl.BlockSpec((D, TILE), lambda i: (0, i))


def sided_block():
    return pl.BlockSpec((2, D // 2, TILE), lambda i: (0, 0, i))


def put_sides(ref, value):
    columns = value.T.reshape(D // 64, 2, 32, value.shape[0])
    for side in range(2):
        ref[side] = columns[:, side].reshape(D // 2, value.shape[0])


def fetch(slots_ref, sources, held, sems, index):
    copies = []
    for number, source in enumerate(sources):
        for half in range(2):
            spot = slots_ref[2 * number + half, 0]
            side = slots_ref[2 * number + half, 1]
            copies.append(
                pltpu.make_async_copy(
                    source.at[half, index], held.at[index, :, spot, side], sems.at[index, 2 * number + half]
                )
            )
    return copies


def held_weight(held, index):
    return held[index].reshape(D, D)


def arrive(slots_ref, sources, held, in_sems, count):
    @pl.when(pl.program_id(0) == 0)
    def _():
        for index in range(count):
            for copy in fetch(slots_ref, sources, held, in_sems, index):
                copy.start()


def ready(slots_ref, sources, held, outs, in_sems, out_sems, index):
    @pl.when(pl.program_id(0) == 0)
    def _():
        for copy in fetch(slots_ref, sources, held, in_sems, index):
            copy.wait()
        pltpu.make_async_copy(held.at[index], outs[index], out_sems.at[index]).start()


def settle(held, outs, out_sems):
    @pl.when(pl.program_id(0) == pl.num_programs(0) - 1)
    def _():
        for index, out in enumerate(outs):
            pltpu.make_async_copy(held.at[index], out, out_sems.at[index]).wait()


def weight_specs(sources):
    _, count, line, rows, columns = sources[0].shape
    shape = (line, SIDE * SIDE, 2, rows, columns)
    anywhere = pl.BlockSpec(memory_space=pl.ANY)
    return (
        [pl.BlockSpec(memory_space=pltpu.SMEM)] + [anywhere] * 4,
        [anywhere] * count,
        [jax.ShapeDtypeStruct(shape, BF)] * count,
        [
            pltpu.VMEM((count,) + shape, BF),
            pltpu.SemaphoreType.DMA((count, 8)),
            pltpu.SemaphoreType.DMA((count,)),
        ],
    )


def enter_kernel(slots_ref, *refs):
    sources = refs[:4]
    x_ref, gain_ref, a_ref, qkv_ref = refs[4:8]
    outs = refs[8:11]
    held, in_sems, out_sems = refs[11:]
    arrive(slots_ref, sources, held, in_sems, 3)
    a = normed(x_ref[...].astype(F32), gain_ref[...])
    put_sides(a_ref, a)
    for index in range(3):
        ready(slots_ref, sources, held, outs, in_sems, out_sems, index)
        qkv_ref[index] = dot(a, held_weight(held, index), (1, 0)).astype(BF)
    settle(held, outs, out_sems)


def enter(stream_low, gain, slots, sources):
    count = stream_low.shape[0]
    weight_ins, weight_outs, weight_shapes, scratch = weight_specs(sources)
    turned, qkv, *weights = pl.pallas_call(
        enter_kernel,
        grid=(count // TILE,),
        in_specs=weight_ins + [row_block(), whole_block(gain)],
        out_specs=[sided_block(), pl.BlockSpec((3, TILE, D), lambda i: (0, i, 0))] + weight_outs,
        out_shape=[jax.ShapeDtypeStruct((2, D // 2, count), BF), jax.ShapeDtypeStruct((3, count, D), BF)] + weight_shapes,
        scratch_shapes=scratch,
        compiler_params=params(),
        cost_estimate=cost(12),
        name="enter",
    )(slots, *sources, stream_low, gain)
    return turned, qkv, [weight.reshape(D, D) for weight in weights]


def middle_kernel(parts, slots_ref, *refs):
    sources = refs[:4]
    x_ref, *mixed_refs = refs[4:5 + parts]
    (gain_two_ref, gain_three_ref, e_ref, x1_ref, x2_ref, a2_ref, a3_ref, q_ref, o_ref, p_ref, kv_ref, a3_t_ref,
     mixed_t_ref, e_t_ref, o_scr, inv_ref, *outs) = refs[5 + parts:26 + parts]
    held, in_sems, out_sems = refs[26 + parts:]
    arrive(slots_ref, sources, held, in_sems, 5)

    def weight(index):
        ready(slots_ref, sources, held, outs, in_sems, out_sems, index)
        return held_weight(held, index)

    for index in range(2):
        w = weight(2 + index)

        @pl.when(pl.program_id(0) == 0)
        def _(index=index, w=w):
            kv_ref[index] = dot(e_ref[...], w, (1, 0)).astype(BF)

    @pl.when(pl.program_id(0) == 0)
    def _():
        put_sides(e_t_ref, e_ref[...])

    w_first = weight(0)
    (mixed_ref,) = mixed_refs
    x1 = x_ref[...].astype(F32) + dot(mixed_ref[...], w_first, (1, 0))
    x1_ref[...] = x1
    a2 = normed(x1, gain_two_ref[...])
    put_sides(mixed_t_ref, mixed_ref[...])
    put_sides(a2_ref, a2)
    q_ref[...] = dot(a2, weight(1), (1, 0)).astype(BF)
    lane = lax.broadcasted_iota(jnp.int32, (TILE, PAIR), 1)
    inverses = jnp.zeros((TILE, PAIR), F32)
    for pair in range(PAIRS):
        columns = slice(pair * PAIR, (pair + 1) * PAIR)
        k = kv_ref[0, :, columns]
        v = kv_ref[1, :, columns]
        s = dot(both_halves(q_ref[:, columns] * BF(HD ** -0.5)), k, (1, 1))
        e = jnp.exp(s - jnp.max(s, axis=1, keepdims=True))
        inverse = 1.0 / jnp.sum(e, axis=1, keepdims=True)
        low = e.astype(BF)
        mixed = dot(low, v, (1, 0)) * inverse
        for half in range(2):
            rows = slice(half * TILE, (half + 1) * TILE)
            p_ref[2 * pair + half] = low[rows]
            inverses = jnp.where(lane == 2 * pair + half, inverse[rows], inverses)
        o_scr[:, columns] = jnp.where(lane < HD, mixed[:TILE], mixed[TILE:]).astype(BF)
    inv_ref[...] = inverses
    put_sides(o_ref, o_scr[...])
    x2 = x1_ref[...] + dot(o_scr[...], weight(4), (1, 0))
    x2_ref[...] = x2
    a3 = normed(x2, gain_three_ref[...])
    a3_ref[...] = a3
    a3_t_ref[...] = a3.T
    settle(held, outs, out_sems)


def middle(stream_low, mixed, gain_two, gain_three, encoder, slots, sources):
    count = stream_low.shape[0]
    enc = encoder.shape[0]
    low = jax.ShapeDtypeStruct((count, D), BF)
    wide = jax.ShapeDtypeStruct((count, D), F32)
    turned = jax.ShapeDtypeStruct((D, count), BF)
    sided = jax.ShapeDtypeStruct((2, D // 2, count), BF)
    weight_ins, weight_outs, weight_shapes, scratch = weight_specs(sources)
    *results, w1, w2, w3, w4, w5 = pl.pallas_call(
        functools.partial(middle_kernel, len(mixed)),
        grid=(count // TILE,),
        in_specs=weight_ins
        + [row_block()]
        + [row_block(part.shape[1]) for part in mixed]
        + [whole_block(value) for value in (gain_two, gain_three, encoder)],
        out_specs=[row_block(), row_block(), sided_block(), row_block(), row_block(), sided_block()]
        + [
            pl.BlockSpec((HEADS, TILE, enc), lambda i: (0, i, 0)),
            pl.BlockSpec((2, enc, D), lambda i: (0, 0, 0)),
            turned_block(),
            sided_block(),
            pl.BlockSpec((2, D // 2, enc), lambda i: (0, 0, 0)),
            row_block(),
            row_block(PAIR),
        ]
        + weight_outs,
        out_shape=[
            wide,
            wide,
            sided,
            low,
            low,
            sided,
            jax.ShapeDtypeStruct((HEADS, count, enc), BF),
            jax.ShapeDtypeStruct((2, enc, D), BF),
            turned,
            sided,
            jax.ShapeDtypeStruct((2, D // 2, enc), BF),
            low,
            jax.ShapeDtypeStruct((count, PAIR), F32),
        ]
        + weight_shapes,
        scratch_shapes=scratch,
        compiler_params=params(),
        cost_estimate=cost(30),
        name="middle",
    )(slots, *sources, stream_low, *mixed, gain_two, gain_three, encoder)
    return results + [[weight.reshape(D, D) for weight in (w1, w2, w3, w4, w5)]]


def middle_back_kernel(dy_ref, da3_ref, x2_ref, x1_ref, q_ref, o_ref, inv_ref, p_ref, kv_ref, gain_two_ref, gain_three_ref, wc_ref, wq_ref,
                       wo_ref, *refs):
    before = refs[:-9]
    low2_ref, dq_ref, dx1_ref, low1_ref, do1_ref, dkv_ref, sums_ref, gains_ref, do_ref = refs[-9:]
    dk_acc, dv_acc = sums_ref.at[0], sums_ref.at[1]
    step = pl.program_id(0)

    @pl.when(step == 0)
    def _():
        sums_ref[...] = before[-2][...] if before else jnp.zeros_like(sums_ref)
        gains_ref[...] = before[-1][...] if before else jnp.zeros_like(gains_ref)

    back, terms = norm_back(x2_ref[...], gain_three_ref[...], da3_ref[...])
    gains_ref[1] += terms
    dx2 = dy_ref[...].astype(F32) + back
    dx1_ref[...] = dx2
    low2 = dx2.astype(BF)
    low2_ref[...] = low2
    do_ref[...] = dot(low2, wo_ref[...], (1, 1)).astype(BF)
    lane = lax.broadcasted_iota(jnp.int32, (TILE, PAIR), 1)
    for pair in range(PAIRS):
        columns = slice(pair * PAIR, (pair + 1) * PAIR)
        k = kv_ref[0, :, columns]
        v = kv_ref[1, :, columns]
        inverse = jnp.where(lane < HD, inv_ref[:, 2 * pair:2 * pair + 1], inv_ref[:, 2 * pair + 1:2 * pair + 2])
        do = (do_ref[:, columns].astype(F32) * inverse).astype(BF)
        drops = do.astype(F32) * o_ref[:, columns].astype(F32)
        q_left, do_left = (q_ref[:, columns] * BF(HD ** -0.5)).T, do.T
        drop = jnp.sum(both_halves(drops), axis=1, keepdims=True)
        low = jnp.concatenate([p_ref[2 * pair], p_ref[2 * pair + 1]], axis=0)
        down = (low.astype(F32) * (dot(both_halves(do), v, (1, 1)) - drop)).astype(BF)
        dq = dot(down, k, (1, 0))
        for half in range(2):
            rows = slice(half * HD, (half + 1) * HD)
            tile = slice(half * TILE, (half + 1) * TILE)
            places = slice(pair * PAIR + half * HD, pair * PAIR + (half + 1) * HD)
            dk_acc[places] += dot(q_left[rows], down[tile], (1, 0))
            dv_acc[places] += dot(do_left[rows], low[tile], (1, 0))
        dq_ref[:, columns] = (jnp.where(lane < HD, dq[:TILE], dq[TILE:]) * (HD ** -0.5)).astype(BF)
    da2 = dot(dq_ref[...], wq_ref[...], (1, 1))
    back, terms = norm_back(x1_ref[...], gain_two_ref[...], da2)
    gains_ref[0] += terms
    dx1 = dx1_ref[...] + back
    dx1_ref[...] = dx1
    low1 = dx1.astype(BF)
    low1_ref[...] = low1
    do1_ref[...] = dot(low1, wc_ref[...], (1, 1)).astype(BF)

    @pl.when(step == pl.num_programs(0) - 1)
    def _():
        dkv_ref[0] = dk_acc[...].T.astype(BF)
        dkv_ref[1] = dv_acc[...].T.astype(BF)


def middle_back(first, blocks, low_up, grad_three, after_two, after_one, query_two, mixed_two, inverse_two, expos_two,
                kv_two, gain_two, gain_three, w_comb_one, w_query_two, w_comb_two, before=None):
    count = low_up.shape[0]
    enc = kv_two.shape[1]
    low = jax.ShapeDtypeStruct((count, D), BF)
    wide = jax.ShapeDtypeStruct((count, D), F32)
    rows = pl.BlockSpec((TILE, D), lambda i: (first + i, 0))
    sums = jax.ShapeDtypeStruct((2, D, enc), F32)
    gains = jax.ShapeDtypeStruct((2, 8, D), F32)
    whole = (kv_two, gain_two, gain_three, w_comb_one, w_query_two, w_comb_two)
    operands = (low_up, grad_three, after_two, after_one, query_two, mixed_two, inverse_two, expos_two) + whole
    more = [] if before is None else list(before[:5]) + list(before[6:])
    aliases = {} if before is None else {len(operands) + index: index for index in range(5)}
    return pl.pallas_call(
        middle_back_kernel,
        grid=(blocks,),
        in_specs=[rows] * 6
        + [
            pl.BlockSpec((TILE, PAIR), lambda i: (first + i, 0)),
            pl.BlockSpec((HEADS, TILE, enc), lambda i: (0, first + i, 0)),
        ]
        + [whole_block(value) for value in whole]
        + ([] if before is None else [pl.BlockSpec(memory_space=pl.ANY)] * 5 + [whole_block(sums), whole_block(gains)]),
        out_specs=[rows] * 5
        + [
            pl.BlockSpec((2, enc, D), lambda i: (0, 0, 0)),
            pl.BlockSpec((2, D, enc), lambda i: (0, 0, 0)),
            pl.BlockSpec((2, 8, D), lambda i: (0, 0, 0)),
        ],
        out_shape=[low, low, wide, low, low, jax.ShapeDtypeStruct((2, enc, D), BF), sums, gains],
        scratch_shapes=[pltpu.VMEM((TILE, D), BF)],
        input_output_aliases=aliases,
        compiler_params=params(),
        cost_estimate=cost(45),
        name="middle_back",
    )(*operands, *more)


def leave_kernel(parts, plan_ref, x_ref, dx1_ref, *refs):
    grads = refs[:3 * parts]
    gain_ref, wq_ref, wk_ref, wv_ref, out_ref, gains_ref = refs[3 * parts:]

    @pl.when(pl.program_id(0) == 0)
    def _():
        gains_ref[...] = jnp.zeros_like(gains_ref)

    da = None
    end = 0
    for index in range(parts):
        columns = slice(end, end + grads[3 * index].shape[1])
        end = columns.stop
        for which, w_ref in enumerate((wq_ref, wk_ref, wv_ref)):
            part = dot(grads[3 * index + which][...], w_ref[:, columns], (1, 1))
            da = part if da is None else da + part
    back, terms = norm_back(x_ref[...].astype(F32), gain_ref[...], da)
    gains_ref[...] += terms
    out_ref[...] = dx1_ref[...] + back


def leave(plan, blocks, stream_low, grad_after_one, parts, gain, w_query, w_key, w_value):
    weights = (w_query, w_key, w_value)
    flat = [value for part in parts for value in part]

    def rows(value):
        return pl.BlockSpec((TILE, value.shape[1]), lambda i, p: (p[i], 0))

    return pl.pallas_call(
        functools.partial(leave_kernel, len(parts)),
        grid_spec=pltpu.PrefetchScalarGridSpec(
            num_scalar_prefetch=1,
            grid=(blocks,),
            in_specs=[rows(stream_low), rows(grad_after_one)]
            + [rows(value) for value in flat]
            + [whole_block(value) for value in (gain,) + weights],
            out_specs=[pl.BlockSpec((TILE, D), lambda i, p: (i, 0)), pl.BlockSpec((8, D), lambda i, p: (0, 0))],
        ),
        out_shape=[jax.ShapeDtypeStruct((blocks * TILE, D), F32), jax.ShapeDtypeStruct((8, D), F32)],
        compiler_params=params(),
        cost_estimate=cost(2),
        name="leave",
    )(plan, stream_low, grad_after_one, *flat, gain, *weights)


def update_kernel(count, lows, factor_ref, *refs):
    ins = refs[:4 * count]
    outs = refs[4 * count:7 * count + lows]
    held = refs[7 * count + lows:11 * count + lows]
    ready = refs[11 * count + lows:14 * count + 2 * lows]
    in_sems, out_sems = refs[14 * count + 2 * lows:]
    arrivals = [pltpu.make_async_copy(ref, kept, in_sems.at[n]) for n, (ref, kept) in enumerate(zip(ins, held))]
    departures = [pltpu.make_async_copy(kept, ref, out_sems.at[n]) for n, (ref, kept) in enumerate(zip(outs, ready))]
    for index in range(count):
        for group in range(4):
            arrivals[group * count + index].start()
    factor = factor_ref[0]
    for index in range(count):
        for group in range(4):
            arrivals[group * count + index].wait()
        weight, first, second, grad = (held[group * count + index] for group in range(4))
        states = adam(weight[...], first[...], second[...], grad[...] * factor, RATES[index])
        for place, value in enumerate(states):
            ready[3 * index + place][...] = value
            departures[3 * index + place].start()
        if index < lows:
            ready[3 * count + index][...] = states[0].astype(BF)
            departures[3 * count + index].start()
    for copy in departures:
        copy.wait()


def update(factor, weights, firsts, seconds, grads, lows=4):
    count = len(weights)
    operands = tuple(weights) + tuple(firsts) + tuple(seconds) + tuple(grads)
    shapes = [jax.ShapeDtypeStruct(weight.shape, F32) for weight in weights for _ in range(3)]
    shapes += [jax.ShapeDtypeStruct(weight.shape, BF) for weight in weights[:lows]]
    anywhere = pl.BlockSpec(memory_space=pl.ANY)
    outs = pl.pallas_call(
        functools.partial(update_kernel, count, lows),
        in_specs=[pl.BlockSpec(memory_space=pltpu.SMEM)] + [anywhere] * len(operands),
        out_specs=[anywhere] * len(shapes),
        out_shape=shapes,
        scratch_shapes=[pltpu.VMEM(value.shape, F32) for value in operands]
        + [pltpu.VMEM(shape.shape, shape.dtype) for shape in shapes]
        + [pltpu.SemaphoreType.DMA((len(operands),)), pltpu.SemaphoreType.DMA((len(shapes),))],
        compiler_params=params(),
        cost_estimate=cost(5),
        name="update",
    )(factor.reshape(1), *operands)
    return [outs[3 * index:3 * index + 3] for index in range(count)], outs[3 * count:]


SIDE = 2
LINE = 4
AXES = ("dp", "fsdp")


def place_of(z, y, x, core):
    return ((z * SIDE + y) * SIDE + x) * 2 + core


def moves(rule):
    every = [(z, y, x, c) for z in range(LINE) for y in range(SIDE) for x in range(SIDE) for c in range(2)]
    return [(place_of(*here), place_of(*rule(*here))) for here in every]


def send(value, rule):
    return lax.ppermute(value, AXES, moves(rule))


def along_line(shift):
    return lambda z, y, x, c: ((z + shift) % LINE, y, x, c)


def line_far(z, y, x, c):
    return (z ^ 2, y, x, c)


def line_near(z, y, x, c):
    return (z ^ 1, y, x, c)


def first_flip(z, y, x, c):
    return (z, y, 1 - x, c) if c == 0 else (z, 1 - y, x, c)


def second_flip(z, y, x, c):
    return (z, 1 - y, x, c) if c == 0 else (z, y, 1 - x, c)


def core_flip(z, y, x, c):
    return (z, y, x, 1 - c)


def spots(y, x, core):
    here = y * SIDE + x
    along_x = y * SIDE + 1 - x
    along_y = (1 - y) * SIDE + x
    across = (1 - y) * SIDE + 1 - x
    near = jnp.where(core == 0, along_x, along_y)
    far = jnp.where(core == 0, along_y, along_x)
    return here, near, far, across


def put_kernel(z_ref, shard, far, near, out, sems):
    z = z_ref[0]
    sources = [(shard, z), (far, z ^ 2), (near.at[0], z ^ 1), (near.at[1], z ^ 3)]
    copies = [
        pltpu.make_async_copy(source, out.at[:, slot], sems.at[index])
        for index, (source, slot) in enumerate(sources)
    ]
    for copy in copies:
        copy.start()
    for copy in copies:
        copy.wait()


def put_in_line(shard, far, near, z):
    count, rows, columns = shard.shape
    return pl.pallas_call(
        put_kernel,
        in_specs=[pl.BlockSpec(memory_space=pltpu.SMEM)] + [pl.BlockSpec(memory_space=pl.ANY)] * 3,
        out_specs=pl.BlockSpec(memory_space=pltpu.VMEM),
        out_shape=jax.ShapeDtypeStruct((count, LINE, rows, columns), shard.dtype),
        scratch_shapes=[pltpu.SemaphoreType.DMA((LINE,))],
        compiler_params=params(40),
        cost_estimate=cost(1),
        name="put_in_line",
    )(z[None], shard, far, near)


def assemble_kernel(slots_ref, *refs):
    sources = refs[:4]
    outs, sems = refs[4:-1], refs[-1]
    copies = []
    for index, source in enumerate(sources):
        for half in range(2):
            spot = slots_ref[2 * index + half, 0]
            side = slots_ref[2 * index + half, 1]
            for k, out in enumerate(outs):
                copies.append(
                    pltpu.make_async_copy(source.at[half, k], out.at[:, spot, side], sems.at[len(copies)])
                )
    for copy in copies:
        copy.start()
    for copy in copies:
        copy.wait()


def assemble(sources, slots):
    _, count, line, rows, columns = sources[0].shape
    shape = (line, SIDE * SIDE, 2, rows, columns)
    outs = pl.pallas_call(
        assemble_kernel,
        in_specs=[pl.BlockSpec(memory_space=pltpu.SMEM)] + [pl.BlockSpec(memory_space=pl.ANY)] * 4,
        out_specs=[pl.BlockSpec(memory_space=pltpu.VMEM)] * count,
        out_shape=[jax.ShapeDtypeStruct(shape, sources[0].dtype)] * count,
        scratch_shapes=[pltpu.SemaphoreType.DMA((8 * count,))],
        compiler_params=params(40),
        cost_estimate=cost(2 * count),
        name="assemble",
    )(slots, *sources)
    return [out.reshape(line * SIDE * SIDE * 2 * rows, columns) for out in outs]


def tie(*values):
    return lax.optimization_barrier(values)


def line_stage(shard):
    return [send(shard, along_line(shift)) for shift in range(1, LINE)]


def piece_slots(place):
    _, y, x, core = place
    mine = spots(y, x, core)
    theirs = spots(y, x, 1 - core)
    order = [(mine[0], core), (mine[1], core), (theirs[0], 1 - core), (theirs[1], 1 - core)]
    order += [(mine[2], core), (mine[3], core), (theirs[2], 1 - core), (theirs[3], 1 - core)]
    return jnp.stack([jnp.stack(pair) for pair in order])


def add_split_kernel(spots_ref, one_ref, two_ref, away_ref, stay_ref):
    slot = pl.program_id(0)
    value = one_ref[...] + two_ref[...]

    for out_ref, here in ((away_ref, slot < 2), (stay_ref, slot >= 2)):
        @pl.when(here)
        def _(out_ref=out_ref):
            for index in range(value.shape[0]):
                out_ref[0, :, index] = value[index, :, 0]


def add_split(keep, received, place):
    _, y, x, core = place
    here, near, far, across = spots(y, x, core)
    count, _, rows, columns = keep.shape
    grid = (count, LINE, SIDE * SIDE, rows, columns)
    wide = columns if columns <= D else columns // 2
    source = pl.BlockSpec((count, LINE, 1, rows, wide), lambda j, t, s: (0, 0, s[j], 0, t))
    out = jax.ShapeDtypeStruct((2, LINE, count, rows, columns), BF)
    block = (1, LINE, count, rows, wide)
    return pl.pallas_call(
        add_split_kernel,
        grid_spec=pltpu.PrefetchScalarGridSpec(
            num_scalar_prefetch=1,
            grid=(4, columns // wide),
            in_specs=[source, source],
            out_specs=[
                pl.BlockSpec(
                    block, lambda j, t, s: (jnp.minimum(j, 1), 0, 0, 0, jnp.where(j < 2, t, columns // wide - 1))
                ),
                pl.BlockSpec(block, lambda j, t, s: (jnp.maximum(j - 2, 0), 0, 0, 0, jnp.where(j < 2, 0, t))),
            ],
        ),
        out_shape=[out, out],
        compiler_params=params(),
        cost_estimate=cost(1),
        name="add_split",
    )(jnp.stack([far, across, here, near]), keep.reshape(grid), received.reshape(grid))


def plus(one, two):
    return (one.astype(F32) + two.astype(F32)).astype(BF)


def line_split(line, place):
    z = place[0]

    def at(index):
        return lax.dynamic_index_in_dim(line, index, 0, keepdims=False)

    return (at(z), at(z ^ 2)), jnp.stack([at(z ^ 1), at(z ^ 3)])


def add_in_order(value, received, own, owners):
    total = None
    for index in range(4):
        term = jnp.where(own == index, value, 0.0)
        for part, owner in zip(received, owners):
            term = term + jnp.where(owner == index, part, 0.0)
        total = term if total is None else total + term
    return total


def sum_everywhere(value, place):
    z, y, x, core = place
    parts = [send(value, along_line(shift)) for shift in range(1, LINE)]
    value = add_in_order(value, parts, z, [(z - shift) % LINE for shift in range(1, LINE)])
    flips = [(0, 1), (1, 0), (1, 1)]
    parts = [send(value, lambda z, y, x, c, dy=dy, dx=dx: (z, y ^ dy, x ^ dx, c)) for dy, dx in flips]
    value = add_in_order(
        value, parts, y * SIDE + x, [jnp.bitwise_xor(y, dy) * SIDE + jnp.bitwise_xor(x, dx) for dy, dx in flips]
    )
    return value + send(value, core_flip)


def swap_halves(parts, core):
    def block(index):
        return jnp.concatenate(
            [lax.dynamic_index_in_dim(part, index, 0, keepdims=False).reshape(-1, D) for part in parts], axis=0
        )

    mine = block(core)
    theirs = send(block(1 - core), core_flip)
    first = jnp.where(core == 0, mine, theirs)
    second = jnp.where(core == 0, theirs, mine)
    whole, begin = [], 0
    for part in parts:
        end = begin + part.size // 2 // D
        whole.append(jnp.concatenate([first[begin:end], second[begin:end]], axis=0))
        begin = end
    return whole


def hand_over(parts, core):
    halves = [part.reshape((2, -1, D)) for part in parts]

    def block(index):
        return jnp.concatenate([lax.dynamic_index_in_dim(part, index, 0, keepdims=False) for part in halves], axis=0)

    return block(core), send(block(1 - core), core_flip)


def both_groups(mine, other, core):
    return jnp.stack([jnp.where(core == 0, mine, other), jnp.where(core == 0, other, mine)])


def matmul(left, right):
    return jnp.dot(left, right, preferred_element_type=F32)


def matmul_t(left, right):
    return lax.dot_general(left, right, (((1,), (1,)), ((), ())), preferred_element_type=F32)


def paired_body(
    prompt_states,
    branch_states,
    encoder_states,
    branch_start,
    bucket_table,
    prompt_cotangent,
    branch_cotangent,
    projections,
    projections_first,
    projections_second,
    combiners,
    combiners_first,
    combiners_second,
    expansion,
    expansion_first,
    expansion_second,
    contraction,
    contraction_first,
    contraction_second,
    norm_gains,
    gains_first,
    gains_second,
    position_bias,
    bias_first,
    bias_second,
):
    rows_here = prompt_states.shape[1]
    prompt = 2 * rows_here
    size = branch_states.shape[2]
    place_index = lax.axis_index("dp")
    core = lax.axis_index("fsdp")
    place = (place_index // (SIDE * SIDE), place_index // SIDE % SIDE, place_index % SIDE, core)

    z = place[0]
    core_ref = core[None]

    shard_qkv = projections[:3].astype(BF)
    shard_mid = jnp.concatenate([combiners[:1], projections[3:], combiners[1:]], axis=0).astype(BF)
    shard_exp = expansion.astype(BF)
    shard_con = contraction[None].astype(BF)
    far_line_qkv = send(shard_qkv, line_far)

    other_start = send(lax.dynamic_index_in_dim(branch_start, 1 - core, 0, keepdims=False), core_flip)
    own_start = lax.dynamic_index_in_dim(branch_start, core, 0, keepdims=False)
    starts = jnp.concatenate(
        [jnp.where(core == 0, own_start, other_start), jnp.where(core == 0, other_start, own_start)]
    )
    gain_rows = [norm_gains[index:index + 1] for index in range(3)]

    bucket_ids = jnp.arange(BUCKETS, dtype=jnp.int32)
    flipped_table = jnp.flip(bucket_table)
    flipped_onehot = (flipped_table[:, None] == bucket_ids[None, :]).astype(F32)
    flipped_bias = jnp.dot(flipped_onehot, position_bias, precision=lax.Precision.HIGHEST).T
    buckets = distance_buckets(flipped_table, starts, prompt, size)
    slots = piece_slots(place)

    far_line_qkv, starts = tie(far_line_qkv, starts)
    near_line_qkv = send(jnp.stack([shard_qkv, far_line_qkv]), line_near)
    near_line_qkv, prompt_states, shard_mid = tie(near_line_qkv, prompt_states, shard_mid)
    far_line_mid = send(shard_mid, line_far)
    prompt_rows, branch_rows, prompt_up, branch_up, encoder = swap_halves(
        [prompt_states, branch_states, prompt_cotangent, branch_cotangent, encoder_states], core
    )
    own_qkv = put_in_line(shard_qkv, far_line_qkv, near_line_qkv, z)
    near_qkv = send(own_qkv, first_flip)
    near_qkv, own_qkv = tie(near_qkv, own_qkv)
    close_qkv = jnp.stack([own_qkv, near_qkv])
    far_qkv = send(close_qkv, second_flip)
    close_qkv, far_line_mid = tie(close_qkv, far_line_mid)
    near_line_mid = send(jnp.stack([shard_mid, far_line_mid]), line_near)
    close_qkv_two = send(close_qkv, core_flip)
    base, branch = bias_rows(flipped_bias, starts, prompt, size)
    stream_low = jnp.concatenate([prompt_rows, branch_rows], axis=0)
    low_up = jnp.concatenate([prompt_up, branch_up], axis=0)
    far_qkv, near_line_mid, close_qkv_two, stream_low, low_up, encoder, base, branch, shard_exp, shard_con = tie(
        far_qkv, near_line_mid, close_qkv_two, stream_low, low_up, encoder, base, branch, shard_exp, shard_con
    )
    far_qkv_two = send(far_qkv, core_flip)
    own_mid = put_in_line(shard_mid, far_line_mid, near_line_mid, z)
    near_mid = send(own_mid, first_flip)
    far_line_exp = send(shard_exp, line_far)
    stream_low, own_mid, far_qkv_two = tie(stream_low, own_mid, far_qkv_two)

    turned_one, qkv, (w_query, w_key, w_value) = enter(
        stream_low, gain_rows[0], slots, [close_qkv, close_qkv_two, far_qkv, far_qkv_two]
    )
    qkv, near_mid, far_line_exp, shard_con = tie(qkv, near_mid, far_line_exp, shard_con)
    close_mid = jnp.stack([own_mid, near_mid])
    far_mid = send(close_mid, second_flip)
    near_line_exp = send(jnp.stack([shard_exp, far_line_exp]), line_near)
    far_line_con = send(shard_con, line_far)
    close_mid_two = send(close_mid, core_flip)
    qkv, close_mid = tie(qkv, close_mid)
    most = PAIRS // 2
    heads = self_forward(qkv, base, branch, starts, prompt, size, 0, most)
    *heads, qkv, far_mid, close_mid_two, near_line_exp, far_line_con = tie(
        *heads, qkv, far_mid, close_mid_two, near_line_exp, far_line_con
    )
    own_exp = put_in_line(shard_exp, far_line_exp, near_line_exp, z)
    near_exp = send(own_exp, first_flip)
    far_mid_two = send(far_mid, core_flip)
    near_line_con = send(jnp.stack([shard_con, far_line_con]), line_near)
    qkv, own_exp, far_mid = tie(qkv, own_exp, far_mid)
    heads = self_forward(qkv, base, branch, starts, prompt, size, most, PAIRS - most, heads)
    *heads, far_mid_two, near_exp, near_line_con = tie(*heads, far_mid_two, near_exp, near_line_con)
    mixed_one, expos, inverse = heads
    close_exp = jnp.stack([own_exp, near_exp])
    far_exp = send(close_exp, second_flip)
    close_exp_two = send(close_exp, core_flip)
    own_con = put_in_line(shard_con, far_line_con, near_line_con, z)
    near_con = send(own_con, first_flip)
    mixed_one, close_exp, own_con = tie(mixed_one, close_exp, own_con)
    (after_one, after_two, turned_two, input_three, query_two, turned_mixed_two, expos_two, kv_two, turned_three,
     turned_mixed_one, turned_encoder, mixed_two, inverse_two, weights_mid) = middle(
        stream_low,
        [mixed_one],
        gain_rows[1],
        gain_rows[2],
        encoder,
        slots,
        [close_mid, close_mid_two, far_mid, far_mid_two],
    )
    w_comb_one, w_query_two, w_key_two, w_value_two, w_comb_two = weights_mid
    input_three, far_exp, near_con, close_exp_two = tie(input_three, far_exp, near_con, close_exp_two)
    far_exp_two = send(far_exp, core_flip)
    close_con = jnp.stack([own_con, near_con])
    far_con = send(close_con, second_flip)
    close_con_two = send(close_con, core_flip)
    w_gate, w_up = assemble([close_exp, close_exp_two, far_exp, far_exp_two], slots)
    w_gate, w_up, far_con, close_con_two = tie(w_gate, w_up, far_con, close_con_two)
    far_con_two = send(far_con, core_flip)
    w_con = assemble([close_con, close_con_two, far_con, far_con_two], slots)[0]

    owners = LINE * SIDE * SIDE * 2
    own_output, output_to_give, grad_three, away_exp, keep_exp, away_con, keep_con = mlp(
        core_ref, after_two, input_three, turned_three, low_up, w_gate, w_up, w_con, owners, 2 * size
    )
    got_exp = send(away_exp, core_flip)
    got_con = send(away_con[None], core_flip)
    other_output = send(output_to_give, core_flip)
    low_up, away_exp, away_con, grad_three = tie(low_up, away_exp, away_con, grad_three)

    def middle_part(first, blocks, before=None):
        return middle_back(
            first,
            blocks,
            low_up,
            grad_three,
            after_two,
            after_one,
            query_two,
            mixed_two,
            inverse_two,
            expos_two,
            kv_two,
            gain_rows[1],
            gain_rows[2],
            w_comb_one,
            w_query_two,
            w_comb_two,
            before,
        )

    before = middle_part(0, 1)
    *before, got_exp, got_con = tie(*before, got_exp, got_con)
    away_con, stay_con = add_split(keep_con[None], got_con, place)
    got_con = send(away_con, second_flip)
    away_exp, stay_exp = add_split(keep_exp, got_exp, place)
    got_exp = send(away_exp, second_flip)
    *before, away_exp, away_con = tie(*before, away_exp, away_con)
    (cross_low, query_two_low, grad_after_one, self_low, grad_mixed_one, kv_two_low, _, gain_back) = middle_part(
        1, prompt // TILE + 2 * size // TILE - 1, before
    )
    _, y, x, _ = place
    here, near, far, across = spots(y, x, core)
    keep_plan = jnp.stack([core, far, across, here, near])
    away_plan = jnp.stack([1 - core, far, across, here, near])
    lefts_mid = [turned_mixed_one, turned_two, turned_encoder, turned_mixed_two]
    jobs_mid = [(0, self_low), (1, query_two_low), (2, kv_two_low[0]), (2, kv_two_low[1]), (3, cross_low)]
    away_mid = weight_part(away_plan, lefts_mid, jobs_mid)
    encoder_grad = matmul_t(kv_two_low[0], w_key_two) + matmul_t(kv_two_low[1], w_value_two)
    away_mid, encoder_grad, other_output, got_exp, got_con = tie(away_mid, encoder_grad, other_output, got_exp, got_con)
    got_mid = send(away_mid, core_flip)
    near_con = plus(stay_con[1], got_con[1])
    got_near_con = send(near_con, first_flip)
    near_exp = plus(stay_exp[1], got_exp[1])
    got_near_exp = send(near_exp, first_flip)
    own_encoder, other_encoder = hand_over([encoder_grad], core)
    grad_mixed_one, away_mid, near_exp, near_con, own_encoder = tie(
        grad_mixed_one, away_mid, near_exp, near_con, own_encoder
    )

    half = PAIRS // 2

    def attend_back(first, pairs, *values):
        part = self_backward(qkv, grad_mixed_one, mixed_one, expos, inverse, prompt, size, first, pairs)
        first, *rest = tie(part[0], grad_mixed_one, *values)
        return ((first,) + tuple(part[1:]), *rest)

    def jobs_of(*parts):
        return [(0, [part[i] for part in parts] if len(parts) > 1 else parts[0][i]) for i in range(3)]

    part_one, grad_mixed_one, got_mid, other_encoder, got_near_con, got_near_exp = attend_back(
        0, half, got_mid, other_encoder, got_near_con, got_near_exp
    )
    line_exp, away_exp = line_split(plus(plus(stay_exp[0], got_exp[0]), got_near_exp), place)
    got_line_exp = send(away_exp, line_near)
    away_mid, stay_mid = weight_part(keep_plan, lefts_mid, jobs_mid, got_mid)
    got_mid = send(away_mid, second_flip)
    line_con, away_con = line_split(plus(plus(stay_con[0], got_con[0]), got_near_con), place)
    got_line_con = send(away_con, line_near)
    away_plan, away_exp, away_con, away_mid = tie(away_plan, away_exp, away_con, away_mid)
    away_one = weight_part(away_plan, [turned_one], jobs_of(part_one))
    got_one = send(away_one, core_flip)
    grad_mixed_one, away_one = tie(grad_mixed_one, away_one)

    part_two, grad_mixed_one, got_one, got_mid, got_line_exp, away_plan = attend_back(
        half, half, got_one, got_mid, got_line_exp, away_plan
    )
    near_mid = plus(stay_mid[1], got_mid[1])
    got_near_mid = send(near_mid, first_flip)
    away_plan, near_mid = tie(away_plan, near_mid)
    away_two = weight_part(away_plan, [turned_one], jobs_of(part_two))
    got_two = send(away_two, core_flip)
    last_exp = plus(line_exp[1], got_line_exp[1])
    got_last_exp = send(last_exp, line_far)
    keep_plan, away_two, last_exp = tie(keep_plan, away_two, last_exp)
    away_one, stay_one = weight_part(keep_plan, [turned_one], jobs_of(part_one), got_one)
    got_one = send(away_one, second_flip)
    leave_values = (
        stream_low,
        grad_after_one,
        [part_one[:3], part_two[:3]],
        gain_rows[0],
        w_query,
        w_key,
        w_value,
    )
    blocks = prompt // TILE // 2
    steps = jnp.arange(blocks, dtype=jnp.int32)
    theirs_plan = jnp.concatenate([(1 - core) * blocks + steps, jnp.full((1,), 2 * blocks, jnp.int32)])
    ours_plan = core * blocks + steps

    theirs_plan, away_one, got_two = tie(theirs_plan, away_one, got_two)
    theirs_grad, gain_one = leave(theirs_plan, blocks + 1, *leave_values)
    theirs_grad, got_one, got_near_mid, keep_plan, got_line_con = tie(
        theirs_grad, got_one, got_near_mid, keep_plan, got_line_con
    )
    away_two, stay_two = weight_part(keep_plan, [turned_one], jobs_of(part_two), got_two)
    got_two = send(away_two, second_flip)
    away_two, stay_one, stay_mid, theirs_grad = tie(away_two, stay_one, stay_mid, theirs_grad)
    near_one = plus(stay_one[1], got_one[1])
    got_near_one = send(near_one, first_flip)
    line_mid, away_mid = line_split(plus(plus(stay_mid[0], got_mid[0]), got_near_mid), place)
    got_line_mid = send(away_mid, line_near)
    last_con = plus(line_con[1], got_line_con[1])
    got_last_con = send(last_con, line_far)
    ours_plan, near_one, away_mid, last_con = tie(ours_plan, near_one, away_mid, last_con)
    ours_grad, gain_more = leave(ours_plan, blocks, *leave_values)
    ours_grad, got_two, got_near_one, got_line_mid = tie(ours_grad, got_two, got_near_one, got_line_mid)
    near_two = plus(stay_two[1], got_two[1])
    got_near_two = send(near_two, first_flip)
    line_one, away_one = line_split(plus(plus(stay_one[0], got_one[0]), got_near_one), place)
    got_line_one = send(away_one, line_near)
    last_mid = plus(line_mid[1], got_line_mid[1])
    got_last_mid = send(last_mid, line_far)
    got_grad = send(theirs_grad, core_flip)
    half_rows = prompt // 2
    prompt_output = both_groups(own_output[:half_rows], other_output[:half_rows], core)
    branch_output = both_groups(own_output[half_rows:], other_output[half_rows:], core)
    encoder_out = both_groups(own_encoder, other_encoder, core)
    got_near_two, got_line_one, got_last_con, got_last_exp, prompt_output, branch_output, encoder_out = tie(
        got_near_two, got_line_one, got_last_con, got_last_exp, prompt_output, branch_output, encoder_out
    )
    line_two, away_two = line_split(plus(plus(stay_two[0], got_two[0]), got_near_two), place)
    got_line_two = send(away_two, line_near)
    got_last_one = send(plus(line_one[1], got_line_one[1]), line_far)

    def owned_part(line, got_line, got_last):
        return line[0].astype(F32) + got_line[0].astype(F32) + got_last.astype(F32)

    def square(value):
        return jnp.sum(value * value)

    owned_exp = owned_part(line_exp, got_line_exp, got_last_exp)
    owned_con = owned_part(line_con, got_line_con, got_last_con)[0]
    squares = square(owned_exp) + square(owned_con)
    prompt_grad = both_groups(ours_grad, got_grad[:half_rows], core)
    squares, got_line_two, got_last_one, got_last_mid, prompt_grad = tie(
        squares, got_line_two, got_last_one, got_last_mid, prompt_grad
    )
    got_last_two = send(plus(line_two[1], got_line_two[1]), line_far)
    owned_mid = owned_part(line_mid, got_line_mid, got_last_mid)
    owned_one = owned_part(line_one, got_line_one, got_last_one)
    squares = squares + square(owned_mid) + square(owned_one)
    grad_bias = bias_gradient(
        jnp.concatenate([part_one[3], part_two[3]]),
        jnp.concatenate([part_one[4], part_two[4]]),
        buckets,
    )
    own_branch = lax.dynamic_slice_in_dim(theirs_grad, half_rows + core * size, size, 0)
    other_branch = lax.dynamic_slice_in_dim(got_grad, half_rows + core * size, size, 0)
    branch_grad = both_groups(own_branch, other_branch, core)
    squares, grad_bias, got_last_two, branch_grad = tie(squares, grad_bias, got_last_two, branch_grad)
    owned_two = owned_part(line_two, got_line_two, got_last_two)
    squares = squares + square(owned_two)
    owned_self = jnp.concatenate([owned_one, owned_two], axis=2)

    owned = (
        jnp.concatenate([owned_self, owned_mid[1:4]], axis=0),
        jnp.stack([owned_mid[0], owned_mid[4]]),
        owned_exp,
        owned_con,
    )
    gain_back = jnp.sum(jnp.concatenate([(gain_one + gain_more)[None], gain_back]), axis=1)
    rest = jnp.concatenate([grad_bias.reshape(-1), squares[None]])
    shared = sum_everywhere(
        jnp.concatenate([gain_back, jnp.pad(rest, (0, D - rest.size))[None]]), place
    )
    gain_total = shared[:3]
    bias_total = shared[3, :grad_bias.size].reshape(grad_bias.shape)
    square_total = shared[3, grad_bias.size]
    grad_norm = jnp.sqrt(
        square_total + jnp.sum(gain_total * gain_total) + jnp.sum(bias_total * bias_total)
    )
    factor = jnp.minimum(1.0, CLIP / (grad_norm + 1e-06))
    weights = (projections, combiners, expansion, contraction, norm_gains, position_bias)
    firsts = (projections_first, combiners_first, expansion_first, contraction_first, gains_first, bias_first)
    seconds = (
        projections_second,
        combiners_second,
        expansion_second,
        contraction_second,
        gains_second,
        bias_second,
    )
    states, copies = update(factor, weights[:5], firsts[:5], seconds[:5], owned + (gain_total,))
    states.append(adam(weights[5], firsts[5], seconds[5], bias_total * factor, RATES[5]))
    branch_shape = (2, 1, size, D)
    return (
        prompt_output,
        branch_output.reshape(branch_shape),
        prompt_grad,
        branch_grad.reshape(branch_shape),
        encoder_out,
        grad_norm,
        *states[0],
        *states[1],
        *states[2],
        *states[3],
        *states[4],
        *states[5],
        copies[0],
        copies[1],
        copies[2],
        copies[3],
    )


def solution(mesh):
    paired = mesh.shape["dp"] == 4 * SIDE * SIDE and mesh.shape["fsdp"] == 2
    return jax.shard_map(
        paired_body if paired else body,
        mesh=mesh,
        in_specs=(
            P("dp", "fsdp", None),
            P("dp", "fsdp", None, None),
            P("dp", "fsdp", None),
            P("dp", "fsdp"),
            P(),
            P("dp", "fsdp", None),
            P("dp", "fsdp", None, None),
            P(None, ("dp", "fsdp"), None),
            P(None, ("dp", "fsdp"), None),
            P(None, ("dp", "fsdp"), None),
            P(None, ("dp", "fsdp"), None),
            P(None, ("dp", "fsdp"), None),
            P(None, ("dp", "fsdp"), None),
            P(None, ("dp", "fsdp"), None),
            P(None, ("dp", "fsdp"), None),
            P(None, ("dp", "fsdp"), None),
            P(("dp", "fsdp"), None),
            P(("dp", "fsdp"), None),
            P(("dp", "fsdp"), None),
            P(),
            P(),
            P(),
            P(),
            P(),
            P(),
        ),
        out_specs=(
            P("dp", "fsdp", None),
            P("dp", "fsdp", None, None),
            P("dp", "fsdp", None),
            P("dp", "fsdp", None, None),
            P("dp", "fsdp", None),
            P(),
            P(None, ("dp", "fsdp"), None),
            P(None, ("dp", "fsdp"), None),
            P(None, ("dp", "fsdp"), None),
            P(None, ("dp", "fsdp"), None),
            P(None, ("dp", "fsdp"), None),
            P(None, ("dp", "fsdp"), None),
            P(None, ("dp", "fsdp"), None),
            P(None, ("dp", "fsdp"), None),
            P(None, ("dp", "fsdp"), None),
            P(("dp", "fsdp"), None),
            P(("dp", "fsdp"), None),
            P(("dp", "fsdp"), None),
            P(),
            P(),
            P(),
            P(),
            P(),
            P(),
            P(None, ("dp", "fsdp"), None),
            P(None, ("dp", "fsdp"), None),
            P(None, ("dp", "fsdp"), None),
            P(("dp", "fsdp"), None),
        ),
        check_vma=False,
    )
```

```python
import functools

import jax
import jax.numpy as jnp
from jax import lax
from jax.experimental import pallas as pl
from jax.experimental.pallas import tpu as pltpu
from jax.sharding import PartitionSpec as P

D = 1024
FF = 2816
HEADS = 16
HD = 64
BUCKETS = 32
PROMPT = 1024
STEP = 10


EPS = 1e-06
CLIP = 1.0
BETA_ONE = 0.9
BETA_TWO = 0.999
ADAM_EPS = 1e-08
DECAY = 0.01
RATES = (0.05, 0.3, 0.05, 0.03, 1.0, 1.0)
MASKED = -1e30


def rms_forward(stream, gain):
    scale = lax.rsqrt(jnp.mean(stream * stream, axis=-1, keepdims=True) + EPS)
    return (stream * scale * gain, scale)


def rms_backward(stream, scale, gain, upstream):
    weighted = upstream * gain
    grad_in = scale * weighted - stream * scale**3 * jnp.mean(
        weighted * stream, axis=-1, keepdims=True
    )
    return (grad_in, jnp.sum(upstream * stream * scale, axis=0))


def gelu_mix(gate, up_value):
    inner = 0.7978845608028654 * (gate + 0.044715 * gate * gate * gate)
    return 0.5 * gate * (1.0 + jnp.tanh(inner)) * up_value


def raw_scores(queries, key_rows):
    qh = queries.reshape(queries.shape[0], HEADS, HD)
    kh = key_rows.reshape(key_rows.shape[0], HEADS, HD)
    return jnp.einsum("rhd,khd->hrk", qh, kh, preferred_element_type=jnp.float32) * HD ** (-0.5)


def softmax_forward(scores, value_rows):
    row_max = jnp.max(scores, axis=-1, keepdims=True)
    expo = jnp.exp(scores - row_max)
    total = jnp.sum(expo, axis=-1, keepdims=True)
    probs = (expo / total).astype(jnp.bfloat16)
    vh = value_rows.reshape(value_rows.shape[0], HEADS, HD)
    mixed = jnp.einsum("hrk,khd->rhd", probs, vh, preferred_element_type=jnp.float32)
    return (mixed.reshape(mixed.shape[0], D).astype(jnp.bfloat16), row_max + jnp.log(total))


def softmax_backward(scores, logsum, queries, key_rows, value_rows, grad_mixed):
    probs = jnp.exp(scores - logsum)
    grad_heads = grad_mixed.reshape(grad_mixed.shape[0], HEADS, HD)
    vh = value_rows.reshape(value_rows.shape[0], HEADS, HD)
    kh = key_rows.reshape(key_rows.shape[0], HEADS, HD)
    qh = queries.reshape(queries.shape[0], HEADS, HD)
    grad_values = jnp.einsum(
        "hrk,rhd->khd", probs.astype(jnp.bfloat16), grad_heads, preferred_element_type=jnp.float32
    )
    grad_probs = jnp.einsum("rhd,khd->hrk", grad_heads, vh, preferred_element_type=jnp.float32)
    grad_scores = probs * (grad_probs - jnp.sum(probs * grad_probs, axis=-1, keepdims=True))
    scaled = (grad_scores * HD ** (-0.5)).astype(jnp.bfloat16)
    grad_queries = jnp.einsum("hrk,khd->rhd", scaled, kh, preferred_element_type=jnp.float32)
    grad_keys = jnp.einsum("hrk,rhd->khd", scaled, qh, preferred_element_type=jnp.float32)
    return (
        grad_queries.reshape(-1, D),
        grad_keys.reshape(-1, D),
        grad_values.reshape(-1, D),
        grad_scores,
    )


def hankel_bias(per_distance, shift, rows, keys):
    heads = per_distance.shape[0]
    front = jnp.broadcast_to(per_distance[:, :1], (heads, keys - 1))
    padded = jnp.concatenate([front, per_distance], axis=1)
    width = rows + keys - 1
    window = lax.dynamic_slice_in_dim(padded, shift, width, 1)
    tiled = jnp.tile(window, (1, rows + 1))[:, : rows * (width + 1)]
    skewed = tiled.reshape(heads, rows, width + 1)[:, :, :keys]
    return jnp.flip(skewed, axis=2)


def distance_grads(grad_block, shift, dist_count):
    heads, rows, keys = grad_block.shape
    width = rows + keys - 1
    flipped = jnp.flip(grad_block, axis=2)
    widened = jnp.concatenate(
        [flipped, jnp.zeros((heads, rows, width + 1 - keys), jnp.float32)], axis=2
    )
    flat = jnp.concatenate(
        [widened.reshape(heads, rows * (width + 1)), jnp.zeros((heads, keys - 1), jnp.float32)],
        axis=1,
    )
    window = jnp.sum(flat.reshape(heads, rows + 1, width), axis=1)
    padded = lax.dynamic_update_slice_in_dim(
        jnp.zeros((heads, dist_count + keys - 1), jnp.float32), window, shift, 1
    )
    head_part = jnp.sum(padded[:, :keys], axis=1, keepdims=True)
    return jnp.concatenate([head_part, padded[:, keys:]], axis=1)


def adam(weight, first, second, grad, rate):
    first_new = BETA_ONE * first + (1.0 - BETA_ONE) * grad
    second_new = BETA_TWO * second + (1.0 - BETA_TWO) * grad * grad
    mean_hat = first_new / (1.0 - BETA_ONE**STEP)
    square_hat = second_new / (1.0 - BETA_TWO**STEP)
    updated = weight - rate * (mean_hat / (jnp.sqrt(square_hat) + ADAM_EPS) + DECAY * weight)
    return (updated, first_new, second_new)


def body(
    prompt_states,
    branch_states,
    encoder_states,
    branch_start,
    bucket_table,
    prompt_cotangent,
    branch_cotangent,
    projections,
    projections_first,
    projections_second,
    combiners,
    combiners_first,
    combiners_second,
    expansion,
    expansion_first,
    expansion_second,
    contraction,
    contraction_first,
    contraction_second,
    norm_gains,
    gains_first,
    gains_second,
    position_bias,
    bias_first,
    bias_second,
):
    rows_here = prompt_states.shape[1]
    branch_count = branch_states.shape[1]
    branch_size = branch_states.shape[2]
    branch_rows = branch_count * branch_size
    dist_count = bucket_table.shape[0]
    offset = lax.axis_index("fsdp") * rows_here
    local_rows = jnp.arange(rows_here, dtype=jnp.int32)
    steps_in = jnp.arange(branch_size, dtype=jnp.int32)
    bucket_ids = jnp.arange(BUCKETS, dtype=jnp.int32)
    bucket_onehot = (bucket_table[:, None] == bucket_ids[None, :]).astype(jnp.float32)
    per_distance = jnp.dot(bucket_onehot, position_bias, precision=lax.Precision.HIGHEST).T
    own_bias = hankel_bias(per_distance, 0, branch_size, branch_size)
    shards = (
        projections.astype(jnp.bfloat16),
        combiners.astype(jnp.bfloat16),
        expansion.astype(jnp.bfloat16),
        contraction.astype(jnp.bfloat16),
    )

    def layout(starts):
        branch_pos = (starts[:, None] + steps_in[None, :]).reshape(-1)
        branch_seg = jnp.arange(branch_rows, dtype=jnp.int32) // branch_size
        query_pos = jnp.concatenate([offset + local_rows, branch_pos])
        query_seg = jnp.concatenate([jnp.full((rows_here,), -1, jnp.int32), branch_seg])
        query_limit = jnp.concatenate(
            [
                jnp.zeros((rows_here,), jnp.int32),
                jnp.broadcast_to(starts[:, None], (branch_count, branch_size)).reshape(-1),
            ]
        )
        key_pos = jnp.concatenate([jnp.arange(PROMPT, dtype=jnp.int32), branch_pos])
        key_seg = jnp.concatenate([jnp.full((PROMPT,), -1, jnp.int32), branch_seg])
        same_seg = (key_seg[None, :] == query_seg[:, None]) & (
            key_pos[None, :] <= query_pos[:, None]
        )
        from_prompt = (key_seg[None, :] == -1) & (key_pos[None, :] < query_limit[:, None])
        return same_seg | from_prompt

    def build_bias(starts):
        prompt_block = hankel_bias(per_distance, offset, rows_here, PROMPT)
        upper = jnp.concatenate(
            [prompt_block, jnp.zeros((HEADS, rows_here, branch_rows), jnp.float32)], axis=2
        )

        def branch_block(start):
            return hankel_bias(per_distance, start, branch_size, PROMPT)

        cross_blocks = lax.map(branch_block, starts)
        cross_blocks = jnp.transpose(cross_blocks, (1, 0, 2, 3)).reshape(HEADS, branch_rows, PROMPT)
        lower = jnp.concatenate(
            [cross_blocks, jnp.tile(own_bias, (1, branch_count, branch_count))], axis=2
        )
        return jnp.concatenate([upper, lower], axis=1)

    def bias_gradient(grad_scores, starts):
        total = distance_grads(grad_scores[:, :rows_here, :PROMPT], offset, dist_count)

        def add_branch(index, running):
            begin = rows_here + index * branch_size
            rows_block = lax.dynamic_slice_in_dim(grad_scores, begin, branch_size, 1)
            running = running + distance_grads(rows_block[:, :, :PROMPT], starts[index], dist_count)
            own_block = lax.dynamic_slice_in_dim(
                rows_block, PROMPT + index * branch_size, branch_size, 2
            )
            return running + distance_grads(own_block, 0, dist_count)

        total = lax.fori_loop(0, branch_count, add_branch, total)
        return jnp.dot(total, bucket_onehot, precision=lax.Precision.HIGHEST).T

    def group_step(running, item):
        big_sum, gain_sum, bias_sum = running
        prompt, branches, encoder, starts, prompt_cot, branch_cot = item
        weights = (
            lax.all_gather(shards[0], ("dp", "fsdp"), axis=1, tiled=True),
            lax.all_gather(shards[1], ("dp", "fsdp"), axis=1, tiled=True),
            lax.all_gather(shards[2], ("dp", "fsdp"), axis=1, tiled=True),
            lax.all_gather(shards[3], ("dp", "fsdp"), axis=0, tiled=True),
        )
        w_proj, w_comb, w_exp, w_con = weights
        pair_mask = layout(starts)
        stream = jnp.concatenate(
            [prompt.astype(jnp.float32), branches.reshape(-1, D).astype(jnp.float32)], axis=0
        )
        normed_one, scale_one = rms_forward(stream, norm_gains[0])
        input_one = normed_one.astype(jnp.bfloat16)
        self_rows = jnp.einsum(
            "td,kde->kte", input_one, w_proj[:3], preferred_element_type=jnp.float32
        ).astype(jnp.bfloat16)
        prompt_keys, prompt_values = (
            lax.all_gather(self_rows[1, :rows_here], "fsdp", axis=0, tiled=True),
            lax.all_gather(self_rows[2, :rows_here], "fsdp", axis=0, tiled=True),
        )
        encoder_rows = jnp.einsum(
            "td,kde->kte", encoder, w_proj[4:], preferred_element_type=jnp.float32
        ).astype(jnp.bfloat16)
        cross_keys, cross_values = (
            lax.all_gather(encoder_rows[0], "fsdp", axis=0, tiled=True),
            lax.all_gather(encoder_rows[1], "fsdp", axis=0, tiled=True),
        )
        key_rows = jnp.concatenate([prompt_keys, self_rows[1, rows_here:]], axis=0)
        value_rows = jnp.concatenate([prompt_values, self_rows[2, rows_here:]], axis=0)
        pair_bias = build_bias(starts)
        scores_one = jnp.where(
            pair_mask[None], raw_scores(self_rows[0], key_rows) + pair_bias, MASKED
        )
        mixed_one, logsum_one = softmax_forward(scores_one, value_rows)
        after_one = stream + jnp.dot(mixed_one, w_comb[0], preferred_element_type=jnp.float32)
        normed_two, scale_two = rms_forward(after_one, norm_gains[1])
        input_two = normed_two.astype(jnp.bfloat16)
        query_two = jnp.dot(input_two, w_proj[3], preferred_element_type=jnp.float32).astype(
            jnp.bfloat16
        )
        scores_two = raw_scores(query_two, cross_keys)
        mixed_two, logsum_two = softmax_forward(scores_two, cross_values)
        after_two = after_one + jnp.dot(mixed_two, w_comb[1], preferred_element_type=jnp.float32)
        normed_three, scale_three = rms_forward(after_two, norm_gains[2])
        input_three = normed_three.astype(jnp.bfloat16)
        gate_up = jnp.einsum("td,kdf->ktf", input_three, w_exp, preferred_element_type=jnp.float32)
        hidden, mix_pull = jax.vjp(gelu_mix, gate_up[0], gate_up[1])
        hidden_low = hidden.astype(jnp.bfloat16)
        output = after_two + jnp.dot(hidden_low, w_con, preferred_element_type=jnp.float32)
        again = (
            lax.all_gather(shards[0], ("dp", "fsdp"), axis=1, tiled=True),
            lax.all_gather(shards[1], ("dp", "fsdp"), axis=1, tiled=True),
            lax.all_gather(shards[2], ("dp", "fsdp"), axis=1, tiled=True),
            lax.all_gather(shards[3], ("dp", "fsdp"), axis=0, tiled=True),
        )
        b_proj, b_comb, b_exp, b_con = again
        upstream = jnp.concatenate(
            [prompt_cot.astype(jnp.float32), branch_cot.reshape(-1, D).astype(jnp.float32)], axis=0
        )
        upstream_low = upstream.astype(jnp.bfloat16)
        grad_con = jnp.einsum(
            "tf,td->fd", hidden_low, upstream_low, preferred_element_type=jnp.float32
        )
        grad_hidden = jnp.einsum(
            "td,fd->tf", upstream_low, b_con, preferred_element_type=jnp.float32
        )
        grad_gate, grad_up = mix_pull(grad_hidden)
        gate_low = jnp.stack([grad_gate, grad_up]).astype(jnp.bfloat16)
        grad_exp = jnp.einsum(
            "td,ktf->kdf", input_three, gate_low, preferred_element_type=jnp.float32
        )
        grad_three = jnp.einsum("ktf,kdf->td", gate_low, b_exp, preferred_element_type=jnp.float32)
        back_three, gain_three = rms_backward(after_two, scale_three, norm_gains[2], grad_three)
        grad_after_two = upstream + back_three
        cross_low = grad_after_two.astype(jnp.bfloat16)
        grad_comb_two = jnp.einsum(
            "te,td->ed", mixed_two, cross_low, preferred_element_type=jnp.float32
        )
        grad_mixed_two = jnp.einsum(
            "td,ed->te", cross_low, b_comb[1], preferred_element_type=jnp.float32
        ).astype(jnp.bfloat16)
        grad_query_two, grad_keys_two, grad_values_two, unused_scores = softmax_backward(
            scores_two, logsum_two, query_two, cross_keys, cross_values, grad_mixed_two
        )
        own_keys, own_values = (
            lax.psum_scatter(
                grad_keys_two.astype(jnp.bfloat16), "fsdp", scatter_dimension=0, tiled=True
            ).astype(jnp.float32),
            lax.psum_scatter(
                grad_values_two.astype(jnp.bfloat16), "fsdp", scatter_dimension=0, tiled=True
            ).astype(jnp.float32),
        )
        encoder_low = jnp.stack([own_keys, own_values]).astype(jnp.bfloat16)
        grad_cross_proj = jnp.einsum(
            "td,kte->kde", encoder, encoder_low, preferred_element_type=jnp.float32
        )
        encoder_grad = jnp.einsum(
            "kte,kde->td", encoder_low, b_proj[4:], preferred_element_type=jnp.float32
        )
        query_two_low = grad_query_two.astype(jnp.bfloat16)
        grad_query_proj = jnp.einsum(
            "td,te->de", input_two, query_two_low, preferred_element_type=jnp.float32
        )
        grad_two = jnp.einsum(
            "te,de->td", query_two_low, b_proj[3], preferred_element_type=jnp.float32
        )
        back_two, gain_two = rms_backward(after_one, scale_two, norm_gains[1], grad_two)
        grad_after_one = grad_after_two + back_two
        self_low = grad_after_one.astype(jnp.bfloat16)
        grad_comb_one = jnp.einsum(
            "te,td->ed", mixed_one, self_low, preferred_element_type=jnp.float32
        )
        grad_mixed_one = jnp.einsum(
            "td,ed->te", self_low, b_comb[0], preferred_element_type=jnp.float32
        ).astype(jnp.bfloat16)
        grad_query, grad_keys, grad_values, grad_scores = softmax_backward(
            scores_one, logsum_one, self_rows[0], key_rows, value_rows, grad_mixed_one
        )
        prompt_key_grad, prompt_value_grad = (
            lax.psum_scatter(
                grad_keys[:PROMPT].astype(jnp.bfloat16), "fsdp", scatter_dimension=0, tiled=True
            ).astype(jnp.float32),
            lax.psum_scatter(
                grad_values[:PROMPT].astype(jnp.bfloat16), "fsdp", scatter_dimension=0, tiled=True
            ).astype(jnp.float32),
        )
        self_grad_low = jnp.stack(
            [
                grad_query,
                jnp.concatenate([prompt_key_grad, grad_keys[PROMPT:]], axis=0),
                jnp.concatenate([prompt_value_grad, grad_values[PROMPT:]], axis=0),
            ]
        ).astype(jnp.bfloat16)
        grad_self_proj = jnp.einsum(
            "td,kte->kde", input_one, self_grad_low, preferred_element_type=jnp.float32
        )
        grad_one = jnp.einsum(
            "kte,kde->td", self_grad_low, b_proj[:3], preferred_element_type=jnp.float32
        )
        back_one, gain_one = rms_backward(stream, scale_one, norm_gains[0], grad_one)
        stream_grad = grad_after_one + back_one
        grad_bias = bias_gradient(grad_scores, starts)
        group_big = (
            jnp.concatenate([grad_self_proj, grad_query_proj[None], grad_cross_proj], axis=0),
            jnp.stack([grad_comb_one, grad_comb_two]),
            grad_exp,
            grad_con,
        )
        big_sum = jax.tree.map(jnp.add, big_sum, group_big)
        gain_sum = gain_sum + jnp.stack([gain_one, gain_two, gain_three])
        bias_sum = bias_sum + grad_bias
        results = (
            output[:rows_here].astype(jnp.bfloat16),
            output[rows_here:].reshape(branch_count, branch_size, D).astype(jnp.bfloat16),
            stream_grad[:rows_here],
            stream_grad[rows_here:].reshape(branch_count, branch_size, D),
            encoder_grad,
        )
        return ((big_sum, gain_sum, bias_sum), results)

    big_start = (
        jnp.zeros((6, D, D), jnp.float32),
        jnp.zeros((2, D, D), jnp.float32),
        jnp.zeros((2, D, FF), jnp.float32),
        jnp.zeros((FF, D), jnp.float32),
    )
    start_state = (
        big_start,
        jnp.zeros(norm_gains.shape, jnp.float32),
        jnp.zeros(position_bias.shape, jnp.float32),
    )
    final_state, results = lax.scan(
        group_step,
        start_state,
        (
            prompt_states,
            branch_states,
            encoder_states,
            branch_start,
            prompt_cotangent,
            branch_cotangent,
        ),
    )
    big_sum, gain_sum, bias_sum = final_state
    owned = (
        lax.psum_scatter(big_sum[0], ("dp", "fsdp"), scatter_dimension=1, tiled=True),
        lax.psum_scatter(big_sum[1], ("dp", "fsdp"), scatter_dimension=1, tiled=True),
        lax.psum_scatter(big_sum[2], ("dp", "fsdp"), scatter_dimension=1, tiled=True),
        lax.psum_scatter(big_sum[3], ("dp", "fsdp"), scatter_dimension=0, tiled=True),
    )
    squares = sum((jnp.sum(grad * grad) for grad in owned))
    gain_total, bias_total, square_total = lax.psum((gain_sum, bias_sum, squares), ("dp", "fsdp"))
    grad_norm = jnp.sqrt(
        square_total + jnp.sum(gain_total * gain_total) + jnp.sum(bias_total * bias_total)
    )
    factor = jnp.minimum(1.0, CLIP / (grad_norm + 1e-06))
    params = (projections, combiners, expansion, contraction, norm_gains, position_bias)
    firsts = (
        projections_first,
        combiners_first,
        expansion_first,
        contraction_first,
        gains_first,
        bias_first,
    )
    seconds = (
        projections_second,
        combiners_second,
        expansion_second,
        contraction_second,
        gains_second,
        bias_second,
    )
    grads = (owned[0], owned[1], owned[2], owned[3], gain_total, bias_total)
    states = [
        adam(params[index], firsts[index], seconds[index], grads[index] * factor, RATES[index])
        for index in range(6)
    ]
    return (
        results[0],
        results[1],
        results[2],
        results[3],
        results[4],
        grad_norm,
        states[0][0],
        states[0][1],
        states[0][2],
        states[1][0],
        states[1][1],
        states[1][2],
        states[2][0],
        states[2][1],
        states[2][2],
        states[3][0],
        states[3][1],
        states[3][2],
        states[4][0],
        states[4][1],
        states[4][2],
        states[5][0],
        states[5][1],
        states[5][2],
        states[0][0].astype(jnp.bfloat16),
        states[1][0].astype(jnp.bfloat16),
        states[2][0].astype(jnp.bfloat16),
        states[3][0].astype(jnp.bfloat16),
    )


BF = jnp.bfloat16
F32 = jnp.float32
PAIR = 2 * HD
PAIRS = HEADS // 2
TILE = 256


def params(limit=60):
    return pltpu.CompilerParams(vmem_limit_bytes=limit * 1024 * 1024)


def cost(microseconds):
    return pl.CostEstimate(flops=int(microseconds), bytes_accessed=1, transcendentals=0)


def dot(left, right, contract):
    return lax.dot_general(
        left, right, ((contract[:1], contract[1:]), ((), ())), preferred_element_type=F32
    )


def bias_rows(flipped, starts, prompt, size):
    base = jnp.pad(flipped[:, size - 1:], ((0, 0), (0, TILE - 1)), constant_values=MASKED)
    padded = jnp.pad(flipped, ((0, 0), (1, prompt)))
    rows = [
        lax.dynamic_slice_in_dim(padded, prompt - starts[index], prompt + size, 1) for index in range(2)
    ]
    return base[:, None], jnp.stack(rows, axis=1)[:, :, None]


def fill_bias(prompt, size, starts_ref, base, branches, strip_ref, cross_ref):
    wide = jnp.broadcast_to(base, (TILE, prompt + TILE))
    strip_ref[...] = pltpu.roll(wide, 0, 1, stride=1, stride_axis=0)[:, TILE:]
    place = lax.broadcasted_iota(jnp.int32, (size, prompt), 1)
    for index, branch in enumerate(branches):
        row = jnp.broadcast_to(branch, (size, prompt + size))
        skewed = pltpu.roll(row, 0, 1, stride=1, stride_axis=0)[:, size:]
        cross_ref[index * size:(index + 1) * size] = jnp.where(place < starts_ref[index], skewed, MASKED)


def lanes_of(value, half):
    lane = lax.broadcasted_iota(jnp.int32, value.shape, 1)
    return jnp.where((lane >= HD) if half else (lane < HD), value, jnp.zeros_like(value))


def both_halves(value):
    return jnp.concatenate([lanes_of(value, 0), lanes_of(value, 1)], axis=0)


def probs_width(prompt, size):
    blocks = prompt // TILE
    return TILE * blocks * (blocks + 1) // 2 + prompt + size


def fold(grid):
    rows, width = grid.shape
    while rows > 1:
        rows //= 2
        grid = grid[:rows] + pltpu.roll(grid[rows:], width - rows, 1)
    return grid


def self_kernel(prompt, size, more, starts_ref, q_ref, k_ref, v_ref, base_ref, branch_ref, *refs):
    o_ref, e_ref, inv_ref, s_ref, strips_ref, crosses_ref = refs[more:]
    blocks = prompt // TILE
    begins = [TILE * i * (i + 1) // 2 for i in range(blocks + 1)]
    lane = lax.broadcasted_iota(jnp.int32, (TILE, PAIR), 1)
    for half in range(2):
        strip_ref, cross_ref = strips_ref.at[half], crosses_ref.at[half]
        branches = [branch_ref[half, index] for index in range(2)]
        fill_bias(prompt, size, starts_ref, base_ref[half], branches, strip_ref, cross_ref)
        for i in range(blocks + 1):
            rows = slice(i * TILE, (i + 1) * TILE)
            q = lanes_of(q_ref[rows] * BF(HD ** -0.5), half)
            tiles = []
            for j in range(min(i + 1, blocks)):
                keys = slice(j * TILE, (j + 1) * TILE)
                begin = prompt - (i + 1 - j) * TILE
                bias = strip_ref.at[:, begin:begin + TILE] if i < blocks else cross_ref.at[:, keys]
                tiles.append((keys, bias))
            top = None
            for j, (keys, bias) in enumerate(tiles):
                s = dot(q, k_ref[keys], (1, 1)) + bias[...]
                s_ref[:, j * TILE:(j + 1) * TILE] = s
                high = jnp.maximum(s[:, :PAIR], s[:, PAIR:])
                top = high if top is None else jnp.maximum(top, high)
            if i == blocks:
                near = strip_ref[:size, prompt - TILE:prompt - TILE + size]
                own = jnp.concatenate(
                    [
                        dot(q[b * size:(b + 1) * size], k_ref[prompt + b * size:prompt + (b + 1) * size], (1, 1)) + near
                        for b in range(2)
                    ],
                    axis=0,
                )
                top = jnp.maximum(top, own)
            top = jnp.max(top, axis=1, keepdims=True)
            total = None
            for j, (keys, _) in enumerate(tiles):
                e = jnp.exp(s_ref[:, j * TILE:(j + 1) * TILE] - top)
                part = e[:, :PAIR] + e[:, PAIR:]
                total = part if total is None else total + part
                low = e.astype(BF)
                e_ref[half, :, begins[i] + j * TILE:begins[i] + (j + 1) * TILE] = low
            seen = len(tiles) * TILE
            out = dot(e_ref[half, :, begins[i]:begins[i] + seen], v_ref[:seen], (1, 0))
            if i == blocks:
                e = jnp.exp(own - top)
                total = total + e
                low = e.astype(BF)
                e_ref[half, :, begins[i] + prompt:] = low
                out = out + jnp.concatenate(
                    [
                        dot(low[b * size:(b + 1) * size], v_ref[prompt + b * size:prompt + (b + 1) * size], (1, 0))
                        for b in range(2)
                    ],
                    axis=0,
                )
            inverse = 1.0 / jnp.sum(total, axis=1, keepdims=True)
            out = out * inverse
            if half == 0:
                o_ref[rows] = out.astype(BF)
                inv_ref[rows] = jnp.broadcast_to(inverse, (TILE, PAIR))
            else:
                o_ref[rows] = jnp.where(lane >= HD, out.astype(BF), o_ref[rows])
                inv_ref[rows] = jnp.where(lane >= HD, inverse, inv_ref[rows])


def self_forward(qkv, base, branch, starts, prompt, size, first, pairs, before=None):
    count = prompt + 2 * size
    width = probs_width(prompt, size)
    column = lambda part: pl.BlockSpec((None, count, PAIR), lambda j, s, part=part: (part, 0, first + j))
    flat = pl.BlockSpec((count, PAIR), lambda j, s: (0, first + j))
    bias = pltpu.VMEM((2, TILE, prompt), F32)
    more = [] if before is None else list(before)
    return pl.pallas_call(
        functools.partial(self_kernel, prompt, size, len(more)),
        grid_spec=pltpu.PrefetchScalarGridSpec(
            num_scalar_prefetch=1,
            grid=(pairs,),
            in_specs=[
                column(0),
                column(1),
                column(2),
                pl.BlockSpec((2, 1, prompt + TILE), lambda j, s: (first + j, 0, 0)),
                pl.BlockSpec((2, 2, 1, prompt + size), lambda j, s: (first + j, 0, 0, 0)),
            ]
            + [pl.BlockSpec(memory_space=pl.ANY)] * len(more),
            out_specs=[flat, pl.BlockSpec((2, TILE, width), lambda j, s: (first + j, 0, 0)), flat],
            scratch_shapes=[pltpu.VMEM((TILE, prompt), F32), bias, bias],
        ),
        out_shape=[
            jax.ShapeDtypeStruct((count, D), BF),
            jax.ShapeDtypeStruct((HEADS, TILE, width), BF),
            jax.ShapeDtypeStruct((count, D), F32),
        ],
        input_output_aliases={6 + index: index for index in range(len(more))},
        compiler_params=params(),
        cost_estimate=cost(6 * pairs),
        name="self_forward",
    )(starts, qkv, qkv, qkv, base, branch, *more)


def self_back_kernel(prompt, size, q_ref, k_ref, v_ref, do_ref, o_ref, e_ref, inv_ref, dq_ref, dk_ref, dv_ref,
                     strip_ref, cross_ref, sums, far_sums, dk_acc, dv_acc, down_ref, low_ref, q_left, do_left):
    blocks = prompt // TILE
    count = prompt + 2 * size
    begins = [TILE * i * (i + 1) // 2 for i in range(blocks + 1)]
    scale = BF(HD ** -0.5)
    lane = lax.broadcasted_iota(jnp.int32, (TILE, PAIR), 1)
    parts = [slice(b * size, (b + 1) * size) for b in range(2)]
    branches = [slice(prompt + b * size, prompt + (b + 1) * size) for b in range(2)]
    for i in range(blocks + 1):
        rows = slice(i * TILE, (i + 1) * TILE)
        q_left[:, rows] = (q_ref[rows] * scale).T
        do_left[:, rows] = (do_ref[rows].astype(F32) * inv_ref[rows]).astype(BF).T
    sums[...] = jnp.zeros_like(sums)
    for i in range(blocks + 1):
        rows = slice(i * TILE, (i + 1) * TILE)
        tiles = min(i + 1, blocks)
        seen = tiles * TILE
        scaled = (do_ref[rows].astype(F32) * inv_ref[rows]).astype(BF)
        do = both_halves(scaled)
        drops = scaled.astype(F32) * o_ref[rows].astype(F32)
        drop = [jnp.sum(lanes_of(drops, half), axis=1, keepdims=True) for half in range(2)]
        for j in range(tiles):
            keys = slice(j * TILE, (j + 1) * TILE)
            both = dot(do, v_ref[keys], (1, 1))
            for half in range(2):
                low = e_ref[half, :, begins[i] + j * TILE:begins[i] + (j + 1) * TILE]
                ds = low.astype(F32) * (both[half * TILE:(half + 1) * TILE] - drop[half])
                if i < blocks:
                    begin = TILE + prompt - (i + 1 - j) * TILE
                    sums[half, :, begin:begin + TILE] += ds
                else:
                    far_sums[half, :, size + j * TILE:size + (j + 1) * TILE] = ds
                down_ref[half, rows, keys] = ds.astype(BF)
                low_ref[half, rows, keys] = low
        down = jnp.concatenate([down_ref[half, rows, :seen] for half in range(2)], axis=0)
        dq = dot(down, k_ref[:seen], (1, 0))
        if i == blocks:
            more = []
            for half in range(2):
                lanes = slice(half * HD, (half + 1) * HD)
                low = e_ref[half, :, begins[i] + prompt:]
                own = jnp.concatenate(
                    [
                        dot(do[half * TILE + b * size:half * TILE + (b + 1) * size], v_ref[branches[b]], (1, 1))
                        for b in range(2)
                    ],
                    axis=0,
                )
                ds = low.astype(F32) * (own - drop[half])
                sums[half, :size, prompt:prompt + size] += ds[:size] + ds[size:]
                down = ds.astype(BF)
                more += [dot(down[parts[b]], k_ref[branches[b]], (1, 0)) for b in range(2)]
                for b in range(2):
                    dk_acc[lanes, branches[b]] = dot(q_left[lanes, branches[b]], down[parts[b]], (1, 0))
                    dv_acc[lanes, branches[b]] = dot(do_left[lanes, branches[b]], low[parts[b]], (1, 0))
            dq = dq + jnp.concatenate(more, axis=0)
        dq_ref[rows] = (jnp.where(lane < HD, dq[:TILE], dq[TILE:]) * (HD ** -0.5)).astype(BF)
    for half in range(2):
        lanes = slice(half * HD, (half + 1) * HD)
        for j in range(blocks):
            keys = slice(j * TILE, (j + 1) * TILE)
            rows = slice(j * TILE, count)
            dk_acc[lanes, keys] = dot(q_left[lanes, rows], down_ref[half, rows, keys], (1, 0))
            dv_acc[lanes, keys] = dot(do_left[lanes, rows], low_ref[half, rows, keys], (1, 0))
        strip_ref[half] = fold(sums[half])
        for b in range(2):
            wide = far_sums[half, b * size:(b + 1) * size]
            place = lax.broadcasted_iota(jnp.int32, wide.shape, 1)
            cross_ref[half, b] = fold(jnp.where(place < size, 0.0, wide))
    dk_ref[...] = dk_acc[...].T.astype(BF)
    dv_ref[...] = dv_acc[...].T.astype(BF)


def self_backward(qkv, do, mixed, expos, inverse, prompt, size, first, pairs):
    count = prompt + 2 * size
    width = probs_width(prompt, size)
    column = lambda part: pl.BlockSpec((None, count, PAIR), lambda j, part=part: (part, 0, first + j))
    flat = pl.BlockSpec((count, PAIR), lambda j: (0, j))
    given = pl.BlockSpec((count, PAIR), lambda j: (0, first + j))
    acc = pltpu.VMEM((PAIR, count), F32)
    return pl.pallas_call(
        functools.partial(self_back_kernel, prompt, size),
        grid=(pairs,),
        in_specs=[
            column(0),
            column(1),
            column(2),
            given,
            given,
            pl.BlockSpec((2, TILE, width), lambda j: (first + j, 0, 0)),
            given,
        ],
        out_specs=[
            flat,
            flat,
            flat,
            pl.BlockSpec((2, 1, prompt + TILE), lambda j: (j, 0, 0)),
            pl.BlockSpec((2, 2, 1, prompt + size), lambda j: (j, 0, 0, 0)),
        ],
        out_shape=[
            jax.ShapeDtypeStruct((count, pairs * PAIR), BF),
            jax.ShapeDtypeStruct((count, pairs * PAIR), BF),
            jax.ShapeDtypeStruct((count, pairs * PAIR), BF),
            jax.ShapeDtypeStruct((2 * pairs, 1, prompt + TILE), F32),
            jax.ShapeDtypeStruct((2 * pairs, 2, 1, prompt + size), F32),
        ],
        scratch_shapes=[
            pltpu.VMEM((2, TILE, prompt + TILE), F32),
            pltpu.VMEM((2, 2 * size, prompt + size), F32),
            acc,
            acc,
            pltpu.VMEM((2, count, prompt), BF),
            pltpu.VMEM((2, count, prompt), BF),
            pltpu.VMEM((PAIR, count), BF),
            pltpu.VMEM((PAIR, count), BF),
        ],
        compiler_params=params(),
        cost_estimate=cost(8 * pairs),
        name="self_backward",
    )(qkv, qkv, qkv, do, mixed, expos, inverse)


def distance_buckets(flipped, starts, prompt, size):
    bucket_ids = jnp.arange(BUCKETS, dtype=jnp.int32)
    whole = jnp.pad(flipped[size - 1:], (0, TILE - 1), constant_values=-1)
    padded = jnp.pad(flipped, (1, prompt), constant_values=-1)
    rows = [lax.dynamic_slice_in_dim(padded, prompt - starts[index], prompt + size, 0) for index in range(2)]
    order = jnp.concatenate([whole] + rows)
    return (order[:, None] == bucket_ids[None, :]).astype(F32)


def bias_gradient(strip, cross, buckets):
    sums = jnp.concatenate([strip[:, 0], cross[:, 0, 0], cross[:, 1, 0]], axis=1)
    return jnp.dot(sums, buckets, precision=lax.Precision.HIGHEST).T


def mlp_kernel(branch_rows, core_ref, x_ref, a_ref, a_t, dy_ref, wg_ref, wu_ref, wd_ref, out_ref_own, out_ref_other, da_ref, away_ref, keep_ref,
               away_con_ref, keep_con_ref, y_ref, hid, dboth, dwd, sem):
    count = a_ref.shape[0]
    step = pl.program_id(0)

    @pl.when(step == 0)
    def _():
        copy = pltpu.make_async_copy(x_ref, y_ref, sem)
        copy.start()
        da_ref[...] = jnp.zeros_like(da_ref)
        copy.wait()

    slope = 0.7978845608028654
    w_both = jnp.concatenate([wg_ref[...], wu_ref[...]], axis=1)
    for i in range(0, count, TILE):
        rows = slice(i, i + TILE)
        both = dot(a_ref[rows], w_both, (1, 0))
        g, u = both[:, :TILE], both[:, TILE:]
        dh = dot(dy_ref[rows], wd_ref[...], (1, 1))
        square = g * g
        th = jnp.tanh(slope * g * (1.0 + 0.044715 * square))
        half = 0.5 + 0.5 * th
        gelu = g * half
        slant = half + (0.5 * slope) * g * (1.0 - th * th) * (1.0 + 0.134145 * square)
        low = (gelu * u).astype(BF)
        dg = (dh * u * slant).astype(BF)
        du = (dh * gelu).astype(BF)
        hid[rows] = low
        dboth[rows, :TILE] = dg
        dboth[rows, TILE:] = du
        y_ref[rows] += dot(low, wd_ref[...], (1, 0))
        da_ref[rows] += dot(dboth[rows], w_both, (1, 1))
    dwd[pl.ds(pl.multiple_of(step * TILE, TILE), TILE)] = dot(hid[...], dy_ref[...], (0, 0))
    core = core_ref[0]
    grads = dot(a_t[...], dboth[...], (1, 0)).astype(BF)
    for index in range(2):
        blocks = grads[:, index * TILE:(index + 1) * TILE].reshape(D // 64, 2, 32, TILE)
        away_ref[index] = jnp.where(core == 0, blocks[:, 1], blocks[:, 0])
        keep_ref[index] = jnp.where(core == 0, blocks[:, 0], blocks[:, 1])

    @pl.when(step == pl.num_programs(0) - 1)
    def _():
        half = (count - branch_rows) // 2
        part = branch_rows // 2
        for out_ref, side in ((out_ref_own, core), (out_ref_other, 1 - core)):
            for i in range(0, half, TILE):
                begin = pl.multiple_of(side * half + i, TILE)
                out_ref[i:i + TILE] = y_ref[pl.ds(begin, TILE)].astype(BF)
            begin = pl.multiple_of(2 * half + side * part, part)
            out_ref[half:] = y_ref[pl.ds(begin, part)].astype(BF)
        pairs, m, _ = keep_con_ref.shape
        for index in range(pairs):
            even = dwd[2 * index * m:(2 * index + 1) * m].astype(BF)
            odd = dwd[(2 * index + 1) * m:(2 * index + 2) * m].astype(BF)
            away_con_ref[index] = jnp.where(core == 0, odd, even)
            keep_con_ref[index] = jnp.where(core == 0, even, odd)


def mlp(core, after_two, inputs, turned, low_up, w_gate, w_up, w_con, owners, branch_rows):
    count = inputs.shape[0]
    hidden = w_gate.shape[1]
    m = hidden // owners
    once = pl.Buffered(1)
    flat = pl.BlockSpec((count, D), lambda t, c: (0, 0), pipeline_mode=once)
    column = pl.BlockSpec((D, TILE), lambda t, c: (0, t))
    row = pl.BlockSpec((TILE, D), lambda t, c: (t, 0))
    shared = pl.BlockSpec((2, D // 64, 32, TILE), lambda t, c: (0, 0, 0, t))
    part = jax.ShapeDtypeStruct((2, D // 64, 32, hidden), BF)
    half_rows = pl.BlockSpec((count // 2, D), lambda t, c: (0, 0), pipeline_mode=once)
    con = pl.BlockSpec((owners // 2, m, D), lambda t, c: (0, 0, 0), pipeline_mode=once)
    con_part = jax.ShapeDtypeStruct((owners // 2, m, D), BF)
    tile = pltpu.VMEM((count, TILE), BF)
    return pl.pallas_call(
        functools.partial(mlp_kernel, branch_rows),
        grid_spec=pltpu.PrefetchScalarGridSpec(
            num_scalar_prefetch=1,
            grid=(hidden // TILE,),
            in_specs=[pl.BlockSpec(memory_space=pl.ANY), flat, whole_block(turned), flat, column, column, row],
            out_specs=[half_rows, half_rows, flat, shared, shared, con, con],
            scratch_shapes=[
                pltpu.VMEM((count, D), F32),
                tile,
                pltpu.VMEM((count, 2 * TILE), BF),
                pltpu.VMEM((hidden, D), F32),
                pltpu.SemaphoreType.DMA,
            ],
        ),
        out_shape=[
            jax.ShapeDtypeStruct((count // 2, D), BF),
            jax.ShapeDtypeStruct((count // 2, D), BF),
            jax.ShapeDtypeStruct((count, D), F32),
            part,
            part,
            con_part,
            con_part,
        ],
        compiler_params=params(),
        cost_estimate=cost(85),
        name="mlp",
    )(core, after_two, inputs, turned, low_up, w_gate, w_up, w_con)


def part_kernel(jobs, counts, plan_ref, *refs):
    lefts = refs[:1 + max(jobs)]
    rights = refs[len(lefts):len(lefts) + sum(counts)]
    rest = refs[len(lefts) + len(rights):]

    def finish(index, value):
        if len(rest) == 1:
            rest[0][index] = value.astype(BF).reshape(rest[0].shape[1:])
        else:
            got, away, stay, held = rest
            held[...] = (value + got[index].astype(F32).reshape(value.shape)).astype(BF).reshape(held.shape)
            for slot in range(2):
                away[slot, :, index] = held[:, plan_ref[1 + slot]]
                stay[slot, :, index] = held[:, plan_ref[3 + slot]]

    first = 0
    for index, left in enumerate(jobs):
        if counts[index] == 1:
            finish(index, dot(lefts[left][...], rights[first][...], (1, 0)))
        else:
            for tile in range(counts[index]):
                @pl.when(pl.program_id(0) == tile)
                def _(index=index, left=left, right=rights[first + tile]):
                    finish(index, dot(lefts[left][...], right[...], (1, 0)))
        first += counts[index]


def weight_part(plan, lefts, jobs, got=None):
    rights = [right if isinstance(right, list) else [right] for _, right in jobs]
    columns = sum(right.shape[1] for right in rights[0])
    counts = [len(right) for right in rights]
    m = 32

    def side(left):
        return pl.BlockSpec((None,) + left.shape[1:], lambda t, p: (p[0], 0, 0), pipeline_mode=pl.Buffered(1))

    def tile(right):
        if isinstance(right, tuple):
            return pl.BlockSpec((None, right[0].shape[1], TILE), lambda t, p: (right[1], 0, t))
        return pl.BlockSpec((right.shape[0], TILE), lambda t, p: (0, t) if right.shape[1] > TILE else (0, 0))

    shared = pl.BlockSpec((len(jobs), D // 64, m, TILE), lambda t, p: (0, 0, 0, t))
    part = jax.ShapeDtypeStruct((len(jobs), D // 64, m, columns), BF)
    split = pl.BlockSpec((2, LINE, len(jobs), m, TILE), lambda t, p: (0, 0, 0, 0, t))
    half = jax.ShapeDtypeStruct((2, LINE, len(jobs), m, columns), BF)
    return pl.pallas_call(
        functools.partial(part_kernel, [left for left, _ in jobs], counts),
        grid_spec=pltpu.PrefetchScalarGridSpec(
            num_scalar_prefetch=1,
            grid=(columns // TILE,),
            in_specs=[side(left) for left in lefts]
            + [tile(value) for right in rights for value in right]
            + ([] if got is None else [shared]),
            out_specs=shared if got is None else [split, split],
            scratch_shapes=[] if got is None else [pltpu.VMEM((LINE, SIDE * SIDE, m, TILE), BF)],
        ),
        out_shape=part if got is None else [half, half],
        compiler_params=params(),
        cost_estimate=cost(2),
        name="weight_part",
    )(plan, *lefts, *(value[0] if isinstance(value, tuple) else value for right in rights for value in right), *([] if got is None else [got]))


def root(value):
    return lax.rsqrt(jnp.mean(value * value, axis=1, keepdims=True) + EPS)


def normed(value, gain):
    return (value * root(value) * gain).astype(BF)


def norm_back(value, gain, upstream):
    scale = root(value)
    weighted = upstream * gain
    grad = scale * weighted - value * (scale * scale * scale) * jnp.mean(weighted * value, axis=1, keepdims=True)
    terms = upstream * value * scale
    return grad, jnp.sum(terms.reshape(-1, 8, D), axis=0)


def whole_block(value):
    zeros = (0,) * len(value.shape)
    return pl.BlockSpec(value.shape, lambda *index: zeros, pipeline_mode=pl.Buffered(1))


def row_block(columns=D):
    return pl.BlockSpec((TILE, columns), lambda i: (i, 0))


def turned_block():
    return pl.BlockSpec((D, TILE), lambda i: (0, i))


def sided_block():
    return pl.BlockSpec((2, D // 2, TILE), lambda i: (0, 0, i))


def put_sides(ref, value):
    columns = value.T.reshape(D // 64, 2, 32, value.shape[0])
    for side in range(2):
        ref[side] = columns[:, side].reshape(D // 2, value.shape[0])


def fetch(slots_ref, sources, held, sems, index):
    copies = []
    for number, source in enumerate(sources):
        for half in range(2):
            spot = slots_ref[2 * number + half, 0]
            side = slots_ref[2 * number + half, 1]
            copies.append(
                pltpu.make_async_copy(
                    source.at[half, index], held.at[index, :, spot, side], sems.at[index, 2 * number + half]
                )
            )
    return copies


def held_weight(held, index):
    return held[index].reshape(D, D)


def arrive(slots_ref, sources, held, in_sems, count):
    @pl.when(pl.program_id(0) == 0)
    def _():
        for index in range(count):
            for copy in fetch(slots_ref, sources, held, in_sems, index):
                copy.start()


def ready(slots_ref, sources, held, outs, in_sems, out_sems, index):
    @pl.when(pl.program_id(0) == 0)
    def _():
        for copy in fetch(slots_ref, sources, held, in_sems, index):
            copy.wait()
        pltpu.make_async_copy(held.at[index], outs[index], out_sems.at[index]).start()


def settle(held, outs, out_sems):
    @pl.when(pl.program_id(0) == pl.num_programs(0) - 1)
    def _():
        for index, out in enumerate(outs):
            pltpu.make_async_copy(held.at[index], out, out_sems.at[index]).wait()


def weight_specs(sources):
    _, count, line, rows, columns = sources[0].shape
    shape = (line, SIDE * SIDE, 2, rows, columns)
    anywhere = pl.BlockSpec(memory_space=pl.ANY)
    return (
        [pl.BlockSpec(memory_space=pltpu.SMEM)] + [anywhere] * 4,
        [anywhere] * count,
        [jax.ShapeDtypeStruct(shape, BF)] * count,
        [
            pltpu.VMEM((count,) + shape, BF),
            pltpu.SemaphoreType.DMA((count, 8)),
            pltpu.SemaphoreType.DMA((count,)),
        ],
    )


def enter_kernel(slots_ref, *refs):
    sources = refs[:4]
    x_ref, gain_ref, a_ref, qkv_ref = refs[4:8]
    outs = refs[8:11]
    held, in_sems, out_sems = refs[11:]
    arrive(slots_ref, sources, held, in_sems, 3)
    a = normed(x_ref[...].astype(F32), gain_ref[...])
    put_sides(a_ref, a)
    for index in range(3):
        ready(slots_ref, sources, held, outs, in_sems, out_sems, index)
        qkv_ref[index] = dot(a, held_weight(held, index), (1, 0)).astype(BF)
    settle(held, outs, out_sems)


def enter(stream_low, gain, slots, sources):
    count = stream_low.shape[0]
    weight_ins, weight_outs, weight_shapes, scratch = weight_specs(sources)
    turned, qkv, *weights = pl.pallas_call(
        enter_kernel,
        grid=(count // TILE,),
        in_specs=weight_ins + [row_block(), whole_block(gain)],
        out_specs=[sided_block(), pl.BlockSpec((3, TILE, D), lambda i: (0, i, 0))] + weight_outs,
        out_shape=[jax.ShapeDtypeStruct((2, D // 2, count), BF), jax.ShapeDtypeStruct((3, count, D), BF)] + weight_shapes,
        scratch_shapes=scratch,
        compiler_params=params(),
        cost_estimate=cost(12),
        name="enter",
    )(slots, *sources, stream_low, gain)
    return turned, qkv, [weight.reshape(D, D) for weight in weights]


def middle_kernel(parts, slots_ref, *refs):
    sources = refs[:4]
    x_ref, *mixed_refs = refs[4:5 + parts]
    (gain_two_ref, gain_three_ref, e_ref, x1_ref, x2_ref, a2_ref, a3_ref, q_ref, o_ref, p_ref, kv_ref, a3_t_ref,
     mixed_t_ref, e_t_ref, o_scr, inv_ref, *outs) = refs[5 + parts:26 + parts]
    held, in_sems, out_sems = refs[26 + parts:]
    arrive(slots_ref, sources, held, in_sems, 5)

    def weight(index):
        ready(slots_ref, sources, held, outs, in_sems, out_sems, index)
        return held_weight(held, index)

    for index in range(2):
        w = weight(2 + index)

        @pl.when(pl.program_id(0) == 0)
        def _(index=index, w=w):
            kv_ref[index] = dot(e_ref[...], w, (1, 0)).astype(BF)

    @pl.when(pl.program_id(0) == 0)
    def _():
        put_sides(e_t_ref, e_ref[...])

    w_first = weight(0)
    (mixed_ref,) = mixed_refs
    x1 = x_ref[...].astype(F32) + dot(mixed_ref[...], w_first, (1, 0))
    x1_ref[...] = x1
    a2 = normed(x1, gain_two_ref[...])
    put_sides(mixed_t_ref, mixed_ref[...])
    put_sides(a2_ref, a2)
    q_ref[...] = dot(a2, weight(1), (1, 0)).astype(BF)
    lane = lax.broadcasted_iota(jnp.int32, (TILE, PAIR), 1)
    inverses = jnp.zeros((TILE, PAIR), F32)
    for pair in range(PAIRS):
        columns = slice(pair * PAIR, (pair + 1) * PAIR)
        k = kv_ref[0, :, columns]
        v = kv_ref[1, :, columns]
        s = dot(both_halves(q_ref[:, columns] * BF(HD ** -0.5)), k, (1, 1))
        e = jnp.exp(s - jnp.max(s, axis=1, keepdims=True))
        inverse = 1.0 / jnp.sum(e, axis=1, keepdims=True)
        low = e.astype(BF)
        mixed = dot(low, v, (1, 0)) * inverse
        for half in range(2):
            rows = slice(half * TILE, (half + 1) * TILE)
            p_ref[2 * pair + half] = low[rows]
            inverses = jnp.where(lane == 2 * pair + half, inverse[rows], inverses)
        o_scr[:, columns] = jnp.where(lane < HD, mixed[:TILE], mixed[TILE:]).astype(BF)
    inv_ref[...] = inverses
    put_sides(o_ref, o_scr[...])
    x2 = x1_ref[...] + dot(o_scr[...], weight(4), (1, 0))
    x2_ref[...] = x2
    a3 = normed(x2, gain_three_ref[...])
    a3_ref[...] = a3
    a3_t_ref[...] = a3.T
    settle(held, outs, out_sems)


def middle(stream_low, mixed, gain_two, gain_three, encoder, slots, sources):
    count = stream_low.shape[0]
    enc = encoder.shape[0]
    low = jax.ShapeDtypeStruct((count, D), BF)
    wide = jax.ShapeDtypeStruct((count, D), F32)
    turned = jax.ShapeDtypeStruct((D, count), BF)
    sided = jax.ShapeDtypeStruct((2, D // 2, count), BF)
    weight_ins, weight_outs, weight_shapes, scratch = weight_specs(sources)
    *results, w1, w2, w3, w4, w5 = pl.pallas_call(
        functools.partial(middle_kernel, len(mixed)),
        grid=(count // TILE,),
        in_specs=weight_ins
        + [row_block()]
        + [row_block(part.shape[1]) for part in mixed]
        + [whole_block(value) for value in (gain_two, gain_three, encoder)],
        out_specs=[row_block(), row_block(), sided_block(), row_block(), row_block(), sided_block()]
        + [
            pl.BlockSpec((HEADS, TILE, enc), lambda i: (0, i, 0)),
            pl.BlockSpec((2, enc, D), lambda i: (0, 0, 0)),
            turned_block(),
            sided_block(),
            pl.BlockSpec((2, D // 2, enc), lambda i: (0, 0, 0)),
            row_block(),
            row_block(PAIR),
        ]
        + weight_outs,
        out_shape=[
            wide,
            wide,
            sided,
            low,
            low,
            sided,
            jax.ShapeDtypeStruct((HEADS, count, enc), BF),
            jax.ShapeDtypeStruct((2, enc, D), BF),
            turned,
            sided,
            jax.ShapeDtypeStruct((2, D // 2, enc), BF),
            low,
            jax.ShapeDtypeStruct((count, PAIR), F32),
        ]
        + weight_shapes,
        scratch_shapes=scratch,
        compiler_params=params(),
        cost_estimate=cost(30),
        name="middle",
    )(slots, *sources, stream_low, *mixed, gain_two, gain_three, encoder)
    return results + [[weight.reshape(D, D) for weight in (w1, w2, w3, w4, w5)]]


def middle_back_kernel(dy_ref, da3_ref, x2_ref, x1_ref, q_ref, o_ref, inv_ref, p_ref, kv_ref, gain_two_ref, gain_three_ref, wc_ref, wq_ref,
                       wo_ref, *refs):
    before = refs[:-9]
    low2_ref, dq_ref, dx1_ref, low1_ref, do1_ref, dkv_ref, sums_ref, gains_ref, do_ref = refs[-9:]
    dk_acc, dv_acc = sums_ref.at[0], sums_ref.at[1]
    step = pl.program_id(0)

    @pl.when(step == 0)
    def _():
        sums_ref[...] = before[-2][...] if before else jnp.zeros_like(sums_ref)
        gains_ref[...] = before[-1][...] if before else jnp.zeros_like(gains_ref)

    back, terms = norm_back(x2_ref[...], gain_three_ref[...], da3_ref[...])
    gains_ref[1] += terms
    dx2 = dy_ref[...].astype(F32) + back
    dx1_ref[...] = dx2
    low2 = dx2.astype(BF)
    low2_ref[...] = low2
    do_ref[...] = dot(low2, wo_ref[...], (1, 1)).astype(BF)
    lane = lax.broadcasted_iota(jnp.int32, (TILE, PAIR), 1)
    for pair in range(PAIRS):
        columns = slice(pair * PAIR, (pair + 1) * PAIR)
        k = kv_ref[0, :, columns]
        v = kv_ref[1, :, columns]
        inverse = jnp.where(lane < HD, inv_ref[:, 2 * pair:2 * pair + 1], inv_ref[:, 2 * pair + 1:2 * pair + 2])
        do = (do_ref[:, columns].astype(F32) * inverse).astype(BF)
        drops = do.astype(F32) * o_ref[:, columns].astype(F32)
        q_left, do_left = (q_ref[:, columns] * BF(HD ** -0.5)).T, do.T
        drop = jnp.sum(both_halves(drops), axis=1, keepdims=True)
        low = jnp.concatenate([p_ref[2 * pair], p_ref[2 * pair + 1]], axis=0)
        down = (low.astype(F32) * (dot(both_halves(do), v, (1, 1)) - drop)).astype(BF)
        dq = dot(down, k, (1, 0))
        for half in range(2):
            rows = slice(half * HD, (half + 1) * HD)
            tile = slice(half * TILE, (half + 1) * TILE)
            places = slice(pair * PAIR + half * HD, pair * PAIR + (half + 1) * HD)
            dk_acc[places] += dot(q_left[rows], down[tile], (1, 0))
            dv_acc[places] += dot(do_left[rows], low[tile], (1, 0))
        dq_ref[:, columns] = (jnp.where(lane < HD, dq[:TILE], dq[TILE:]) * (HD ** -0.5)).astype(BF)
    da2 = dot(dq_ref[...], wq_ref[...], (1, 1))
    back, terms = norm_back(x1_ref[...], gain_two_ref[...], da2)
    gains_ref[0] += terms
    dx1 = dx1_ref[...] + back
    dx1_ref[...] = dx1
    low1 = dx1.astype(BF)
    low1_ref[...] = low1
    do1_ref[...] = dot(low1, wc_ref[...], (1, 1)).astype(BF)

    @pl.when(step == pl.num_programs(0) - 1)
    def _():
        dkv_ref[0] = dk_acc[...].T.astype(BF)
        dkv_ref[1] = dv_acc[...].T.astype(BF)


def middle_back(first, blocks, low_up, grad_three, after_two, after_one, query_two, mixed_two, inverse_two, expos_two,
                kv_two, gain_two, gain_three, w_comb_one, w_query_two, w_comb_two, before=None):
    count = low_up.shape[0]
    enc = kv_two.shape[1]
    low = jax.ShapeDtypeStruct((count, D), BF)
    wide = jax.ShapeDtypeStruct((count, D), F32)
    rows = pl.BlockSpec((TILE, D), lambda i: (first + i, 0))
    sums = jax.ShapeDtypeStruct((2, D, enc), F32)
    gains = jax.ShapeDtypeStruct((2, 8, D), F32)
    whole = (kv_two, gain_two, gain_three, w_comb_one, w_query_two, w_comb_two)
    operands = (low_up, grad_three, after_two, after_one, query_two, mixed_two, inverse_two, expos_two) + whole
    more = [] if before is None else list(before[:5]) + list(before[6:])
    aliases = {} if before is None else {len(operands) + index: index for index in range(5)}
    return pl.pallas_call(
        middle_back_kernel,
        grid=(blocks,),
        in_specs=[rows] * 6
        + [
            pl.BlockSpec((TILE, PAIR), lambda i: (first + i, 0)),
            pl.BlockSpec((HEADS, TILE, enc), lambda i: (0, first + i, 0)),
        ]
        + [whole_block(value) for value in whole]
        + ([] if before is None else [pl.BlockSpec(memory_space=pl.ANY)] * 5 + [whole_block(sums), whole_block(gains)]),
        out_specs=[rows] * 5
        + [
            pl.BlockSpec((2, enc, D), lambda i: (0, 0, 0)),
            pl.BlockSpec((2, D, enc), lambda i: (0, 0, 0)),
            pl.BlockSpec((2, 8, D), lambda i: (0, 0, 0)),
        ],
        out_shape=[low, low, wide, low, low, jax.ShapeDtypeStruct((2, enc, D), BF), sums, gains],
        scratch_shapes=[pltpu.VMEM((TILE, D), BF)],
        input_output_aliases=aliases,
        compiler_params=params(),
        cost_estimate=cost(45),
        name="middle_back",
    )(*operands, *more)


def leave_kernel(parts, plan_ref, x_ref, dx1_ref, *refs):
    grads = refs[:3 * parts]
    gain_ref, wq_ref, wk_ref, wv_ref, out_ref, gains_ref = refs[3 * parts:]

    @pl.when(pl.program_id(0) == 0)
    def _():
        gains_ref[...] = jnp.zeros_like(gains_ref)

    da = None
    end = 0
    for index in range(parts):
        columns = slice(end, end + grads[3 * index].shape[1])
        end = columns.stop
        for which, w_ref in enumerate((wq_ref, wk_ref, wv_ref)):
            part = dot(grads[3 * index + which][...], w_ref[:, columns], (1, 1))
            da = part if da is None else da + part
    back, terms = norm_back(x_ref[...].astype(F32), gain_ref[...], da)
    gains_ref[...] += terms
    out_ref[...] = dx1_ref[...] + back


def leave(plan, blocks, stream_low, grad_after_one, parts, gain, w_query, w_key, w_value):
    weights = (w_query, w_key, w_value)
    flat = [value for part in parts for value in part]

    def rows(value):
        return pl.BlockSpec((TILE, value.shape[1]), lambda i, p: (p[i], 0))

    return pl.pallas_call(
        functools.partial(leave_kernel, len(parts)),
        grid_spec=pltpu.PrefetchScalarGridSpec(
            num_scalar_prefetch=1,
            grid=(blocks,),
            in_specs=[rows(stream_low), rows(grad_after_one)]
            + [rows(value) for value in flat]
            + [whole_block(value) for value in (gain,) + weights],
            out_specs=[pl.BlockSpec((TILE, D), lambda i, p: (i, 0)), pl.BlockSpec((8, D), lambda i, p: (0, 0))],
        ),
        out_shape=[jax.ShapeDtypeStruct((blocks * TILE, D), F32), jax.ShapeDtypeStruct((8, D), F32)],
        compiler_params=params(),
        cost_estimate=cost(2),
        name="leave",
    )(plan, stream_low, grad_after_one, *flat, gain, *weights)


def update_kernel(count, lows, factor_ref, *refs):
    ins = refs[:4 * count]
    outs = refs[4 * count:7 * count + lows]
    held = refs[7 * count + lows:11 * count + lows]
    ready = refs[11 * count + lows:14 * count + 2 * lows]
    in_sems, out_sems = refs[14 * count + 2 * lows:]
    arrivals = [pltpu.make_async_copy(ref, kept, in_sems.at[n]) for n, (ref, kept) in enumerate(zip(ins, held))]
    departures = [pltpu.make_async_copy(kept, ref, out_sems.at[n]) for n, (ref, kept) in enumerate(zip(outs, ready))]
    for index in range(count):
        for group in range(4):
            arrivals[group * count + index].start()
    factor = factor_ref[0]
    for index in range(count):
        for group in range(4):
            arrivals[group * count + index].wait()
        weight, first, second, grad = (held[group * count + index] for group in range(4))
        states = adam(weight[...], first[...], second[...], grad[...] * factor, RATES[index])
        for place, value in enumerate(states):
            ready[3 * index + place][...] = value
            departures[3 * index + place].start()
        if index < lows:
            ready[3 * count + index][...] = states[0].astype(BF)
            departures[3 * count + index].start()
    for copy in departures:
        copy.wait()


def update(factor, weights, firsts, seconds, grads, lows=4):
    count = len(weights)
    operands = tuple(weights) + tuple(firsts) + tuple(seconds) + tuple(grads)
    shapes = [jax.ShapeDtypeStruct(weight.shape, F32) for weight in weights for _ in range(3)]
    shapes += [jax.ShapeDtypeStruct(weight.shape, BF) for weight in weights[:lows]]
    anywhere = pl.BlockSpec(memory_space=pl.ANY)
    outs = pl.pallas_call(
        functools.partial(update_kernel, count, lows),
        in_specs=[pl.BlockSpec(memory_space=pltpu.SMEM)] + [anywhere] * len(operands),
        out_specs=[anywhere] * len(shapes),
        out_shape=shapes,
        scratch_shapes=[pltpu.VMEM(value.shape, F32) for value in operands]
        + [pltpu.VMEM(shape.shape, shape.dtype) for shape in shapes]
        + [pltpu.SemaphoreType.DMA((len(operands),)), pltpu.SemaphoreType.DMA((len(shapes),))],
        compiler_params=params(),
        cost_estimate=cost(5),
        name="update",
    )(factor.reshape(1), *operands)
    return [outs[3 * index:3 * index + 3] for index in range(count)], outs[3 * count:]


SIDE = 2
LINE = 4
AXES = ("dp", "fsdp")


def place_of(z, y, x, core):
    return ((z * SIDE + y) * SIDE + x) * 2 + core


def moves(rule):
    every = [(z, y, x, c) for z in range(LINE) for y in range(SIDE) for x in range(SIDE) for c in range(2)]
    return [(place_of(*here), place_of(*rule(*here))) for here in every]


def send(value, rule):
    return lax.ppermute(value, AXES, moves(rule))


def along_line(shift):
    return lambda z, y, x, c: ((z + shift) % LINE, y, x, c)


def line_far(z, y, x, c):
    return (z ^ 2, y, x, c)


def line_near(z, y, x, c):
    return (z ^ 1, y, x, c)


def first_flip(z, y, x, c):
    return (z, y, 1 - x, c) if c == 0 else (z, 1 - y, x, c)


def second_flip(z, y, x, c):
    return (z, 1 - y, x, c) if c == 0 else (z, y, 1 - x, c)


def core_flip(z, y, x, c):
    return (z, y, x, 1 - c)


def spots(y, x, core):
    here = y * SIDE + x
    along_x = y * SIDE + 1 - x
    along_y = (1 - y) * SIDE + x
    across = (1 - y) * SIDE + 1 - x
    near = jnp.where(core == 0, along_x, along_y)
    far = jnp.where(core == 0, along_y, along_x)
    return here, near, far, across


def put_kernel(z_ref, shard, far, near, out, sems):
    z = z_ref[0]
    sources = [(shard, z), (far, z ^ 2), (near.at[0], z ^ 1), (near.at[1], z ^ 3)]
    copies = [
        pltpu.make_async_copy(source, out.at[:, slot], sems.at[index])
        for index, (source, slot) in enumerate(sources)
    ]
    for copy in copies:
        copy.start()
    for copy in copies:
        copy.wait()


def put_in_line(shard, far, near, z):
    count, rows, columns = shard.shape
    return pl.pallas_call(
        put_kernel,
        in_specs=[pl.BlockSpec(memory_space=pltpu.SMEM)] + [pl.BlockSpec(memory_space=pl.ANY)] * 3,
        out_specs=pl.BlockSpec(memory_space=pltpu.VMEM),
        out_shape=jax.ShapeDtypeStruct((count, LINE, rows, columns), shard.dtype),
        scratch_shapes=[pltpu.SemaphoreType.DMA((LINE,))],
        compiler_params=params(40),
        cost_estimate=cost(1),
        name="put_in_line",
    )(z[None], shard, far, near)


def assemble_kernel(slots_ref, *refs):
    sources = refs[:4]
    outs, sems = refs[4:-1], refs[-1]
    copies = []
    for index, source in enumerate(sources):
        for half in range(2):
            spot = slots_ref[2 * index + half, 0]
            side = slots_ref[2 * index + half, 1]
            for k, out in enumerate(outs):
                copies.append(
                    pltpu.make_async_copy(source.at[half, k], out.at[:, spot, side], sems.at[len(copies)])
                )
    for copy in copies:
        copy.start()
    for copy in copies:
        copy.wait()


def assemble(sources, slots):
    _, count, line, rows, columns = sources[0].shape
    shape = (line, SIDE * SIDE, 2, rows, columns)
    outs = pl.pallas_call(
        assemble_kernel,
        in_specs=[pl.BlockSpec(memory_space=pltpu.SMEM)] + [pl.BlockSpec(memory_space=pl.ANY)] * 4,
        out_specs=[pl.BlockSpec(memory_space=pltpu.VMEM)] * count,
        out_shape=[jax.ShapeDtypeStruct(shape, sources[0].dtype)] * count,
        scratch_shapes=[pltpu.SemaphoreType.DMA((8 * count,))],
        compiler_params=params(40),
        cost_estimate=cost(2 * count),
        name="assemble",
    )(slots, *sources)
    return [out.reshape(line * SIDE * SIDE * 2 * rows, columns) for out in outs]


def tie(*values):
    return lax.optimization_barrier(values)


def line_stage(shard):
    return [send(shard, along_line(shift)) for shift in range(1, LINE)]


def piece_slots(place):
    _, y, x, core = place
    mine = spots(y, x, core)
    theirs = spots(y, x, 1 - core)
    order = [(mine[0], core), (mine[1], core), (theirs[0], 1 - core), (theirs[1], 1 - core)]
    order += [(mine[2], core), (mine[3], core), (theirs[2], 1 - core), (theirs[3], 1 - core)]
    return jnp.stack([jnp.stack(pair) for pair in order])


def add_split_kernel(spots_ref, one_ref, two_ref, away_ref, stay_ref):
    slot = pl.program_id(0)
    value = one_ref[...] + two_ref[...]

    for out_ref, here in ((away_ref, slot < 2), (stay_ref, slot >= 2)):
        @pl.when(here)
        def _(out_ref=out_ref):
            for index in range(value.shape[0]):
                out_ref[0, :, index] = value[index, :, 0]


def add_split(keep, received, place):
    _, y, x, core = place
    here, near, far, across = spots(y, x, core)
    count, _, rows, columns = keep.shape
    grid = (count, LINE, SIDE * SIDE, rows, columns)
    wide = columns if columns <= D else columns // 2
    source = pl.BlockSpec((count, LINE, 1, rows, wide), lambda j, t, s: (0, 0, s[j], 0, t))
    out = jax.ShapeDtypeStruct((2, LINE, count, rows, columns), BF)
    block = (1, LINE, count, rows, wide)
    return pl.pallas_call(
        add_split_kernel,
        grid_spec=pltpu.PrefetchScalarGridSpec(
            num_scalar_prefetch=1,
            grid=(4, columns // wide),
            in_specs=[source, source],
            out_specs=[
                pl.BlockSpec(
                    block, lambda j, t, s: (jnp.minimum(j, 1), 0, 0, 0, jnp.where(j < 2, t, columns // wide - 1))
                ),
                pl.BlockSpec(block, lambda j, t, s: (jnp.maximum(j - 2, 0), 0, 0, 0, jnp.where(j < 2, 0, t))),
            ],
        ),
        out_shape=[out, out],
        compiler_params=params(),
        cost_estimate=cost(1),
        name="add_split",
    )(jnp.stack([far, across, here, near]), keep.reshape(grid), received.reshape(grid))


def plus(one, two):
    return (one.astype(F32) + two.astype(F32)).astype(BF)


def line_split(line, place):
    z = place[0]

    def at(index):
        return lax.dynamic_index_in_dim(line, index, 0, keepdims=False)

    return (at(z), at(z ^ 2)), jnp.stack([at(z ^ 1), at(z ^ 3)])


def add_in_order(value, received, own, owners):
    total = None
    for index in range(4):
        term = jnp.where(own == index, value, 0.0)
        for part, owner in zip(received, owners):
            term = term + jnp.where(owner == index, part, 0.0)
        total = term if total is None else total + term
    return total


def sum_everywhere(value, place):
    z, y, x, core = place
    parts = [send(value, along_line(shift)) for shift in range(1, LINE)]
    value = add_in_order(value, parts, z, [(z - shift) % LINE for shift in range(1, LINE)])
    flips = [(0, 1), (1, 0), (1, 1)]
    parts = [send(value, lambda z, y, x, c, dy=dy, dx=dx: (z, y ^ dy, x ^ dx, c)) for dy, dx in flips]
    value = add_in_order(
        value, parts, y * SIDE + x, [jnp.bitwise_xor(y, dy) * SIDE + jnp.bitwise_xor(x, dx) for dy, dx in flips]
    )
    return value + send(value, core_flip)


def swap_halves(parts, core):
    def block(index):
        return jnp.concatenate(
            [lax.dynamic_index_in_dim(part, index, 0, keepdims=False).reshape(-1, D) for part in parts], axis=0
        )

    mine = block(core)
    theirs = send(block(1 - core), core_flip)
    first = jnp.where(core == 0, mine, theirs)
    second = jnp.where(core == 0, theirs, mine)
    whole, begin = [], 0
    for part in parts:
        end = begin + part.size // 2 // D
        whole.append(jnp.concatenate([first[begin:end], second[begin:end]], axis=0))
        begin = end
    return whole


def hand_over(parts, core):
    halves = [part.reshape((2, -1, D)) for part in parts]

    def block(index):
        return jnp.concatenate([lax.dynamic_index_in_dim(part, index, 0, keepdims=False) for part in halves], axis=0)

    return block(core), send(block(1 - core), core_flip)


def both_groups(mine, other, core):
    return jnp.stack([jnp.where(core == 0, mine, other), jnp.where(core == 0, other, mine)])


def matmul(left, right):
    return jnp.dot(left, right, preferred_element_type=F32)


def matmul_t(left, right):
    return lax.dot_general(left, right, (((1,), (1,)), ((), ())), preferred_element_type=F32)


def paired_body(
    prompt_states,
    branch_states,
    encoder_states,
    branch_start,
    bucket_table,
    prompt_cotangent,
    branch_cotangent,
    projections,
    projections_first,
    projections_second,
    combiners,
    combiners_first,
    combiners_second,
    expansion,
    expansion_first,
    expansion_second,
    contraction,
    contraction_first,
    contraction_second,
    norm_gains,
    gains_first,
    gains_second,
    position_bias,
    bias_first,
    bias_second,
):
    rows_here = prompt_states.shape[1]
    prompt = 2 * rows_here
    size = branch_states.shape[2]
    place_index = lax.axis_index("dp")
    core = lax.axis_index("fsdp")
    place = (place_index // (SIDE * SIDE), place_index // SIDE % SIDE, place_index % SIDE, core)

    z = place[0]
    core_ref = core[None]

    shard_qkv = projections[:3].astype(BF)
    shard_mid = jnp.concatenate([combiners[:1], projections[3:], combiners[1:]], axis=0).astype(BF)
    shard_exp = expansion.astype(BF)
    shard_con = contraction[None].astype(BF)
    far_line_qkv = send(shard_qkv, line_far)

    other_start = send(lax.dynamic_index_in_dim(branch_start, 1 - core, 0, keepdims=False), core_flip)
    own_start = lax.dynamic_index_in_dim(branch_start, core, 0, keepdims=False)
    starts = jnp.concatenate(
        [jnp.where(core == 0, own_start, other_start), jnp.where(core == 0, other_start, own_start)]
    )
    gain_rows = [norm_gains[index:index + 1] for index in range(3)]

    bucket_ids = jnp.arange(BUCKETS, dtype=jnp.int32)
    flipped_table = jnp.flip(bucket_table)
    flipped_onehot = (flipped_table[:, None] == bucket_ids[None, :]).astype(F32)
    flipped_bias = jnp.dot(flipped_onehot, position_bias, precision=lax.Precision.HIGHEST).T
    buckets = distance_buckets(flipped_table, starts, prompt, size)
    slots = piece_slots(place)

    far_line_qkv, starts = tie(far_line_qkv, starts)
    near_line_qkv = send(jnp.stack([shard_qkv, far_line_qkv]), line_near)
    near_line_qkv, prompt_states, shard_mid = tie(near_line_qkv, prompt_states, shard_mid)
    far_line_mid = send(shard_mid, line_far)
    prompt_rows, branch_rows, prompt_up, branch_up, encoder = swap_halves(
        [prompt_states, branch_states, prompt_cotangent, branch_cotangent, encoder_states], core
    )
    own_qkv = put_in_line(shard_qkv, far_line_qkv, near_line_qkv, z)
    near_qkv = send(own_qkv, first_flip)
    near_qkv, own_qkv = tie(near_qkv, own_qkv)
    close_qkv = jnp.stack([own_qkv, near_qkv])
    far_qkv = send(close_qkv, second_flip)
    close_qkv, far_line_mid = tie(close_qkv, far_line_mid)
    near_line_mid = send(jnp.stack([shard_mid, far_line_mid]), line_near)
    close_qkv_two = send(close_qkv, core_flip)
    base, branch = bias_rows(flipped_bias, starts, prompt, size)
    stream_low = jnp.concatenate([prompt_rows, branch_rows], axis=0)
    low_up = jnp.concatenate([prompt_up, branch_up], axis=0)
    far_qkv, near_line_mid, close_qkv_two, stream_low, low_up, encoder, base, branch, shard_exp, shard_con = tie(
        far_qkv, near_line_mid, close_qkv_two, stream_low, low_up, encoder, base, branch, shard_exp, shard_con
    )
    far_qkv_two = send(far_qkv, core_flip)
    own_mid = put_in_line(shard_mid, far_line_mid, near_line_mid, z)
    near_mid = send(own_mid, first_flip)
    far_line_exp = send(shard_exp, line_far)
    stream_low, own_mid, far_qkv_two = tie(stream_low, own_mid, far_qkv_two)

    turned_one, qkv, (w_query, w_key, w_value) = enter(
        stream_low, gain_rows[0], slots, [close_qkv, close_qkv_two, far_qkv, far_qkv_two]
    )
    qkv, near_mid, far_line_exp, shard_con = tie(qkv, near_mid, far_line_exp, shard_con)
    close_mid = jnp.stack([own_mid, near_mid])
    far_mid = send(close_mid, second_flip)
    near_line_exp = send(jnp.stack([shard_exp, far_line_exp]), line_near)
    far_line_con = send(shard_con, line_far)
    close_mid_two = send(close_mid, core_flip)
    qkv, close_mid = tie(qkv, close_mid)
    most = PAIRS // 2
    heads = self_forward(qkv, base, branch, starts, prompt, size, 0, most)
    *heads, qkv, far_mid, close_mid_two, near_line_exp, far_line_con = tie(
        *heads, qkv, far_mid, close_mid_two, near_line_exp, far_line_con
    )
    own_exp = put_in_line(shard_exp, far_line_exp, near_line_exp, z)
    near_exp = send(own_exp, first_flip)
    far_mid_two = send(far_mid, core_flip)
    near_line_con = send(jnp.stack([shard_con, far_line_con]), line_near)
    qkv, own_exp, far_mid = tie(qkv, own_exp, far_mid)
    heads = self_forward(qkv, base, branch, starts, prompt, size, most, PAIRS - most, heads)
    *heads, far_mid_two, near_exp, near_line_con = tie(*heads, far_mid_two, near_exp, near_line_con)
    mixed_one, expos, inverse = heads
    close_exp = jnp.stack([own_exp, near_exp])
    far_exp = send(close_exp, second_flip)
    close_exp_two = send(close_exp, core_flip)
    own_con = put_in_line(shard_con, far_line_con, near_line_con, z)
    near_con = send(own_con, first_flip)
    mixed_one, close_exp, own_con = tie(mixed_one, close_exp, own_con)
    (after_one, after_two, turned_two, input_three, query_two, turned_mixed_two, expos_two, kv_two, turned_three,
     turned_mixed_one, turned_encoder, mixed_two, inverse_two, weights_mid) = middle(
        stream_low,
        [mixed_one],
        gain_rows[1],
        gain_rows[2],
        encoder,
        slots,
        [close_mid, close_mid_two, far_mid, far_mid_two],
    )
    w_comb_one, w_query_two, w_key_two, w_value_two, w_comb_two = weights_mid
    input_three, far_exp, near_con, close_exp_two = tie(input_three, far_exp, near_con, close_exp_two)
    far_exp_two = send(far_exp, core_flip)
    close_con = jnp.stack([own_con, near_con])
    far_con = send(close_con, second_flip)
    close_con_two = send(close_con, core_flip)
    w_gate, w_up = assemble([close_exp, close_exp_two, far_exp, far_exp_two], slots)
    w_gate, w_up, far_con, close_con_two = tie(w_gate, w_up, far_con, close_con_two)
    far_con_two = send(far_con, core_flip)
    w_con = assemble([close_con, close_con_two, far_con, far_con_two], slots)[0]

    owners = LINE * SIDE * SIDE * 2
    own_output, output_to_give, grad_three, away_exp, keep_exp, away_con, keep_con = mlp(
        core_ref, after_two, input_three, turned_three, low_up, w_gate, w_up, w_con, owners, 2 * size
    )
    got_exp = send(away_exp, core_flip)
    got_con = send(away_con[None], core_flip)
    other_output = send(output_to_give, core_flip)
    low_up, away_exp, away_con, grad_three = tie(low_up, away_exp, away_con, grad_three)

    def middle_part(first, blocks, before=None):
        return middle_back(
            first,
            blocks,
            low_up,
            grad_three,
            after_two,
            after_one,
            query_two,
            mixed_two,
            inverse_two,
            expos_two,
            kv_two,
            gain_rows[1],
            gain_rows[2],
            w_comb_one,
            w_query_two,
            w_comb_two,
            before,
        )

    before = middle_part(0, 1)
    *before, got_exp, got_con = tie(*before, got_exp, got_con)
    away_con, stay_con = add_split(keep_con[None], got_con, place)
    got_con = send(away_con, second_flip)
    away_exp, stay_exp = add_split(keep_exp, got_exp, place)
    got_exp = send(away_exp, second_flip)
    *before, away_exp, away_con = tie(*before, away_exp, away_con)
    (cross_low, query_two_low, grad_after_one, self_low, grad_mixed_one, kv_two_low, _, gain_back) = middle_part(
        1, prompt // TILE + 2 * size // TILE - 1, before
    )
    _, y, x, _ = place
    here, near, far, across = spots(y, x, core)
    keep_plan = jnp.stack([core, far, across, here, near])
    away_plan = jnp.stack([1 - core, far, across, here, near])
    lefts_mid = [turned_mixed_one, turned_two, turned_encoder, turned_mixed_two]
    jobs_mid = [(0, self_low), (1, query_two_low), (2, (kv_two_low, 0)), (2, (kv_two_low, 1)), (3, cross_low)]
    away_mid = weight_part(away_plan, lefts_mid, jobs_mid)
    encoder_grad = matmul_t(kv_two_low[0], w_key_two) + matmul_t(kv_two_low[1], w_value_two)
    away_mid, encoder_grad, other_output, got_exp, got_con = tie(away_mid, encoder_grad, other_output, got_exp, got_con)
    got_mid = send(away_mid, core_flip)
    near_con = plus(stay_con[1], got_con[1])
    got_near_con = send(near_con, first_flip)
    near_exp = plus(stay_exp[1], got_exp[1])
    got_near_exp = send(near_exp, first_flip)
    own_encoder, other_encoder = hand_over([encoder_grad], core)
    grad_mixed_one, away_mid, near_exp, near_con, own_encoder = tie(
        grad_mixed_one, away_mid, near_exp, near_con, own_encoder
    )

    half = PAIRS // 2

    def attend_back(first, pairs, *values):
        part = self_backward(qkv, grad_mixed_one, mixed_one, expos, inverse, prompt, size, first, pairs)
        first, *rest = tie(part[0], grad_mixed_one, *values)
        return ((first,) + tuple(part[1:]), *rest)

    def jobs_of(*parts):
        return [(0, [part[i] for part in parts] if len(parts) > 1 else parts[0][i]) for i in range(3)]

    part_one, grad_mixed_one, got_mid, other_encoder, got_near_con, got_near_exp = attend_back(
        0, half, got_mid, other_encoder, got_near_con, got_near_exp
    )
    line_exp, away_exp = line_split(plus(plus(stay_exp[0], got_exp[0]), got_near_exp), place)
    got_line_exp = send(away_exp, line_near)
    away_mid, stay_mid = weight_part(keep_plan, lefts_mid, jobs_mid, got_mid)
    got_mid = send(away_mid, second_flip)
    line_con, away_con = line_split(plus(plus(stay_con[0], got_con[0]), got_near_con), place)
    got_line_con = send(away_con, line_near)
    away_plan, away_exp, away_con, away_mid = tie(away_plan, away_exp, away_con, away_mid)
    away_one = weight_part(away_plan, [turned_one], jobs_of(part_one))
    got_one = send(away_one, core_flip)
    grad_mixed_one, away_one = tie(grad_mixed_one, away_one)

    part_two, grad_mixed_one, got_one, got_mid, got_line_exp, away_plan = attend_back(
        half, half, got_one, got_mid, got_line_exp, away_plan
    )
    near_mid = plus(stay_mid[1], got_mid[1])
    got_near_mid = send(near_mid, first_flip)
    away_plan, near_mid = tie(away_plan, near_mid)
    away_two = weight_part(away_plan, [turned_one], jobs_of(part_two))
    got_two = send(away_two, core_flip)
    last_exp = plus(line_exp[1], got_line_exp[1])
    got_last_exp = send(last_exp, line_far)
    keep_plan, away_two, last_exp = tie(keep_plan, away_two, last_exp)
    away_one, stay_one = weight_part(keep_plan, [turned_one], jobs_of(part_one), got_one)
    got_one = send(away_one, second_flip)
    leave_values = (
        stream_low,
        grad_after_one,
        [part_one[:3], part_two[:3]],
        gain_rows[0],
        w_query,
        w_key,
        w_value,
    )
    blocks = prompt // TILE // 2
    steps = jnp.arange(blocks, dtype=jnp.int32)
    theirs_plan = jnp.concatenate([(1 - core) * blocks + steps, jnp.full((1,), 2 * blocks, jnp.int32)])
    ours_plan = core * blocks + steps

    theirs_plan, away_one, got_two = tie(theirs_plan, away_one, got_two)
    theirs_grad, gain_one = leave(theirs_plan, blocks + 1, *leave_values)
    theirs_grad, got_one, got_near_mid, keep_plan, got_line_con = tie(
        theirs_grad, got_one, got_near_mid, keep_plan, got_line_con
    )
    away_two, stay_two = weight_part(keep_plan, [turned_one], jobs_of(part_two), got_two)
    got_two = send(away_two, second_flip)
    away_two, stay_one, stay_mid, theirs_grad = tie(away_two, stay_one, stay_mid, theirs_grad)
    near_one = plus(stay_one[1], got_one[1])
    got_near_one = send(near_one, first_flip)
    line_mid, away_mid = line_split(plus(plus(stay_mid[0], got_mid[0]), got_near_mid), place)
    got_line_mid = send(away_mid, line_near)
    last_con = plus(line_con[1], got_line_con[1])
    got_last_con = send(last_con, line_far)
    ours_plan, near_one, away_mid, last_con = tie(ours_plan, near_one, away_mid, last_con)
    ours_grad, gain_more = leave(ours_plan, blocks, *leave_values)
    ours_grad, got_two, got_near_one, got_line_mid = tie(ours_grad, got_two, got_near_one, got_line_mid)
    near_two = plus(stay_two[1], got_two[1])
    got_near_two = send(near_two, first_flip)
    line_one, away_one = line_split(plus(plus(stay_one[0], got_one[0]), got_near_one), place)
    got_line_one = send(away_one, line_near)
    last_mid = plus(line_mid[1], got_line_mid[1])
    got_last_mid = send(last_mid, line_far)
    got_grad = send(theirs_grad, core_flip)
    half_rows = prompt // 2
    prompt_output = both_groups(own_output[:half_rows], other_output[:half_rows], core)
    branch_output = both_groups(own_output[half_rows:], other_output[half_rows:], core)
    encoder_out = both_groups(own_encoder, other_encoder, core)
    got_near_two, got_line_one, got_last_con, got_last_exp, prompt_output, branch_output, encoder_out = tie(
        got_near_two, got_line_one, got_last_con, got_last_exp, prompt_output, branch_output, encoder_out
    )
    line_two, away_two = line_split(plus(plus(stay_two[0], got_two[0]), got_near_two), place)
    got_line_two = send(away_two, line_near)
    got_last_one = send(plus(line_one[1], got_line_one[1]), line_far)

    def owned_part(line, got_line, got_last):
        return line[0].astype(F32) + got_line[0].astype(F32) + got_last.astype(F32)

    def square(value):
        return jnp.sum(value * value)

    owned_exp = owned_part(line_exp, got_line_exp, got_last_exp)
    owned_con = owned_part(line_con, got_line_con, got_last_con)[0]
    squares = square(owned_exp) + square(owned_con)
    prompt_grad = both_groups(ours_grad, got_grad[:half_rows], core)
    squares, got_line_two, got_last_one, got_last_mid, prompt_grad = tie(
        squares, got_line_two, got_last_one, got_last_mid, prompt_grad
    )
    got_last_two = send(plus(line_two[1], got_line_two[1]), line_far)
    owned_mid = owned_part(line_mid, got_line_mid, got_last_mid)
    owned_one = owned_part(line_one, got_line_one, got_last_one)
    squares = squares + square(owned_mid) + square(owned_one)
    grad_bias = bias_gradient(
        jnp.concatenate([part_one[3], part_two[3]]),
        jnp.concatenate([part_one[4], part_two[4]]),
        buckets,
    )
    own_branch = lax.dynamic_slice_in_dim(theirs_grad, half_rows + core * size, size, 0)
    other_branch = lax.dynamic_slice_in_dim(got_grad, half_rows + core * size, size, 0)
    branch_grad = both_groups(own_branch, other_branch, core)
    squares, grad_bias, got_last_two, branch_grad = tie(squares, grad_bias, got_last_two, branch_grad)
    owned_two = owned_part(line_two, got_line_two, got_last_two)
    squares = squares + square(owned_two)
    owned_self = jnp.concatenate([owned_one, owned_two], axis=2)

    owned = (
        jnp.concatenate([owned_self, owned_mid[1:4]], axis=0),
        jnp.stack([owned_mid[0], owned_mid[4]]),
        owned_exp,
        owned_con,
    )
    gain_back = jnp.sum(jnp.concatenate([(gain_one + gain_more)[None], gain_back]), axis=1)
    rest = jnp.concatenate([grad_bias.reshape(-1), squares[None]])
    shared = sum_everywhere(
        jnp.concatenate([gain_back, jnp.pad(rest, (0, D - rest.size))[None]]), place
    )
    gain_total = shared[:3]
    bias_total = shared[3, :grad_bias.size].reshape(grad_bias.shape)
    square_total = shared[3, grad_bias.size]
    grad_norm = jnp.sqrt(
        square_total + jnp.sum(gain_total * gain_total) + jnp.sum(bias_total * bias_total)
    )
    factor = jnp.minimum(1.0, CLIP / (grad_norm + 1e-06))
    weights = (projections, combiners, expansion, contraction, norm_gains, position_bias)
    firsts = (projections_first, combiners_first, expansion_first, contraction_first, gains_first, bias_first)
    seconds = (
        projections_second,
        combiners_second,
        expansion_second,
        contraction_second,
        gains_second,
        bias_second,
    )
    states, copies = update(factor, weights[:5], firsts[:5], seconds[:5], owned + (gain_total,))
    states.append(adam(weights[5], firsts[5], seconds[5], bias_total * factor, RATES[5]))
    branch_shape = (2, 1, size, D)
    return (
        prompt_output,
        branch_output.reshape(branch_shape),
        prompt_grad,
        branch_grad.reshape(branch_shape),
        encoder_out,
        grad_norm,
        *states[0],
        *states[1],
        *states[2],
        *states[3],
        *states[4],
        *states[5],
        copies[0],
        copies[1],
        copies[2],
        copies[3],
    )


def solution(mesh):
    paired = mesh.shape["dp"] == 4 * SIDE * SIDE and mesh.shape["fsdp"] == 2
    return jax.shard_map(
        paired_body if paired else body,
        mesh=mesh,
        in_specs=(
            P("dp", "fsdp", None),
            P("dp", "fsdp", None, None),
            P("dp", "fsdp", None),
            P("dp", "fsdp"),
            P(),
            P("dp", "fsdp", None),
            P("dp", "fsdp", None, None),
            P(None, ("dp", "fsdp"), None),
            P(None, ("dp", "fsdp"), None),
            P(None, ("dp", "fsdp"), None),
            P(None, ("dp", "fsdp"), None),
            P(None, ("dp", "fsdp"), None),
            P(None, ("dp", "fsdp"), None),
            P(None, ("dp", "fsdp"), None),
            P(None, ("dp", "fsdp"), None),
            P(None, ("dp", "fsdp"), None),
            P(("dp", "fsdp"), None),
            P(("dp", "fsdp"), None),
            P(("dp", "fsdp"), None),
            P(),
            P(),
            P(),
            P(),
            P(),
            P(),
        ),
        out_specs=(
            P("dp", "fsdp", None),
            P("dp", "fsdp", None, None),
            P("dp", "fsdp", None),
            P("dp", "fsdp", None, None),
            P("dp", "fsdp", None),
            P(),
            P(None, ("dp", "fsdp"), None),
            P(None, ("dp", "fsdp"), None),
            P(None, ("dp", "fsdp"), None),
            P(None, ("dp", "fsdp"), None),
            P(None, ("dp", "fsdp"), None),
            P(None, ("dp", "fsdp"), None),
            P(None, ("dp", "fsdp"), None),
            P(None, ("dp", "fsdp"), None),
            P(None, ("dp", "fsdp"), None),
            P(("dp", "fsdp"), None),
            P(("dp", "fsdp"), None),
            P(("dp", "fsdp"), None),
            P(),
            P(),
            P(),
            P(),
            P(),
            P(),
            P(None, ("dp", "fsdp"), None),
            P(None, ("dp", "fsdp"), None),
            P(None, ("dp", "fsdp"), None),
            P(("dp", "fsdp"), None),
        ),
        check_vma=False,
    )
```
